32 devices in a mesh: mem: 4 (over z), lev: 4 (over y, x), row: 2 (over core).
Axes of the slice: x: 2, y: 2, z: 4, core: 2. Of those that a mesh axis runs over, the one named last changes fastest.
Arguments:
- control: bfloat16 [8, 8, 64, 256], P('mem', 'lev', 'row'), may hold values from -6 to 6
- members: bfloat16 [8, 8, 16384], P('mem', None, ('row', 'lev')), may hold values from -3 to 3
- east_coef: float32 [8, 64, 256], P('lev', 'row'), may hold values from 0.12 to 0.245
- south_coef: float32 [8, 64, 256], P('lev', 'row'), may hold values from 0.12 to 0.245
- innovation: float32 [8, 16384], P(None, ('row', 'lev')), may hold values from -6 to 6
- huber_class: int32 [8, 16384], P(None, ('row', 'lev')), may hold values 0 or 1
- band: float32 [7, 8], replicated, may hold values from -0.4 to 0.4
- level_group_index: int32 [8], replicated, may hold values from 0 to 2, never falling along the last dimension, each value on 1 to 4 neighbouring positions
Outputs:
- gradient: float32 [8, 8, 64, 256], P('mem', 'lev', 'row')
The draws below stay inside these ranges and needn't reach their ends.
Inputs may be any that keep to these rules, and one draw needn't show every extreme that they name: `level_group_index`: never falls along the levels; every group 0 to 2 holds 1 to 4 consecutive levels.
All inputs are finite; a program needn't handle non-finite values. No bound on the sum of `huber_class` on one device may be relied on, other than what follows from the above.
Results may differ from the reference program's by a relative error of at most 0.0003.
Values sent between devices are 32-bit elements; how exact they have to be, the bound alone decides.
No kernel may reach another device: no remote copies, remote signals or barrier semaphores. Data moves between devices by JAX's collectives and lax.ppermute only.
A program may use at most 64 MiB of HBM per device.

```python
import math
import jax
import jax.numpy as jnp
import numpy as np
from jax import lax

LON = 256
PASSES = 8
MEMBERS = 8
LEV = 8
LAT = 64
CELLS = 16384
GROUPS = 3
GROUP_MOST = 4


def draw_control(key, part):
    cell_key = jax.random.fold_in(key, 11)
    zonal_key = jax.random.fold_in(key, 12)
    cell = 0.7 * jnp.clip(jax.random.normal(cell_key, (MEMBERS, LEV, LAT, LON), jnp.float32), -4.0, 4.0)
    zonal = 0.7 * jnp.clip(jax.random.normal(zonal_key, (MEMBERS, LEV, LAT, 1), jnp.float32), -4.0, 4.0)
    field = cell + zonal
    return field.astype(jnp.bfloat16)


def set_ends(entries, key, low, top_value):
    longest = entries.shape.index(max(entries.shape))
    spots = []
    for shift in (0, 1):
        where = [jax.random.randint(jax.random.fold_in(key, axis), (), 0, length) for axis, length in enumerate(entries.shape)]
        where[longest] = (where[longest] + shift) % entries.shape[longest]
        spots.append(tuple(where))
    return entries.at[spots[0]].set(low).at[spots[1]].set(top_value)


def level_of(stream_key, dims, split, low, top_value):
    def one(axis_at, parts):
        heights = jax.random.uniform(jax.random.fold_in(jax.random.fold_in(stream_key, 6), axis_at), (parts,), jnp.float32, low / len(split), top_value / len(split))
        return jnp.repeat(jnp.exp(heights), dims[axis_at] // parts).reshape((-1,) + (1,) * (len(dims) - axis_at - 1))

    loudness = one(*split[0])
    for cut in split[1:]:
        loudness = loudness * one(*cut)
    return loudness


def split_up(amount, total, reach, lean):
    weights = [(1 << 20) // math.isqrt(grade ** lean) + 1 for grade in range(2, amount + 1)]
    spare, given = total - reach - (amount - 1), [1] * (amount - 1)
    while spare > 0:
        free = [i for i in range(amount - 1) if given[i] < reach]
        mass, budget = sum([weights[i] for i in free]), spare
        for i in free:
            extra = min(reach - given[i], max(1, budget * weights[i] // mass), spare)
            given[i] = given[i] + extra
            spare = spare - extra
    return np.array([reach] + given)


def ragged(stream_key, amount, total, limit, lean):
    if amount == 2:
        one = jax.random.randint(stream_key, (), max(1, total - limit), min(limit, total - 1) + 1)
        return jnp.stack([one, total - one])
    lengths = jnp.asarray(split_up(amount, total, limit, lean), jnp.int32)
    twos = (amount - 1) // 2
    giver, receiver = lengths[1:1 + 2 * twos:2], lengths[2:2 + 2 * twos:2]
    margin = jnp.minimum(giver - 1, limit - receiver)
    moved = jax.random.randint(jax.random.fold_in(stream_key, 1), (twos,), 0, 1 << 20) % (margin + 1)
    lengths = lengths.at[1:1 + 2 * twos:2].set(giver - moved).at[2:2 + 2 * twos:2].set(receiver + moved)
    return lengths[jax.random.permutation(jax.random.fold_in(stream_key, 2), amount)]


def noise(own_key, dims, scale, bound, shards=(), held_as=jnp.bfloat16):
    factor_of = level_of(own_key, dims, shards, -0.22, 0.18) if shards else 1.0
    result = jax.random.normal(own_key, dims, jnp.float32) * scale * factor_of
    return jnp.minimum(jnp.maximum(result, -bound), bound).astype(held_as)


def setup_inputs(seed: int = 0) -> dict:
    streams_of = jax.random.split(jax.random.key(seed), 9)
    return {
        "control": draw_control(jax.random.fold_in(streams_of[8], 71), 0),
        "members": noise(streams_of[1], (MEMBERS, LEV, CELLS), 0.5, 3.0, ((0, 4), (2, 8))),
        "east_coef": jnp.clip(jnp.exp(math.log(0.245) - 0.7137665 * jax.random.uniform(streams_of[2], (LEV, LAT, LON), jnp.float32) ** level_of(streams_of[2], (LEV, LAT, LON), ((0, 4), (1, 2)), -0.2, 0.2)), 0.12, 0.245),
        "south_coef": jnp.clip(jnp.exp(math.log(0.245) - 0.7137665 * jax.random.uniform(streams_of[3], (LEV, LAT, LON), jnp.float32) ** level_of(streams_of[3], (LEV, LAT, LON), ((0, 4), (1, 2)), -0.2, 0.2)), 0.12, 0.245),
        "innovation": noise(streams_of[4], (LEV, CELLS), 1.0, 6.0, ((1, 8),), jnp.float32),
        "huber_class": set_ends((jax.random.randint(streams_of[5], (LEV, CELLS), 0, 2) < 1).astype(jnp.int32), jax.random.fold_in(streams_of[5], 1), 0, 1),
        "band": jnp.clip(jax.random.uniform(streams_of[6], (7, LEV), jnp.float32, -0.4, 0.4), -0.4, 0.4),
        "level_group_index": jnp.searchsorted(jnp.cumsum(ragged(streams_of[7], GROUPS, LEV, GROUP_MOST, 2)), jnp.arange(LEV), side="right").astype(jnp.int32),
    }


HUBER = 1.0


def smooth_rows(extended, east, south):
    center = extended[..., 1:-1, :]
    flux_x = east * (jnp.roll(center, -1, axis=-1) - center)
    flux_y = south * (extended[..., 1:, :] - extended[..., :-1, :])
    return center + flux_x - jnp.roll(flux_x, 1, axis=-1) + flux_y[..., 1:, :] - flux_y[..., :-1, :]


def pad_rows(field):
    widths = [(0, 0)] * (field.ndim - 2) + [(1, 1), (0, 0)]
    return jnp.pad(field, widths)


def vertical_level_matrix(band, level_group_index):
    count = band.shape[1]
    rows = jnp.arange(count)[:, None]
    cols = jnp.arange(count)[None, :]
    same = level_group_index[:, None] == level_group_index[None, :]
    matrix = jnp.zeros((count, count), jnp.float32)
    for offset in range(7):
        coef = band[offset] + (1.0 if offset == 3 else 0.0)
        hit = (cols == rows + offset - 3) & same
        matrix = matrix + jnp.where(hit, coef[:, None], jnp.float32(0.0))
    return matrix


def huber_weight(residual, classes):
    scale = HUBER / jnp.maximum(jnp.abs(residual), HUBER)
    return jnp.where(classes == 1, scale, jnp.float32(1.0)) * residual


def reference(control, members, east_coef, south_coef, innovation, huber_class, band, level_group_index):
    zero_row = jnp.zeros((LEV, 1, LON), jnp.float32)
    south_faces = jnp.concatenate([south_coef, zero_row], axis=1)
    vertical_matrix = vertical_level_matrix(band, level_group_index)

    def diffuse(field):
        for step in range(PASSES):
            field = smooth_rows(pad_rows(field), east_coef, south_faces)
        return field

    def forward_member(carry, pair):
        ctrl, ensemble_states = pair
        smoothed_field = diffuse(ctrl.astype(jnp.float32)).reshape(LEV, LAT * LON)
        filtered_field = jnp.dot(vertical_matrix, smoothed_field, precision=lax.Precision.HIGHEST)
        return carry + ensemble_states.astype(jnp.float32) * filtered_field, None

    increment, unused = lax.scan(forward_member, jnp.zeros((LEV, LAT * LON), jnp.float32), (control, members))
    weighted_field = huber_weight(increment - innovation, huber_class)

    def backward_member(pair):
        ctrl, ensemble_states = pair
        lifted_field = jnp.dot(vertical_matrix.T, ensemble_states.astype(jnp.float32) * weighted_field, precision=lax.Precision.HIGHEST)
        return ctrl.astype(jnp.float32) + diffuse(lifted_field.reshape(LEV, LAT, LON))

    return lax.map(backward_member, (control, members))
```

```python
import functools

import jax
import jax.numpy as jnp
from jax import lax
from jax.experimental import pallas as pl
from jax.experimental.pallas import tpu as pltpu
from jax.sharding import PartitionSpec as P

PASSES = 8
HUBER = 1.0
OFFSETS = 7
REACH = 3
LANES = 128

VMEM = pl.BlockSpec(memory_space=pltpu.VMEM)
SMEM = pl.BlockSpec(memory_space=pltpu.SMEM)


def vmem_array(*shape):
    return pltpu.VMEM(shape, jnp.float32)


def call(body, outs, operands, scratch=(), specs=None, out_specs=None, flops=0):
    total = sum(op.size * op.dtype.itemsize for op in operands)
    return pl.pallas_call(
        body,
        out_shape=outs,
        in_specs=specs or [VMEM] * len(operands),
        out_specs=out_specs or [VMEM] * len(outs),
        scratch_shapes=list(scratch),
        compiler_params=pltpu.CompilerParams(vmem_limit_bytes=32 * 1024 * 1024),
        cost_estimate=pl.CostEstimate(flops=flops, bytes_accessed=2 * total, transcendentals=0),
    )(*operands)


def resident(array):
    return pltpu.with_memory_space_constraint(array, pltpu.VMEM)


def exchange(chunks, axis):
    count = len(chunks)
    received = [chunks[0]]
    for step in range(1, count):
        received.append(lax.ppermute(chunks[step], axis, [(i, i ^ step) for i in range(count)]))
    return received


def swap_edges(edges, axis):
    count = lax.axis_size(axis)
    if len(edges) == 1:
        return [lax.ppermute(edges[0], axis, [(0, 1), (1, 0)])]
    head, tail = edges
    south = lax.ppermute(head, axis, [(i + 1, i) for i in range(count - 1)])
    north = lax.ppermute(tail, axis, [(i, i + 1) for i in range(count - 1)])
    return [south, north]


def write_edges(field, first, send_refs, base):
    head = field[:, :PASSES, :]
    tail = field[:, field.shape[1] - PASSES :, :]
    block = slice(base, base + field.shape[0])
    if len(send_refs) == 1:
        send_refs[0][block] = jnp.where(first, tail, head)
    else:
        send_refs[0][block] = head
        send_refs[1][block] = tail


def pack_body(control_ref, east_ref, south_ref, field_ref, east_out, south_out, *send_refs):
    first = lax.axis_index("row") == 0
    fields = field_ref.shape[0]
    levels = east_ref.shape[0]
    field = control_ref[...].astype(jnp.float32).reshape(field_ref.shape)
    field_ref[...] = field
    write_edges(field, first, send_refs, 0)
    for coef_ref, out_ref, base in ((east_ref, east_out, fields), (south_ref, south_out, fields + levels)):
        coef = coef_ref[...]
        out_ref[...] = coef
        write_edges(coef, first, send_refs, base)


def columns_body(members_ref, innovation_ref, huber_ref, band_ref, group_ref, members_out, innovation_out, huber_out, matrix_out):
    count, levels, rows, lon = members_out.shape
    for row in range(rows):
        cells = slice(row * lon, (row + 1) * lon)
        for member in range(count):
            members_out[member, :, row, :] = members_ref[member, :, cells].astype(jnp.float32)
        innovation_out[:, row, :] = innovation_ref[:, cells]
        huber_out[:, row, :] = huber_ref[:, cells].astype(jnp.float32)
    for level in range(levels):
        for offset in range(OFFSETS):
            other = level + offset - REACH
            if 0 <= other < levels:
                entry = band_ref[offset, level] + jnp.float32(1.0 if offset == REACH else 0.0)
                entry = jnp.where(group_ref[level] == group_ref[other], entry, jnp.float32(0.0))
                matrix_out[level, offset] = jnp.full(matrix_out.shape[2:], entry, jnp.float32)


def run_passes(field_ref, center_ref, east_ref, west_ref, south_ref, north_ref):
    fields, rows, lon = field_ref.shape
    levels = center_ref.shape[0]

    def one_pass(_, carry):
        for level in range(levels):
            center, east, west = center_ref[level], east_ref[level], west_ref[level]
            south, north = south_ref[level], north_ref[level]
            for index in range(level, fields, levels):
                u = field_ref[index]
                total = center * u
                total = total + east * pltpu.roll(u, lon - 1, 1)
                total = total + west * pltpu.roll(u, 1, 1)
                total = total + south * pltpu.roll(u, rows - 1, 0)
                field_ref[index] = total + north * pltpu.roll(u, 1, 0)
        return carry

    lax.fori_loop(0, PASSES, one_pass, 0)


def forward_body(halos, field_ref, east_ref, south_ref, *refs):
    halo_refs, refs = refs[:halos], refs[halos:]
    chunks = len(refs) - 7
    chunk_refs, refs = refs[:chunks], refs[chunks:]
    center_out, east_out, west_out, south_out, north_out, work, sorted_ref = refs
    fields, own, lon = field_ref.shape
    levels = east_ref.shape[0]
    rows = work.shape[1]
    row_at, row_count = lax.axis_index("row"), lax.axis_size("row")
    lev_at = lax.axis_index("lev")

    work[:, :own, :] = field_ref[...]
    east_out[:, :own, :] = east_ref[...]
    north_out[:, :own, :] = south_ref[...]
    for halo, halo_ref in enumerate(halo_refs):
        at = slice(own + halo * PASSES, own + (halo + 1) * PASSES)
        work[:, at, :] = halo_ref[:fields]
        east_out[:, at, :] = halo_ref[fields : fields + levels]
        north_out[:, at, :] = halo_ref[fields + levels : fields + 2 * levels]
    place = lax.broadcasted_iota(jnp.int32, (rows, lon), 0)
    top = (place == 0) & (row_at == 0)
    bottom = (place == own - 1) & (row_at == row_count - 1)
    for level in range(levels):
        east = east_out[level]
        west = pltpu.roll(east, 1, 1)
        face = north_out[level]
        south = jnp.where(bottom, 0.0, pltpu.roll(face, rows - 1, 0))
        west_out[level] = west
        south_out[level] = south
        north_out[level] = jnp.where(top, 0.0, face)
        center_out[level] = 1.0 - east - west - south - face
    run_passes(work, center_out, east_out, west_out, south_out, north_out)
    part = own // chunks
    for dest in range(chunks):
        sorted_ref[dest] = work[:, dest * part : (dest + 1) * part, :]
    for step, chunk_ref in enumerate(chunk_refs):
        chunk_ref[...] = sorted_ref[lax.bitwise_xor(lev_at, step)]


def filter_body(chunks, *refs):
    chunk_refs = refs[:chunks]
    members_ref, matrix_ref, partial_ref, columns = refs[chunks:]
    count, levels, rows, lon = members_ref.shape
    held = levels // chunks
    lev_at = lax.axis_index("lev")
    for step, chunk_ref in enumerate(chunk_refs):
        columns[lax.bitwise_xor(lev_at, step)] = chunk_ref[...]
    for start in range(0, lon, LANES):
        lanes = slice(start, start + LANES)
        for level in range(levels):
            total = None
            for member in range(count):
                filtered = None
                for offset in range(OFFSETS):
                    other = level + offset - REACH
                    if 0 <= other < levels:
                        cells = columns[other // held, member * held + other % held, :, lanes]
                        term = matrix_ref[level, offset, :rows] * cells
                        filtered = term if filtered is None else filtered + term
                filtered = members_ref[member, level, :, lanes] * filtered
                total = filtered if total is None else total + filtered
            partial_ref[level, :, lanes] = total


def lift_body(chunks, parts, *refs):
    part_refs = refs[:parts]
    innovation_ref, huber_ref, members_ref, matrix_ref = refs[parts : parts + 4]
    chunk_refs = refs[parts + 4 : parts + 4 + chunks]
    weighted_ref, sorted_ref = refs[parts + 4 + chunks :]
    count, levels, rows, lon = members_ref.shape
    held = levels // chunks
    lev_at = lax.axis_index("lev")
    increment = part_refs[0][...]
    for part_ref in part_refs[1:]:
        increment = increment + part_ref[...]
    residual = increment - innovation_ref[...]
    scale = HUBER / jnp.maximum(jnp.abs(residual), HUBER)
    weighted_ref[...] = jnp.where(huber_ref[...] == 1.0, scale, 1.0) * residual
    for start in range(0, lon, LANES):
        lanes = slice(start, start + LANES)
        for member in range(count):
            for level in range(levels):
                lifted = None
                for offset in range(OFFSETS):
                    other = level - offset + REACH
                    if 0 <= other < levels:
                        adjoint = members_ref[member, other, :, lanes] * weighted_ref[other, :, lanes]
                        term = matrix_ref[other, offset, :rows] * adjoint
                        lifted = term if lifted is None else lifted + term
                sorted_ref[level // held, member * held + level % held, :, lanes] = lifted
    for step, chunk_ref in enumerate(chunk_refs):
        chunk_ref[...] = sorted_ref[lax.bitwise_xor(lev_at, step)]


def gather_body(chunks, *refs):
    chunk_refs = refs[:chunks]
    field_ref, refs = refs[chunks], refs[chunks + 1 :]
    send_refs, sorted_ref = refs[:-1], refs[-1]
    lev_at = lax.axis_index("lev")
    first = lax.axis_index("row") == 0
    part = field_ref.shape[1] // chunks
    for step, chunk_ref in enumerate(chunk_refs):
        sorted_ref[lax.bitwise_xor(lev_at, step)] = chunk_ref[...]
    for source in range(chunks):
        field_ref[:, source * part : (source + 1) * part, :] = sorted_ref[source]
    write_edges(field_ref, first, send_refs, 0)


def backward_body(halos, control_ref, field_ref, center_ref, east_ref, west_ref, south_ref, north_ref, *refs):
    halo_refs = refs[:halos]
    gradient_ref, work = refs[halos:]
    fields, own, lon = field_ref.shape
    work[:, :own, :] = field_ref[...]
    for halo, halo_ref in enumerate(halo_refs):
        work[:, own + halo * PASSES : own + (halo + 1) * PASSES, :] = halo_ref[...]
    run_passes(work, center_ref, east_ref, west_ref, south_ref, north_ref)
    gradient_ref[...] = control_ref[...].astype(jnp.float32) + work[:, :own, :].reshape(gradient_ref.shape)


def per_device(control, members, east_coef, south_coef, innovation, huber_class, band, level_group_index):
    count, held, own, lon = control.shape
    levels = members.shape[1]
    chunks, parts, row_count = (lax.axis_size(axis) for axis in ("lev", "mem", "row"))
    part = own // chunks
    fields = count * held
    halos = 1 if row_count == 2 else 2
    rows = own + halos * PASSES
    coefs = vmem_array(held, rows, lon)

    packed = call(
        pack_body,
        [vmem_array(fields, own, lon), vmem_array(held, own, lon), vmem_array(held, own, lon)]
        + [vmem_array(fields + 2 * held, PASSES, lon)] * halos,
        [control, east_coef, south_coef],
    )
    field, east, south = packed[:3]
    halo = swap_edges(packed[3:], "row")
    members_rows, innovation_rows, huber_rows, matrix = call(
        columns_body,
        [
            vmem_array(count, levels, part, lon),
            vmem_array(levels, part, lon),
            vmem_array(levels, part, lon),
            vmem_array(levels, OFFSETS, 8, LANES),
        ],
        [members, innovation, huber_class, band, level_group_index],
        specs=[VMEM, VMEM, VMEM, SMEM, SMEM],
    )
    chunk = vmem_array(fields, part, lon)
    ordered = vmem_array(chunks, fields, part, lon)
    work = vmem_array(fields, rows, lon)
    results = call(
        functools.partial(forward_body, halos),
        [chunk] * chunks + [coefs] * 5,
        [resident(x) for x in (field, east, south, *halo)],
        [work, ordered],
    )
    stencil = results[chunks:]
    columns = exchange(results[:chunks], "lev")
    (partial,) = call(
        functools.partial(filter_body, chunks),
        [vmem_array(levels, part, lon)],
        [resident(x) for x in (*columns, members_rows, matrix)],
        [ordered],
    )
    partials = exchange([partial] * parts, "mem")
    lifted = call(
        functools.partial(lift_body, chunks, parts),
        [chunk] * chunks,
        [resident(x) for x in (*partials, innovation_rows, huber_rows, members_rows, matrix)],
        [vmem_array(levels, part, lon), ordered],
    )
    returned = exchange(lifted, "lev")
    gathered = call(
        functools.partial(gather_body, chunks),
        [vmem_array(fields, own, lon)] + [vmem_array(fields, PASSES, lon)] * halos,
        [resident(x) for x in returned],
        [ordered],
    )
    halo = swap_edges(gathered[1:], "row")
    (gradient,) = call(
        functools.partial(backward_body, halos),
        [jax.ShapeDtypeStruct(control.shape, jnp.float32)],
        [control] + [resident(x) for x in (gathered[0], *stencil, *halo)],
        [work],
    )
    return gradient


def solution(mesh):
    placed = (
        P("mem", "lev", "row", None),
        P("mem", None, ("row", "lev")),
        P("lev", "row", None),
        P("lev", "row", None),
        P(None, ("row", "lev")),
        P(None, ("row", "lev")),
        P(),
        P(),
    )
    return jax.shard_map(
        per_device,
        mesh=mesh,
        in_specs=placed,
        out_specs=P("mem", "lev", "row", None),
        check_vma=False,
    )
```

```python
import functools

import jax
import jax.numpy as jnp
from jax import lax
from jax.experimental import pallas as pl
from jax.experimental.pallas import tpu as pltpu
from jax.sharding import PartitionSpec as P

PASSES = 8
HUBER = 1.0
REACH = 3
LANES = 128
TILE = 8
HALVES = 2
HELD = 2
FIELDS = 4

VMEM = pl.BlockSpec(memory_space=pltpu.VMEM)
SMEM = pl.BlockSpec(memory_space=pltpu.SMEM)
HBM = pl.BlockSpec(memory_space=pltpu.HBM)


def planes(count):
    return pltpu.VMEM((count * TILE, LANES), jnp.float32)


def call(body, outs, operands, scratch=(), specs=None, out_specs=None, flops=0):
    total = sum(op.size * op.dtype.itemsize for op in operands)
    return pl.pallas_call(
        body,
        out_shape=outs,
        in_specs=specs or [VMEM] * len(operands),
        out_specs=out_specs or [VMEM] * len(outs),
        scratch_shapes=list(scratch),
        compiler_params=pltpu.CompilerParams(vmem_limit_bytes=32 * 1024 * 1024),
        cost_estimate=pl.CostEstimate(flops=flops, bytes_accessed=2 * total, transcendentals=0),
    )(*operands)


def resident(*arrays):
    return [pltpu.with_memory_space_constraint(array, pltpu.VMEM) for array in arrays]


def remote(*arrays):
    return [pltpu.with_memory_space_constraint(array, pltpu.HBM) for array in arrays]


def exchange(chunks, axis):
    count = len(chunks)
    received = [chunks[0]]
    for step in range(1, count):
        received.append(lax.ppermute(chunks[step], axis, [(i, i ^ step) for i in range(count)]))
    return received


def swap_edges(edges, axis):
    count = lax.axis_size(axis)
    if len(edges) == 1:
        return [lax.ppermute(edges[0], axis, [(0, 1), (1, 0)])]
    head, tail = edges
    south = lax.ppermute(head, axis, [(i + 1, i) for i in range(count - 1)])
    north = lax.ppermute(tail, axis, [(i, i + 1) for i in range(count - 1)])
    return [south, north]


def tile(ref, row):
    return ref[row * TILE : (row + 1) * TILE, :]


def set_tile(ref, row, value):
    ref[row * TILE : (row + 1) * TILE, :] = value


def block(first_row, rows):
    return pl.ds(pl.multiple_of(first_row * TILE, TILE), rows * TILE)


def spread(ref, row, sublane, values):
    ref[pl.ds(row * TILE + sublane, values.shape[0], stride=TILE), :] = values


def places():
    return lax.broadcasted_iota(jnp.int32, (TILE, LANES), 0)


def east_west(value):
    lane = lax.broadcasted_iota(jnp.int32, (TILE, LANES), 1)
    other = pltpu.roll(value, FIELDS, 0)
    east = pltpu.roll(jnp.where(lane == 0, other, value), LANES - 1, 1)
    west = pltpu.roll(jnp.where(lane == LANES - 1, other, value), 1, 1)
    return east, west


def west_of(value):
    lane = lax.broadcasted_iota(jnp.int32, (TILE, LANES), 1)
    return pltpu.roll(jnp.where(lane == LANES - 1, pltpu.roll(value, FIELDS, 0), value), 1, 1)


def halves():
    return [(half, slice(half * LANES, (half + 1) * LANES)) for half in range(HALVES)]


def pack_body(control_hbm, east_hbm, south_hbm, control_ref, east_ref, south_ref, *refs):
    send_refs, semaphores = refs[:-1], refs[-1]
    copies = [
        pltpu.make_async_copy(source, target, semaphores.at[index])
        for index, (source, target) in enumerate(
            ((control_hbm, control_ref), (east_hbm, east_ref), (south_hbm, south_ref))
        )
    ]
    for copy in copies:
        copy.start()
    for copy in copies:
        copy.wait()
    own = control_ref.shape[2]
    first = lax.axis_index("row") == 0

    def edges(load):
        head = load(slice(0, 2 * PASSES))[:PASSES].astype(jnp.float32)
        tail = load(slice(own - 2 * PASSES, own))[PASSES:].astype(jnp.float32)
        return [jnp.where(first, tail, head)] if len(send_refs) == 1 else [head, tail]

    for half, lanes in halves():
        for field in range(FIELDS):
            member, level = divmod(field, HELD)
            at = half * FIELDS + field
            values = edges(lambda rows: control_ref[member, level, rows, lanes])
            for send_ref, value in zip(send_refs, values):
                spread(send_ref, 0, at, value)
            for kind, coef_ref in enumerate((east_ref, south_ref)):
                values = edges(lambda rows: coef_ref[level, rows, lanes])
                for send_ref, value in zip(send_refs, values):
                    spread(send_ref, (kind + 1) * PASSES, at, value)


def prepare_body(control_ref, east_ref, south_ref, field_out, center_out, east_out, west_out, south_out, north_out):
    own = control_ref.shape[2]
    first = lax.axis_index("row") == 0
    for half, lanes in halves():
        for field in range(FIELDS):
            member, level = divmod(field, HELD)
            at = half * FIELDS + field
            spread(field_out, 0, at, control_ref[member, level, :, lanes].astype(jnp.float32))
            spread(east_out, 0, at, east_ref[level, :, lanes])
            spread(north_out, 0, at, south_ref[level, :, lanes])
    for row in range(own):
        east, face = tile(east_out, row), tile(north_out, row)
        west = west_of(east)
        set_tile(west_out, row, west)
        south = tile(north_out, row + 1) if row + 1 < own else jnp.zeros_like(face)
        set_tile(south_out, row, south)
        set_tile(center_out, row, 1.0 - east - west - south - face)
    set_tile(north_out, 0, jnp.where(first, 0.0, tile(north_out, 0)))


def finish_stencil(halo_refs, own_refs, tail_refs, own):
    _, east_own, west_own, _, north_own = own_refs
    center_tail, east_tail, west_tail, south_tail, north_tail = tail_refs
    last = lax.axis_index("row") == lax.axis_size("row") - 1
    east, west = [tile(east_own, own - 1)], [tile(west_own, own - 1)]
    faces = [tile(north_own, own - 1)]
    for halo_ref in halo_refs:
        for row in range(PASSES):
            east.append(tile(halo_ref, PASSES + row))
            west.append(west_of(east[-1]))
            faces.append(tile(halo_ref, 2 * PASSES + row))
    for row, face in enumerate(faces):
        if row == 0:
            south = jnp.where(last, 0.0, faces[1])
        else:
            south = faces[row + 1] if row + 1 < len(faces) else tile(north_own, 0)
        set_tile(east_tail, row, east[row])
        set_tile(west_tail, row, west[row])
        set_tile(south_tail, row, south)
        set_tile(north_tail, row, face)
        set_tile(center_tail, row, 1.0 - east[row] - west[row] - south - face)


def run_passes(values, own_refs, tail_refs, own):
    rows = len(values)

    def coefficient(kind, row):
        return tile(own_refs[kind], row) if row < own - 1 else tile(tail_refs[kind], row - own + 1)

    def one_pass(_, now):
        after = []
        for row, value in enumerate(now):
            east, west = east_west(value)
            total = coefficient(0, row) * value
            total = total + coefficient(1, row) * east
            total = total + coefficient(2, row) * west
            total = total + coefficient(3, row) * now[(row + 1) % rows]
            after.append(total + coefficient(4, row) * now[row - 1])
        return tuple(after)

    return lax.fori_loop(0, PASSES, one_pass, tuple(values))


def forward_body(halos, field_ref, *refs):
    own_refs, halo_refs, refs = refs[:5], refs[5 : 5 + halos], refs[5 + halos :]
    tail_refs, chunk_refs, sorted_ref = refs[:5], refs[5:-1], refs[-1]
    own = field_ref.shape[0] // TILE
    lev_at = lax.axis_index("lev")
    finish_stencil(halo_refs, own_refs, tail_refs, own)
    values = [tile(field_ref, row) for row in range(own)]
    values += [tile(halo_ref, row) for halo_ref in halo_refs for row in range(PASSES)]
    values = run_passes(values, own_refs, tail_refs, own)
    for row in range(own):
        set_tile(sorted_ref, row, values[row])
    part = own // len(chunk_refs)
    for step, chunk_ref in enumerate(chunk_refs):
        chunk_ref[...] = sorted_ref[block(lax.bitwise_xor(lev_at, step) * part, part), :]


def matrix_terms(groups):
    return [
        (group, other, cross)
        for group in range(groups)
        for other in range(max(0, group - 2), min(groups, group + 3))
        for cross in range(2)
        if abs(group - other) < 2 or cross
    ]


def swap_levels(value, sublane):
    return jnp.where(sublane % HELD == 0, pltpu.roll(value, TILE - 1, 0), pltpu.roll(value, 1, 0))


def columns_body(members_ref, innovation_ref, huber_ref, band_ref, group_ref, *refs):
    members_out, innovation_out, huber_out, matrix_out, transposed_out, levels_ref = refs
    count, levels, cells = members_ref.shape
    groups, lon = levels // HELD, HALVES * LANES
    rows, packed = cells // lon, levels // FIELDS
    sublane = places()
    for member in range(count):
        for row in range(rows):
            for half in range(HALVES):
                lanes = slice(row * lon + half * LANES, row * lon + (half + 1) * LANES)
                start = ((member * rows + row) * HALVES + half) * levels
                levels_ref[start : start + levels, :] = members_ref[member, :, lanes].astype(jnp.float32)
                for level in range(HELD):
                    at = half * FIELDS + member * HELD + level
                    spread(members_out, row * groups, at, levels_ref[pl.ds(start + level, groups, stride=HELD), :])
    for row in range(rows):
        for half in range(HALVES):
            lanes = slice(row * lon + half * LANES, row * lon + (half + 1) * LANES)
            for pack in range(packed):
                source = slice(pack * FIELDS, (pack + 1) * FIELDS)
                start = (row * packed + pack) * TILE + half * FIELDS
                innovation_out[start : start + FIELDS, :] = innovation_ref[source, lanes]
                huber_out[start : start + FIELDS, :] = huber_ref[source, lanes].astype(jnp.float32)

    def entry(level, other):
        offset = other - level + REACH
        if not 0 <= offset < 2 * REACH + 1:
            return jnp.float32(0.0)
        value = band_ref[offset, level] + jnp.float32(1.0 if offset == REACH else 0.0)
        return jnp.where(group_ref[level] == group_ref[other], value, jnp.float32(0.0))

    for slot, (group, other, cross) in enumerate(matrix_terms(groups)):
        pairs = [(group * HELD + level, other * HELD + (level ^ cross)) for level in range(HELD)]
        even, odd = (entry(a, b) for a, b in pairs)
        set_tile(matrix_out, slot, jnp.where(sublane % HELD == 0, even, odd))
        even, odd = (entry(b, a) for a, b in pairs)
        set_tile(transposed_out, slot, jnp.where(sublane % HELD == 0, even, odd))


def apply_matrix(matrix_ref, values, sublane):
    crossed = [swap_levels(value, sublane) for value in values]
    totals = [None] * len(values)
    for slot, (group, other, cross) in enumerate(matrix_terms(len(values))):
        term = tile(matrix_ref, slot) * (crossed if cross else values)[other]
        totals[group] = term if totals[group] is None else totals[group] + term
    return totals


def filter_body(chunks, *refs):
    chunk_refs = refs[:chunks]
    members_ref, matrix_ref, partial_ref, columns = refs[chunks:]
    rows = chunk_refs[0].shape[0] // TILE
    lev_at = lax.axis_index("lev")
    sublane = places()
    first_member = sublane % FIELDS < HELD
    for step, chunk_ref in enumerate(chunk_refs):
        columns[block(lax.bitwise_xor(lev_at, step) * rows, rows), :] = chunk_ref[...]
    for row in range(rows):
        filtered = apply_matrix(matrix_ref, [tile(columns, group * rows + row) for group in range(chunks)], sublane)
        terms = [tile(members_ref, row * chunks + group) * value for group, value in enumerate(filtered)]
        for pack in range(chunks // 2):
            lower, upper = terms[2 * pack], terms[2 * pack + 1]
            total = jnp.where(first_member, lower, upper)
            total = total + jnp.where(first_member, pltpu.roll(lower, TILE - HELD, 0), pltpu.roll(upper, HELD, 0))
            set_tile(partial_ref, row * (chunks // 2) + pack, total)


def lift_body(chunks, parts, *refs):
    part_refs, refs = refs[:parts], refs[parts:]
    innovation_ref, huber_ref, members_ref, transposed_ref = refs[:4]
    chunk_refs, (weighted_ref, sorted_ref) = refs[4 : 4 + chunks], refs[4 + chunks :]
    rows = chunk_refs[0].shape[0] // TILE
    lev_at = lax.axis_index("lev")
    sublane = places()
    first_member = sublane % FIELDS < HELD
    increment = part_refs[0][...]
    for part_ref in part_refs[1:]:
        increment = increment + part_ref[...]
    residual = increment - innovation_ref[...]
    scale = HUBER / jnp.maximum(jnp.abs(residual), HUBER)
    weighted_ref[...] = jnp.where(huber_ref[...] == 1.0, scale, 1.0) * residual
    for row in range(rows):
        adjoint = []
        for pack in range(chunks // 2):
            weighted = tile(weighted_ref, row * (chunks // 2) + pack)
            lower = jnp.where(first_member, weighted, pltpu.roll(weighted, HELD, 0))
            upper = jnp.where(first_member, pltpu.roll(weighted, TILE - HELD, 0), weighted)
            for value in (lower, upper):
                adjoint.append(value * tile(members_ref, row * chunks + len(adjoint)))
        for group, value in enumerate(apply_matrix(transposed_ref, adjoint, sublane)):
            set_tile(sorted_ref, group * rows + row, value)
    for step, chunk_ref in enumerate(chunk_refs):
        chunk_ref[...] = sorted_ref[block(lax.bitwise_xor(lev_at, step) * rows, rows), :]


def gather_body(chunks, *refs):
    chunk_refs, field_ref, send_refs = refs[:chunks], refs[chunks], refs[chunks + 1 :]
    lev_at = lax.axis_index("lev")
    first = lax.axis_index("row") == 0
    rows = chunk_refs[0].shape[0] // TILE
    own = rows * chunks
    for step, chunk_ref in enumerate(chunk_refs):
        field_ref[block(lax.bitwise_xor(lev_at, step) * rows, rows), :] = chunk_ref[...]
    if len(send_refs) == 1:
        send_refs[0][...] = field_ref[block(jnp.where(first, own - PASSES, 0), PASSES), :]
    else:
        send_refs[0][...] = field_ref[: PASSES * TILE, :]
        send_refs[1][...] = field_ref[(own - PASSES) * TILE :, :]


def backward_body(halos, control_ref, field_ref, *refs):
    own_refs, tail_refs, halo_refs = refs[:5], refs[5:10], refs[10 : 10 + halos]
    gradient_hbm, result_ref, gradient_ref, semaphores = refs[10 + halos :]
    own = field_ref.shape[0] // TILE
    values = [tile(field_ref, row) for row in range(own)]
    values += [tile(halo_ref, row) for halo_ref in halo_refs for row in range(PASSES)]
    values = run_passes(values, own_refs, tail_refs, own)
    for row in range(own):
        set_tile(result_ref, row, values[row])
    copies = []
    for field in range(FIELDS):
        member, level = divmod(field, HELD)
        for half, lanes in halves():
            result = result_ref[pl.ds(half * FIELDS + field, own, stride=TILE), :]
            gradient_ref[member, level, :, lanes] = control_ref[member, level, :, lanes].astype(jnp.float32) + result
        copy = pltpu.make_async_copy(
            gradient_ref.at[member, level], gradient_hbm.at[member, level], semaphores.at[field]
        )
        copy.start()
        copies.append(copy)
    for copy in copies:
        copy.wait()


def per_device(control, members, east_coef, south_coef, innovation, huber_class, band, level_group_index):
    count, held, own, lon = control.shape
    levels, cells = members.shape[1:]
    chunks, parts, row_count = (lax.axis_size(axis) for axis in ("lev", "mem", "row"))
    assert (count * held, held, lon) == (FIELDS, HELD, HALVES * LANES)
    part = own // chunks
    halos = 1 if row_count == 2 else 2
    tail = 1 + halos * PASSES
    terms = len(matrix_terms(chunks))
    packed = part * levels // FIELDS

    control_near, east_near, south_near, *edges = call(
        pack_body,
        [pltpu.VMEM(x.shape, x.dtype) for x in (control, east_coef, south_coef)] + [planes(3 * PASSES)] * halos,
        remote(control, east_coef, south_coef),
        [pltpu.SemaphoreType.DMA((3,))],
        specs=[HBM] * 3,
    )
    halo = swap_edges(edges, "row")
    field, *own_stencil = call(
        prepare_body, [planes(own)] * 6, resident(control_near, east_near, south_near)
    )
    members_planes, innovation_planes, huber_planes, matrix, transposed = call(
        columns_body,
        [planes(part * chunks), planes(packed), planes(packed), planes(terms), planes(terms)],
        [members, innovation, huber_class, band, level_group_index],
        [planes(part * chunks)],
        specs=[VMEM, VMEM, VMEM, SMEM, SMEM],
    )
    results = call(
        functools.partial(forward_body, halos),
        [planes(tail)] * 5 + [planes(part)] * chunks,
        resident(field, *own_stencil, *halo),
        [planes(own)],
    )
    tail_stencil = results[:5]
    columns = exchange(results[5:], "lev")
    (partial,) = call(
        functools.partial(filter_body, chunks),
        [planes(packed)],
        resident(*columns, members_planes, matrix),
        [planes(part * chunks)],
    )
    partials = exchange([partial] * parts, "mem")
    lifted = call(
        functools.partial(lift_body, chunks, parts),
        [planes(part)] * chunks,
        resident(*partials, innovation_planes, huber_planes, members_planes, transposed),
        [planes(packed), planes(part * chunks)],
    )
    returned = exchange(lifted, "lev")
    gathered, *edges = call(
        functools.partial(gather_body, chunks),
        [planes(own)] + [planes(PASSES)] * halos,
        resident(*returned),
    )
    halo = swap_edges(edges, "row")
    (gradient,) = call(
        functools.partial(backward_body, halos),
        [jax.ShapeDtypeStruct(control.shape, jnp.float32)],
        resident(control_near, gathered, *own_stencil, *tail_stencil, *halo),
        [planes(own), pltpu.VMEM(control.shape, jnp.float32), pltpu.SemaphoreType.DMA((FIELDS,))],
        out_specs=[HBM],
    )
    return gradient


def solution(mesh):
    placed = (
        P("mem", "lev", "row", None),
        P("mem", None, ("row", "lev")),
        P("lev", "row", None),
        P("lev", "row", None),
        P(None, ("row", "lev")),
        P(None, ("row", "lev")),
        P(),
        P(),
    )
    return jax.shard_map(
        per_device,
        mesh=mesh,
        in_specs=placed,
        out_specs=P("mem", "lev", "row", None),
        check_vma=False,
    )
```

```python
import functools

import jax
import jax.numpy as jnp
from jax import lax
from jax.experimental import pallas as pl
from jax.experimental.pallas import tpu as pltpu
from jax.sharding import PartitionSpec as P

PASSES = 8
HUBER = 1.0
REACH = 3
LANES = 128
TILE = 8
HALVES = 2
HELD = 2
FIELDS = 4

VMEM = pl.BlockSpec(memory_space=pltpu.VMEM)
SMEM = pl.BlockSpec(memory_space=pltpu.SMEM)
HBM = pl.BlockSpec(memory_space=pltpu.HBM)


def planes(count):
    return pltpu.VMEM((count * TILE, LANES), jnp.float32)


def call(body, outs, operands, scratch=(), specs=None, out_specs=None, flops=0):
    total = sum(op.size * op.dtype.itemsize for op in operands)
    return pl.pallas_call(
        body,
        out_shape=outs,
        in_specs=specs or [VMEM] * len(operands),
        out_specs=out_specs or [VMEM] * len(outs),
        scratch_shapes=list(scratch),
        compiler_params=pltpu.CompilerParams(vmem_limit_bytes=32 * 1024 * 1024),
        cost_estimate=pl.CostEstimate(flops=flops, bytes_accessed=2 * total, transcendentals=0),
    )(*operands)


def resident(*arrays):
    return [pltpu.with_memory_space_constraint(array, pltpu.VMEM) for array in arrays]


def remote(*arrays):
    return [pltpu.with_memory_space_constraint(array, pltpu.HBM) for array in arrays]


def exchange(chunks, axis):
    count = len(chunks)
    received = list(chunks)
    for step in reversed(range(1, count)):
        received[step] = lax.ppermute(chunks[step], axis, [(i, i ^ step) for i in range(count)])
    return received


def swap_edges(edges, axis):
    count = lax.axis_size(axis)
    if len(edges) == 1:
        return [lax.ppermute(edges[0], axis, [(0, 1), (1, 0)])]
    head, tail = edges
    south = lax.ppermute(head, axis, [(i + 1, i) for i in range(count - 1)])
    north = lax.ppermute(tail, axis, [(i, i + 1) for i in range(count - 1)])
    return [south, north]


def tile(ref, row):
    return ref[row * TILE : (row + 1) * TILE, :]


def set_tile(ref, row, value):
    ref[row * TILE : (row + 1) * TILE, :] = value


def block(first_row, rows):
    return pl.ds(pl.multiple_of(first_row * TILE, TILE), rows * TILE)


def spread(ref, row, sublane, values):
    ref[pl.ds(row * TILE + sublane, values.shape[0], stride=TILE), :] = values


def places():
    return lax.broadcasted_iota(jnp.int32, (TILE, LANES), 0)


def east_west(value):
    lane = lax.broadcasted_iota(jnp.int32, (TILE, LANES), 1)
    other = pltpu.roll(value, FIELDS, 0)
    east = pltpu.roll(jnp.where(lane == 0, other, value), LANES - 1, 1)
    west = pltpu.roll(jnp.where(lane == LANES - 1, other, value), 1, 1)
    return east, west


def west_of(value):
    lane = lax.broadcasted_iota(jnp.int32, (TILE, LANES), 1)
    return pltpu.roll(jnp.where(lane == LANES - 1, pltpu.roll(value, FIELDS, 0), value), 1, 1)


def halves():
    return [(half, slice(half * LANES, (half + 1) * LANES)) for half in range(HALVES)]


def pack_body(control_hbm, east_hbm, south_hbm, control_ref, east_ref, south_ref, *refs):
    send_refs, semaphores = refs[:-1], refs[-1]
    copies = [
        pltpu.make_async_copy(source, target, semaphores.at[index])
        for index, (source, target) in enumerate(
            ((control_hbm, control_ref), (east_hbm, east_ref), (south_hbm, south_ref))
        )
    ]
    for copy in copies:
        copy.start()
    for copy in copies:
        copy.wait()
    own = control_ref.shape[2]
    first = lax.axis_index("row") == 0

    def edges(load):
        head = load(slice(0, 2 * PASSES))[:PASSES].astype(jnp.float32)
        tail = load(slice(own - 2 * PASSES, own))[PASSES:].astype(jnp.float32)
        return [jnp.where(first, tail, head)] if len(send_refs) == 1 else [head, tail]

    for half, lanes in halves():
        for field in range(FIELDS):
            member, level = divmod(field, HELD)
            at = half * FIELDS + field
            values = edges(lambda rows: control_ref[member, level, rows, lanes])
            for send_ref, value in zip(send_refs, values):
                spread(send_ref, 0, at, value)
            for kind, coef_ref in enumerate((east_ref, south_ref)):
                values = edges(lambda rows: coef_ref[level, rows, lanes])
                for send_ref, value in zip(send_refs, values):
                    spread(send_ref, (kind + 1) * PASSES, at, value)


def prepare_body(control_ref, east_ref, south_ref, field_out, center_out, east_out, west_out, south_out, north_out):
    own = control_ref.shape[2]
    first = lax.axis_index("row") == 0
    for half, lanes in halves():
        for field in range(FIELDS):
            member, level = divmod(field, HELD)
            at = half * FIELDS + field
            spread(field_out, 0, at, control_ref[member, level, :, lanes].astype(jnp.float32))
            spread(east_out, 0, at, east_ref[level, :, lanes])
            spread(north_out, 0, at, south_ref[level, :, lanes])
    for row in range(own):
        east, face = tile(east_out, row), tile(north_out, row)
        west = west_of(east)
        set_tile(west_out, row, west)
        south = tile(north_out, row + 1) if row + 1 < own else jnp.zeros_like(face)
        set_tile(south_out, row, south)
        set_tile(center_out, row, 1.0 - east - west - south - face)
    set_tile(north_out, 0, jnp.where(first, 0.0, tile(north_out, 0)))


def finish_stencil(halo_refs, own_refs, tail_refs, own):
    _, east_own, west_own, _, north_own = own_refs
    center_tail, east_tail, west_tail, south_tail, north_tail = tail_refs
    last = lax.axis_index("row") == lax.axis_size("row") - 1
    east, west = [tile(east_own, own - 1)], [tile(west_own, own - 1)]
    faces = [tile(north_own, own - 1)]
    for halo_ref in halo_refs:
        for row in range(PASSES):
            east.append(tile(halo_ref, PASSES + row))
            west.append(west_of(east[-1]))
            faces.append(tile(halo_ref, 2 * PASSES + row))
    for row, face in enumerate(faces):
        if row == 0:
            south = jnp.where(last, 0.0, faces[1])
        else:
            south = faces[row + 1] if row + 1 < len(faces) else tile(north_own, 0)
        set_tile(east_tail, row, east[row])
        set_tile(west_tail, row, west[row])
        set_tile(south_tail, row, south)
        set_tile(north_tail, row, face)
        set_tile(center_tail, row, 1.0 - east[row] - west[row] - south - face)


def run_passes(values, own_refs, tail_refs, own):
    rows = len(values)

    def coefficient(kind, row):
        return tile(own_refs[kind], row) if row < own - 1 else tile(tail_refs[kind], row - own + 1)

    def one_pass(_, now):
        after = []
        for row, value in enumerate(now):
            east, west = east_west(value)
            total = coefficient(0, row) * value
            total = total + coefficient(1, row) * east
            total = total + coefficient(2, row) * west
            total = total + coefficient(3, row) * now[(row + 1) % rows]
            after.append(total + coefficient(4, row) * now[row - 1])
        return tuple(after)

    return lax.fori_loop(0, PASSES, one_pass, tuple(values))


def forward_body(halos, field_ref, *refs):
    own_refs, halo_refs, refs = refs[:5], refs[5 : 5 + halos], refs[5 + halos :]
    tail_refs, chunk_refs, sorted_ref = refs[:5], refs[5:-1], refs[-1]
    own = field_ref.shape[0] // TILE
    lev_at = lax.axis_index("lev")
    finish_stencil(halo_refs, own_refs, tail_refs, own)
    values = [tile(field_ref, row) for row in range(own)]
    values += [tile(halo_ref, row) for halo_ref in halo_refs for row in range(PASSES)]
    values = run_passes(values, own_refs, tail_refs, own)
    for row in range(own):
        set_tile(sorted_ref, row, values[row])
    part = own // len(chunk_refs)
    for step, chunk_ref in enumerate(reversed(chunk_refs)):
        chunk_ref[...] = sorted_ref[block(lax.bitwise_xor(lev_at, step) * part, part), :]


def matrix_terms(groups):
    return [
        (group, other, cross)
        for group in range(groups)
        for other in range(max(0, group - 2), min(groups, group + 3))
        for cross in range(2)
        if abs(group - other) < 2 or cross
    ]


def swap_levels(value, sublane):
    return jnp.where(sublane % HELD == 0, pltpu.roll(value, TILE - 1, 0), pltpu.roll(value, 1, 0))


def columns_body(members_ref, innovation_ref, huber_ref, band_ref, group_ref, *refs):
    members_out, innovation_out, huber_out, matrix_out, transposed_out, levels_ref = refs
    count, levels, cells = members_ref.shape
    groups, lon = levels // HELD, HALVES * LANES
    rows, packed = cells // lon, levels // FIELDS
    sublane = places()
    for member in range(count):
        for row in range(rows):
            for half in range(HALVES):
                lanes = slice(row * lon + half * LANES, row * lon + (half + 1) * LANES)
                start = ((member * rows + row) * HALVES + half) * levels
                levels_ref[start : start + levels, :] = members_ref[member, :, lanes].astype(jnp.float32)
                for level in range(HELD):
                    at = half * FIELDS + member * HELD + level
                    spread(members_out, row * groups, at, levels_ref[pl.ds(start + level, groups, stride=HELD), :])
    for row in range(rows):
        for half in range(HALVES):
            lanes = slice(row * lon + half * LANES, row * lon + (half + 1) * LANES)
            for pack in range(packed):
                source = slice(pack * FIELDS, (pack + 1) * FIELDS)
                start = (row * packed + pack) * TILE + half * FIELDS
                innovation_out[start : start + FIELDS, :] = innovation_ref[source, lanes]
                huber_out[start : start + FIELDS, :] = huber_ref[source, lanes].astype(jnp.float32)

    def entry(level, other):
        offset = other - level + REACH
        if not 0 <= offset < 2 * REACH + 1:
            return jnp.float32(0.0)
        value = band_ref[offset, level] + jnp.float32(1.0 if offset == REACH else 0.0)
        return jnp.where(group_ref[level] == group_ref[other], value, jnp.float32(0.0))

    for slot, (group, other, cross) in enumerate(matrix_terms(groups)):
        pairs = [(group * HELD + level, other * HELD + (level ^ cross)) for level in range(HELD)]
        even, odd = (entry(a, b) for a, b in pairs)
        set_tile(matrix_out, slot, jnp.where(sublane % HELD == 0, even, odd))
        even, odd = (entry(b, a) for a, b in pairs)
        set_tile(transposed_out, slot, jnp.where(sublane % HELD == 0, even, odd))


def apply_matrix(matrix_ref, values, sublane):
    crossed = [swap_levels(value, sublane) for value in values]
    totals = [None] * len(values)
    for slot, (group, other, cross) in enumerate(matrix_terms(len(values))):
        term = tile(matrix_ref, slot) * (crossed if cross else values)[other]
        totals[group] = term if totals[group] is None else totals[group] + term
    return totals


def filter_body(chunks, *refs):
    chunk_refs = refs[:chunks]
    members_ref, matrix_ref, partial_ref, columns = refs[chunks:]
    rows = chunk_refs[0].shape[0] // TILE
    lev_at = lax.axis_index("lev")
    sublane = places()
    first_member = sublane % FIELDS < HELD
    for step, chunk_ref in enumerate(reversed(chunk_refs)):
        columns[block(lax.bitwise_xor(lev_at, step) * rows, rows), :] = chunk_ref[...]
    for row in range(rows):
        filtered = apply_matrix(matrix_ref, [tile(columns, group * rows + row) for group in range(chunks)], sublane)
        terms = [tile(members_ref, row * chunks + group) * value for group, value in enumerate(filtered)]
        for pack in range(chunks // 2):
            lower, upper = terms[2 * pack], terms[2 * pack + 1]
            total = jnp.where(first_member, lower, upper)
            total = total + jnp.where(first_member, pltpu.roll(lower, TILE - HELD, 0), pltpu.roll(upper, HELD, 0))
            set_tile(partial_ref, row * (chunks // 2) + pack, total)


def lift_body(chunks, parts, *refs):
    part_refs, refs = refs[:parts], refs[parts:]
    innovation_ref, huber_ref, members_ref, transposed_ref = refs[:4]
    chunk_refs, (weighted_ref, sorted_ref) = refs[4 : 4 + chunks], refs[4 + chunks :]
    rows = chunk_refs[0].shape[0] // TILE
    lev_at = lax.axis_index("lev")
    sublane = places()
    first_member = sublane % FIELDS < HELD
    increment = part_refs[0][...]
    for part_ref in part_refs[1:]:
        increment = increment + part_ref[...]
    residual = increment - innovation_ref[...]
    scale = HUBER / jnp.maximum(jnp.abs(residual), HUBER)
    weighted_ref[...] = jnp.where(huber_ref[...] == 1.0, scale, 1.0) * residual
    for row in range(rows):
        adjoint = []
        for pack in range(chunks // 2):
            weighted = tile(weighted_ref, row * (chunks // 2) + pack)
            lower = jnp.where(first_member, weighted, pltpu.roll(weighted, HELD, 0))
            upper = jnp.where(first_member, pltpu.roll(weighted, TILE - HELD, 0), weighted)
            for value in (lower, upper):
                adjoint.append(value * tile(members_ref, row * chunks + len(adjoint)))
        for group, value in enumerate(apply_matrix(transposed_ref, adjoint, sublane)):
            set_tile(sorted_ref, group * rows + row, value)
    for step, chunk_ref in enumerate(reversed(chunk_refs)):
        chunk_ref[...] = sorted_ref[block(lax.bitwise_xor(lev_at, step) * rows, rows), :]


def gather_body(chunks, *refs):
    chunk_refs, field_ref, send_refs = refs[:chunks], refs[chunks], refs[chunks + 1 :]
    lev_at = lax.axis_index("lev")
    first = lax.axis_index("row") == 0
    rows = chunk_refs[0].shape[0] // TILE
    own = rows * chunks
    for step, chunk_ref in enumerate(reversed(chunk_refs)):
        field_ref[block(lax.bitwise_xor(lev_at, step) * rows, rows), :] = chunk_ref[...]
    if len(send_refs) == 1:
        send_refs[0][...] = field_ref[block(jnp.where(first, own - PASSES, 0), PASSES), :]
    else:
        send_refs[0][...] = field_ref[: PASSES * TILE, :]
        send_refs[1][...] = field_ref[(own - PASSES) * TILE :, :]


def backward_body(halos, control_ref, field_ref, *refs):
    own_refs, tail_refs, halo_refs = refs[:5], refs[5:10], refs[10 : 10 + halos]
    gradient_hbm, result_ref, gradient_ref, semaphores = refs[10 + halos :]
    own = field_ref.shape[0] // TILE
    values = [tile(field_ref, row) for row in range(own)]
    values += [tile(halo_ref, row) for halo_ref in halo_refs for row in range(PASSES)]
    values = run_passes(values, own_refs, tail_refs, own)
    for row in range(own):
        set_tile(result_ref, row, values[row])
    copies = []
    for field in range(FIELDS):
        member, level = divmod(field, HELD)
        for half, lanes in halves():
            result = result_ref[pl.ds(half * FIELDS + field, own, stride=TILE), :]
            gradient_ref[member, level, :, lanes] = control_ref[member, level, :, lanes].astype(jnp.float32) + result
        copy = pltpu.make_async_copy(
            gradient_ref.at[member, level], gradient_hbm.at[member, level], semaphores.at[field]
        )
        copy.start()
        copies.append(copy)
    for copy in copies:
        copy.wait()


def per_device(control, members, east_coef, south_coef, innovation, huber_class, band, level_group_index):
    count, held, own, lon = control.shape
    levels, cells = members.shape[1:]
    chunks, parts, row_count = (lax.axis_size(axis) for axis in ("lev", "mem", "row"))
    assert (count * held, held, lon) == (FIELDS, HELD, HALVES * LANES)
    part = own // chunks
    halos = 1 if row_count == 2 else 2
    tail = 1 + halos * PASSES
    terms = len(matrix_terms(chunks))
    packed = part * levels // FIELDS

    control_near, east_near, south_near, *edges = call(
        pack_body,
        [pltpu.VMEM(x.shape, x.dtype) for x in (control, east_coef, south_coef)] + [planes(3 * PASSES)] * halos,
        remote(control, east_coef, south_coef),
        [pltpu.SemaphoreType.DMA((3,))],
        specs=[HBM] * 3,
    )
    halo = swap_edges(edges, "row")
    field, *own_stencil = call(
        prepare_body, [planes(own)] * 6, resident(control_near, east_near, south_near)
    )
    members_planes, innovation_planes, huber_planes, matrix, transposed = call(
        columns_body,
        [planes(part * chunks), planes(packed), planes(packed), planes(terms), planes(terms)],
        [members, innovation, huber_class, band, level_group_index],
        [planes(part * chunks)],
        specs=[VMEM, VMEM, VMEM, SMEM, SMEM],
    )
    results = call(
        functools.partial(forward_body, halos),
        [planes(tail)] * 5 + [planes(part)] * chunks,
        resident(field, *own_stencil, *halo),
        [planes(own)],
    )
    tail_stencil = results[:5]
    columns = exchange(results[:4:-1], "lev")
    (partial,) = call(
        functools.partial(filter_body, chunks),
        [planes(packed)],
        resident(*columns[::-1], members_planes, matrix),
        [planes(part * chunks)],
    )
    partials = exchange([partial] * parts, "mem")
    lifted = call(
        functools.partial(lift_body, chunks, parts),
        [planes(part)] * chunks,
        resident(*partials, innovation_planes, huber_planes, members_planes, transposed),
        [planes(packed), planes(part * chunks)],
    )
    returned = exchange(lifted[::-1], "lev")
    gathered, *edges = call(
        functools.partial(gather_body, chunks),
        [planes(own)] + [planes(PASSES)] * halos,
        resident(*returned[::-1]),
    )
    halo = swap_edges(edges, "row")
    (gradient,) = call(
        functools.partial(backward_body, halos),
        [jax.ShapeDtypeStruct(control.shape, jnp.float32)],
        resident(control_near, gathered, *own_stencil, *tail_stencil, *halo),
        [planes(own), pltpu.VMEM(control.shape, jnp.float32), pltpu.SemaphoreType.DMA((FIELDS,))],
        out_specs=[HBM],
    )
    return gradient


def solution(mesh):
    placed = (
        P("mem", "lev", "row", None),
        P("mem", None, ("row", "lev")),
        P("lev", "row", None),
        P("lev", "row", None),
        P(None, ("row", "lev")),
        P(None, ("row", "lev")),
        P(),
        P(),
    )
    return jax.shard_map(
        per_device,
        mesh=mesh,
        in_specs=placed,
        out_specs=P("mem", "lev", "row", None),
        check_vma=False,
    )
```

```python
import functools

import jax
import jax.numpy as jnp
from jax import lax
from jax.experimental import pallas as pl
from jax.experimental.pallas import tpu as pltpu
from jax.sharding import PartitionSpec as P

PASSES = 8
HUBER = 1.0
REACH = 3
LANES = 128
TILE = 8
HALVES = 2
HELD = 2
FIELDS = 4

VMEM = pl.BlockSpec(memory_space=pltpu.VMEM)
SMEM = pl.BlockSpec(memory_space=pltpu.SMEM)
HBM = pl.BlockSpec(memory_space=pltpu.HBM)


def planes(count):
    return pltpu.VMEM((count * TILE, LANES), jnp.float32)


def call(body, outs, operands, scratch=(), specs=None, out_specs=None, flops=0):
    total = sum(op.size * op.dtype.itemsize for op in operands)
    return pl.pallas_call(
        body,
        out_shape=outs,
        in_specs=specs or [VMEM] * len(operands),
        out_specs=out_specs or [VMEM] * len(outs),
        scratch_shapes=list(scratch),
        compiler_params=pltpu.CompilerParams(vmem_limit_bytes=32 * 1024 * 1024),
        cost_estimate=pl.CostEstimate(flops=flops, bytes_accessed=2 * total, transcendentals=0),
    )(*operands)


def resident(*arrays):
    return [pltpu.with_memory_space_constraint(array, pltpu.VMEM) for array in arrays]


def remote(*arrays):
    return [pltpu.with_memory_space_constraint(array, pltpu.HBM) for array in arrays]


def exchange(chunks, axis):
    count = len(chunks)
    received = list(chunks)
    for step in reversed(range(1, count)):
        received[step] = lax.ppermute(chunks[step], axis, [(i, i ^ step) for i in range(count)])
    return received


def swap_edges(edges, axis):
    count = lax.axis_size(axis)
    if len(edges) == 1:
        return [lax.ppermute(edges[0], axis, [(0, 1), (1, 0)])]
    head, tail = edges
    south = lax.ppermute(head, axis, [(i + 1, i) for i in range(count - 1)])
    north = lax.ppermute(tail, axis, [(i, i + 1) for i in range(count - 1)])
    return [south, north]


def tile(ref, row):
    return ref[row * TILE : (row + 1) * TILE, :]


def set_tile(ref, row, value):
    ref[row * TILE : (row + 1) * TILE, :] = value


def block(first_row, rows):
    return pl.ds(pl.multiple_of(first_row * TILE, TILE), rows * TILE)


def spread(ref, row, sublane, values):
    ref[pl.ds(row * TILE + sublane, values.shape[0], stride=TILE), :] = values


def places():
    return lax.broadcasted_iota(jnp.int32, (TILE, LANES), 0)


def east_west(value):
    lane = lax.broadcasted_iota(jnp.int32, (TILE, LANES), 1)
    other = pltpu.roll(value, FIELDS, 0)
    east = pltpu.roll(jnp.where(lane == 0, other, value), LANES - 1, 1)
    west = pltpu.roll(jnp.where(lane == LANES - 1, other, value), 1, 1)
    return east, west


def west_of(value):
    lane = lax.broadcasted_iota(jnp.int32, (TILE, LANES), 1)
    return pltpu.roll(jnp.where(lane == LANES - 1, pltpu.roll(value, FIELDS, 0), value), 1, 1)


def halves():
    return [(half, slice(half * LANES, (half + 1) * LANES)) for half in range(HALVES)]


def pack_body(control_hbm, east_hbm, south_hbm, control_ref, east_ref, south_ref, *refs):
    send_refs, semaphores = refs[:-1], refs[-1]
    copies = [
        pltpu.make_async_copy(source, target, semaphores.at[index])
        for index, (source, target) in enumerate(
            ((control_hbm, control_ref), (east_hbm, east_ref), (south_hbm, south_ref))
        )
    ]
    for copy in copies:
        copy.start()
    for copy in copies:
        copy.wait()
    own = control_ref.shape[2]
    first = lax.axis_index("row") == 0

    def edges(load):
        head = load(slice(0, 2 * PASSES))[:PASSES].astype(jnp.float32)
        tail = load(slice(own - 2 * PASSES, own))[PASSES:].astype(jnp.float32)
        return [jnp.where(first, tail, head)] if len(send_refs) == 1 else [head, tail]

    for half, lanes in halves():
        for field in range(FIELDS):
            member, level = divmod(field, HELD)
            at = half * FIELDS + field
            values = edges(lambda rows: control_ref[member, level, rows, lanes])
            for send_ref, value in zip(send_refs, values):
                spread(send_ref, 0, at, value)
            for kind, coef_ref in enumerate((east_ref, south_ref)):
                values = edges(lambda rows: coef_ref[level, rows, lanes])
                for send_ref, value in zip(send_refs, values):
                    spread(send_ref, (kind + 1) * PASSES, at, value)


def is_mirrored(halos):
    return halos == 1 and lax.axis_index("row") == 1


def pick(mirrored, count, row):
    return row if mirrored is False else jnp.where(mirrored, count - 1 - row, row)


def stencil(values, row, center, east, west, above, below):
    to_east, to_west = east_west(values[row])
    total = center * values[row]
    total = total + east * to_east
    total = total + west * to_west
    total = total + below * values[row + 1]
    return total if above is None else total + above * values[row - 1]


def interior_passes(halos, field_ref, own_refs, saved_ref):
    center_ref, east_ref, west_ref, face_ref = own_refs
    own = field_ref.shape[0] // TILE
    values = {row: tile(field_ref, row) for row in range(own)}
    for step in range(1, PASSES + 1):
        for side in range(halos):
            kept = (own - 1 - step, own - step) if side == 0 else (step - 1, step)
            for index, row in enumerate(kept):
                set_tile(saved_ref, (side * PASSES + step - 1) * 2 + index, values[row])
        after = {}
        for row in range(step if halos == 2 else 0, own - step):
            after[row] = stencil(
                values,
                row,
                tile(center_ref, row),
                tile(east_ref, row),
                tile(west_ref, row),
                tile(face_ref, row) if row else None,
                tile(face_ref, row + 1),
            )
        values = after
    return values


def wedge_passes(halos, halo_rows, own, saved_ref, coefficient, top):
    done = {}
    for side in range(halos):
        values = dict(halo_rows[side])
        for step in range(1, PASSES + 1):
            kept = (own - 1 - step, own - step) if side == 0 else (step - 1, step)
            for index, row in enumerate(kept):
                values[row] = tile(saved_ref, (side * PASSES + step - 1) * 2 + index)
            after = {}
            for row in range(own - step, own + PASSES - step) if side == 0 else range(step - PASSES, step):
                center, east, west, above = (coefficient(kind, row) for kind in range(4))
                after[row] = stencil(values, row, center, east, west, top if row == 0 else above, coefficient(3, row + 1))
            values = after
        done.update(values)
    return done


def prepare_body(halos, control_ref, east_ref, south_ref, *refs):
    own_refs, (rows_out, saved_out, field_ref, raw_east, raw_face) = refs[:4], refs[4:]
    center_out, east_out, west_out, face_out = own_refs
    own = control_ref.shape[2]
    mirrored = is_mirrored(halos)
    for half, lanes in halves():
        for field in range(FIELDS):
            member, level = divmod(field, HELD)
            at = half * FIELDS + field
            spread(rows_out, 0, at, control_ref[member, level, :, lanes].astype(jnp.float32))
            spread(raw_east, 0, at, east_ref[level, :, lanes])
            spread(raw_face, 0, at, south_ref[level, :, lanes])
    for row in range(own):
        source = pick(mirrored, own, row)
        set_tile(field_ref, row, rows_out[block(source, 1), :])
        east = raw_east[block(source, 1), :]
        set_tile(east_out, row, east)
        set_tile(west_out, row, west_of(east))
        if row == 0:
            face = tile(raw_face, 0)
            face = face if mirrored is False else jnp.where(mirrored, 0.0, face)
        else:
            face = raw_face[block(row if mirrored is False else jnp.where(mirrored, own - row, row), 1), :]
        set_tile(face_out, row, face)
    set_tile(face_out, own, tile(raw_face, 0))
    for row in range(own - 1):
        total = 1.0 - tile(east_out, row) - tile(west_out, row)
        set_tile(center_out, row, total - tile(face_out, row + 1) - tile(face_out, row))
    for row, value in interior_passes(halos, field_ref, own_refs, saved_out).items():
        set_tile(rows_out, row, value)


def finish_coefficients(halos, halo_refs, own_refs, tail_refs, own):
    _, east_own, west_own, face_own = own_refs
    center_tail, east_tail, west_tail, face_tail = tail_refs
    mirrored = is_mirrored(halos)

    def halo_tile(side, kind, row):
        return halo_refs[side][block(kind * PASSES + row, 1), :]

    set_tile(east_tail, 0, tile(east_own, own - 1))
    set_tile(west_tail, 0, tile(west_own, own - 1))
    set_tile(face_tail, 0, tile(face_own, own - 1))
    for row in range(PASSES):
        east = halo_tile(0, 1, pick(mirrored, PASSES, row))
        set_tile(east_tail, 1 + row, east)
        set_tile(west_tail, 1 + row, west_of(east))
        if mirrored is False:
            face = halo_tile(0, 2, row)
        elif row == 0:
            face = jnp.where(mirrored, tile(face_own, own), halo_tile(0, 2, 0))
        else:
            face = halo_tile(0, 2, jnp.where(mirrored, PASSES - row, row))
        set_tile(face_tail, 1 + row, face)
    for row in range(PASSES):
        total = 1.0 - tile(east_tail, row) - tile(west_tail, row)
        set_tile(center_tail, row, total - tile(face_tail, row + 1) - tile(face_tail, row))
    if halos == 2:
        for row in range(PASSES):
            at = 1 + PASSES + row
            east, face = halo_tile(1, 1, row), halo_tile(1, 2, row)
            below = halo_tile(1, 2, row + 1) if row + 1 < PASSES else tile(face_own, 0)
            west = west_of(east)
            for ref, value in zip(tail_refs, (1.0 - east - west - below - face, east, west, face)):
                set_tile(ref, at, value)


def coefficient_reader(own_refs, tail_refs, own):
    def coefficient(kind, row):
        if row < 0:
            return tile(tail_refs[kind], 1 + 2 * PASSES + row)
        return tile(own_refs[kind], row) if row < own - 1 else tile(tail_refs[kind], row - own + 1)

    return coefficient


def top_coefficient(halos, own_refs):
    return None if halos == 1 else jnp.where(lax.axis_index("row") == 0, 0.0, tile(own_refs[3], 0))


def forward_body(halos, rows_ref, saved_ref, *refs):
    own_refs, halo_refs, refs = refs[:4], refs[4 : 4 + halos], refs[4 + halos :]
    tail_refs, chunk_refs, sorted_ref = refs[:4], refs[4:-1], refs[-1]
    own = rows_ref.shape[0] // TILE
    lev_at = lax.axis_index("lev")
    mirrored = is_mirrored(halos)
    finish_coefficients(halos, halo_refs, own_refs, tail_refs, own)
    halo_rows = [{own + row: halo_refs[0][block(pick(mirrored, PASSES, row), 1), :] for row in range(PASSES)}]
    if halos == 2:
        halo_rows.append({row - PASSES: tile(halo_refs[1], row) for row in range(PASSES)})
    coefficient = coefficient_reader(own_refs, tail_refs, own)
    top = top_coefficient(halos, own_refs)
    done = wedge_passes(halos, halo_rows, own, saved_ref, coefficient, top)
    for row in range(own):
        value = done[row] if row in done else tile(rows_ref, row)
        sorted_ref[block(pick(mirrored, own, row), 1), :] = value
    part = own // len(chunk_refs)
    for step, chunk_ref in enumerate(reversed(chunk_refs)):
        chunk_ref[...] = sorted_ref[block(lax.bitwise_xor(lev_at, step) * part, part), :]


def matrix_terms(groups):
    return [
        (group, other, cross)
        for group in range(groups)
        for other in range(max(0, group - 2), min(groups, group + 3))
        for cross in range(2)
        if abs(group - other) < 2 or cross
    ]


def swap_levels(value, sublane):
    return jnp.where(sublane % HELD == 0, pltpu.roll(value, TILE - 1, 0), pltpu.roll(value, 1, 0))


def columns_body(members_ref, innovation_ref, huber_ref, band_ref, group_ref, *refs):
    members_out, innovation_out, huber_out, matrix_out, transposed_out, levels_ref = refs
    count, levels, cells = members_ref.shape
    groups, lon = levels // HELD, HALVES * LANES
    rows, packed = cells // lon, levels // FIELDS
    sublane = places()
    for member in range(count):
        for row in range(rows):
            for half in range(HALVES):
                lanes = slice(row * lon + half * LANES, row * lon + (half + 1) * LANES)
                start = ((member * rows + row) * HALVES + half) * levels
                levels_ref[start : start + levels, :] = members_ref[member, :, lanes].astype(jnp.float32)
                for level in range(HELD):
                    at = half * FIELDS + member * HELD + level
                    spread(members_out, row * groups, at, levels_ref[pl.ds(start + level, groups, stride=HELD), :])
    for row in range(rows):
        for half in range(HALVES):
            lanes = slice(row * lon + half * LANES, row * lon + (half + 1) * LANES)
            for pack in range(packed):
                source = slice(pack * FIELDS, (pack + 1) * FIELDS)
                start = (row * packed + pack) * TILE + half * FIELDS
                innovation_out[start : start + FIELDS, :] = innovation_ref[source, lanes]
                huber_out[start : start + FIELDS, :] = huber_ref[source, lanes].astype(jnp.float32)

    def entry(level, other):
        offset = other - level + REACH
        if not 0 <= offset < 2 * REACH + 1:
            return jnp.float32(0.0)
        value = band_ref[offset, level] + jnp.float32(1.0 if offset == REACH else 0.0)
        return jnp.where(group_ref[level] == group_ref[other], value, jnp.float32(0.0))

    for slot, (group, other, cross) in enumerate(matrix_terms(groups)):
        pairs = [(group * HELD + level, other * HELD + (level ^ cross)) for level in range(HELD)]
        even, odd = (entry(a, b) for a, b in pairs)
        set_tile(matrix_out, slot, jnp.where(sublane % HELD == 0, even, odd))
        even, odd = (entry(b, a) for a, b in pairs)
        set_tile(transposed_out, slot, jnp.where(sublane % HELD == 0, even, odd))


def apply_matrix(matrix_ref, values, sublane):
    crossed = [swap_levels(value, sublane) for value in values]
    totals = [None] * len(values)
    for slot, (group, other, cross) in enumerate(matrix_terms(len(values))):
        term = tile(matrix_ref, slot) * (crossed if cross else values)[other]
        totals[group] = term if totals[group] is None else totals[group] + term
    return totals


def filter_body(chunks, *refs):
    chunk_refs = refs[:chunks]
    members_ref, matrix_ref, partial_ref, columns = refs[chunks:]
    rows = chunk_refs[0].shape[0] // TILE
    lev_at = lax.axis_index("lev")
    sublane = places()
    first_member = sublane % FIELDS < HELD
    for step, chunk_ref in enumerate(reversed(chunk_refs)):
        columns[block(lax.bitwise_xor(lev_at, step) * rows, rows), :] = chunk_ref[...]
    for row in range(rows):
        filtered = apply_matrix(matrix_ref, [tile(columns, group * rows + row) for group in range(chunks)], sublane)
        terms = [tile(members_ref, row * chunks + group) * value for group, value in enumerate(filtered)]
        for pack in range(chunks // 2):
            lower, upper = terms[2 * pack], terms[2 * pack + 1]
            total = jnp.where(first_member, lower, upper)
            total = total + jnp.where(first_member, pltpu.roll(lower, TILE - HELD, 0), pltpu.roll(upper, HELD, 0))
            set_tile(partial_ref, row * (chunks // 2) + pack, total)


def lift_body(chunks, parts, *refs):
    part_refs, refs = refs[:parts], refs[parts:]
    innovation_ref, huber_ref, members_ref, transposed_ref = refs[:4]
    chunk_refs, (weighted_ref, sorted_ref) = refs[4 : 4 + chunks], refs[4 + chunks :]
    rows = chunk_refs[0].shape[0] // TILE
    lev_at = lax.axis_index("lev")
    sublane = places()
    first_member = sublane % FIELDS < HELD
    increment = part_refs[0][...]
    for part_ref in part_refs[1:]:
        increment = increment + part_ref[...]
    residual = increment - innovation_ref[...]
    scale = HUBER / jnp.maximum(jnp.abs(residual), HUBER)
    weighted_ref[...] = jnp.where(huber_ref[...] == 1.0, scale, 1.0) * residual
    for row in range(rows):
        adjoint = []
        for pack in range(chunks // 2):
            weighted = tile(weighted_ref, row * (chunks // 2) + pack)
            lower = jnp.where(first_member, weighted, pltpu.roll(weighted, HELD, 0))
            upper = jnp.where(first_member, pltpu.roll(weighted, TILE - HELD, 0), weighted)
            for value in (lower, upper):
                adjoint.append(value * tile(members_ref, row * chunks + len(adjoint)))
        for group, value in enumerate(apply_matrix(transposed_ref, adjoint, sublane)):
            set_tile(sorted_ref, group * rows + row, value)
    for step, chunk_ref in enumerate(reversed(chunk_refs)):
        chunk_ref[...] = sorted_ref[block(lax.bitwise_xor(lev_at, step) * rows, rows), :]


def gather_body(halos, chunks, *refs):
    chunk_refs, field_ref, send_refs, sorted_ref = refs[:chunks], refs[chunks], refs[chunks + 1 : -1], refs[-1]
    lev_at = lax.axis_index("lev")
    mirrored = is_mirrored(halos)
    rows = chunk_refs[0].shape[0] // TILE
    own = rows * chunks
    for step, chunk_ref in enumerate(reversed(chunk_refs)):
        sorted_ref[block(lax.bitwise_xor(lev_at, step) * rows, rows), :] = chunk_ref[...]
    for row in range(own):
        set_tile(field_ref, row, sorted_ref[block(pick(mirrored, own, row), 1), :])
    for row in range(PASSES):
        if halos == 1:
            set_tile(send_refs[0], row, tile(field_ref, own - 1 - row))
        else:
            set_tile(send_refs[0], row, tile(field_ref, row))
            set_tile(send_refs[1], row, tile(field_ref, own - PASSES + row))


def interior_body(halos, field_ref, *refs):
    own_refs, (rows_out, saved_out) = refs[:4], refs[4:]
    for row, value in interior_passes(halos, field_ref, own_refs, saved_out).items():
        set_tile(rows_out, row, value)


def backward_body(halos, control_ref, rows_ref, saved_ref, *refs):
    own_refs, tail_refs, halo_refs = refs[:4], refs[4:8], refs[8 : 8 + halos]
    gradient_hbm, result_ref, gradient_ref, semaphores = refs[8 + halos :]
    own = rows_ref.shape[0] // TILE
    mirrored = is_mirrored(halos)
    halo_rows = [{own + row: tile(halo_refs[0], row) for row in range(PASSES)}]
    if halos == 2:
        halo_rows.append({row - PASSES: tile(halo_refs[1], row) for row in range(PASSES)})
    coefficient = coefficient_reader(own_refs, tail_refs, own)
    top = top_coefficient(halos, own_refs)
    done = wedge_passes(halos, halo_rows, own, saved_ref, coefficient, top)
    for row in range(own):
        value = done[row] if row in done else tile(rows_ref, row)
        result_ref[block(pick(mirrored, own, row), 1), :] = value
    copies = []
    for field in range(FIELDS):
        member, level = divmod(field, HELD)
        for half, lanes in halves():
            result = result_ref[pl.ds(half * FIELDS + field, own, stride=TILE), :]
            gradient_ref[member, level, :, lanes] = control_ref[member, level, :, lanes].astype(jnp.float32) + result
        copy = pltpu.make_async_copy(
            gradient_ref.at[member, level], gradient_hbm.at[member, level], semaphores.at[field]
        )
        copy.start()
        copies.append(copy)
    for copy in copies:
        copy.wait()


def per_device(control, members, east_coef, south_coef, innovation, huber_class, band, level_group_index):
    count, held, own, lon = control.shape
    levels, cells = members.shape[1:]
    chunks, parts, row_count = (lax.axis_size(axis) for axis in ("lev", "mem", "row"))
    assert (count * held, held, lon) == (FIELDS, HELD, HALVES * LANES)
    part = own // chunks
    halos = 1 if row_count == 2 else 2
    tail = 1 + halos * PASSES
    terms = len(matrix_terms(chunks))
    packed = part * levels // FIELDS

    control_near, east_near, south_near, *edges = call(
        pack_body,
        [pltpu.VMEM(x.shape, x.dtype) for x in (control, east_coef, south_coef)] + [planes(3 * PASSES)] * halos,
        remote(control, east_coef, south_coef),
        [pltpu.SemaphoreType.DMA((3,))],
        specs=[HBM] * 3,
    )
    halo = swap_edges(edges, "row")
    kept = halos * PASSES * 2
    *own_stencil, done_rows, saved = call(
        functools.partial(prepare_body, halos),
        [planes(own)] * 3 + [planes(own + 1), planes(own), planes(kept)],
        resident(control_near, east_near, south_near),
        [planes(own)] * 3,
    )
    members_planes, innovation_planes, huber_planes, matrix, transposed = call(
        columns_body,
        [planes(part * chunks), planes(packed), planes(packed), planes(terms), planes(terms)],
        [members, innovation, huber_class, band, level_group_index],
        [planes(part * chunks)],
        specs=[VMEM, VMEM, VMEM, SMEM, SMEM],
    )
    results = call(
        functools.partial(forward_body, halos),
        [planes(tail)] * 4 + [planes(part)] * chunks,
        resident(done_rows, saved, *own_stencil, *halo),
        [planes(own)],
    )
    tail_stencil = results[:4]
    columns = exchange(results[:3:-1], "lev")
    (partial,) = call(
        functools.partial(filter_body, chunks),
        [planes(packed)],
        resident(*columns[::-1], members_planes, matrix),
        [planes(part * chunks)],
    )
    partials = exchange([partial] * parts, "mem")
    lifted = call(
        functools.partial(lift_body, chunks, parts),
        [planes(part)] * chunks,
        resident(*partials, innovation_planes, huber_planes, members_planes, transposed),
        [planes(packed), planes(part * chunks)],
    )
    returned = exchange(lifted[::-1], "lev")
    gathered, *edges = call(
        functools.partial(gather_body, halos, chunks),
        [planes(own)] + [planes(PASSES)] * halos,
        resident(*returned[::-1]),
        [planes(own)],
    )
    halo = swap_edges(edges, "row")
    done_rows, saved = call(
        functools.partial(interior_body, halos),
        [planes(own), planes(kept)],
        resident(gathered, *own_stencil),
    )
    (gradient,) = call(
        functools.partial(backward_body, halos),
        [jax.ShapeDtypeStruct(control.shape, jnp.float32)],
        resident(control_near, done_rows, saved, *own_stencil, *tail_stencil, *halo),
        [planes(own), pltpu.VMEM(control.shape, jnp.float32), pltpu.SemaphoreType.DMA((FIELDS,))],
        out_specs=[HBM],
    )
    return gradient


def solution(mesh):
    placed = (
        P("mem", "lev", "row", None),
        P("mem", None, ("row", "lev")),
        P("lev", "row", None),
        P("lev", "row", None),
        P(None, ("row", "lev")),
        P(None, ("row", "lev")),
        P(),
        P(),
    )
    return jax.shard_map(
        per_device,
        mesh=mesh,
        in_specs=placed,
        out_specs=P("mem", "lev", "row", None),
        check_vma=False,
    )
```

```python
import functools

import jax
import jax.numpy as jnp
from jax import lax
from jax.experimental import pallas as pl
from jax.experimental.pallas import tpu as pltpu
from jax.sharding import PartitionSpec as P

PASSES = 8
HUBER = 1.0
REACH = 3
LANES = 128
TILE = 8
HALVES = 2
HELD = 2
FIELDS = 4

VMEM = pl.BlockSpec(memory_space=pltpu.VMEM)
SMEM = pl.BlockSpec(memory_space=pltpu.SMEM)
HBM = pl.BlockSpec(memory_space=pltpu.HBM)


def planes(count):
    return pltpu.VMEM((count * TILE, LANES), jnp.float32)


def call(body, outs, operands, scratch=(), specs=None, out_specs=None, flops=0):
    total = sum(op.size * op.dtype.itemsize for op in operands)
    return pl.pallas_call(
        body,
        out_shape=outs,
        in_specs=specs or [VMEM] * len(operands),
        out_specs=out_specs or [VMEM] * len(outs),
        scratch_shapes=list(scratch),
        compiler_params=pltpu.CompilerParams(vmem_limit_bytes=32 * 1024 * 1024),
        cost_estimate=pl.CostEstimate(flops=flops, bytes_accessed=2 * total, transcendentals=0),
    )(*operands)


def resident(*arrays):
    return [pltpu.with_memory_space_constraint(array, pltpu.VMEM) for array in arrays]


def remote(*arrays):
    return [pltpu.with_memory_space_constraint(array, pltpu.HBM) for array in arrays]


def exchange(chunks, axis):
    count = len(chunks)
    received = list(chunks)
    for step in reversed(range(1, count)):
        received[step] = lax.ppermute(chunks[step], axis, [(i, i ^ step) for i in range(count)])
    return received


def swap_edges(edges, axis):
    count = lax.axis_size(axis)
    if len(edges) == 1:
        return [lax.ppermute(edges[0], axis, [(0, 1), (1, 0)])]
    head, tail = edges
    south = lax.ppermute(head, axis, [(i + 1, i) for i in range(count - 1)])
    north = lax.ppermute(tail, axis, [(i, i + 1) for i in range(count - 1)])
    return [south, north]


def tile(ref, row):
    return ref[row * TILE : (row + 1) * TILE, :]


def set_tile(ref, row, value):
    ref[row * TILE : (row + 1) * TILE, :] = value


def block(first_row, rows):
    return pl.ds(pl.multiple_of(first_row * TILE, TILE), rows * TILE)


def spread(ref, row, sublane, values):
    ref[pl.ds(row * TILE + sublane, values.shape[0], stride=TILE), :] = values


def places():
    return lax.broadcasted_iota(jnp.int32, (TILE, LANES), 0)


def east_west(value):
    lane = lax.broadcasted_iota(jnp.int32, (TILE, LANES), 1)
    other = pltpu.roll(value, FIELDS, 0)
    east = pltpu.roll(jnp.where(lane == 0, other, value), LANES - 1, 1)
    west = pltpu.roll(jnp.where(lane == LANES - 1, other, value), 1, 1)
    return east, west


def west_of(value):
    lane = lax.broadcasted_iota(jnp.int32, (TILE, LANES), 1)
    return pltpu.roll(jnp.where(lane == LANES - 1, pltpu.roll(value, FIELDS, 0), value), 1, 1)


def halves():
    return [(half, slice(half * LANES, (half + 1) * LANES)) for half in range(HALVES)]


def pack_body(control_hbm, east_hbm, south_hbm, control_ref, east_ref, south_ref, *refs):
    send_refs, semaphores = refs[:-1], refs[-1]
    pieces = [(east_hbm.at[level], east_ref.at[level]) for level in range(HELD)]
    pieces += [(south_hbm.at[level], south_ref.at[level]) for level in range(HELD)]
    for field in range(FIELDS):
        member, level = divmod(field, HELD)
        pieces.append((control_hbm.at[member, level], control_ref.at[member, level]))
    copies = [
        pltpu.make_async_copy(source, target, semaphores.at[index]) for index, (source, target) in enumerate(pieces)
    ]
    for copy in copies:
        copy.start()
    for copy in copies:
        copy.wait()
    own = control_ref.shape[2]
    first = lax.axis_index("row") == 0

    def edges(load):
        head = load(slice(0, 2 * PASSES))[:PASSES].astype(jnp.float32)
        tail = load(slice(own - 2 * PASSES, own))[PASSES:].astype(jnp.float32)
        return [jnp.where(first, tail, head)] if len(send_refs) == 1 else [head, tail]

    for half, lanes in halves():
        for field in range(FIELDS):
            member, level = divmod(field, HELD)
            at = half * FIELDS + field
            values = edges(lambda rows: control_ref[member, level, rows, lanes])
            for send_ref, value in zip(send_refs, values):
                spread(send_ref, 0, at, value)
            for kind, coef_ref in enumerate((east_ref, south_ref)):
                values = edges(lambda rows: coef_ref[level, rows, lanes])
                for send_ref, value in zip(send_refs, values):
                    spread(send_ref, (kind + 1) * PASSES, at, value)


def is_mirrored(halos):
    return halos == 1 and lax.axis_index("row") == 1


def pick(mirrored, count, row):
    return row if mirrored is False else jnp.where(mirrored, count - 1 - row, row)


def stencil(values, row, center, east, west, above, below):
    to_east, to_west = east_west(values[row])
    total = center * values[row] + below * values[row + 1]
    if above is not None:
        total = total + above * values[row - 1]
    return total + (east * to_east + west * to_west)


def interior_passes(halos, field_ref, own_refs, saved_ref):
    center_ref, east_ref, west_ref, face_ref = own_refs
    own = field_ref.shape[0] // TILE
    values = {row: tile(field_ref, row) for row in range(own)}
    for step in range(1, PASSES + 1):
        for side in range(halos):
            kept = (own - 1 - step, own - step) if side == 0 else (step - 1, step)
            for index, row in enumerate(kept):
                set_tile(saved_ref, (side * PASSES + step - 1) * 2 + index, values[row])
        after = {}
        for row in range(step if halos == 2 else 0, own - step):
            after[row] = stencil(
                values,
                row,
                tile(center_ref, row),
                tile(east_ref, row),
                tile(west_ref, row),
                tile(face_ref, row) if row else None,
                tile(face_ref, row + 1),
            )
        values = after
    return values


def wedge_passes(halos, halo_rows, own, saved_ref, coefficient, top):
    done = {}
    for side in range(halos):
        values = dict(halo_rows[side])
        for step in range(1, PASSES + 1):
            kept = (own - 1 - step, own - step) if side == 0 else (step - 1, step)
            for index, row in enumerate(kept):
                values[row] = tile(saved_ref, (side * PASSES + step - 1) * 2 + index)
            after = {}
            for row in range(own - step, own + PASSES - step) if side == 0 else range(step - PASSES, step):
                center, east, west, above = (coefficient(kind, row) for kind in range(4))
                after[row] = stencil(values, row, center, east, west, top if row == 0 else above, coefficient(3, row + 1))
            values = after
        done.update(values)
    return done


def prepare_body(halos, control_ref, east_ref, south_ref, *refs):
    own_refs, (rows_out, saved_out, field_ref, raw_east, raw_face) = refs[:4], refs[4:]
    center_out, east_out, west_out, face_out = own_refs
    own = control_ref.shape[2]
    mirrored = is_mirrored(halos)
    for half, lanes in halves():
        for field in range(FIELDS):
            member, level = divmod(field, HELD)
            at = half * FIELDS + field
            spread(rows_out, 0, at, control_ref[member, level, :, lanes].astype(jnp.float32))
            spread(raw_east, 0, at, east_ref[level, :, lanes])
            spread(raw_face, 0, at, south_ref[level, :, lanes])
    for row in range(own):
        source = pick(mirrored, own, row)
        set_tile(field_ref, row, rows_out[block(source, 1), :])
        east = raw_east[block(source, 1), :]
        set_tile(east_out, row, east)
        set_tile(west_out, row, west_of(east))
        if row == 0:
            face = tile(raw_face, 0)
            face = face if mirrored is False else jnp.where(mirrored, 0.0, face)
        else:
            face = raw_face[block(row if mirrored is False else jnp.where(mirrored, own - row, row), 1), :]
        set_tile(face_out, row, face)
    set_tile(face_out, own, tile(raw_face, 0))
    for row in range(own - 1):
        total = 1.0 - tile(east_out, row) - tile(west_out, row)
        set_tile(center_out, row, total - tile(face_out, row + 1) - tile(face_out, row))
    for row, value in interior_passes(halos, field_ref, own_refs, saved_out).items():
        set_tile(rows_out, row, value)


def finish_coefficients(halos, halo_refs, own_refs, tail_refs, own):
    _, east_own, west_own, face_own = own_refs
    center_tail, east_tail, west_tail, face_tail = tail_refs
    mirrored = is_mirrored(halos)

    def halo_tile(side, kind, row):
        return halo_refs[side][block(kind * PASSES + row, 1), :]

    set_tile(east_tail, 0, tile(east_own, own - 1))
    set_tile(west_tail, 0, tile(west_own, own - 1))
    set_tile(face_tail, 0, tile(face_own, own - 1))
    for row in range(PASSES):
        east = halo_tile(0, 1, pick(mirrored, PASSES, row))
        set_tile(east_tail, 1 + row, east)
        set_tile(west_tail, 1 + row, west_of(east))
        if mirrored is False:
            face = halo_tile(0, 2, row)
        elif row == 0:
            face = jnp.where(mirrored, tile(face_own, own), halo_tile(0, 2, 0))
        else:
            face = halo_tile(0, 2, jnp.where(mirrored, PASSES - row, row))
        set_tile(face_tail, 1 + row, face)
    for row in range(PASSES):
        total = 1.0 - tile(east_tail, row) - tile(west_tail, row)
        set_tile(center_tail, row, total - tile(face_tail, row + 1) - tile(face_tail, row))
    if halos == 2:
        for row in range(PASSES):
            at = 1 + PASSES + row
            east, face = halo_tile(1, 1, row), halo_tile(1, 2, row)
            below = halo_tile(1, 2, row + 1) if row + 1 < PASSES else tile(face_own, 0)
            west = west_of(east)
            for ref, value in zip(tail_refs, (1.0 - east - west - below - face, east, west, face)):
                set_tile(ref, at, value)


def coefficient_reader(own_refs, tail_refs, own):
    def coefficient(kind, row):
        if row < 0:
            return tile(tail_refs[kind], 1 + 2 * PASSES + row)
        return tile(own_refs[kind], row) if row < own - 1 else tile(tail_refs[kind], row - own + 1)

    return coefficient


def top_coefficient(halos, own_refs):
    return None if halos == 1 else jnp.where(lax.axis_index("row") == 0, 0.0, tile(own_refs[3], 0))


def forward_body(halos, rows_ref, saved_ref, *refs):
    own_refs, halo_refs, refs = refs[:4], refs[4 : 4 + halos], refs[4 + halos :]
    tail_refs, chunk_refs, sorted_ref = refs[:4], refs[4:-1], refs[-1]
    own = rows_ref.shape[0] // TILE
    lev_at = lax.axis_index("lev")
    mirrored = is_mirrored(halos)
    finish_coefficients(halos, halo_refs, own_refs, tail_refs, own)
    halo_rows = [{own + row: halo_refs[0][block(pick(mirrored, PASSES, row), 1), :] for row in range(PASSES)}]
    if halos == 2:
        halo_rows.append({row - PASSES: tile(halo_refs[1], row) for row in range(PASSES)})
    coefficient = coefficient_reader(own_refs, tail_refs, own)
    top = top_coefficient(halos, own_refs)
    done = wedge_passes(halos, halo_rows, own, saved_ref, coefficient, top)
    for row in range(own):
        value = done[row] if row in done else tile(rows_ref, row)
        sorted_ref[block(pick(mirrored, own, row), 1), :] = value
    part = own // len(chunk_refs)
    for step, chunk_ref in enumerate(reversed(chunk_refs)):
        chunk_ref[...] = sorted_ref[block(lax.bitwise_xor(lev_at, step) * part, part), :]


def matrix_terms(groups):
    return [
        (group, other, cross)
        for group in range(groups)
        for other in range(max(0, group - 2), min(groups, group + 3))
        for cross in range(2)
        if abs(group - other) < 2 or cross
    ]


def swap_levels(value, sublane):
    return jnp.where(sublane % HELD == 0, pltpu.roll(value, TILE - 1, 0), pltpu.roll(value, 1, 0))


def columns_body(members_ref, innovation_ref, huber_ref, band_ref, group_ref, *refs):
    members_out, innovation_out, huber_out, matrix_out, transposed_out, levels_ref = refs
    count, levels, cells = members_ref.shape
    groups, lon = levels // HELD, HALVES * LANES
    rows, packed = cells // lon, levels // FIELDS
    sublane = places()
    for member in range(count):
        for row in range(rows):
            for half in range(HALVES):
                lanes = slice(row * lon + half * LANES, row * lon + (half + 1) * LANES)
                start = ((member * rows + row) * HALVES + half) * levels
                levels_ref[start : start + levels, :] = members_ref[member, :, lanes].astype(jnp.float32)
                for level in range(HELD):
                    at = half * FIELDS + member * HELD + level
                    spread(members_out, row * groups, at, levels_ref[pl.ds(start + level, groups, stride=HELD), :])
    for row in range(rows):
        for half in range(HALVES):
            lanes = slice(row * lon + half * LANES, row * lon + (half + 1) * LANES)
            for pack in range(packed):
                source = slice(pack * FIELDS, (pack + 1) * FIELDS)
                start = (row * packed + pack) * TILE + half * FIELDS
                innovation_out[start : start + FIELDS, :] = innovation_ref[source, lanes]
                huber_out[start : start + FIELDS, :] = huber_ref[source, lanes].astype(jnp.float32)

    def entry(level, other):
        offset = other - level + REACH
        if not 0 <= offset < 2 * REACH + 1:
            return jnp.float32(0.0)
        value = band_ref[offset, level] + jnp.float32(1.0 if offset == REACH else 0.0)
        return jnp.where(group_ref[level] == group_ref[other], value, jnp.float32(0.0))

    for slot, (group, other, cross) in enumerate(matrix_terms(groups)):
        pairs = [(group * HELD + level, other * HELD + (level ^ cross)) for level in range(HELD)]
        even, odd = (entry(a, b) for a, b in pairs)
        set_tile(matrix_out, slot, jnp.where(sublane % HELD == 0, even, odd))
        even, odd = (entry(b, a) for a, b in pairs)
        set_tile(transposed_out, slot, jnp.where(sublane % HELD == 0, even, odd))


def apply_matrix(matrix_ref, values, sublane):
    crossed = [swap_levels(value, sublane) for value in values]
    totals = [None] * len(values)
    for slot, (group, other, cross) in enumerate(matrix_terms(len(values))):
        term = tile(matrix_ref, slot) * (crossed if cross else values)[other]
        totals[group] = term if totals[group] is None else totals[group] + term
    return totals


def filter_body(chunks, *refs):
    chunk_refs = refs[:chunks]
    members_ref, matrix_ref, partial_ref, columns = refs[chunks:]
    rows = chunk_refs[0].shape[0] // TILE
    lev_at = lax.axis_index("lev")
    sublane = places()
    first_member = sublane % FIELDS < HELD
    for step, chunk_ref in enumerate(reversed(chunk_refs)):
        columns[block(lax.bitwise_xor(lev_at, step) * rows, rows), :] = chunk_ref[...]
    for row in range(rows):
        filtered = apply_matrix(matrix_ref, [tile(columns, group * rows + row) for group in range(chunks)], sublane)
        terms = [tile(members_ref, row * chunks + group) * value for group, value in enumerate(filtered)]
        for pack in range(chunks // 2):
            lower, upper = terms[2 * pack], terms[2 * pack + 1]
            total = jnp.where(first_member, lower, upper)
            total = total + jnp.where(first_member, pltpu.roll(lower, TILE - HELD, 0), pltpu.roll(upper, HELD, 0))
            set_tile(partial_ref, row * (chunks // 2) + pack, total)


def lift_body(chunks, parts, *refs):
    part_refs, refs = refs[:parts], refs[parts:]
    innovation_ref, huber_ref, members_ref, transposed_ref = refs[:4]
    chunk_refs, (weighted_ref, sorted_ref) = refs[4 : 4 + chunks], refs[4 + chunks :]
    rows = chunk_refs[0].shape[0] // TILE
    lev_at = lax.axis_index("lev")
    sublane = places()
    first_member = sublane % FIELDS < HELD
    increment = part_refs[0][...]
    for part_ref in part_refs[1:]:
        increment = increment + part_ref[...]
    residual = increment - innovation_ref[...]
    scale = HUBER / jnp.maximum(jnp.abs(residual), HUBER)
    weighted_ref[...] = jnp.where(huber_ref[...] == 1.0, scale, 1.0) * residual
    for row in range(rows):
        adjoint = []
        for pack in range(chunks // 2):
            weighted = tile(weighted_ref, row * (chunks // 2) + pack)
            lower = jnp.where(first_member, weighted, pltpu.roll(weighted, HELD, 0))
            upper = jnp.where(first_member, pltpu.roll(weighted, TILE - HELD, 0), weighted)
            for value in (lower, upper):
                adjoint.append(value * tile(members_ref, row * chunks + len(adjoint)))
        for group, value in enumerate(apply_matrix(transposed_ref, adjoint, sublane)):
            set_tile(sorted_ref, group * rows + row, value)
    for step, chunk_ref in enumerate(reversed(chunk_refs)):
        chunk_ref[...] = sorted_ref[block(lax.bitwise_xor(lev_at, step) * rows, rows), :]


def gather_body(halos, chunks, *refs):
    chunk_refs, field_ref, send_refs, sorted_ref = refs[:chunks], refs[chunks], refs[chunks + 1 : -1], refs[-1]
    lev_at = lax.axis_index("lev")
    mirrored = is_mirrored(halos)
    rows = chunk_refs[0].shape[0] // TILE
    own = rows * chunks
    for step, chunk_ref in enumerate(reversed(chunk_refs)):
        sorted_ref[block(lax.bitwise_xor(lev_at, step) * rows, rows), :] = chunk_ref[...]
    for row in range(own):
        set_tile(field_ref, row, sorted_ref[block(pick(mirrored, own, row), 1), :])
    for row in range(PASSES):
        if halos == 1:
            set_tile(send_refs[0], row, tile(field_ref, own - 1 - row))
        else:
            set_tile(send_refs[0], row, tile(field_ref, row))
            set_tile(send_refs[1], row, tile(field_ref, own - PASSES + row))


def to_fields(planes_ref, fields_ref, rows):
    for field in range(FIELDS):
        member, level = divmod(field, HELD)
        for half, lanes in halves():
            fields_ref[member, level, :, lanes] = planes_ref[pl.ds(half * FIELDS + field, rows, stride=TILE), :]


def interior_body(halos, field_ref, control_ref, *refs):
    own_refs, (fields_out, saved_out, result_ref) = refs[:4], refs[4:]
    own = field_ref.shape[0] // TILE
    mirrored = is_mirrored(halos)
    done = interior_passes(halos, field_ref, own_refs, saved_out)
    for row in range(own):
        value = done[row] + tile(control_ref, row) if row in done else jnp.zeros((TILE, LANES), jnp.float32)
        result_ref[block(pick(mirrored, own, row), 1), :] = value
    to_fields(result_ref, fields_out, own)


def backward_body(halos, control_ref, fields_ref, saved_ref, *refs):
    own_refs, tail_refs, halo_refs = refs[:4], refs[4:8], refs[8 : 8 + halos]
    gradient_hbm, refs = refs[8 + halos], refs[9 + halos :]
    result_refs, edge_refs, semaphores = refs[:halos], refs[halos : 2 * halos], refs[-1]
    own = fields_ref.shape[2]
    mirrored = is_mirrored(halos)
    if halos == 1:
        spans = [(PASSES * mirrored.astype(jnp.int32), own - PASSES)]
        spans.append((jnp.where(mirrored, 0, own - PASSES), PASSES))
    else:
        spans = [(PASSES, own - 2 * PASSES), (own - PASSES, PASSES), (0, PASSES)]
    copies = []

    def send(source_ref, source_start, start, rows):
        for field in range(FIELDS):
            member, level = divmod(field, HELD)
            copy = pltpu.make_async_copy(
                source_ref.at[member, level, pl.ds(source_start, rows), :],
                gradient_hbm.at[member, level, pl.ds(start, rows), :],
                semaphores.at[len(copies)],
            )
            copy.start()
            copies.append(copy)

    start = pl.multiple_of(spans[0][0], TILE)
    send(fields_ref, start, start, spans[0][1])
    halo_rows = [{own + row: tile(halo_refs[0], row) for row in range(PASSES)}]
    if halos == 2:
        halo_rows.append({row - PASSES: tile(halo_refs[1], row) for row in range(PASSES)})
    coefficient = coefficient_reader(own_refs, tail_refs, own)
    top = top_coefficient(halos, own_refs)
    done = wedge_passes(halos, halo_rows, own, saved_ref, coefficient, top)
    for side in range(halos):
        for row in range(PASSES):
            value = done[own - PASSES + row] + tile(control_ref, own - PASSES + row) if side == 0 else done[row] + tile(control_ref, row)
            result_refs[side][block(pick(mirrored, PASSES, row), 1), :] = value
        to_fields(result_refs[side], edge_refs[side], PASSES)
        send(edge_refs[side], 0, pl.multiple_of(spans[1 + side][0], TILE), PASSES)
    for copy in copies:
        copy.wait()


def per_device(control, members, east_coef, south_coef, innovation, huber_class, band, level_group_index):
    count, held, own, lon = control.shape
    levels, cells = members.shape[1:]
    chunks, parts, row_count = (lax.axis_size(axis) for axis in ("lev", "mem", "row"))
    assert (count * held, held, lon) == (FIELDS, HELD, HALVES * LANES)
    part = own // chunks
    halos = 1 if row_count == 2 else 2
    tail = 1 + halos * PASSES
    terms = len(matrix_terms(chunks))
    packed = part * levels // FIELDS

    control_near, east_near, south_near, *edges = call(
        pack_body,
        [pltpu.VMEM(x.shape, x.dtype) for x in (control, east_coef, south_coef)] + [planes(3 * PASSES)] * halos,
        remote(control, east_coef, south_coef),
        [pltpu.SemaphoreType.DMA((FIELDS + 2 * HELD,))],
        specs=[HBM] * 3,
    )
    halo = swap_edges(edges, "row")
    kept = halos * PASSES * 2
    *own_stencil, done_rows, saved, control_planes = call(
        functools.partial(prepare_body, halos),
        [planes(own)] * 3 + [planes(own + 1), planes(own), planes(kept), planes(own)],
        resident(control_near, east_near, south_near),
        [planes(own)] * 2,
    )
    members_planes, innovation_planes, huber_planes, matrix, transposed = call(
        columns_body,
        [planes(part * chunks), planes(packed), planes(packed), planes(terms), planes(terms)],
        [members, innovation, huber_class, band, level_group_index],
        [planes(part * chunks)],
        specs=[VMEM, VMEM, VMEM, SMEM, SMEM],
    )
    results = call(
        functools.partial(forward_body, halos),
        [planes(tail)] * 4 + [planes(part)] * chunks,
        resident(done_rows, saved, *own_stencil, *halo),
        [planes(own)],
    )
    tail_stencil = results[:4]
    columns = exchange(results[:3:-1], "lev")
    (partial,) = call(
        functools.partial(filter_body, chunks),
        [planes(packed)],
        resident(*columns[::-1], members_planes, matrix),
        [planes(part * chunks)],
    )
    partials = exchange([partial] * parts, "mem")
    lifted = call(
        functools.partial(lift_body, chunks, parts),
        [planes(part)] * chunks,
        resident(*partials, innovation_planes, huber_planes, members_planes, transposed),
        [planes(packed), planes(part * chunks)],
    )
    returned = exchange(lifted[::-1], "lev")
    gathered, *edges = call(
        functools.partial(gather_body, halos, chunks),
        [planes(own)] + [planes(PASSES)] * halos,
        resident(*returned[::-1]),
        [planes(own)],
    )
    halo = swap_edges(edges, "row")
    early, saved = call(
        functools.partial(interior_body, halos),
        [pltpu.VMEM(control.shape, jnp.float32), planes(kept)],
        resident(gathered, control_planes, *own_stencil),
        [planes(own)],
    )
    (gradient,) = call(
        functools.partial(backward_body, halos),
        [jax.ShapeDtypeStruct(control.shape, jnp.float32)],
        resident(control_planes, early, saved, *own_stencil, *tail_stencil, *halo),
        [planes(PASSES)] * halos
        + [pltpu.VMEM((count, held, PASSES, lon), jnp.float32)] * halos
        + [pltpu.SemaphoreType.DMA((FIELDS * (1 + halos),))],
        out_specs=[HBM],
    )
    return gradient


def solution(mesh):
    placed = (
        P("mem", "lev", "row", None),
        P("mem", None, ("row", "lev")),
        P("lev", "row", None),
        P("lev", "row", None),
        P(None, ("row", "lev")),
        P(None, ("row", "lev")),
        P(),
        P(),
    )
    return jax.shard_map(
        per_device,
        mesh=mesh,
        in_specs=placed,
        out_specs=P("mem", "lev", "row", None),
        check_vma=False,
    )
```

```python
import functools

import jax
import jax.numpy as jnp
from jax import lax
from jax.experimental import pallas as pl
from jax.experimental.pallas import tpu as pltpu
from jax.sharding import PartitionSpec as P

PASSES = 8
HUBER = 1.0
REACH = 3
LANES = 128
TILE = 8
HALVES = 2
HELD = 2
FIELDS = 4

VMEM = pl.BlockSpec(memory_space=pltpu.VMEM)
SMEM = pl.BlockSpec(memory_space=pltpu.SMEM)
HBM = pl.BlockSpec(memory_space=pltpu.HBM)


def planes(count):
    return pltpu.VMEM((count * TILE, LANES), jnp.float32)


def call(body, outs, operands, scratch=(), specs=None, out_specs=None, flops=0):
    total = sum(op.size * op.dtype.itemsize for op in operands)
    return pl.pallas_call(
        body,
        out_shape=outs,
        in_specs=specs or [VMEM] * len(operands),
        out_specs=out_specs or [VMEM] * len(outs),
        scratch_shapes=list(scratch),
        compiler_params=pltpu.CompilerParams(vmem_limit_bytes=32 * 1024 * 1024),
        cost_estimate=pl.CostEstimate(flops=flops, bytes_accessed=2 * total, transcendentals=0),
    )(*operands)


def resident(*arrays):
    return [pltpu.with_memory_space_constraint(array, pltpu.VMEM) for array in arrays]


def remote(*arrays):
    return [pltpu.with_memory_space_constraint(array, pltpu.HBM) for array in arrays]


def exchange(chunks, axis):
    count = len(chunks)
    received = list(chunks)
    for step in reversed(range(1, count)):
        received[step] = lax.ppermute(chunks[step], axis, [(i, i ^ step) for i in range(count)])
    return received


def swap_edges(edges, axis):
    count = lax.axis_size(axis)
    if len(edges) == 1:
        return [lax.ppermute(edges[0], axis, [(0, 1), (1, 0)])]
    head, tail = edges
    south = lax.ppermute(head, axis, [(i + 1, i) for i in range(count - 1)])
    north = lax.ppermute(tail, axis, [(i, i + 1) for i in range(count - 1)])
    return [south, north]


def tile(ref, row):
    return ref[row * TILE : (row + 1) * TILE, :]


def set_tile(ref, row, value):
    ref[row * TILE : (row + 1) * TILE, :] = value


def block(first_row, rows):
    return pl.ds(pl.multiple_of(first_row * TILE, TILE), rows * TILE)


def spread(ref, row, sublane, values):
    ref[pl.ds(row * TILE + sublane, values.shape[0], stride=TILE), :] = values


def places():
    return lax.broadcasted_iota(jnp.int32, (TILE, LANES), 0)


def east_west(value):
    lane = lax.broadcasted_iota(jnp.int32, (TILE, LANES), 1)
    other = pltpu.roll(value, FIELDS, 0)
    east = pltpu.roll(jnp.where(lane == 0, other, value), LANES - 1, 1)
    west = pltpu.roll(jnp.where(lane == LANES - 1, other, value), 1, 1)
    return east, west


def west_of(value):
    lane = lax.broadcasted_iota(jnp.int32, (TILE, LANES), 1)
    return pltpu.roll(jnp.where(lane == LANES - 1, pltpu.roll(value, FIELDS, 0), value), 1, 1)


def halves():
    return [(half, slice(half * LANES, (half + 1) * LANES)) for half in range(HALVES)]


def pack_body(control_hbm, east_hbm, south_hbm, control_ref, east_ref, south_ref, *refs):
    send_refs, semaphores = refs[:-1], refs[-1]
    pieces = [(east_hbm.at[level], east_ref.at[level]) for level in range(HELD)]
    pieces += [(south_hbm.at[level], south_ref.at[level]) for level in range(HELD)]
    for field in range(FIELDS):
        member, level = divmod(field, HELD)
        pieces.append((control_hbm.at[member, level], control_ref.at[member, level]))
    copies = [
        pltpu.make_async_copy(source, target, semaphores.at[index]) for index, (source, target) in enumerate(pieces)
    ]
    for copy in copies:
        copy.start()
    for copy in copies:
        copy.wait()
    own = control_ref.shape[2]
    first = lax.axis_index("row") == 0

    def edges(load):
        head = load(slice(0, 2 * PASSES))[:PASSES].astype(jnp.float32)
        tail = load(slice(own - 2 * PASSES, own))[PASSES:].astype(jnp.float32)
        return [jnp.where(first, tail, head)] if len(send_refs) == 1 else [head, tail]

    for half, lanes in halves():
        for field in range(FIELDS):
            member, level = divmod(field, HELD)
            at = half * FIELDS + field
            values = edges(lambda rows: control_ref[member, level, rows, lanes])
            for send_ref, value in zip(send_refs, values):
                spread(send_ref, 0, at, value)
            for kind, coef_ref in enumerate((east_ref, south_ref)):
                values = edges(lambda rows: coef_ref[level, rows, lanes])
                for send_ref, value in zip(send_refs, values):
                    spread(send_ref, (kind + 1) * PASSES, at, value)


def is_mirrored(halos):
    return halos == 1 and lax.axis_index("row") == 1


def pick(mirrored, count, row):
    return row if mirrored is False else jnp.where(mirrored, count - 1 - row, row)


def stencil(values, row, center, east, west, above, below):
    to_east, to_west = east_west(values[row])
    total = center * values[row] + below * values[row + 1]
    if above is not None:
        total = total + above * values[row - 1]
    return total + (east * to_east + west * to_west)


def interior_passes(halos, field_ref, own_refs, saved_ref):
    center_ref, east_ref, west_ref, face_ref = own_refs
    own = field_ref.shape[0] // TILE
    values = {row: tile(field_ref, row) for row in range(own)}
    for step in range(1, PASSES + 1):
        for side in range(halos):
            kept = (own - 1 - step, own - step) if side == 0 else (step - 1, step)
            for index, row in enumerate(kept):
                set_tile(saved_ref, (side * PASSES + step - 1) * 2 + index, values[row])
        after = {}
        for row in range(step if halos == 2 else 0, own - step):
            after[row] = stencil(
                values,
                row,
                tile(center_ref, row),
                tile(east_ref, row),
                tile(west_ref, row),
                tile(face_ref, row) if row else None,
                tile(face_ref, row + 1),
            )
        values = after
    return values


def wedge_passes(halos, halo_rows, own, saved_ref, coefficient, top):
    done = {}
    for side in range(halos):
        values = dict(halo_rows[side])
        for step in range(1, PASSES + 1):
            kept = (own - 1 - step, own - step) if side == 0 else (step - 1, step)
            for index, row in enumerate(kept):
                values[row] = tile(saved_ref, (side * PASSES + step - 1) * 2 + index)
            after = {}
            for row in range(own - step, own + PASSES - step) if side == 0 else range(step - PASSES, step):
                center, east, west, above = (coefficient(kind, row) for kind in range(4))
                after[row] = stencil(values, row, center, east, west, top if row == 0 else above, coefficient(3, row + 1))
            values = after
        done.update(values)
    return done


def prepare_body(halos, control_ref, east_ref, south_ref, *refs):
    own_refs, (rows_out, saved_out, field_ref, raw_east, raw_face) = refs[:4], refs[4:]
    center_out, east_out, west_out, face_out = own_refs
    own = control_ref.shape[2]
    mirrored = is_mirrored(halos)
    for half, lanes in halves():
        for field in range(FIELDS):
            member, level = divmod(field, HELD)
            at = half * FIELDS + field
            spread(rows_out, 0, at, control_ref[member, level, :, lanes].astype(jnp.float32))
            spread(raw_east, 0, at, east_ref[level, :, lanes])
            spread(raw_face, 0, at, south_ref[level, :, lanes])
    for row in range(own):
        source = pick(mirrored, own, row)
        set_tile(field_ref, row, rows_out[block(source, 1), :])
        east = raw_east[block(source, 1), :]
        set_tile(east_out, row, east)
        set_tile(west_out, row, west_of(east))
        if row == 0:
            face = tile(raw_face, 0)
            face = face if mirrored is False else jnp.where(mirrored, 0.0, face)
        else:
            face = raw_face[block(row if mirrored is False else jnp.where(mirrored, own - row, row), 1), :]
        set_tile(face_out, row, face)
    set_tile(face_out, own, tile(raw_face, 0))
    for row in range(own - 1):
        total = 1.0 - tile(east_out, row) - tile(west_out, row)
        set_tile(center_out, row, total - tile(face_out, row + 1) - tile(face_out, row))
    for row, value in interior_passes(halos, field_ref, own_refs, saved_out).items():
        set_tile(rows_out, row, value)


def finish_coefficients(halos, halo_refs, own_refs, tail_refs, own):
    _, east_own, west_own, face_own = own_refs
    center_tail, east_tail, west_tail, face_tail = tail_refs
    mirrored = is_mirrored(halos)

    def halo_tile(side, kind, row):
        return halo_refs[side][block(kind * PASSES + row, 1), :]

    set_tile(east_tail, 0, tile(east_own, own - 1))
    set_tile(west_tail, 0, tile(west_own, own - 1))
    set_tile(face_tail, 0, tile(face_own, own - 1))
    for row in range(PASSES):
        east = halo_tile(0, 1, pick(mirrored, PASSES, row))
        set_tile(east_tail, 1 + row, east)
        set_tile(west_tail, 1 + row, west_of(east))
        if mirrored is False:
            face = halo_tile(0, 2, row)
        elif row == 0:
            face = jnp.where(mirrored, tile(face_own, own), halo_tile(0, 2, 0))
        else:
            face = halo_tile(0, 2, jnp.where(mirrored, PASSES - row, row))
        set_tile(face_tail, 1 + row, face)
    for row in range(PASSES):
        total = 1.0 - tile(east_tail, row) - tile(west_tail, row)
        set_tile(center_tail, row, total - tile(face_tail, row + 1) - tile(face_tail, row))
    if halos == 2:
        for row in range(PASSES):
            at = 1 + PASSES + row
            east, face = halo_tile(1, 1, row), halo_tile(1, 2, row)
            below = halo_tile(1, 2, row + 1) if row + 1 < PASSES else tile(face_own, 0)
            west = west_of(east)
            for ref, value in zip(tail_refs, (1.0 - east - west - below - face, east, west, face)):
                set_tile(ref, at, value)


def coefficient_reader(own_refs, tail_refs, own):
    def coefficient(kind, row):
        if row < 0:
            return tile(tail_refs[kind], 1 + 2 * PASSES + row)
        return tile(own_refs[kind], row) if row < own - 1 else tile(tail_refs[kind], row - own + 1)

    return coefficient


def top_coefficient(halos, own_refs):
    return None if halos == 1 else jnp.where(lax.axis_index("row") == 0, 0.0, tile(own_refs[3], 0))


def forward_body(halos, rows_ref, saved_ref, *refs):
    own_refs, halo_refs, refs = refs[:4], refs[4 : 4 + halos], refs[4 + halos :]
    tail_refs, chunk_refs, sorted_ref = refs[:4], refs[4:-1], refs[-1]
    own = rows_ref.shape[0] // TILE
    lev_at = lax.axis_index("lev")
    mirrored = is_mirrored(halos)
    finish_coefficients(halos, halo_refs, own_refs, tail_refs, own)
    halo_rows = [{own + row: halo_refs[0][block(pick(mirrored, PASSES, row), 1), :] for row in range(PASSES)}]
    if halos == 2:
        halo_rows.append({row - PASSES: tile(halo_refs[1], row) for row in range(PASSES)})
    coefficient = coefficient_reader(own_refs, tail_refs, own)
    top = top_coefficient(halos, own_refs)
    done = wedge_passes(halos, halo_rows, own, saved_ref, coefficient, top)
    for row in range(own):
        value = done[row] if row in done else tile(rows_ref, row)
        sorted_ref[block(pick(mirrored, own, row), 1), :] = value
    part = own // len(chunk_refs)
    for step, chunk_ref in enumerate(reversed(chunk_refs)):
        chunk_ref[...] = sorted_ref[block(lax.bitwise_xor(lev_at, step) * part, part), :]


def matrix_terms(groups):
    return [
        (group, other, cross)
        for group in range(groups)
        for other in range(max(0, group - 2), min(groups, group + 3))
        for cross in range(2)
        if abs(group - other) < 2 or cross
    ]


def swap_levels(value, sublane):
    return jnp.where(sublane % HELD == 0, pltpu.roll(value, TILE - 1, 0), pltpu.roll(value, 1, 0))


def columns_body(members_ref, innovation_ref, huber_ref, band_ref, group_ref, *refs):
    members_out, innovation_out, huber_out, matrix_out, transposed_out, levels_ref = refs
    count, levels, cells = members_ref.shape
    groups, lon = levels // HELD, HALVES * LANES
    rows, packed = cells // lon, levels // FIELDS
    sublane = places()
    for member in range(count):
        for row in range(rows):
            for half in range(HALVES):
                lanes = slice(row * lon + half * LANES, row * lon + (half + 1) * LANES)
                start = ((member * rows + row) * HALVES + half) * levels
                levels_ref[start : start + levels, :] = members_ref[member, :, lanes].astype(jnp.float32)
                for level in range(HELD):
                    at = half * FIELDS + member * HELD + level
                    spread(members_out, row * groups, at, levels_ref[pl.ds(start + level, groups, stride=HELD), :])
    for row in range(rows):
        for half in range(HALVES):
            lanes = slice(row * lon + half * LANES, row * lon + (half + 1) * LANES)
            for pack in range(packed):
                source = slice(pack * FIELDS, (pack + 1) * FIELDS)
                start = (row * packed + pack) * TILE + half * FIELDS
                innovation_out[start : start + FIELDS, :] = innovation_ref[source, lanes]
                huber_out[start : start + FIELDS, :] = huber_ref[source, lanes].astype(jnp.float32)

    def entry(level, other):
        offset = other - level + REACH
        if not 0 <= offset < 2 * REACH + 1:
            return jnp.float32(0.0)
        value = band_ref[offset, level] + jnp.float32(1.0 if offset == REACH else 0.0)
        return jnp.where(group_ref[level] == group_ref[other], value, jnp.float32(0.0))

    for slot, (group, other, cross) in enumerate(matrix_terms(groups)):
        pairs = [(group * HELD + level, other * HELD + (level ^ cross)) for level in range(HELD)]
        even, odd = (entry(a, b) for a, b in pairs)
        set_tile(matrix_out, slot, jnp.where(sublane % HELD == 0, even, odd))
        even, odd = (entry(b, a) for a, b in pairs)
        set_tile(transposed_out, slot, jnp.where(sublane % HELD == 0, even, odd))


def apply_matrix(matrix_ref, values, sublane):
    crossed = [swap_levels(value, sublane) for value in values]
    totals = [None] * len(values)
    for slot, (group, other, cross) in enumerate(matrix_terms(len(values))):
        term = tile(matrix_ref, slot) * (crossed if cross else values)[other]
        totals[group] = term if totals[group] is None else totals[group] + term
    return totals


def filter_body(chunks, *refs):
    chunk_refs = refs[:chunks]
    members_ref, matrix_ref, partial_ref, columns = refs[chunks:]
    rows = chunk_refs[0].shape[0] // TILE
    lev_at = lax.axis_index("lev")
    sublane = places()
    first_member = sublane % FIELDS < HELD
    for step, chunk_ref in enumerate(reversed(chunk_refs)):
        columns[block(lax.bitwise_xor(lev_at, step) * rows, rows), :] = chunk_ref[...]
    for row in range(rows):
        filtered = apply_matrix(matrix_ref, [tile(columns, group * rows + row) for group in range(chunks)], sublane)
        terms = [tile(members_ref, row * chunks + group) * value for group, value in enumerate(filtered)]
        for pack in range(chunks // 2):
            lower, upper = terms[2 * pack], terms[2 * pack + 1]
            total = jnp.where(first_member, lower, upper)
            total = total + jnp.where(first_member, pltpu.roll(lower, TILE - HELD, 0), pltpu.roll(upper, HELD, 0))
            set_tile(partial_ref, row * (chunks // 2) + pack, total)


def lift_body(chunks, parts, *refs):
    part_refs, refs = refs[:parts], refs[parts:]
    innovation_ref, huber_ref, members_ref, transposed_ref = refs[:4]
    chunk_refs, (weighted_ref, sorted_ref) = refs[4 : 4 + chunks], refs[4 + chunks :]
    rows = chunk_refs[0].shape[0] // TILE
    lev_at = lax.axis_index("lev")
    sublane = places()
    first_member = sublane % FIELDS < HELD
    increment = part_refs[0][...]
    for part_ref in part_refs[1:]:
        increment = increment + part_ref[...]
    residual = increment - innovation_ref[...]
    scale = HUBER / jnp.maximum(jnp.abs(residual), HUBER)
    weighted_ref[...] = jnp.where(huber_ref[...] == 1.0, scale, 1.0) * residual
    for row in range(rows):
        adjoint = []
        for pack in range(chunks // 2):
            weighted = tile(weighted_ref, row * (chunks // 2) + pack)
            lower = jnp.where(first_member, weighted, pltpu.roll(weighted, HELD, 0))
            upper = jnp.where(first_member, pltpu.roll(weighted, TILE - HELD, 0), weighted)
            for value in (lower, upper):
                adjoint.append(value * tile(members_ref, row * chunks + len(adjoint)))
        for group, value in enumerate(apply_matrix(transposed_ref, adjoint, sublane)):
            set_tile(sorted_ref, group * rows + row, value)
    for step, chunk_ref in enumerate(reversed(chunk_refs)):
        chunk_ref[...] = sorted_ref[block(lax.bitwise_xor(lev_at, step) * rows, rows), :]


def gather_body(halos, chunks, *refs):
    chunk_refs, field_ref, send_refs, sorted_ref = refs[:chunks], refs[chunks], refs[chunks + 1 : -1], refs[-1]
    lev_at = lax.axis_index("lev")
    mirrored = is_mirrored(halos)
    rows = chunk_refs[0].shape[0] // TILE
    own = rows * chunks
    for step, chunk_ref in enumerate(reversed(chunk_refs)):
        sorted_ref[block(lax.bitwise_xor(lev_at, step) * rows, rows), :] = chunk_ref[...]
    for row in range(own):
        set_tile(field_ref, row, sorted_ref[block(pick(mirrored, own, row), 1), :])
    for row in range(PASSES):
        if halos == 1:
            set_tile(send_refs[0], row, tile(field_ref, own - 1 - row))
        else:
            set_tile(send_refs[0], row, tile(field_ref, row))
            set_tile(send_refs[1], row, tile(field_ref, own - PASSES + row))


def to_fields(planes_ref, fields_ref, rows):
    for field in range(FIELDS):
        member, level = divmod(field, HELD)
        for half, lanes in halves():
            fields_ref[member, level, :, lanes] = planes_ref[pl.ds(half * FIELDS + field, rows, stride=TILE), :]


def interior_body(halos, field_ref, control_ref, *refs):
    own_refs, (fields_out, saved_out, result_ref) = refs[:4], refs[4:]
    own = field_ref.shape[0] // TILE
    mirrored = is_mirrored(halos)
    done = interior_passes(halos, field_ref, own_refs, saved_out)
    for row in range(own):
        value = done[row] + tile(control_ref, row) if row in done else jnp.zeros((TILE, LANES), jnp.float32)
        result_ref[block(pick(mirrored, own, row), 1), :] = value
    to_fields(result_ref, fields_out, own)


def backward_body(halos, control_ref, fields_ref, saved_ref, *refs):
    own_refs, tail_refs, halo_refs = refs[:4], refs[4:8], refs[8 : 8 + halos]
    gradient_hbm, refs = refs[8 + halos], refs[9 + halos :]
    result_refs, edge_refs, semaphores = refs[:halos], refs[halos : 2 * halos], refs[-1]
    own = fields_ref.shape[2]
    mirrored = is_mirrored(halos)
    if halos == 1:
        spans = [(PASSES * mirrored.astype(jnp.int32), own - PASSES)]
        spans.append((jnp.where(mirrored, 0, own - PASSES), PASSES))
    else:
        spans = [(PASSES, own - 2 * PASSES), (own - PASSES, PASSES), (0, PASSES)]
    copies = []

    def send(source_ref, source_start, start, rows):
        for field in range(FIELDS):
            member, level = divmod(field, HELD)
            copy = pltpu.make_async_copy(
                source_ref.at[member, level, pl.ds(source_start, rows), :],
                gradient_hbm.at[member, level, pl.ds(start, rows), :],
                semaphores.at[len(copies)],
            )
            copy.start()
            copies.append(copy)

    start = pl.multiple_of(spans[0][0], TILE)
    send(fields_ref, start, start, spans[0][1])
    halo_rows = [{own + row: tile(halo_refs[0], row) for row in range(PASSES)}]
    if halos == 2:
        halo_rows.append({row - PASSES: tile(halo_refs[1], row) for row in range(PASSES)})
    coefficient = coefficient_reader(own_refs, tail_refs, own)
    top = top_coefficient(halos, own_refs)
    done = wedge_passes(halos, halo_rows, own, saved_ref, coefficient, top)
    for side in range(halos):
        for row in range(PASSES):
            value = done[own - PASSES + row] + tile(control_ref, own - PASSES + row) if side == 0 else done[row] + tile(control_ref, row)
            result_refs[side][block(pick(mirrored, PASSES, row), 1), :] = value
        to_fields(result_refs[side], edge_refs[side], PASSES)
        send(edge_refs[side], 0, pl.multiple_of(spans[1 + side][0], TILE), PASSES)
    for copy in copies:
        copy.wait()


def per_device(control, members, east_coef, south_coef, innovation, huber_class, band, level_group_index):
    count, held, own, lon = control.shape
    levels, cells = members.shape[1:]
    chunks, parts, row_count = (lax.axis_size(axis) for axis in ("lev", "mem", "row"))
    assert (count * held, held, lon) == (FIELDS, HELD, HALVES * LANES)
    part = own // chunks
    halos = 1 if row_count == 2 else 2
    tail = 1 + halos * PASSES
    terms = len(matrix_terms(chunks))
    packed = part * levels // FIELDS

    control_near, east_near, south_near, *edges = call(
        pack_body,
        [pltpu.VMEM(x.shape, x.dtype) for x in (control, east_coef, south_coef)] + [planes(3 * PASSES)] * halos,
        remote(control, east_coef, south_coef),
        [pltpu.SemaphoreType.DMA((FIELDS + 2 * HELD,))],
        specs=[HBM] * 3,
    )
    halo = swap_edges(edges, "row")
    kept = halos * PASSES * 2
    *own_stencil, done_rows, saved, control_planes = call(
        functools.partial(prepare_body, halos),
        [planes(own)] * 3 + [planes(own + 1), planes(own), planes(kept), planes(own)],
        resident(control_near, east_near, south_near),
        [planes(own)] * 2,
    )
    members_planes, innovation_planes, huber_planes, matrix, transposed = call(
        columns_body,
        [planes(part * chunks), planes(packed), planes(packed), planes(terms), planes(terms)],
        [members, innovation, huber_class, band, level_group_index],
        [planes(part * chunks)],
        specs=[VMEM, VMEM, VMEM, SMEM, SMEM],
    )
    results = call(
        functools.partial(forward_body, halos),
        [planes(tail)] * 4 + [planes(part)] * chunks,
        resident(done_rows, saved, *own_stencil, *halo),
        [planes(own)],
    )
    tail_stencil = results[:4]
    columns = exchange(results[:3:-1], "lev")
    (partial,) = call(
        functools.partial(filter_body, chunks),
        [planes(packed)],
        resident(*columns[::-1], members_planes, matrix),
        [planes(part * chunks)],
    )
    partials = exchange([partial] * parts, "mem")
    far = parts // 2
    partials = [partials[step] for step in (0, far, *(step for step in range(1, parts) if step != far))]
    lifted = call(
        functools.partial(lift_body, chunks, parts),
        [planes(part)] * chunks,
        resident(*partials, innovation_planes, huber_planes, members_planes, transposed),
        [planes(packed), planes(part * chunks)],
    )
    returned = exchange(lifted[::-1], "lev")
    gathered, *edges = call(
        functools.partial(gather_body, halos, chunks),
        [planes(own)] + [planes(PASSES)] * halos,
        resident(*returned[::-1]),
        [planes(own)],
    )
    halo = swap_edges(edges, "row")
    early, saved = call(
        functools.partial(interior_body, halos),
        [pltpu.VMEM(control.shape, jnp.float32), planes(kept)],
        resident(gathered, control_planes, *own_stencil),
        [planes(own)],
    )
    (gradient,) = call(
        functools.partial(backward_body, halos),
        [jax.ShapeDtypeStruct(control.shape, jnp.float32)],
        resident(control_planes, early, saved, *own_stencil, *tail_stencil, *halo),
        [planes(PASSES)] * halos
        + [pltpu.VMEM((count, held, PASSES, lon), jnp.float32)] * halos
        + [pltpu.SemaphoreType.DMA((FIELDS * (1 + halos),))],
        out_specs=[HBM],
    )
    return gradient


def solution(mesh):
    placed = (
        P("mem", "lev", "row", None),
        P("mem", None, ("row", "lev")),
        P("lev", "row", None),
        P("lev", "row", None),
        P(None, ("row", "lev")),
        P(None, ("row", "lev")),
        P(),
        P(),
    )
    return jax.shard_map(
        per_device,
        mesh=mesh,
        in_specs=placed,
        out_specs=P("mem", "lev", "row", None),
        check_vma=False,
    )
```

```python
import functools

import jax
import jax.numpy as jnp
from jax import lax
from jax.experimental import pallas as pl
from jax.experimental.pallas import tpu as pltpu
from jax.sharding import PartitionSpec as P

PASSES = 8
HUBER = 1.0
REACH = 3
LANES = 128
TILE = 8
HALVES = 2
HELD = 2
FIELDS = 4

VMEM = pl.BlockSpec(memory_space=pltpu.VMEM)
SMEM = pl.BlockSpec(memory_space=pltpu.SMEM)
HBM = pl.BlockSpec(memory_space=pltpu.HBM)


def planes(count):
    return pltpu.VMEM((count * TILE, LANES), jnp.float32)


def call(body, outs, operands, scratch=(), specs=None, out_specs=None, flops=0):
    total = sum(op.size * op.dtype.itemsize for op in operands)
    return pl.pallas_call(
        body,
        out_shape=outs,
        in_specs=specs or [VMEM] * len(operands),
        out_specs=out_specs or [VMEM] * len(outs),
        scratch_shapes=list(scratch),
        compiler_params=pltpu.CompilerParams(vmem_limit_bytes=32 * 1024 * 1024),
        cost_estimate=pl.CostEstimate(flops=flops, bytes_accessed=2 * total, transcendentals=0),
    )(*operands)


def resident(*arrays):
    return [pltpu.with_memory_space_constraint(array, pltpu.VMEM) for array in arrays]


def remote(*arrays):
    return [pltpu.with_memory_space_constraint(array, pltpu.HBM) for array in arrays]


def exchange(chunks, axis):
    count = len(chunks)
    received = list(chunks)
    for step in reversed(range(1, count)):
        received[step] = lax.ppermute(chunks[step], axis, [(i, i ^ step) for i in range(count)])
    return received


def collect(array, axis):
    count = lax.axis_size(axis)
    shifts = [[(i, (i + step) % count) for i in range(count)] for step in range(1, count)]
    return [array] + [lax.ppermute(array, axis, shift) for shift in shifts]


def swap_edges(edges, axis):
    count = lax.axis_size(axis)
    if len(edges) == 1:
        return [lax.ppermute(edges[0], axis, [(0, 1), (1, 0)])]
    head, tail = edges
    south = lax.ppermute(head, axis, [(i + 1, i) for i in range(count - 1)])
    north = lax.ppermute(tail, axis, [(i, i + 1) for i in range(count - 1)])
    return [south, north]


def tile(ref, row):
    return ref[row * TILE : (row + 1) * TILE, :]


def set_tile(ref, row, value):
    ref[row * TILE : (row + 1) * TILE, :] = value


def block(first_row, rows):
    return pl.ds(pl.multiple_of(first_row * TILE, TILE), rows * TILE)


def spread(ref, row, sublane, values):
    ref[pl.ds(row * TILE + sublane, values.shape[0], stride=TILE), :] = values


def places():
    return lax.broadcasted_iota(jnp.int32, (TILE, LANES), 0)


def east_west(value):
    lane = lax.broadcasted_iota(jnp.int32, (TILE, LANES), 1)
    other = pltpu.roll(value, FIELDS, 0)
    east = pltpu.roll(jnp.where(lane == 0, other, value), LANES - 1, 1)
    west = pltpu.roll(jnp.where(lane == LANES - 1, other, value), 1, 1)
    return east, west


def west_of(value):
    lane = lax.broadcasted_iota(jnp.int32, (TILE, LANES), 1)
    return pltpu.roll(jnp.where(lane == LANES - 1, pltpu.roll(value, FIELDS, 0), value), 1, 1)


def halves():
    return [(half, slice(half * LANES, (half + 1) * LANES)) for half in range(HALVES)]


def pack_body(control_hbm, east_hbm, south_hbm, control_ref, east_ref, south_ref, *refs):
    send_refs, semaphores = refs[:-1], refs[-1]
    pieces = [(east_hbm.at[level], east_ref.at[level]) for level in range(HELD)]
    pieces += [(south_hbm.at[level], south_ref.at[level]) for level in range(HELD)]
    for field in range(FIELDS):
        member, level = divmod(field, HELD)
        pieces.append((control_hbm.at[member, level], control_ref.at[member, level]))
    copies = [
        pltpu.make_async_copy(source, target, semaphores.at[index]) for index, (source, target) in enumerate(pieces)
    ]
    for copy in copies:
        copy.start()
    for copy in copies:
        copy.wait()
    own = control_ref.shape[2]
    first = lax.axis_index("row") == 0

    def edges(load):
        head = load(slice(0, 2 * PASSES))[:PASSES].astype(jnp.float32)
        tail = load(slice(own - 2 * PASSES, own))[PASSES:].astype(jnp.float32)
        return [jnp.where(first, tail, head)] if len(send_refs) == 1 else [head, tail]

    for half, lanes in halves():
        for field in range(FIELDS):
            member, level = divmod(field, HELD)
            at = half * FIELDS + field
            values = edges(lambda rows: control_ref[member, level, rows, lanes])
            for send_ref, value in zip(send_refs, values):
                spread(send_ref, 0, at, value)
            for kind, coef_ref in enumerate((east_ref, south_ref)):
                values = edges(lambda rows: coef_ref[level, rows, lanes])
                for send_ref, value in zip(send_refs, values):
                    spread(send_ref, (kind + 1) * PASSES, at, value)


def is_mirrored(halos):
    return halos == 1 and lax.axis_index("row") == 1


def pick(mirrored, count, row):
    return row if mirrored is False else jnp.where(mirrored, count - 1 - row, row)


def stencil(values, row, center, east, west, above, below):
    to_east, to_west = east_west(values[row])
    total = center * values[row] + below * values[row + 1]
    if above is not None:
        total = total + above * values[row - 1]
    return total + (east * to_east + west * to_west)


def interior_passes(halos, field_ref, own_refs, saved_ref):
    center_ref, east_ref, west_ref, face_ref = own_refs
    own = field_ref.shape[0] // TILE
    values = {row: tile(field_ref, row) for row in range(own)}
    for step in range(1, PASSES + 1):
        for side in range(halos):
            kept = (own - 1 - step, own - step) if side == 0 else (step - 1, step)
            for index, row in enumerate(kept):
                set_tile(saved_ref, (side * PASSES + step - 1) * 2 + index, values[row])
        after = {}
        for row in range(step if halos == 2 else 0, own - step):
            after[row] = stencil(
                values,
                row,
                tile(center_ref, row),
                tile(east_ref, row),
                tile(west_ref, row),
                tile(face_ref, row) if row else None,
                tile(face_ref, row + 1),
            )
        values = after
    return values


def wedge_passes(halos, halo_rows, own, saved_ref, coefficient, top):
    done = {}
    for side in range(halos):
        values = dict(halo_rows[side])
        for step in range(1, PASSES + 1):
            kept = (own - 1 - step, own - step) if side == 0 else (step - 1, step)
            for index, row in enumerate(kept):
                values[row] = tile(saved_ref, (side * PASSES + step - 1) * 2 + index)
            after = {}
            for row in range(own - step, own + PASSES - step) if side == 0 else range(step - PASSES, step):
                center, east, west, above = (coefficient(kind, row) for kind in range(4))
                after[row] = stencil(values, row, center, east, west, top if row == 0 else above, coefficient(3, row + 1))
            values = after
        done.update(values)
    return done


def prepare_body(halos, control_ref, east_ref, south_ref, *refs):
    own_refs, (rows_out, saved_out, field_ref, raw_east, raw_face) = refs[:4], refs[4:]
    center_out, east_out, west_out, face_out = own_refs
    own = control_ref.shape[2]
    mirrored = is_mirrored(halos)
    for half, lanes in halves():
        for field in range(FIELDS):
            member, level = divmod(field, HELD)
            at = half * FIELDS + field
            spread(rows_out, 0, at, control_ref[member, level, :, lanes].astype(jnp.float32))
            spread(raw_east, 0, at, east_ref[level, :, lanes])
            spread(raw_face, 0, at, south_ref[level, :, lanes])
    for row in range(own):
        source = pick(mirrored, own, row)
        set_tile(field_ref, row, rows_out[block(source, 1), :])
        east = raw_east[block(source, 1), :]
        set_tile(east_out, row, east)
        set_tile(west_out, row, west_of(east))
        if row == 0:
            face = tile(raw_face, 0)
            face = face if mirrored is False else jnp.where(mirrored, 0.0, face)
        else:
            face = raw_face[block(row if mirrored is False else jnp.where(mirrored, own - row, row), 1), :]
        set_tile(face_out, row, face)
    set_tile(face_out, own, tile(raw_face, 0))
    for row in range(own - 1):
        total = 1.0 - tile(east_out, row) - tile(west_out, row)
        set_tile(center_out, row, total - tile(face_out, row + 1) - tile(face_out, row))
    for row, value in interior_passes(halos, field_ref, own_refs, saved_out).items():
        set_tile(rows_out, row, value)


def finish_coefficients(halos, halo_refs, own_refs, tail_refs, own):
    _, east_own, west_own, face_own = own_refs
    center_tail, east_tail, west_tail, face_tail = tail_refs
    mirrored = is_mirrored(halos)

    def halo_tile(side, kind, row):
        return halo_refs[side][block(kind * PASSES + row, 1), :]

    set_tile(east_tail, 0, tile(east_own, own - 1))
    set_tile(west_tail, 0, tile(west_own, own - 1))
    set_tile(face_tail, 0, tile(face_own, own - 1))
    for row in range(PASSES):
        east = halo_tile(0, 1, pick(mirrored, PASSES, row))
        set_tile(east_tail, 1 + row, east)
        set_tile(west_tail, 1 + row, west_of(east))
        if mirrored is False:
            face = halo_tile(0, 2, row)
        elif row == 0:
            face = jnp.where(mirrored, tile(face_own, own), halo_tile(0, 2, 0))
        else:
            face = halo_tile(0, 2, jnp.where(mirrored, PASSES - row, row))
        set_tile(face_tail, 1 + row, face)
    for row in range(PASSES):
        total = 1.0 - tile(east_tail, row) - tile(west_tail, row)
        set_tile(center_tail, row, total - tile(face_tail, row + 1) - tile(face_tail, row))
    if halos == 2:
        for row in range(PASSES):
            at = 1 + PASSES + row
            east, face = halo_tile(1, 1, row), halo_tile(1, 2, row)
            below = halo_tile(1, 2, row + 1) if row + 1 < PASSES else tile(face_own, 0)
            west = west_of(east)
            for ref, value in zip(tail_refs, (1.0 - east - west - below - face, east, west, face)):
                set_tile(ref, at, value)


def coefficient_reader(own_refs, tail_refs, own):
    def coefficient(kind, row):
        if row < 0:
            return tile(tail_refs[kind], 1 + 2 * PASSES + row)
        return tile(own_refs[kind], row) if row < own - 1 else tile(tail_refs[kind], row - own + 1)

    return coefficient


def top_coefficient(halos, own_refs):
    return None if halos == 1 else jnp.where(lax.axis_index("row") == 0, 0.0, tile(own_refs[3], 0))


def forward_body(halos, rows_ref, saved_ref, *refs):
    own_refs, halo_refs, refs = refs[:4], refs[4 : 4 + halos], refs[4 + halos :]
    tail_refs, chunk_refs, sorted_ref = refs[:4], refs[4:-1], refs[-1]
    own = rows_ref.shape[0] // TILE
    lev_at = lax.axis_index("lev")
    mirrored = is_mirrored(halos)
    finish_coefficients(halos, halo_refs, own_refs, tail_refs, own)
    halo_rows = [{own + row: halo_refs[0][block(pick(mirrored, PASSES, row), 1), :] for row in range(PASSES)}]
    if halos == 2:
        halo_rows.append({row - PASSES: tile(halo_refs[1], row) for row in range(PASSES)})
    coefficient = coefficient_reader(own_refs, tail_refs, own)
    top = top_coefficient(halos, own_refs)
    done = wedge_passes(halos, halo_rows, own, saved_ref, coefficient, top)
    for row in range(own):
        value = done[row] if row in done else tile(rows_ref, row)
        sorted_ref[block(pick(mirrored, own, row), 1), :] = value
    part = own // len(chunk_refs)
    for step, chunk_ref in enumerate(reversed(chunk_refs)):
        chunk_ref[...] = sorted_ref[block(lax.bitwise_xor(lev_at, step) * part, part), :]


def matrix_terms(groups):
    return [
        (group, other, cross)
        for group in range(groups)
        for other in range(max(0, group - 2), min(groups, group + 3))
        for cross in range(2)
        if abs(group - other) < 2 or cross
    ]


def swap_levels(value, sublane):
    return jnp.where(sublane % HELD == 0, pltpu.roll(value, TILE - 1, 0), pltpu.roll(value, 1, 0))


def columns_body(members_ref, innovation_ref, huber_ref, band_ref, group_ref, *refs):
    members_out, innovation_out, huber_out, matrix_out, transposed_out, levels_ref = refs
    count, levels, cells = members_ref.shape
    groups, lon = levels // HELD, HALVES * LANES
    rows, packed = cells // lon, levels // FIELDS
    sublane = places()
    for member in range(count):
        for row in range(rows):
            for half in range(HALVES):
                lanes = slice(row * lon + half * LANES, row * lon + (half + 1) * LANES)
                start = ((member * rows + row) * HALVES + half) * levels
                levels_ref[start : start + levels, :] = members_ref[member, :, lanes].astype(jnp.float32)
                for level in range(HELD):
                    at = half * FIELDS + member * HELD + level
                    spread(members_out, row * groups, at, levels_ref[pl.ds(start + level, groups, stride=HELD), :])
    for row in range(rows):
        for half in range(HALVES):
            lanes = slice(row * lon + half * LANES, row * lon + (half + 1) * LANES)
            for pack in range(packed):
                source = slice(pack * FIELDS, (pack + 1) * FIELDS)
                start = (row * packed + pack) * TILE + half * FIELDS
                innovation_out[start : start + FIELDS, :] = innovation_ref[source, lanes]
                huber_out[start : start + FIELDS, :] = huber_ref[source, lanes].astype(jnp.float32)

    def entry(level, other):
        offset = other - level + REACH
        if not 0 <= offset < 2 * REACH + 1:
            return jnp.float32(0.0)
        value = band_ref[offset, level] + jnp.float32(1.0 if offset == REACH else 0.0)
        return jnp.where(group_ref[level] == group_ref[other], value, jnp.float32(0.0))

    for slot, (group, other, cross) in enumerate(matrix_terms(groups)):
        pairs = [(group * HELD + level, other * HELD + (level ^ cross)) for level in range(HELD)]
        even, odd = (entry(a, b) for a, b in pairs)
        set_tile(matrix_out, slot, jnp.where(sublane % HELD == 0, even, odd))
        even, odd = (entry(b, a) for a, b in pairs)
        set_tile(transposed_out, slot, jnp.where(sublane % HELD == 0, even, odd))


def apply_matrix(matrix_ref, values, sublane):
    crossed = [swap_levels(value, sublane) for value in values]
    totals = [None] * len(values)
    for slot, (group, other, cross) in enumerate(matrix_terms(len(values))):
        term = tile(matrix_ref, slot) * (crossed if cross else values)[other]
        totals[group] = term if totals[group] is None else totals[group] + term
    return totals


def filter_body(chunks, *refs):
    chunk_refs = refs[:chunks]
    members_ref, matrix_ref, partial_ref, columns = refs[chunks:]
    rows = chunk_refs[0].shape[0] // TILE
    lev_at = lax.axis_index("lev")
    sublane = places()
    first_member = sublane % FIELDS < HELD
    for step, chunk_ref in enumerate(reversed(chunk_refs)):
        columns[block(lax.bitwise_xor(lev_at, step) * rows, rows), :] = chunk_ref[...]
    for row in range(rows):
        filtered = apply_matrix(matrix_ref, [tile(columns, group * rows + row) for group in range(chunks)], sublane)
        terms = [tile(members_ref, row * chunks + group) * value for group, value in enumerate(filtered)]
        for pack in range(chunks // 2):
            lower, upper = terms[2 * pack], terms[2 * pack + 1]
            total = jnp.where(first_member, lower, upper)
            total = total + jnp.where(first_member, pltpu.roll(lower, TILE - HELD, 0), pltpu.roll(upper, HELD, 0))
            set_tile(partial_ref, row * (chunks // 2) + pack, total)


def lift_body(chunks, parts, *refs):
    part_refs, refs = refs[:parts], refs[parts:]
    innovation_ref, huber_ref, members_ref, transposed_ref = refs[:4]
    chunk_refs, (weighted_ref, sorted_ref) = refs[4 : 4 + chunks], refs[4 + chunks :]
    rows = chunk_refs[0].shape[0] // TILE
    lev_at = lax.axis_index("lev")
    sublane = places()
    first_member = sublane % FIELDS < HELD
    increment = part_refs[0][...]
    for part_ref in part_refs[1:]:
        increment = increment + part_ref[...]
    residual = increment - innovation_ref[...]
    scale = HUBER / jnp.maximum(jnp.abs(residual), HUBER)
    weighted_ref[...] = jnp.where(huber_ref[...] == 1.0, scale, 1.0) * residual
    for row in range(rows):
        adjoint = []
        for pack in range(chunks // 2):
            weighted = tile(weighted_ref, row * (chunks // 2) + pack)
            lower = jnp.where(first_member, weighted, pltpu.roll(weighted, HELD, 0))
            upper = jnp.where(first_member, pltpu.roll(weighted, TILE - HELD, 0), weighted)
            for value in (lower, upper):
                adjoint.append(value * tile(members_ref, row * chunks + len(adjoint)))
        for group, value in enumerate(apply_matrix(transposed_ref, adjoint, sublane)):
            set_tile(sorted_ref, group * rows + row, value)
    for step, chunk_ref in enumerate(reversed(chunk_refs)):
        chunk_ref[...] = sorted_ref[block(lax.bitwise_xor(lev_at, step) * rows, rows), :]


def gather_body(halos, chunks, *refs):
    chunk_refs, field_ref, send_refs, sorted_ref = refs[:chunks], refs[chunks], refs[chunks + 1 : -1], refs[-1]
    lev_at = lax.axis_index("lev")
    mirrored = is_mirrored(halos)
    rows = chunk_refs[0].shape[0] // TILE
    own = rows * chunks
    for step, chunk_ref in enumerate(reversed(chunk_refs)):
        sorted_ref[block(lax.bitwise_xor(lev_at, step) * rows, rows), :] = chunk_ref[...]
    for row in range(own):
        set_tile(field_ref, row, sorted_ref[block(pick(mirrored, own, row), 1), :])
    for row in range(PASSES):
        if halos == 1:
            set_tile(send_refs[0], row, tile(field_ref, own - 1 - row))
        else:
            set_tile(send_refs[0], row, tile(field_ref, row))
            set_tile(send_refs[1], row, tile(field_ref, own - PASSES + row))


def to_fields(planes_ref, fields_ref, rows):
    for field in range(FIELDS):
        member, level = divmod(field, HELD)
        for half, lanes in halves():
            fields_ref[member, level, :, lanes] = planes_ref[pl.ds(half * FIELDS + field, rows, stride=TILE), :]


def interior_body(halos, field_ref, control_ref, *refs):
    own_refs, (fields_out, saved_out, result_ref) = refs[:4], refs[4:]
    own = field_ref.shape[0] // TILE
    mirrored = is_mirrored(halos)
    done = interior_passes(halos, field_ref, own_refs, saved_out)
    for row in range(own):
        value = done[row] + tile(control_ref, row) if row in done else jnp.zeros((TILE, LANES), jnp.float32)
        result_ref[block(pick(mirrored, own, row), 1), :] = value
    to_fields(result_ref, fields_out, own)


def backward_body(halos, control_ref, fields_ref, saved_ref, *refs):
    own_refs, tail_refs, halo_refs = refs[:4], refs[4:8], refs[8 : 8 + halos]
    gradient_hbm, refs = refs[8 + halos], refs[9 + halos :]
    result_refs, edge_refs, semaphores = refs[:halos], refs[halos : 2 * halos], refs[-1]
    own = fields_ref.shape[2]
    mirrored = is_mirrored(halos)
    if halos == 1:
        spans = [(PASSES * mirrored.astype(jnp.int32), own - PASSES)]
        spans.append((jnp.where(mirrored, 0, own - PASSES), PASSES))
    else:
        spans = [(PASSES, own - 2 * PASSES), (own - PASSES, PASSES), (0, PASSES)]
    copies = []

    def send(source_ref, source_start, start, rows):
        for field in range(FIELDS):
            member, level = divmod(field, HELD)
            copy = pltpu.make_async_copy(
                source_ref.at[member, level, pl.ds(source_start, rows), :],
                gradient_hbm.at[member, level, pl.ds(start, rows), :],
                semaphores.at[len(copies)],
            )
            copy.start()
            copies.append(copy)

    start = pl.multiple_of(spans[0][0], TILE)
    send(fields_ref, start, start, spans[0][1])
    halo_rows = [{own + row: tile(halo_refs[0], row) for row in range(PASSES)}]
    if halos == 2:
        halo_rows.append({row - PASSES: tile(halo_refs[1], row) for row in range(PASSES)})
    coefficient = coefficient_reader(own_refs, tail_refs, own)
    top = top_coefficient(halos, own_refs)
    done = wedge_passes(halos, halo_rows, own, saved_ref, coefficient, top)
    for side in range(halos):
        for row in range(PASSES):
            value = done[own - PASSES + row] + tile(control_ref, own - PASSES + row) if side == 0 else done[row] + tile(control_ref, row)
            result_refs[side][block(pick(mirrored, PASSES, row), 1), :] = value
        to_fields(result_refs[side], edge_refs[side], PASSES)
        send(edge_refs[side], 0, pl.multiple_of(spans[1 + side][0], TILE), PASSES)
    for copy in copies:
        copy.wait()


def per_device(control, members, east_coef, south_coef, innovation, huber_class, band, level_group_index):
    count, held, own, lon = control.shape
    levels, cells = members.shape[1:]
    chunks, parts, row_count = (lax.axis_size(axis) for axis in ("lev", "mem", "row"))
    assert (count * held, held, lon) == (FIELDS, HELD, HALVES * LANES)
    part = own // chunks
    halos = 1 if row_count == 2 else 2
    tail = 1 + halos * PASSES
    terms = len(matrix_terms(chunks))
    packed = part * levels // FIELDS

    control_near, east_near, south_near, *edges = call(
        pack_body,
        [pltpu.VMEM(x.shape, x.dtype) for x in (control, east_coef, south_coef)] + [planes(3 * PASSES)] * halos,
        remote(control, east_coef, south_coef),
        [pltpu.SemaphoreType.DMA((FIELDS + 2 * HELD,))],
        specs=[HBM] * 3,
    )
    halo = swap_edges(edges, "row")
    kept = halos * PASSES * 2
    *own_stencil, done_rows, saved, control_planes = call(
        functools.partial(prepare_body, halos),
        [planes(own)] * 3 + [planes(own + 1), planes(own), planes(kept), planes(own)],
        resident(control_near, east_near, south_near),
        [planes(own)] * 2,
    )
    members_planes, innovation_planes, huber_planes, matrix, transposed = call(
        columns_body,
        [planes(part * chunks), planes(packed), planes(packed), planes(terms), planes(terms)],
        [members, innovation, huber_class, band, level_group_index],
        [planes(part * chunks)],
        specs=[VMEM, VMEM, VMEM, SMEM, SMEM],
    )
    results = call(
        functools.partial(forward_body, halos),
        [planes(tail)] * 4 + [planes(part)] * chunks,
        resident(done_rows, saved, *own_stencil, *halo),
        [planes(own)],
    )
    tail_stencil = results[:4]
    columns = exchange(results[:3:-1], "lev")
    (partial,) = call(
        functools.partial(filter_body, chunks),
        [planes(packed)],
        resident(*columns[::-1], members_planes, matrix),
        [planes(part * chunks)],
    )
    partials = collect(partial, "mem")
    lifted = call(
        functools.partial(lift_body, chunks, parts),
        [planes(part)] * chunks,
        resident(*partials, innovation_planes, huber_planes, members_planes, transposed),
        [planes(packed), planes(part * chunks)],
    )
    returned = exchange(lifted[::-1], "lev")
    gathered, *edges = call(
        functools.partial(gather_body, halos, chunks),
        [planes(own)] + [planes(PASSES)] * halos,
        resident(*returned[::-1]),
        [planes(own)],
    )
    halo = swap_edges(edges, "row")
    early, saved = call(
        functools.partial(interior_body, halos),
        [pltpu.VMEM(control.shape, jnp.float32), planes(kept)],
        resident(gathered, control_planes, *own_stencil),
        [planes(own)],
    )
    (gradient,) = call(
        functools.partial(backward_body, halos),
        [jax.ShapeDtypeStruct(control.shape, jnp.float32)],
        resident(control_planes, early, saved, *own_stencil, *tail_stencil, *halo),
        [planes(PASSES)] * halos
        + [pltpu.VMEM((count, held, PASSES, lon), jnp.float32)] * halos
        + [pltpu.SemaphoreType.DMA((FIELDS * (1 + halos),))],
        out_specs=[HBM],
    )
    return gradient


def solution(mesh):
    placed = (
        P("mem", "lev", "row", None),
        P("mem", None, ("row", "lev")),
        P("lev", "row", None),
        P("lev", "row", None),
        P(None, ("row", "lev")),
        P(None, ("row", "lev")),
        P(),
        P(),
    )
    return jax.shard_map(
        per_device,
        mesh=mesh,
        in_specs=placed,
        out_specs=P("mem", "lev", "row", None),
        check_vma=False,
    )
```

```python
import functools

import jax
import jax.numpy as jnp
from jax import lax
from jax.experimental import pallas as pl
from jax.experimental.pallas import tpu as pltpu
from jax.sharding import PartitionSpec as P

PASSES = 8
HUBER = 1.0
REACH = 3
LANES = 128
TILE = 8
HALVES = 2
HELD = 2
FIELDS = 4

VMEM = pl.BlockSpec(memory_space=pltpu.VMEM)
SMEM = pl.BlockSpec(memory_space=pltpu.SMEM)
HBM = pl.BlockSpec(memory_space=pltpu.HBM)


def planes(count):
    return pltpu.VMEM((count * TILE, LANES), jnp.float32)


def call(body, outs, operands, scratch=(), specs=None, out_specs=None, flops=0, aliases=None):
    total = sum(op.size * op.dtype.itemsize for op in operands)
    return pl.pallas_call(
        body,
        out_shape=outs,
        in_specs=specs or [VMEM] * len(operands),
        out_specs=out_specs or [VMEM] * len(outs),
        scratch_shapes=list(scratch),
        input_output_aliases=aliases or {},
        compiler_params=pltpu.CompilerParams(vmem_limit_bytes=32 * 1024 * 1024),
        cost_estimate=pl.CostEstimate(flops=flops, bytes_accessed=2 * total, transcendentals=0),
    )(*operands)


def resident(*arrays):
    return [pltpu.with_memory_space_constraint(array, pltpu.VMEM) for array in arrays]


def remote(*arrays):
    return [pltpu.with_memory_space_constraint(array, pltpu.HBM) for array in arrays]


def send(array, axis, pairs, paired):
    if not paired:
        return lax.ppermute(array, axis, pairs)
    both = [(2 * source + 1, 2 * target + 1) for source, target in pairs]
    both += [(2 * source, 2 * source) for source, _ in pairs]
    return lax.ppermute(array, (axis, "row"), both)


def exchange(chunks, axis, paired):
    count = len(chunks)
    received = list(chunks)
    for step in reversed(range(1, count)):
        received[step] = send(chunks[step], axis, [(i, i ^ step) for i in range(count)], paired)
    return received


def collect(array, axis, paired):
    count = lax.axis_size(axis)
    shifts = [[(i, (i + step) % count) for i in range(count)] for step in range(1, count)]
    return [array] + [send(array, axis, shift, paired) for shift in shifts]


def swap(array):
    return lax.ppermute(array, "row", [(0, 1), (1, 0)])


def swap_edges(edges, axis):
    count = lax.axis_size(axis)
    if len(edges) == 1:
        return [lax.ppermute(edges[0], axis, [(0, 1), (1, 0)])]
    head, tail = edges
    south = lax.ppermute(head, axis, [(i + 1, i) for i in range(count - 1)])
    north = lax.ppermute(tail, axis, [(i, i + 1) for i in range(count - 1)])
    return [south, north]


def tile(ref, row):
    return ref[row * TILE : (row + 1) * TILE, :]


def set_tile(ref, row, value):
    ref[row * TILE : (row + 1) * TILE, :] = value


def block(first_row, rows):
    return pl.ds(pl.multiple_of(first_row * TILE, TILE), rows * TILE)


def spread(ref, row, sublane, values):
    ref[pl.ds(row * TILE + sublane, values.shape[0], stride=TILE), :] = values


def places():
    return lax.broadcasted_iota(jnp.int32, (TILE, LANES), 0)


def east_west(value):
    lane = lax.broadcasted_iota(jnp.int32, (TILE, LANES), 1)
    other = pltpu.roll(value, FIELDS, 0)
    east = pltpu.roll(jnp.where(lane == 0, other, value), LANES - 1, 1)
    west = pltpu.roll(jnp.where(lane == LANES - 1, other, value), 1, 1)
    return east, west


def west_of(value):
    lane = lax.broadcasted_iota(jnp.int32, (TILE, LANES), 1)
    return pltpu.roll(jnp.where(lane == LANES - 1, pltpu.roll(value, FIELDS, 0), value), 1, 1)


def halves():
    return [(half, slice(half * LANES, (half + 1) * LANES)) for half in range(HALVES)]


def pack_body(control_hbm, east_hbm, south_hbm, control_ref, east_ref, south_ref, *refs):
    send_refs, semaphores = refs[:-1], refs[-1]
    pieces = [(east_hbm.at[level], east_ref.at[level]) for level in range(HELD)]
    pieces += [(south_hbm.at[level], south_ref.at[level]) for level in range(HELD)]
    for field in range(FIELDS):
        member, level = divmod(field, HELD)
        pieces.append((control_hbm.at[member, level], control_ref.at[member, level]))
    copies = [
        pltpu.make_async_copy(source, target, semaphores.at[index]) for index, (source, target) in enumerate(pieces)
    ]
    for copy in copies:
        copy.start()
    for copy in copies:
        copy.wait()
    own = control_ref.shape[2]
    first = lax.axis_index("row") == 0

    def edges(load):
        head = load(slice(0, 2 * PASSES))[:PASSES].astype(jnp.float32)
        tail = load(slice(own - 2 * PASSES, own))[PASSES:].astype(jnp.float32)
        return [jnp.where(first, tail, head)] if len(send_refs) == 1 else [head, tail]

    for half, lanes in halves():
        for field in range(FIELDS):
            member, level = divmod(field, HELD)
            at = half * FIELDS + field
            values = edges(lambda rows: control_ref[member, level, rows, lanes])
            for send_ref, value in zip(send_refs, values):
                spread(send_ref, 0, at, value)
            for kind, coef_ref in enumerate((east_ref, south_ref)):
                values = edges(lambda rows: coef_ref[level, rows, lanes])
                for send_ref, value in zip(send_refs, values):
                    spread(send_ref, (kind + 1) * PASSES, at, value)


def is_mirrored(halos):
    return halos == 1 and lax.axis_index("row") == 1


def pick(mirrored, count, row):
    return row if mirrored is False else jnp.where(mirrored, count - 1 - row, row)


def stencil(values, row, center, east, west, above, below):
    to_east, to_west = east_west(values[row])
    total = center * values[row] + below * values[row + 1]
    if above is not None:
        total = total + above * values[row - 1]
    return total + (east * to_east + west * to_west)


def interior_passes(halos, field_ref, own_refs, saved_ref):
    center_ref, east_ref, west_ref, face_ref = own_refs
    own = field_ref.shape[0] // TILE
    values = {row: tile(field_ref, row) for row in range(own)}
    for step in range(1, PASSES + 1):
        for side in range(halos):
            kept = (own - 1 - step, own - step) if side == 0 else (step - 1, step)
            for index, row in enumerate(kept):
                set_tile(saved_ref, (side * PASSES + step - 1) * 2 + index, values[row])
        after = {}
        for row in range(step if halos == 2 else 0, own - step):
            after[row] = stencil(
                values,
                row,
                tile(center_ref, row),
                tile(east_ref, row),
                tile(west_ref, row),
                tile(face_ref, row) if row else None,
                tile(face_ref, row + 1),
            )
        values = after
    return values


def wedge_passes(halos, halo_rows, own, saved_ref, coefficient, top):
    done = {}
    for side in range(halos):
        values = dict(halo_rows[side])
        for step in range(1, PASSES + 1):
            kept = (own - 1 - step, own - step) if side == 0 else (step - 1, step)
            for index, row in enumerate(kept):
                values[row] = tile(saved_ref, (side * PASSES + step - 1) * 2 + index)
            after = {}
            for row in range(own - step, own + PASSES - step) if side == 0 else range(step - PASSES, step):
                center, east, west, above = (coefficient(kind, row) for kind in range(4))
                after[row] = stencil(values, row, center, east, west, top if row == 0 else above, coefficient(3, row + 1))
            values = after
        done.update(values)
    return done


def prepare_body(halos, control_ref, east_ref, south_ref, *refs):
    own_refs, (rows_out, saved_out, field_ref, raw_east, raw_face) = refs[:4], refs[4:]
    center_out, east_out, west_out, face_out = own_refs
    own = control_ref.shape[2]
    mirrored = is_mirrored(halos)
    for half, lanes in halves():
        for field in range(FIELDS):
            member, level = divmod(field, HELD)
            at = half * FIELDS + field
            spread(rows_out, 0, at, control_ref[member, level, :, lanes].astype(jnp.float32))
            spread(raw_east, 0, at, east_ref[level, :, lanes])
            spread(raw_face, 0, at, south_ref[level, :, lanes])
    for row in range(own):
        source = pick(mirrored, own, row)
        set_tile(field_ref, row, rows_out[block(source, 1), :])
        east = raw_east[block(source, 1), :]
        set_tile(east_out, row, east)
        set_tile(west_out, row, west_of(east))
        if row == 0:
            face = tile(raw_face, 0)
            face = face if mirrored is False else jnp.where(mirrored, 0.0, face)
        else:
            face = raw_face[block(row if mirrored is False else jnp.where(mirrored, own - row, row), 1), :]
        set_tile(face_out, row, face)
    set_tile(face_out, own, tile(raw_face, 0))
    for row in range(own - 1):
        total = 1.0 - tile(east_out, row) - tile(west_out, row)
        set_tile(center_out, row, total - tile(face_out, row + 1) - tile(face_out, row))
    for row, value in interior_passes(halos, field_ref, own_refs, saved_out).items():
        set_tile(rows_out, row, value)


def finish_coefficients(halos, halo_refs, own_refs, tail_refs, own):
    _, east_own, west_own, face_own = own_refs
    center_tail, east_tail, west_tail, face_tail = tail_refs
    mirrored = is_mirrored(halos)

    def halo_tile(side, kind, row):
        return halo_refs[side][block(kind * PASSES + row, 1), :]

    set_tile(east_tail, 0, tile(east_own, own - 1))
    set_tile(west_tail, 0, tile(west_own, own - 1))
    set_tile(face_tail, 0, tile(face_own, own - 1))
    for row in range(PASSES):
        east = halo_tile(0, 1, pick(mirrored, PASSES, row))
        set_tile(east_tail, 1 + row, east)
        set_tile(west_tail, 1 + row, west_of(east))
        if mirrored is False:
            face = halo_tile(0, 2, row)
        elif row == 0:
            face = jnp.where(mirrored, tile(face_own, own), halo_tile(0, 2, 0))
        else:
            face = halo_tile(0, 2, jnp.where(mirrored, PASSES - row, row))
        set_tile(face_tail, 1 + row, face)
    for row in range(PASSES):
        total = 1.0 - tile(east_tail, row) - tile(west_tail, row)
        set_tile(center_tail, row, total - tile(face_tail, row + 1) - tile(face_tail, row))
    if halos == 2:
        for row in range(PASSES):
            at = 1 + PASSES + row
            east, face = halo_tile(1, 1, row), halo_tile(1, 2, row)
            below = halo_tile(1, 2, row + 1) if row + 1 < PASSES else tile(face_own, 0)
            west = west_of(east)
            for ref, value in zip(tail_refs, (1.0 - east - west - below - face, east, west, face)):
                set_tile(ref, at, value)


def coefficient_reader(own_refs, tail_refs, own):
    def coefficient(kind, row):
        if row < 0:
            return tile(tail_refs[kind], 1 + 2 * PASSES + row)
        return tile(own_refs[kind], row) if row < own - 1 else tile(tail_refs[kind], row - own + 1)

    return coefficient


def top_coefficient(halos, own_refs):
    return None if halos == 1 else jnp.where(lax.axis_index("row") == 0, 0.0, tile(own_refs[3], 0))


def forward_body(halos, rows_ref, saved_ref, *refs):
    own_refs, halo_refs, refs = refs[:4], refs[4 : 4 + halos], refs[4 + halos :]
    tail_refs, chunk_refs, sorted_ref = refs[:4], refs[4:-1], refs[-1]
    own = rows_ref.shape[0] // TILE
    lev_at = lax.axis_index("lev")
    mirrored = is_mirrored(halos)
    finish_coefficients(halos, halo_refs, own_refs, tail_refs, own)
    halo_rows = [{own + row: halo_refs[0][block(pick(mirrored, PASSES, row), 1), :] for row in range(PASSES)}]
    if halos == 2:
        halo_rows.append({row - PASSES: tile(halo_refs[1], row) for row in range(PASSES)})
    coefficient = coefficient_reader(own_refs, tail_refs, own)
    top = top_coefficient(halos, own_refs)
    done = wedge_passes(halos, halo_rows, own, saved_ref, coefficient, top)
    for row in range(own):
        value = done[row] if row in done else tile(rows_ref, row)
        sorted_ref[block(pick(mirrored, own, row), 1), :] = value
    for step, chunk_ref in enumerate(reversed(chunk_refs)):
        part = own // len(chunk_refs)
        chunk_ref[...] = sorted_ref[block(lax.bitwise_xor(lev_at, step) * part, part), :]


def assemble_body(chunks, own_ref, other_ref, _, *refs):
    chunk_refs = refs[:chunks]
    lev_at = lax.axis_index("lev")
    part = own_ref.shape[0] // TILE // chunks
    for step, chunk_ref in enumerate(reversed(chunk_refs)):
        source = block(lax.bitwise_xor(lev_at, step) * part, part)
        chunk_ref[: part * TILE, :] = own_ref[source, :]
        chunk_ref[part * TILE :, :] = other_ref[source, :]


def matrix_terms(groups):
    return [
        (group, other, cross)
        for group in range(groups)
        for other in range(max(0, group - 2), min(groups, group + 3))
        for cross in range(2)
        if abs(group - other) < 2 or cross
    ]


def swap_levels(value, sublane):
    return jnp.where(sublane % HELD == 0, pltpu.roll(value, TILE - 1, 0), pltpu.roll(value, 1, 0))


def columns_body(members_ref, innovation_ref, huber_ref, band_ref, group_ref, _, *refs):
    columns_out, matrix_out, transposed_out, levels_ref = refs
    count, levels, cells = members_ref.shape
    groups, lon = levels // HELD, HALVES * LANES
    rows, packed = cells // lon, levels // FIELDS
    sublane = places()
    for member in range(count):
        for row in range(rows):
            for half in range(HALVES):
                lanes = slice(row * lon + half * LANES, row * lon + (half + 1) * LANES)
                start = ((member * rows + row) * HALVES + half) * levels
                levels_ref[start : start + levels, :] = members_ref[member, :, lanes].astype(jnp.float32)
                for level in range(HELD):
                    at = half * FIELDS + member * HELD + level
                    spread(columns_out, row * groups, at, levels_ref[pl.ds(start + level, groups, stride=HELD), :])
    for row in range(rows):
        for half in range(HALVES):
            lanes = slice(row * lon + half * LANES, row * lon + (half + 1) * LANES)
            for pack in range(packed):
                source = slice(pack * FIELDS, (pack + 1) * FIELDS)
                start = (rows * groups + row * packed + pack) * TILE + half * FIELDS
                columns_out[start : start + FIELDS, :] = innovation_ref[source, lanes]
                start = start + rows * packed * TILE
                columns_out[start : start + FIELDS, :] = huber_ref[source, lanes].astype(jnp.float32)

    def entry(level, other):
        offset = other - level + REACH
        if not 0 <= offset < 2 * REACH + 1:
            return jnp.float32(0.0)
        value = band_ref[offset, level] + jnp.float32(1.0 if offset == REACH else 0.0)
        return jnp.where(group_ref[level] == group_ref[other], value, jnp.float32(0.0))

    for slot, (group, other, cross) in enumerate(matrix_terms(groups)):
        pairs = [(group * HELD + level, other * HELD + (level ^ cross)) for level in range(HELD)]
        even, odd = (entry(a, b) for a, b in pairs)
        set_tile(matrix_out, slot, jnp.where(sublane % HELD == 0, even, odd))
        even, odd = (entry(b, a) for a, b in pairs)
        set_tile(transposed_out, slot, jnp.where(sublane % HELD == 0, even, odd))


def apply_matrix(matrix_ref, values, sublane):
    crossed = [swap_levels(value, sublane) for value in values]
    totals = [None] * len(values)
    for slot, (group, other, cross) in enumerate(matrix_terms(len(values))):
        term = tile(matrix_ref, slot) * (crossed if cross else values)[other]
        totals[group] = term if totals[group] is None else totals[group] + term
    return totals


def filter_body(chunks, sets, *refs):
    chunk_refs, columns_refs, refs = refs[:chunks], refs[chunks : chunks + sets], refs[chunks + sets :]
    matrix_ref, partial_ref, sorted_ref = refs
    held = chunk_refs[0].shape[0] // TILE
    rows = held // sets
    lev_at = lax.axis_index("lev")
    sublane = places()
    first_member = sublane % FIELDS < HELD
    for step, chunk_ref in enumerate(reversed(chunk_refs)):
        sorted_ref[block(lax.bitwise_xor(lev_at, step) * held, held), :] = chunk_ref[...]
    for at in range(held):
        columns_ref, row = columns_refs[at // rows], at % rows
        filtered = apply_matrix(matrix_ref, [tile(sorted_ref, group * held + at) for group in range(chunks)], sublane)
        terms = [tile(columns_ref, row * chunks + group) * value for group, value in enumerate(filtered)]
        for pack in range(chunks // 2):
            lower, upper = terms[2 * pack], terms[2 * pack + 1]
            total = jnp.where(first_member, lower, upper)
            total = total + jnp.where(first_member, pltpu.roll(lower, TILE - HELD, 0), pltpu.roll(upper, HELD, 0))
            set_tile(partial_ref, at * (chunks // 2) + pack, total)


def lift_body(chunks, parts, sets, *refs):
    part_refs, columns_refs, refs = refs[:parts], refs[parts : parts + sets], refs[parts + sets :]
    transposed_ref, chunk_refs, (weighted_ref, sorted_ref) = refs[0], refs[1 : 1 + chunks], refs[1 + chunks :]
    held = chunk_refs[0].shape[0] // TILE
    rows = held // sets
    size = rows * (chunks // 2) * TILE
    lev_at = lax.axis_index("lev")
    sublane = places()
    first_member = sublane % FIELDS < HELD
    for index, columns_ref in enumerate(columns_refs):
        own = slice(index * size, (index + 1) * size)
        increment = part_refs[0][own, :]
        for part_ref in part_refs[1:]:
            increment = increment + part_ref[own, :]
        start = rows * chunks * TILE
        residual = increment - columns_ref[start : start + size, :]
        scale = HUBER / jnp.maximum(jnp.abs(residual), HUBER)
        classes = columns_ref[start + size : start + 2 * size, :]
        weighted_ref[own, :] = jnp.where(classes == 1.0, scale, 1.0) * residual
    for at in range(held):
        columns_ref, row = columns_refs[at // rows], at % rows
        adjoint = []
        for pack in range(chunks // 2):
            weighted = tile(weighted_ref, at * (chunks // 2) + pack)
            lower = jnp.where(first_member, weighted, pltpu.roll(weighted, HELD, 0))
            upper = jnp.where(first_member, pltpu.roll(weighted, TILE - HELD, 0), weighted)
            for value in (lower, upper):
                adjoint.append(value * tile(columns_ref, row * chunks + len(adjoint)))
        for group, value in enumerate(apply_matrix(transposed_ref, adjoint, sublane)):
            set_tile(sorted_ref, group * held + at, value)
    for step, chunk_ref in enumerate(reversed(chunk_refs)):
        chunk_ref[...] = sorted_ref[block(lax.bitwise_xor(lev_at, step) * held, held), :]


def gather_body(halos, chunks, *refs):
    chunk_refs, field_ref, send_refs, sorted_ref = refs[:chunks], refs[chunks], refs[chunks + 1 : -1], refs[-1]
    lev_at = lax.axis_index("lev")
    mirrored = is_mirrored(halos)
    rows = chunk_refs[0].shape[0] // TILE
    own = rows * chunks
    for step, chunk_ref in enumerate(reversed(chunk_refs)):
        sorted_ref[block(lax.bitwise_xor(lev_at, step) * rows, rows), :] = chunk_ref[...]
    for row in range(own):
        set_tile(field_ref, row, sorted_ref[block(pick(mirrored, own, row), 1), :])
    for row in range(PASSES):
        if halos == 1:
            set_tile(send_refs[0], row, tile(field_ref, own - 1 - row))
        else:
            set_tile(send_refs[0], row, tile(field_ref, row))
            set_tile(send_refs[1], row, tile(field_ref, own - PASSES + row))


def to_fields(planes_ref, fields_ref, rows):
    for field in range(FIELDS):
        member, level = divmod(field, HELD)
        for half, lanes in halves():
            fields_ref[member, level, :, lanes] = planes_ref[pl.ds(half * FIELDS + field, rows, stride=TILE), :]


def interior_body(halos, field_ref, control_ref, *refs):
    own_refs, (fields_out, saved_out, result_ref) = refs[:4], refs[4:]
    own = field_ref.shape[0] // TILE
    mirrored = is_mirrored(halos)
    done = interior_passes(halos, field_ref, own_refs, saved_out)
    for row in range(own):
        value = done[row] + tile(control_ref, row) if row in done else jnp.zeros((TILE, LANES), jnp.float32)
        result_ref[block(pick(mirrored, own, row), 1), :] = value
    to_fields(result_ref, fields_out, own)


def backward_body(halos, control_ref, fields_ref, saved_ref, *refs):
    own_refs, tail_refs, halo_refs = refs[:4], refs[4:8], refs[8 : 8 + halos]
    gradient_hbm, refs = refs[8 + halos], refs[9 + halos :]
    result_refs, edge_refs, semaphores = refs[:halos], refs[halos : 2 * halos], refs[-1]
    own = fields_ref.shape[2]
    mirrored = is_mirrored(halos)
    if halos == 1:
        spans = [(PASSES * mirrored.astype(jnp.int32), own - PASSES)]
        spans.append((jnp.where(mirrored, 0, own - PASSES), PASSES))
    else:
        spans = [(PASSES, own - 2 * PASSES), (own - PASSES, PASSES), (0, PASSES)]
    copies = []

    def send(source_ref, source_start, start, rows):
        for field in range(FIELDS):
            member, level = divmod(field, HELD)
            copy = pltpu.make_async_copy(
                source_ref.at[member, level, pl.ds(source_start, rows), :],
                gradient_hbm.at[member, level, pl.ds(start, rows), :],
                semaphores.at[len(copies)],
            )
            copy.start()
            copies.append(copy)

    start = pl.multiple_of(spans[0][0], TILE)
    send(fields_ref, start, start, spans[0][1])
    halo_rows = [{own + row: tile(halo_refs[0], row) for row in range(PASSES)}]
    if halos == 2:
        halo_rows.append({row - PASSES: tile(halo_refs[1], row) for row in range(PASSES)})
    coefficient = coefficient_reader(own_refs, tail_refs, own)
    top = top_coefficient(halos, own_refs)
    done = wedge_passes(halos, halo_rows, own, saved_ref, coefficient, top)
    for side in range(halos):
        for row in range(PASSES):
            value = done[own - PASSES + row] + tile(control_ref, own - PASSES + row) if side == 0 else done[row] + tile(control_ref, row)
            result_refs[side][block(pick(mirrored, PASSES, row), 1), :] = value
        to_fields(result_refs[side], edge_refs[side], PASSES)
        send(edge_refs[side], 0, pl.multiple_of(spans[1 + side][0], TILE), PASSES)
    for copy in copies:
        copy.wait()


def gather_both_body(chunks, *refs):
    chunk_refs, (local_out, other_out, own_ref, other_ref) = refs[:chunks], refs[chunks:]
    lev_at = lax.axis_index("lev")
    part = chunk_refs[0].shape[0] // TILE // 2
    own = part * chunks
    for step, chunk_ref in enumerate(reversed(chunk_refs)):
        target = block(lax.bitwise_xor(lev_at, step) * part, part)
        own_ref[target, :] = chunk_ref[: part * TILE, :]
        other_ref[target, :] = chunk_ref[part * TILE :, :]
    second = lax.axis_index("row") == 1
    for out_ref, rows_ref, halo_ref, mirrored in (
        (local_out, own_ref, other_ref, second),
        (other_out, other_ref, own_ref, jnp.logical_not(second)),
    ):
        for row in range(own):
            set_tile(out_ref, row, rows_ref[block(pick(mirrored, own, row), 1), :])
        for row in range(PASSES):
            set_tile(out_ref, own + row, halo_ref[block(pick(mirrored, own, row), 1), :])


def backward_both_body(local_ref, given_ref, control_ref, *refs):
    own_refs, tail_refs = refs[:4], refs[4:8]
    gradient_hbm, result_ref, gradient_ref, semaphores = refs[8:]
    own = control_ref.shape[0] // TILE
    second = lax.axis_index("row") == 1
    coefficient = coefficient_reader(own_refs, tail_refs, own)
    values = {row: jnp.where(second, tile(local_ref, row), tile(given_ref, row)) for row in range(own + PASSES)}
    for step in range(1, PASSES + 1):
        after = {}
        for row in range(own + PASSES - step):
            center, east, west, above = (coefficient(kind, row) for kind in range(4))
            after[row] = stencil(values, row, center, east, west, above if row else None, coefficient(3, row + 1))
        values = after
    for row in range(own):
        result_ref[block(pick(second, own, row), 1), :] = values[row] + tile(control_ref, row)
    copies = []
    for field in range(FIELDS):
        member, level = divmod(field, HELD)
        for half, lanes in halves():
            gradient_ref[member, level, :, lanes] = result_ref[pl.ds(half * FIELDS + field, own, stride=TILE), :]
        copy = pltpu.make_async_copy(
            gradient_ref.at[member, level], gradient_hbm.at[member, level], semaphores.at[field]
        )
        copy.start()
        copies.append(copy)
    for copy in copies:
        copy.wait()


def per_device(control, members, east_coef, south_coef, innovation, huber_class, band, level_group_index):
    count, held, own, lon = control.shape
    levels, cells = members.shape[1:]
    chunks, parts, row_count = (lax.axis_size(axis) for axis in ("lev", "mem", "row"))
    assert (count * held, held, lon) == (FIELDS, HELD, HALVES * LANES)
    paired = row_count == 2
    sets = 2 if paired else 1
    part = own // chunks
    halos = 1 if paired else 2
    tail = 1 + halos * PASSES
    kept = halos * PASSES * 2
    terms = len(matrix_terms(chunks))
    packed = part * levels // FIELDS
    gradient_shape = [jax.ShapeDtypeStruct(control.shape, jnp.float32)]

    control_near, east_near, south_near, *edges = call(
        pack_body,
        [pltpu.VMEM(x.shape, x.dtype) for x in (control, east_coef, south_coef)] + [planes(3 * PASSES)] * halos,
        remote(control, east_coef, south_coef),
        [pltpu.SemaphoreType.DMA((FIELDS + 2 * HELD,))],
        specs=[HBM] * 3,
    )
    halo = swap_edges(edges, "row")
    *own_stencil, done_rows, saved, control_planes = call(
        functools.partial(prepare_body, halos),
        [planes(own)] * 3 + [planes(own + 1), planes(own), planes(kept), planes(own)],
        resident(control_near, east_near, south_near),
        [planes(own)] * 2,
    )
    results = call(
        functools.partial(forward_body, halos),
        [planes(tail)] * 4 + ([planes(own)] if paired else [planes(part)] * chunks),
        resident(done_rows, saved, *own_stencil, *halo),
        [] if paired else [planes(own)],
    )
    tail_stencil, smoothed = results[:4], results[4:]
    columns, matrix, transposed = call(
        columns_body,
        [planes(part * chunks + 2 * packed), planes(terms), planes(terms)],
        [members, innovation, huber_class, band, level_group_index, *resident(results[4])],
        [planes(part * chunks)],
        specs=[VMEM, VMEM, VMEM, SMEM, SMEM, VMEM],
    )
    if paired:
        *smoothed, columns = call(
            functools.partial(assemble_body, chunks),
            [planes(sets * part)] * chunks + [planes(part * chunks + 2 * packed)],
            resident(smoothed[0], swap(smoothed[0]), columns),
            aliases={2: chunks},
        )
    columns = [columns, swap(columns)] if paired else [columns]
    received = exchange(smoothed[::-1], "lev", paired)
    (partial,) = call(
        functools.partial(filter_body, chunks, sets),
        [planes(sets * packed)],
        resident(*received[::-1], *columns, matrix),
        [planes(sets * part * chunks)],
    )
    own_part, *partials = collect(partial, "mem", paired)
    lifted = call(
        functools.partial(lift_body, chunks, parts, sets),
        [planes(sets * part)] * chunks,
        resident(own_part, *partials[::-1], *columns, transposed),
        [planes(sets * packed), planes(sets * part * chunks)],
    )
    returned = exchange(lifted[::-1], "lev", paired)
    if paired:
        local, other = call(
            functools.partial(gather_both_body, chunks),
            [planes(own + PASSES)] * 2,
            resident(*returned[::-1]),
            [planes(own)] * 2,
        )
        (gradient,) = call(
            backward_both_body,
            gradient_shape,
            resident(local, swap(other), control_planes, *own_stencil, *tail_stencil),
            [planes(own), pltpu.VMEM(control.shape, jnp.float32), pltpu.SemaphoreType.DMA((FIELDS,))],
            out_specs=[HBM],
        )
        return gradient
    gathered, *edges = call(
        functools.partial(gather_body, halos, chunks),
        [planes(own)] + [planes(PASSES)] * halos,
        resident(*returned[::-1]),
        [planes(own)],
    )
    halo = swap_edges(edges, "row")
    early, saved = call(
        functools.partial(interior_body, halos),
        [pltpu.VMEM(control.shape, jnp.float32), planes(kept)],
        resident(gathered, control_planes, *own_stencil),
        [planes(own)],
    )
    (gradient,) = call(
        functools.partial(backward_body, halos),
        gradient_shape,
        resident(control_planes, early, saved, *own_stencil, *tail_stencil, *halo),
        [planes(PASSES)] * halos
        + [pltpu.VMEM((count, held, PASSES, lon), jnp.float32)] * halos
        + [pltpu.SemaphoreType.DMA((FIELDS * (1 + halos),))],
        out_specs=[HBM],
    )
    return gradient


def solution(mesh):
    placed = (
        P("mem", "lev", "row", None),
        P("mem", None, ("row", "lev")),
        P("lev", "row", None),
        P("lev", "row", None),
        P(None, ("row", "lev")),
        P(None, ("row", "lev")),
        P(),
        P(),
    )
    return jax.shard_map(
        per_device,
        mesh=mesh,
        in_specs=placed,
        out_specs=P("mem", "lev", "row", None),
        check_vma=False,
    )
```

```python
import functools

import jax
import jax.numpy as jnp
from jax import lax
from jax.experimental import pallas as pl
from jax.experimental.pallas import tpu as pltpu
from jax.sharding import PartitionSpec as P

PASSES = 8
HUBER = 1.0
REACH = 3
POINTS = 13
LANES = 128
TILE = 8
HALVES = 2
HELD = 2
FIELDS = 4

VMEM = pl.BlockSpec(memory_space=pltpu.VMEM)
SMEM = pl.BlockSpec(memory_space=pltpu.SMEM)
HBM = pl.BlockSpec(memory_space=pltpu.HBM)


def planes(count):
    return pltpu.VMEM((count * TILE, LANES), jnp.float32)


def call(body, outs, operands, scratch=(), specs=None, out_specs=None, flops=0):
    total = sum(op.size * op.dtype.itemsize for op in operands)
    return pl.pallas_call(
        body,
        out_shape=outs,
        in_specs=specs or [VMEM] * len(operands),
        out_specs=out_specs or [VMEM] * len(outs),
        scratch_shapes=list(scratch),
        compiler_params=pltpu.CompilerParams(vmem_limit_bytes=32 * 1024 * 1024),
        cost_estimate=pl.CostEstimate(flops=flops, bytes_accessed=2 * total, transcendentals=0),
    )(*operands)


def resident(*arrays):
    return [pltpu.with_memory_space_constraint(array, pltpu.VMEM) for array in arrays]


def remote(*arrays):
    return [pltpu.with_memory_space_constraint(array, pltpu.HBM) for array in arrays]


def exchange(chunks, axis):
    count = len(chunks)
    received = list(chunks)
    for step in reversed(range(1, count)):
        received[step] = lax.ppermute(chunks[step], axis, [(i, i ^ step) for i in range(count)])
    return received


def collect(array, axis):
    count = lax.axis_size(axis)
    shifts = [[(i, (i + step) % count) for i in range(count)] for step in range(1, count)]
    return [array] + [lax.ppermute(array, axis, shift) for shift in shifts]


def swap_edges(edges, axis):
    count = lax.axis_size(axis)
    if len(edges) == 1:
        return [lax.ppermute(edges[0], axis, [(0, 1), (1, 0)])]
    head, tail = edges
    south = lax.ppermute(head, axis, [(i + 1, i) for i in range(count - 1)])
    north = lax.ppermute(tail, axis, [(i, i + 1) for i in range(count - 1)])
    return [south, north]


def tile(ref, row):
    return ref[row * TILE : (row + 1) * TILE, :]


def set_tile(ref, row, value):
    ref[row * TILE : (row + 1) * TILE, :] = value


def block(first_row, rows):
    return pl.ds(pl.multiple_of(first_row * TILE, TILE), rows * TILE)


def spread(ref, row, sublane, values):
    ref[pl.ds(row * TILE + sublane, values.shape[0], stride=TILE), :] = values


def places():
    return lax.broadcasted_iota(jnp.int32, (TILE, LANES), 0)


def east_west(value):
    lane = lax.broadcasted_iota(jnp.int32, (TILE, LANES), 1)
    other = pltpu.roll(value, FIELDS, 0)
    east = pltpu.roll(jnp.where(lane == 0, other, value), LANES - 1, 1)
    west = pltpu.roll(jnp.where(lane == LANES - 1, other, value), 1, 1)
    return east, west


def west_of(value):
    lane = lax.broadcasted_iota(jnp.int32, (TILE, LANES), 1)
    return pltpu.roll(jnp.where(lane == LANES - 1, pltpu.roll(value, FIELDS, 0), value), 1, 1)


def halves():
    return [(half, slice(half * LANES, (half + 1) * LANES)) for half in range(HALVES)]


def pack_body(control_hbm, east_hbm, south_hbm, control_ref, east_ref, south_ref, *refs):
    send_refs, semaphores = refs[:-1], refs[-1]
    pieces = [(east_hbm.at[level], east_ref.at[level]) for level in range(HELD)]
    pieces += [(south_hbm.at[level], south_ref.at[level]) for level in range(HELD)]
    for field in range(FIELDS):
        member, level = divmod(field, HELD)
        pieces.append((control_hbm.at[member, level], control_ref.at[member, level]))
    copies = [
        pltpu.make_async_copy(source, target, semaphores.at[index]) for index, (source, target) in enumerate(pieces)
    ]
    for copy in copies:
        copy.start()
    for copy in copies:
        copy.wait()
    own = control_ref.shape[2]
    first = lax.axis_index("row") == 0

    def edges(load):
        head = load(slice(0, 2 * PASSES))[:PASSES].astype(jnp.float32)
        tail = load(slice(own - 2 * PASSES, own))[PASSES:].astype(jnp.float32)
        return [jnp.where(first, tail, head)] if len(send_refs) == 1 else [head, tail]

    for half, lanes in halves():
        for field in range(FIELDS):
            member, level = divmod(field, HELD)
            at = half * FIELDS + field
            values = edges(lambda rows: control_ref[member, level, rows, lanes])
            for send_ref, value in zip(send_refs, values):
                spread(send_ref, 0, at, value)
            for kind, coef_ref in enumerate((east_ref, south_ref)):
                values = edges(lambda rows: coef_ref[level, rows, lanes])
                for send_ref, value in zip(send_refs, values):
                    spread(send_ref, (kind + 1) * PASSES, at, value)


def is_mirrored(halos):
    return halos == 1 and lax.axis_index("row") == 1


def pick(mirrored, count, row):
    return row if mirrored is False else jnp.where(mirrored, count - 1 - row, row)


def stencil(values, row, center, east, west, above, below):
    to_east, to_west = east_west(values[row])
    total = center * values[row] + below * values[row + 1]
    if above is not None:
        total = total + above * values[row - 1]
    return total + (east * to_east + west * to_west)


def interior_passes(halos, field_ref, own_refs, saved_ref, double=False):
    center_ref, east_ref, west_ref, face_ref = own_refs
    own = field_ref.shape[0] // TILE
    values = {row: tile(field_ref, row) for row in range(own)}
    for step in range(1, PASSES + 1):
        for side in range(halos):
            kept = (own - 1 - step, own - step) if side == 0 else (step - 1, step)
            if double:
                kept = range(own - 3 - step, own + 1 - step) if step % 2 else ()
            for index, row in enumerate(kept):
                set_tile(saved_ref, (side * PASSES + step - 1) * 2 + index, values[row])
        after = {}
        for row in range(step if halos == 2 else 0, own - step):
            after[row] = stencil(
                values,
                row,
                tile(center_ref, row),
                tile(east_ref, row),
                tile(west_ref, row),
                tile(face_ref, row) if row else None,
                tile(face_ref, row + 1),
            )
        values = after
    return values


def wedge_passes(halos, halo_rows, own, saved_ref, coefficient, top):
    done = {}
    for side in range(halos):
        values = dict(halo_rows[side])
        for step in range(1, PASSES + 1):
            kept = (own - 1 - step, own - step) if side == 0 else (step - 1, step)
            for index, row in enumerate(kept):
                values[row] = tile(saved_ref, (side * PASSES + step - 1) * 2 + index)
            after = {}
            for row in range(own - step, own + PASSES - step) if side == 0 else range(step - PASSES, step):
                center, east, west, above = (coefficient(kind, row) for kind in range(4))
                after[row] = stencil(values, row, center, east, west, top if row == 0 else above, coefficient(3, row + 1))
            values = after
        done.update(values)
    return done


def shifted(value, distance):
    lane = lax.broadcasted_iota(jnp.int32, (TILE, LANES), 1)
    other = pltpu.roll(value, FIELDS, 0)
    east = pltpu.roll(jnp.where(lane < distance, other, value), LANES - distance, 1)
    west = pltpu.roll(jnp.where(lane >= LANES - distance, other, value), distance, 1)
    return east, west


def compose_body(*refs):
    own_refs, tail_refs, composed_out = refs[:4], refs[4:8], refs[-1]
    own = own_refs[0].shape[0] // TILE
    coefficient = coefficient_reader(own_refs, tail_refs, own)
    for index in range(2 * PASSES - 2):
        row = own - PASSES + index
        center, east, west, above = (coefficient(kind, row) for kind in range(4))
        below = coefficient(3, row + 1)
        (center_e, center_w), (east_e, east_w), (west_e, west_w), (below_e, below_w), (above_e, above_w) = (
            shifted(value, 1) for value in (center, east, west, below, above)
        )
        tiles = (
            center * center + east * west_e + west * east_w + below * below + above * above,
            east * (center + center_e),
            west * (center + center_w),
            east * east_e,
            west * west_w,
            below * (center + coefficient(0, row + 1)),
            east * below_e + below * coefficient(1, row + 1),
            west * below_w + below * coefficient(2, row + 1),
            above * (center + coefficient(0, row - 1)),
            east * above_e + above * coefficient(1, row - 1),
            west * above_w + above * coefficient(2, row - 1),
            below * coefficient(3, row + 2),
            above * coefficient(3, row - 1),
        )
        for place, value in enumerate(tiles):
            set_tile(composed_out, index * POINTS + place, value)


def double_wedge(values, own, saved_ref, composed_ref):
    for step in range(1, PASSES // 2 + 1):
        first = own - 2 * step
        for index in range(4):
            values[first - 2 + index] = tile(saved_ref, (step - 1) * 4 + index)
        near = {row: shifted(values[row], 1) for row in range(first - 1, first + PASSES + 1)}
        after = {}
        for row in range(first, first + PASSES):
            def coefficient(place):
                return tile(composed_ref, (row - own + PASSES) * POINTS + place)

            east, west = shifted(values[row], 2)
            total = coefficient(0) * values[row] + coefficient(5) * values[row + 1]
            total = total + (coefficient(8) * values[row - 1] + coefficient(11) * values[row + 2])
            total = total + coefficient(12) * values[row - 2]
            sides = coefficient(1) * near[row][0] + coefficient(2) * near[row][1]
            lower = coefficient(6) * near[row + 1][0] + coefficient(7) * near[row + 1][1]
            upper = coefficient(9) * near[row - 1][0] + coefficient(10) * near[row - 1][1]
            far = coefficient(3) * east + coefficient(4) * west
            after[row] = (total + sides) + ((lower + upper) + far)
        values = after
    return values


def prepare_body(halos, control_ref, east_ref, south_ref, *refs):
    own_refs, (rows_out, saved_out, field_ref, raw_east, raw_face) = refs[:4], refs[4:]
    center_out, east_out, west_out, face_out = own_refs
    own = control_ref.shape[2]
    mirrored = is_mirrored(halos)
    for half, lanes in halves():
        for field in range(FIELDS):
            member, level = divmod(field, HELD)
            at = half * FIELDS + field
            spread(rows_out, 0, at, control_ref[member, level, :, lanes].astype(jnp.float32))
            spread(raw_east, 0, at, east_ref[level, :, lanes])
            spread(raw_face, 0, at, south_ref[level, :, lanes])
    for row in range(own):
        source = pick(mirrored, own, row)
        set_tile(field_ref, row, rows_out[block(source, 1), :])
        east = raw_east[block(source, 1), :]
        set_tile(east_out, row, east)
        set_tile(west_out, row, west_of(east))
        if row == 0:
            face = tile(raw_face, 0)
            face = face if mirrored is False else jnp.where(mirrored, 0.0, face)
        else:
            face = raw_face[block(row if mirrored is False else jnp.where(mirrored, own - row, row), 1), :]
        set_tile(face_out, row, face)
    set_tile(face_out, own, tile(raw_face, 0))
    for row in range(own - 1):
        total = 1.0 - tile(east_out, row) - tile(west_out, row)
        set_tile(center_out, row, total - tile(face_out, row + 1) - tile(face_out, row))
    for row, value in interior_passes(halos, field_ref, own_refs, saved_out).items():
        set_tile(rows_out, row, value)


def finish_coefficients(halos, halo_refs, own_refs, tail_refs, own):
    _, east_own, west_own, face_own = own_refs
    center_tail, east_tail, west_tail, face_tail = tail_refs
    mirrored = is_mirrored(halos)

    def halo_tile(side, kind, row):
        return halo_refs[side][block(kind * PASSES + row, 1), :]

    set_tile(east_tail, 0, tile(east_own, own - 1))
    set_tile(west_tail, 0, tile(west_own, own - 1))
    set_tile(face_tail, 0, tile(face_own, own - 1))
    for row in range(PASSES):
        east = halo_tile(0, 1, pick(mirrored, PASSES, row))
        set_tile(east_tail, 1 + row, east)
        set_tile(west_tail, 1 + row, west_of(east))
        if mirrored is False:
            face = halo_tile(0, 2, row)
        elif row == 0:
            face = jnp.where(mirrored, tile(face_own, own), halo_tile(0, 2, 0))
        else:
            face = halo_tile(0, 2, jnp.where(mirrored, PASSES - row, row))
        set_tile(face_tail, 1 + row, face)
    for row in range(PASSES):
        total = 1.0 - tile(east_tail, row) - tile(west_tail, row)
        set_tile(center_tail, row, total - tile(face_tail, row + 1) - tile(face_tail, row))
    if halos == 2:
        for row in range(PASSES):
            at = 1 + PASSES + row
            east, face = halo_tile(1, 1, row), halo_tile(1, 2, row)
            below = halo_tile(1, 2, row + 1) if row + 1 < PASSES else tile(face_own, 0)
            west = west_of(east)
            for ref, value in zip(tail_refs, (1.0 - east - west - below - face, east, west, face)):
                set_tile(ref, at, value)


def coefficient_reader(own_refs, tail_refs, own):
    def coefficient(kind, row):
        if row < 0:
            return tile(tail_refs[kind], 1 + 2 * PASSES + row)
        return tile(own_refs[kind], row) if row < own - 1 else tile(tail_refs[kind], row - own + 1)

    return coefficient


def top_coefficient(halos, own_refs):
    return None if halos == 1 else jnp.where(lax.axis_index("row") == 0, 0.0, tile(own_refs[3], 0))


def forward_body(halos, rows_ref, saved_ref, *refs):
    own_refs, halo_refs, refs = refs[:4], refs[4 : 4 + halos], refs[4 + halos :]
    tail_refs, chunk_refs, sorted_ref = refs[:4], refs[4:-1], refs[-1]
    own = rows_ref.shape[0] // TILE
    lev_at = lax.axis_index("lev")
    mirrored = is_mirrored(halos)
    finish_coefficients(halos, halo_refs, own_refs, tail_refs, own)
    halo_rows = [{own + row: halo_refs[0][block(pick(mirrored, PASSES, row), 1), :] for row in range(PASSES)}]
    if halos == 2:
        halo_rows.append({row - PASSES: tile(halo_refs[1], row) for row in range(PASSES)})
    coefficient = coefficient_reader(own_refs, tail_refs, own)
    top = top_coefficient(halos, own_refs)
    done = wedge_passes(halos, halo_rows, own, saved_ref, coefficient, top)
    for row in range(own):
        value = done[row] if row in done else tile(rows_ref, row)
        sorted_ref[block(pick(mirrored, own, row), 1), :] = value
    part = own // len(chunk_refs)
    for step, chunk_ref in enumerate(reversed(chunk_refs)):
        chunk_ref[...] = sorted_ref[block(lax.bitwise_xor(lev_at, step) * part, part), :]


def matrix_terms(groups):
    return [
        (group, other, cross)
        for group in range(groups)
        for other in range(max(0, group - 2), min(groups, group + 3))
        for cross in range(2)
        if abs(group - other) < 2 or cross
    ]


def swap_levels(value, sublane):
    return jnp.where(sublane % HELD == 0, pltpu.roll(value, TILE - 1, 0), pltpu.roll(value, 1, 0))


def columns_body(members_ref, innovation_ref, huber_ref, band_ref, group_ref, *refs):
    members_out, innovation_out, huber_out, matrix_out, transposed_out, levels_ref = refs
    count, levels, cells = members_ref.shape
    groups, lon = levels // HELD, HALVES * LANES
    rows, packed = cells // lon, levels // FIELDS
    sublane = places()
    for member in range(count):
        for row in range(rows):
            for half in range(HALVES):
                lanes = slice(row * lon + half * LANES, row * lon + (half + 1) * LANES)
                start = ((member * rows + row) * HALVES + half) * levels
                levels_ref[start : start + levels, :] = members_ref[member, :, lanes].astype(jnp.float32)
                for level in range(HELD):
                    at = half * FIELDS + member * HELD + level
                    spread(members_out, row * groups, at, levels_ref[pl.ds(start + level, groups, stride=HELD), :])
    for row in range(rows):
        for half in range(HALVES):
            lanes = slice(row * lon + half * LANES, row * lon + (half + 1) * LANES)
            for pack in range(packed):
                source = slice(pack * FIELDS, (pack + 1) * FIELDS)
                start = (row * packed + pack) * TILE + half * FIELDS
                innovation_out[start : start + FIELDS, :] = innovation_ref[source, lanes]
                huber_out[start : start + FIELDS, :] = huber_ref[source, lanes].astype(jnp.float32)

    def entry(level, other):
        offset = other - level + REACH
        if not 0 <= offset < 2 * REACH + 1:
            return jnp.float32(0.0)
        value = band_ref[offset, level] + jnp.float32(1.0 if offset == REACH else 0.0)
        return jnp.where(group_ref[level] == group_ref[other], value, jnp.float32(0.0))

    for slot, (group, other, cross) in enumerate(matrix_terms(groups)):
        pairs = [(group * HELD + level, other * HELD + (level ^ cross)) for level in range(HELD)]
        even, odd = (entry(a, b) for a, b in pairs)
        set_tile(matrix_out, slot, jnp.where(sublane % HELD == 0, even, odd))
        even, odd = (entry(b, a) for a, b in pairs)
        set_tile(transposed_out, slot, jnp.where(sublane % HELD == 0, even, odd))


def apply_matrix(matrix_ref, values, sublane):
    crossed = [swap_levels(value, sublane) for value in values]
    totals = [None] * len(values)
    for slot, (group, other, cross) in enumerate(matrix_terms(len(values))):
        term = tile(matrix_ref, slot) * (crossed if cross else values)[other]
        totals[group] = term if totals[group] is None else totals[group] + term
    return totals


def filter_body(chunks, *refs):
    chunk_refs = refs[:chunks]
    members_ref, matrix_ref, partial_ref, columns = refs[chunks:]
    rows = chunk_refs[0].shape[0] // TILE
    lev_at = lax.axis_index("lev")
    sublane = places()
    first_member = sublane % FIELDS < HELD
    for step, chunk_ref in enumerate(reversed(chunk_refs)):
        columns[block(lax.bitwise_xor(lev_at, step) * rows, rows), :] = chunk_ref[...]
    for row in range(rows):
        filtered = apply_matrix(matrix_ref, [tile(columns, group * rows + row) for group in range(chunks)], sublane)
        terms = [tile(members_ref, row * chunks + group) * value for group, value in enumerate(filtered)]
        for pack in range(chunks // 2):
            lower, upper = terms[2 * pack], terms[2 * pack + 1]
            total = jnp.where(first_member, lower, upper)
            total = total + jnp.where(first_member, pltpu.roll(lower, TILE - HELD, 0), pltpu.roll(upper, HELD, 0))
            set_tile(partial_ref, row * (chunks // 2) + pack, total)


def lift_body(chunks, parts, extra, *refs):
    part_refs, refs = refs[:parts], refs[parts:]
    innovation_ref, huber_ref, members_ref, transposed_ref = refs[:4]
    refs = refs[4 + extra :]
    chunk_refs, (weighted_ref, sorted_ref) = refs[:chunks], refs[chunks:]
    rows = chunk_refs[0].shape[0] // TILE
    lev_at = lax.axis_index("lev")
    sublane = places()
    first_member = sublane % FIELDS < HELD
    increment = part_refs[0][...]
    for part_ref in part_refs[1:]:
        increment = increment + part_ref[...]
    residual = increment - innovation_ref[...]
    scale = HUBER / jnp.maximum(jnp.abs(residual), HUBER)
    weighted_ref[...] = jnp.where(huber_ref[...] == 1.0, scale, 1.0) * residual
    for row in range(rows):
        adjoint = []
        for pack in range(chunks // 2):
            weighted = tile(weighted_ref, row * (chunks // 2) + pack)
            lower = jnp.where(first_member, weighted, pltpu.roll(weighted, HELD, 0))
            upper = jnp.where(first_member, pltpu.roll(weighted, TILE - HELD, 0), weighted)
            for value in (lower, upper):
                adjoint.append(value * tile(members_ref, row * chunks + len(adjoint)))
        for group, value in enumerate(apply_matrix(transposed_ref, adjoint, sublane)):
            set_tile(sorted_ref, group * rows + row, value)
    for step, chunk_ref in enumerate(reversed(chunk_refs)):
        chunk_ref[...] = sorted_ref[block(lax.bitwise_xor(lev_at, step) * rows, rows), :]


def gather_body(halos, chunks, *refs):
    chunk_refs, field_ref, send_refs, sorted_ref = refs[:chunks], refs[chunks], refs[chunks + 1 : -1], refs[-1]
    lev_at = lax.axis_index("lev")
    mirrored = is_mirrored(halos)
    rows = chunk_refs[0].shape[0] // TILE
    own = rows * chunks
    for step, chunk_ref in enumerate(reversed(chunk_refs)):
        sorted_ref[block(lax.bitwise_xor(lev_at, step) * rows, rows), :] = chunk_ref[...]
    for row in range(own):
        set_tile(field_ref, row, sorted_ref[block(pick(mirrored, own, row), 1), :])
    for row in range(PASSES):
        if halos == 1:
            set_tile(send_refs[0], row, tile(field_ref, own - 1 - row))
        else:
            set_tile(send_refs[0], row, tile(field_ref, row))
            set_tile(send_refs[1], row, tile(field_ref, own - PASSES + row))


def to_fields(planes_ref, fields_ref, rows):
    for field in range(FIELDS):
        member, level = divmod(field, HELD)
        for half, lanes in halves():
            fields_ref[member, level, :, lanes] = planes_ref[pl.ds(half * FIELDS + field, rows, stride=TILE), :]


def interior_body(halos, field_ref, control_ref, *refs):
    own_refs, (fields_out, saved_out, result_ref) = refs[:4], refs[4:]
    own = field_ref.shape[0] // TILE
    mirrored = is_mirrored(halos)
    done = interior_passes(halos, field_ref, own_refs, saved_out, halos == 1)
    for row in range(own):
        value = done[row] + tile(control_ref, row) if row in done else jnp.zeros((TILE, LANES), jnp.float32)
        result_ref[block(pick(mirrored, own, row), 1), :] = value
    to_fields(result_ref, fields_out, own)


def backward_body(halos, control_ref, fields_ref, saved_ref, *refs):
    halo_refs, refs = refs[:halos], refs[halos:]
    coefficient_refs, refs = (refs[:1], refs[1:]) if halos == 1 else (refs[:8], refs[8:])
    gradient_hbm, refs = refs[0], refs[1:]
    result_refs, edge_refs, semaphores = refs[:halos], refs[halos : 2 * halos], refs[-1]
    own = fields_ref.shape[2]
    mirrored = is_mirrored(halos)
    if halos == 1:
        spans = [(PASSES * mirrored.astype(jnp.int32), own - PASSES)]
        spans.append((jnp.where(mirrored, 0, own - PASSES), PASSES))
    else:
        spans = [(PASSES, own - 2 * PASSES), (own - PASSES, PASSES), (0, PASSES)]
    copies = []

    def send(source_ref, source_start, start, rows):
        for field in range(FIELDS):
            member, level = divmod(field, HELD)
            copy = pltpu.make_async_copy(
                source_ref.at[member, level, pl.ds(source_start, rows), :],
                gradient_hbm.at[member, level, pl.ds(start, rows), :],
                semaphores.at[len(copies)],
            )
            copy.start()
            copies.append(copy)

    start = pl.multiple_of(spans[0][0], TILE)
    send(fields_ref, start, start, spans[0][1])
    halo_rows = [{own + row: tile(halo_refs[0], row) for row in range(PASSES)}]
    if halos == 1:
        done = double_wedge(halo_rows[0], own, saved_ref, coefficient_refs[0])
    else:
        halo_rows.append({row - PASSES: tile(halo_refs[1], row) for row in range(PASSES)})
        own_refs, tail_refs = coefficient_refs[:4], coefficient_refs[4:]
        coefficient = coefficient_reader(own_refs, tail_refs, own)
        top = top_coefficient(halos, own_refs)
        done = wedge_passes(halos, halo_rows, own, saved_ref, coefficient, top)
    for side in range(halos):
        for row in range(PASSES):
            value = done[own - PASSES + row] + tile(control_ref, own - PASSES + row) if side == 0 else done[row] + tile(control_ref, row)
            result_refs[side][block(pick(mirrored, PASSES, row), 1), :] = value
        to_fields(result_refs[side], edge_refs[side], PASSES)
        send(edge_refs[side], 0, pl.multiple_of(spans[1 + side][0], TILE), PASSES)
    for copy in copies:
        copy.wait()


def per_device(control, members, east_coef, south_coef, innovation, huber_class, band, level_group_index):
    count, held, own, lon = control.shape
    levels, cells = members.shape[1:]
    chunks, parts, row_count = (lax.axis_size(axis) for axis in ("lev", "mem", "row"))
    assert (count * held, held, lon) == (FIELDS, HELD, HALVES * LANES)
    part = own // chunks
    halos = 1 if row_count == 2 else 2
    tail = 1 + halos * PASSES
    terms = len(matrix_terms(chunks))
    packed = part * levels // FIELDS

    control_near, east_near, south_near, *edges = call(
        pack_body,
        [pltpu.VMEM(x.shape, x.dtype) for x in (control, east_coef, south_coef)] + [planes(3 * PASSES)] * halos,
        remote(control, east_coef, south_coef),
        [pltpu.SemaphoreType.DMA((FIELDS + 2 * HELD,))],
        specs=[HBM] * 3,
    )
    halo = swap_edges(edges, "row")
    kept = halos * PASSES * 2
    *own_stencil, done_rows, saved, control_planes = call(
        functools.partial(prepare_body, halos),
        [planes(own)] * 3 + [planes(own + 1), planes(own), planes(kept), planes(own)],
        resident(control_near, east_near, south_near),
        [planes(own)] * 2,
    )
    members_planes, innovation_planes, huber_planes, matrix, transposed = call(
        columns_body,
        [planes(part * chunks), planes(packed), planes(packed), planes(terms), planes(terms)],
        [members, innovation, huber_class, band, level_group_index],
        [planes(part * chunks)],
        specs=[VMEM, VMEM, VMEM, SMEM, SMEM],
    )
    results = call(
        functools.partial(forward_body, halos),
        [planes(tail)] * 4 + [planes(part)] * chunks,
        resident(done_rows, saved, *own_stencil, *halo),
        [planes(own)],
    )
    tail_stencil = results[:4]
    columns = exchange(results[:3:-1], "lev")
    (partial,) = call(
        functools.partial(filter_body, chunks),
        [planes(packed)],
        resident(*columns[::-1], members_planes, matrix),
        [planes(part * chunks)],
    )
    partials = collect(partial, "mem")
    last_coefs, behind = [*own_stencil, *tail_stencil], []
    if halos == 1:
        last_coefs = call(compose_body, [planes((2 * PASSES - 2) * POINTS)], resident(*last_coefs, partial))
        behind = last_coefs
    lifted = call(
        functools.partial(lift_body, chunks, parts, len(behind)),
        [planes(part)] * chunks,
        resident(*partials, innovation_planes, huber_planes, members_planes, transposed, *behind),
        [planes(packed), planes(part * chunks)],
    )
    returned = exchange(lifted[::-1], "lev")
    gathered, *edges = call(
        functools.partial(gather_body, halos, chunks),
        [planes(own)] + [planes(PASSES)] * halos,
        resident(*returned[::-1]),
        [planes(own)],
    )
    halo = swap_edges(edges, "row")
    early, saved = call(
        functools.partial(interior_body, halos),
        [pltpu.VMEM(control.shape, jnp.float32), planes(kept)],
        resident(gathered, control_planes, *own_stencil),
        [planes(own)],
    )
    (gradient,) = call(
        functools.partial(backward_body, halos),
        [jax.ShapeDtypeStruct(control.shape, jnp.float32)],
        resident(control_planes, early, saved, *halo, *last_coefs),
        [planes(PASSES)] * halos
        + [pltpu.VMEM((count, held, PASSES, lon), jnp.float32)] * halos
        + [pltpu.SemaphoreType.DMA((FIELDS * (1 + halos),))],
        out_specs=[HBM],
    )
    return gradient


def solution(mesh):
    placed = (
        P("mem", "lev", "row", None),
        P("mem", None, ("row", "lev")),
        P("lev", "row", None),
        P("lev", "row", None),
        P(None, ("row", "lev")),
        P(None, ("row", "lev")),
        P(),
        P(),
    )
    return jax.shard_map(
        per_device,
        mesh=mesh,
        in_specs=placed,
        out_specs=P("mem", "lev", "row", None),
        check_vma=False,
    )
```

```python
import functools

import jax
import jax.numpy as jnp
from jax import lax
from jax.experimental import pallas as pl
from jax.experimental.pallas import tpu as pltpu
from jax.sharding import PartitionSpec as P

PASSES = 8
HUBER = 1.0
REACH = 3
POINTS = 13
LANES = 128
TILE = 8
HALVES = 2
HELD = 2
FIELDS = 4

VMEM = pl.BlockSpec(memory_space=pltpu.VMEM)
SMEM = pl.BlockSpec(memory_space=pltpu.SMEM)
HBM = pl.BlockSpec(memory_space=pltpu.HBM)


def planes(count):
    return pltpu.VMEM((count * TILE, LANES), jnp.float32)


def call(body, outs, operands, scratch=(), specs=None, out_specs=None, flops=0):
    total = sum(op.size * op.dtype.itemsize for op in operands)
    return pl.pallas_call(
        body,
        out_shape=outs,
        in_specs=specs or [VMEM] * len(operands),
        out_specs=out_specs or [VMEM] * len(outs),
        scratch_shapes=list(scratch),
        compiler_params=pltpu.CompilerParams(vmem_limit_bytes=32 * 1024 * 1024),
        cost_estimate=pl.CostEstimate(flops=flops, bytes_accessed=2 * total, transcendentals=0),
    )(*operands)


def resident(*arrays):
    return [pltpu.with_memory_space_constraint(array, pltpu.VMEM) for array in arrays]


def remote(*arrays):
    return [pltpu.with_memory_space_constraint(array, pltpu.HBM) for array in arrays]


def exchange(chunks, axis):
    count = len(chunks)
    received = list(chunks)
    for step in reversed(range(1, count)):
        received[step] = lax.ppermute(chunks[step], axis, [(i, i ^ step) for i in range(count)])
    return received


def collect(array, axis):
    count, rows = lax.axis_size(axis), lax.axis_size("row")
    received = [array]
    for step in range(1, count):
        steps = [step if row % 2 == 0 else step % (count - 1) + 1 for row in range(rows)]
        pairs = [(i * rows + row, (i + steps[row]) % count * rows + row) for i in range(count) for row in range(rows)]
        received.append(lax.ppermute(array, (axis, "row"), pairs))
    return received


def swap_edges(edges, axis):
    count = lax.axis_size(axis)
    if len(edges) == 1:
        return [lax.ppermute(edges[0], axis, [(0, 1), (1, 0)])]
    head, tail = edges
    south = lax.ppermute(head, axis, [(i + 1, i) for i in range(count - 1)])
    north = lax.ppermute(tail, axis, [(i, i + 1) for i in range(count - 1)])
    return [south, north]


def tile(ref, row):
    return ref[row * TILE : (row + 1) * TILE, :]


def set_tile(ref, row, value):
    ref[row * TILE : (row + 1) * TILE, :] = value


def block(first_row, rows):
    return pl.ds(pl.multiple_of(first_row * TILE, TILE), rows * TILE)


def spread(ref, row, sublane, values):
    ref[pl.ds(row * TILE + sublane, values.shape[0], stride=TILE), :] = values


def places():
    return lax.broadcasted_iota(jnp.int32, (TILE, LANES), 0)


def east_west(value):
    lane = lax.broadcasted_iota(jnp.int32, (TILE, LANES), 1)
    other = pltpu.roll(value, FIELDS, 0)
    east = pltpu.roll(jnp.where(lane == 0, other, value), LANES - 1, 1)
    west = pltpu.roll(jnp.where(lane == LANES - 1, other, value), 1, 1)
    return east, west


def west_of(value):
    lane = lax.broadcasted_iota(jnp.int32, (TILE, LANES), 1)
    return pltpu.roll(jnp.where(lane == LANES - 1, pltpu.roll(value, FIELDS, 0), value), 1, 1)


def halves():
    return [(half, slice(half * LANES, (half + 1) * LANES)) for half in range(HALVES)]


def pack_body(control_hbm, east_hbm, south_hbm, control_ref, east_ref, south_ref, *refs):
    send_refs, semaphores = refs[:-1], refs[-1]
    pieces = [(east_hbm.at[level], east_ref.at[level]) for level in range(HELD)]
    pieces += [(south_hbm.at[level], south_ref.at[level]) for level in range(HELD)]
    for field in range(FIELDS):
        member, level = divmod(field, HELD)
        pieces.append((control_hbm.at[member, level], control_ref.at[member, level]))
    copies = [
        pltpu.make_async_copy(source, target, semaphores.at[index]) for index, (source, target) in enumerate(pieces)
    ]
    for copy in copies:
        copy.start()
    for copy in copies:
        copy.wait()
    own = control_ref.shape[2]
    first = lax.axis_index("row") == 0

    def edges(load):
        head = load(slice(0, 2 * PASSES))[:PASSES].astype(jnp.float32)
        tail = load(slice(own - 2 * PASSES, own))[PASSES:].astype(jnp.float32)
        return [jnp.where(first, tail, head)] if len(send_refs) == 1 else [head, tail]

    for half, lanes in halves():
        for field in range(FIELDS):
            member, level = divmod(field, HELD)
            at = half * FIELDS + field
            values = edges(lambda rows: control_ref[member, level, rows, lanes])
            for send_ref, value in zip(send_refs, values):
                spread(send_ref, 0, at, value)
            for kind, coef_ref in enumerate((east_ref, south_ref)):
                values = edges(lambda rows: coef_ref[level, rows, lanes])
                for send_ref, value in zip(send_refs, values):
                    spread(send_ref, (kind + 1) * PASSES, at, value)


def is_mirrored(halos):
    return halos == 1 and lax.axis_index("row") == 1


def pick(mirrored, count, row):
    return row if mirrored is False else jnp.where(mirrored, count - 1 - row, row)


def stencil(values, row, center, east, west, above, below):
    to_east, to_west = east_west(values[row])
    total = center * values[row] + below * values[row + 1]
    if above is not None:
        total = total + above * values[row - 1]
    return total + (east * to_east + west * to_west)


def interior_passes(halos, field_ref, own_refs, saved_ref, double=False):
    center_ref, east_ref, west_ref, face_ref = own_refs
    own = field_ref.shape[0] // TILE
    values = {row: tile(field_ref, row) for row in range(own)}
    for step in range(1, PASSES + 1):
        for side in range(halos):
            kept = (own - 1 - step, own - step) if side == 0 else (step - 1, step)
            if double:
                kept = range(own - 3 - step, own + 1 - step) if step % 2 else ()
            for index, row in enumerate(kept):
                set_tile(saved_ref, (side * PASSES + step - 1) * 2 + index, values[row])
        after = {}
        for row in range(step if halos == 2 else 0, own - step):
            after[row] = stencil(
                values,
                row,
                tile(center_ref, row),
                tile(east_ref, row),
                tile(west_ref, row),
                tile(face_ref, row) if row else None,
                tile(face_ref, row + 1),
            )
        values = after
    return values


def wedge_passes(halos, halo_rows, own, saved_ref, coefficient, top):
    done = {}
    for side in range(halos):
        values = dict(halo_rows[side])
        for step in range(1, PASSES + 1):
            kept = (own - 1 - step, own - step) if side == 0 else (step - 1, step)
            for index, row in enumerate(kept):
                values[row] = tile(saved_ref, (side * PASSES + step - 1) * 2 + index)
            after = {}
            for row in range(own - step, own + PASSES - step) if side == 0 else range(step - PASSES, step):
                center, east, west, above = (coefficient(kind, row) for kind in range(4))
                after[row] = stencil(values, row, center, east, west, top if row == 0 else above, coefficient(3, row + 1))
            values = after
        done.update(values)
    return done


def shifted(value, distance):
    lane = lax.broadcasted_iota(jnp.int32, (TILE, LANES), 1)
    other = pltpu.roll(value, FIELDS, 0)
    east = pltpu.roll(jnp.where(lane < distance, other, value), LANES - distance, 1)
    west = pltpu.roll(jnp.where(lane >= LANES - distance, other, value), distance, 1)
    return east, west


def compose_body(*refs):
    own_refs, tail_refs, composed_out = refs[:4], refs[4:8], refs[-1]
    own = own_refs[0].shape[0] // TILE
    coefficient = coefficient_reader(own_refs, tail_refs, own)
    for index in range(2 * PASSES - 2):
        row = own - PASSES + index
        center, east, west, above = (coefficient(kind, row) for kind in range(4))
        below = coefficient(3, row + 1)
        (center_e, center_w), (east_e, east_w), (west_e, west_w), (below_e, below_w), (above_e, above_w) = (
            shifted(value, 1) for value in (center, east, west, below, above)
        )
        tiles = (
            center * center + east * west_e + west * east_w + below * below + above * above,
            east * (center + center_e),
            west * (center + center_w),
            east * east_e,
            west * west_w,
            below * (center + coefficient(0, row + 1)),
            east * below_e + below * coefficient(1, row + 1),
            west * below_w + below * coefficient(2, row + 1),
            above * (center + coefficient(0, row - 1)),
            east * above_e + above * coefficient(1, row - 1),
            west * above_w + above * coefficient(2, row - 1),
            below * coefficient(3, row + 2),
            above * coefficient(3, row - 1),
        )
        for place, value in enumerate(tiles):
            set_tile(composed_out, index * POINTS + place, value)


def double_wedge(values, own, saved_ref, composed_ref):
    for step in range(1, PASSES // 2 + 1):
        first = own - 2 * step
        for index in range(4):
            values[first - 2 + index] = tile(saved_ref, (step - 1) * 4 + index)
        near = {row: shifted(values[row], 1) for row in range(first - 1, first + PASSES + 1)}
        after = {}
        for row in range(first, first + PASSES):
            def coefficient(place):
                return tile(composed_ref, (row - own + PASSES) * POINTS + place)

            east, west = shifted(values[row], 2)
            total = coefficient(0) * values[row] + coefficient(5) * values[row + 1]
            total = total + (coefficient(8) * values[row - 1] + coefficient(11) * values[row + 2])
            total = total + coefficient(12) * values[row - 2]
            sides = coefficient(1) * near[row][0] + coefficient(2) * near[row][1]
            lower = coefficient(6) * near[row + 1][0] + coefficient(7) * near[row + 1][1]
            upper = coefficient(9) * near[row - 1][0] + coefficient(10) * near[row - 1][1]
            far = coefficient(3) * east + coefficient(4) * west
            after[row] = (total + sides) + ((lower + upper) + far)
        values = after
    return values


def prepare_body(halos, control_ref, east_ref, south_ref, *refs):
    own_refs, (rows_out, saved_out, field_ref, raw_east, raw_face) = refs[:4], refs[4:]
    center_out, east_out, west_out, face_out = own_refs
    own = control_ref.shape[2]
    mirrored = is_mirrored(halos)
    for half, lanes in halves():
        for field in range(FIELDS):
            member, level = divmod(field, HELD)
            at = half * FIELDS + field
            spread(rows_out, 0, at, control_ref[member, level, :, lanes].astype(jnp.float32))
            spread(raw_east, 0, at, east_ref[level, :, lanes])
            spread(raw_face, 0, at, south_ref[level, :, lanes])
    for row in range(own):
        source = pick(mirrored, own, row)
        set_tile(field_ref, row, rows_out[block(source, 1), :])
        east = raw_east[block(source, 1), :]
        set_tile(east_out, row, east)
        set_tile(west_out, row, west_of(east))
        if row == 0:
            face = tile(raw_face, 0)
            face = face if mirrored is False else jnp.where(mirrored, 0.0, face)
        else:
            face = raw_face[block(row if mirrored is False else jnp.where(mirrored, own - row, row), 1), :]
        set_tile(face_out, row, face)
    set_tile(face_out, own, tile(raw_face, 0))
    for row in range(own - 1):
        total = 1.0 - tile(east_out, row) - tile(west_out, row)
        set_tile(center_out, row, total - tile(face_out, row + 1) - tile(face_out, row))
    for row, value in interior_passes(halos, field_ref, own_refs, saved_out).items():
        set_tile(rows_out, row, value)


def finish_coefficients(halos, halo_refs, own_refs, tail_refs, own):
    _, east_own, west_own, face_own = own_refs
    center_tail, east_tail, west_tail, face_tail = tail_refs
    mirrored = is_mirrored(halos)

    def halo_tile(side, kind, row):
        return halo_refs[side][block(kind * PASSES + row, 1), :]

    set_tile(east_tail, 0, tile(east_own, own - 1))
    set_tile(west_tail, 0, tile(west_own, own - 1))
    set_tile(face_tail, 0, tile(face_own, own - 1))
    for row in range(PASSES):
        east = halo_tile(0, 1, pick(mirrored, PASSES, row))
        set_tile(east_tail, 1 + row, east)
        set_tile(west_tail, 1 + row, west_of(east))
        if mirrored is False:
            face = halo_tile(0, 2, row)
        elif row == 0:
            face = jnp.where(mirrored, tile(face_own, own), halo_tile(0, 2, 0))
        else:
            face = halo_tile(0, 2, jnp.where(mirrored, PASSES - row, row))
        set_tile(face_tail, 1 + row, face)
    for row in range(PASSES):
        total = 1.0 - tile(east_tail, row) - tile(west_tail, row)
        set_tile(center_tail, row, total - tile(face_tail, row + 1) - tile(face_tail, row))
    if halos == 2:
        for row in range(PASSES):
            at = 1 + PASSES + row
            east, face = halo_tile(1, 1, row), halo_tile(1, 2, row)
            below = halo_tile(1, 2, row + 1) if row + 1 < PASSES else tile(face_own, 0)
            west = west_of(east)
            for ref, value in zip(tail_refs, (1.0 - east - west - below - face, east, west, face)):
                set_tile(ref, at, value)


def coefficient_reader(own_refs, tail_refs, own):
    def coefficient(kind, row):
        if row < 0:
            return tile(tail_refs[kind], 1 + 2 * PASSES + row)
        return tile(own_refs[kind], row) if row < own - 1 else tile(tail_refs[kind], row - own + 1)

    return coefficient


def top_coefficient(halos, own_refs):
    return None if halos == 1 else jnp.where(lax.axis_index("row") == 0, 0.0, tile(own_refs[3], 0))


def forward_body(halos, rows_ref, saved_ref, *refs):
    own_refs, halo_refs, refs = refs[:4], refs[4 : 4 + halos], refs[4 + halos :]
    tail_refs, chunk_refs, sorted_ref = refs[:4], refs[4:-1], refs[-1]
    own = rows_ref.shape[0] // TILE
    lev_at = lax.axis_index("lev")
    mirrored = is_mirrored(halos)
    finish_coefficients(halos, halo_refs, own_refs, tail_refs, own)
    halo_rows = [{own + row: halo_refs[0][block(pick(mirrored, PASSES, row), 1), :] for row in range(PASSES)}]
    if halos == 2:
        halo_rows.append({row - PASSES: tile(halo_refs[1], row) for row in range(PASSES)})
    coefficient = coefficient_reader(own_refs, tail_refs, own)
    top = top_coefficient(halos, own_refs)
    done = wedge_passes(halos, halo_rows, own, saved_ref, coefficient, top)
    for row in range(own):
        value = done[row] if row in done else tile(rows_ref, row)
        sorted_ref[block(pick(mirrored, own, row), 1), :] = value
    part = own // len(chunk_refs)
    for step, chunk_ref in enumerate(reversed(chunk_refs)):
        chunk_ref[...] = sorted_ref[block(lax.bitwise_xor(lev_at, step) * part, part), :]


def matrix_terms(groups):
    return [
        (group, other, cross)
        for group in range(groups)
        for other in range(max(0, group - 2), min(groups, group + 3))
        for cross in range(2)
        if abs(group - other) < 2 or cross
    ]


def swap_levels(value, sublane):
    return jnp.where(sublane % HELD == 0, pltpu.roll(value, TILE - 1, 0), pltpu.roll(value, 1, 0))


def columns_body(members_ref, innovation_ref, huber_ref, band_ref, group_ref, *refs):
    members_out, innovation_out, huber_out, matrix_out, transposed_out, levels_ref = refs
    count, levels, cells = members_ref.shape
    groups, lon = levels // HELD, HALVES * LANES
    rows, packed = cells // lon, levels // FIELDS
    sublane = places()
    for member in range(count):
        for row in range(rows):
            for half in range(HALVES):
                lanes = slice(row * lon + half * LANES, row * lon + (half + 1) * LANES)
                start = ((member * rows + row) * HALVES + half) * levels
                levels_ref[start : start + levels, :] = members_ref[member, :, lanes].astype(jnp.float32)
                for level in range(HELD):
                    at = half * FIELDS + member * HELD + level
                    spread(members_out, row * groups, at, levels_ref[pl.ds(start + level, groups, stride=HELD), :])
    for row in range(rows):
        for half in range(HALVES):
            lanes = slice(row * lon + half * LANES, row * lon + (half + 1) * LANES)
            for pack in range(packed):
                source = slice(pack * FIELDS, (pack + 1) * FIELDS)
                start = (row * packed + pack) * TILE + half * FIELDS
                innovation_out[start : start + FIELDS, :] = innovation_ref[source, lanes]
                huber_out[start : start + FIELDS, :] = huber_ref[source, lanes].astype(jnp.float32)

    def entry(level, other):
        offset = other - level + REACH
        if not 0 <= offset < 2 * REACH + 1:
            return jnp.float32(0.0)
        value = band_ref[offset, level] + jnp.float32(1.0 if offset == REACH else 0.0)
        return jnp.where(group_ref[level] == group_ref[other], value, jnp.float32(0.0))

    for slot, (group, other, cross) in enumerate(matrix_terms(groups)):
        pairs = [(group * HELD + level, other * HELD + (level ^ cross)) for level in range(HELD)]
        even, odd = (entry(a, b) for a, b in pairs)
        set_tile(matrix_out, slot, jnp.where(sublane % HELD == 0, even, odd))
        even, odd = (entry(b, a) for a, b in pairs)
        set_tile(transposed_out, slot, jnp.where(sublane % HELD == 0, even, odd))


def apply_matrix(matrix_ref, values, sublane):
    crossed = [swap_levels(value, sublane) for value in values]
    totals = [None] * len(values)
    for slot, (group, other, cross) in enumerate(matrix_terms(len(values))):
        term = tile(matrix_ref, slot) * (crossed if cross else values)[other]
        totals[group] = term if totals[group] is None else totals[group] + term
    return totals


def filter_body(chunks, *refs):
    chunk_refs = refs[:chunks]
    members_ref, matrix_ref, partial_ref, columns = refs[chunks:]
    rows = chunk_refs[0].shape[0] // TILE
    lev_at = lax.axis_index("lev")
    sublane = places()
    first_member = sublane % FIELDS < HELD
    for step, chunk_ref in enumerate(reversed(chunk_refs)):
        columns[block(lax.bitwise_xor(lev_at, step) * rows, rows), :] = chunk_ref[...]
    for row in range(rows):
        filtered = apply_matrix(matrix_ref, [tile(columns, group * rows + row) for group in range(chunks)], sublane)
        terms = [tile(members_ref, row * chunks + group) * value for group, value in enumerate(filtered)]
        for pack in range(chunks // 2):
            lower, upper = terms[2 * pack], terms[2 * pack + 1]
            total = jnp.where(first_member, lower, upper)
            total = total + jnp.where(first_member, pltpu.roll(lower, TILE - HELD, 0), pltpu.roll(upper, HELD, 0))
            set_tile(partial_ref, row * (chunks // 2) + pack, total)


def lift_body(chunks, parts, extra, *refs):
    part_refs, refs = refs[:parts], refs[parts:]
    innovation_ref, huber_ref, members_ref, transposed_ref = refs[:4]
    refs = refs[4 + extra :]
    chunk_refs, (weighted_ref, sorted_ref) = refs[:chunks], refs[chunks:]
    rows = chunk_refs[0].shape[0] // TILE
    lev_at = lax.axis_index("lev")
    sublane = places()
    first_member = sublane % FIELDS < HELD
    increment = part_refs[0][...]
    for part_ref in part_refs[1:]:
        increment = increment + part_ref[...]
    residual = increment - innovation_ref[...]
    scale = HUBER / jnp.maximum(jnp.abs(residual), HUBER)
    weighted_ref[...] = jnp.where(huber_ref[...] == 1.0, scale, 1.0) * residual
    for row in range(rows):
        adjoint = []
        for pack in range(chunks // 2):
            weighted = tile(weighted_ref, row * (chunks // 2) + pack)
            lower = jnp.where(first_member, weighted, pltpu.roll(weighted, HELD, 0))
            upper = jnp.where(first_member, pltpu.roll(weighted, TILE - HELD, 0), weighted)
            for value in (lower, upper):
                adjoint.append(value * tile(members_ref, row * chunks + len(adjoint)))
        for group, value in enumerate(apply_matrix(transposed_ref, adjoint, sublane)):
            set_tile(sorted_ref, group * rows + row, value)
    for step, chunk_ref in enumerate(reversed(chunk_refs)):
        chunk_ref[...] = sorted_ref[block(lax.bitwise_xor(lev_at, step) * rows, rows), :]


def gather_body(halos, chunks, *refs):
    chunk_refs, field_ref, send_refs, sorted_ref = refs[:chunks], refs[chunks], refs[chunks + 1 : -1], refs[-1]
    lev_at = lax.axis_index("lev")
    mirrored = is_mirrored(halos)
    rows = chunk_refs[0].shape[0] // TILE
    own = rows * chunks
    for step, chunk_ref in enumerate(reversed(chunk_refs)):
        sorted_ref[block(lax.bitwise_xor(lev_at, step) * rows, rows), :] = chunk_ref[...]
    for row in range(own):
        set_tile(field_ref, row, sorted_ref[block(pick(mirrored, own, row), 1), :])
    for row in range(PASSES):
        if halos == 1:
            set_tile(send_refs[0], row, tile(field_ref, own - 1 - row))
        else:
            set_tile(send_refs[0], row, tile(field_ref, row))
            set_tile(send_refs[1], row, tile(field_ref, own - PASSES + row))


def to_fields(planes_ref, fields_ref, rows):
    for field in range(FIELDS):
        member, level = divmod(field, HELD)
        for half, lanes in halves():
            fields_ref[member, level, :, lanes] = planes_ref[pl.ds(half * FIELDS + field, rows, stride=TILE), :]


def interior_body(halos, field_ref, control_ref, *refs):
    own_refs, (fields_out, saved_out, result_ref) = refs[:4], refs[4:]
    own = field_ref.shape[0] // TILE
    mirrored = is_mirrored(halos)
    done = interior_passes(halos, field_ref, own_refs, saved_out, halos == 1)
    for row in range(own):
        value = done[row] + tile(control_ref, row) if row in done else jnp.zeros((TILE, LANES), jnp.float32)
        result_ref[block(pick(mirrored, own, row), 1), :] = value
    to_fields(result_ref, fields_out, own)


def backward_body(halos, control_ref, fields_ref, saved_ref, *refs):
    halo_refs, refs = refs[:halos], refs[halos:]
    coefficient_refs, refs = (refs[:1], refs[1:]) if halos == 1 else (refs[:8], refs[8:])
    gradient_hbm, refs = refs[0], refs[1:]
    result_refs, edge_refs, semaphores = refs[:halos], refs[halos : 2 * halos], refs[-1]
    own = fields_ref.shape[2]
    mirrored = is_mirrored(halos)
    if halos == 1:
        spans = [(PASSES * mirrored.astype(jnp.int32), own - PASSES)]
        spans.append((jnp.where(mirrored, 0, own - PASSES), PASSES))
    else:
        spans = [(PASSES, own - 2 * PASSES), (own - PASSES, PASSES), (0, PASSES)]
    copies = []

    def send(source_ref, source_start, start, rows):
        for field in range(FIELDS):
            member, level = divmod(field, HELD)
            copy = pltpu.make_async_copy(
                source_ref.at[member, level, pl.ds(source_start, rows), :],
                gradient_hbm.at[member, level, pl.ds(start, rows), :],
                semaphores.at[len(copies)],
            )
            copy.start()
            copies.append(copy)

    start = pl.multiple_of(spans[0][0], TILE)
    send(fields_ref, start, start, spans[0][1])
    halo_rows = [{own + row: tile(halo_refs[0], row) for row in range(PASSES)}]
    if halos == 1:
        done = double_wedge(halo_rows[0], own, saved_ref, coefficient_refs[0])
    else:
        halo_rows.append({row - PASSES: tile(halo_refs[1], row) for row in range(PASSES)})
        own_refs, tail_refs = coefficient_refs[:4], coefficient_refs[4:]
        coefficient = coefficient_reader(own_refs, tail_refs, own)
        top = top_coefficient(halos, own_refs)
        done = wedge_passes(halos, halo_rows, own, saved_ref, coefficient, top)
    for side in range(halos):
        for row in range(PASSES):
            value = done[own - PASSES + row] + tile(control_ref, own - PASSES + row) if side == 0 else done[row] + tile(control_ref, row)
            result_refs[side][block(pick(mirrored, PASSES, row), 1), :] = value
        to_fields(result_refs[side], edge_refs[side], PASSES)
        send(edge_refs[side], 0, pl.multiple_of(spans[1 + side][0], TILE), PASSES)
    for copy in copies:
        copy.wait()


def per_device(control, members, east_coef, south_coef, innovation, huber_class, band, level_group_index):
    count, held, own, lon = control.shape
    levels, cells = members.shape[1:]
    chunks, parts, row_count = (lax.axis_size(axis) for axis in ("lev", "mem", "row"))
    assert (count * held, held, lon) == (FIELDS, HELD, HALVES * LANES)
    part = own // chunks
    halos = 1 if row_count == 2 else 2
    tail = 1 + halos * PASSES
    terms = len(matrix_terms(chunks))
    packed = part * levels // FIELDS

    control_near, east_near, south_near, *edges = call(
        pack_body,
        [pltpu.VMEM(x.shape, x.dtype) for x in (control, east_coef, south_coef)] + [planes(3 * PASSES)] * halos,
        remote(control, east_coef, south_coef),
        [pltpu.SemaphoreType.DMA((FIELDS + 2 * HELD,))],
        specs=[HBM] * 3,
    )
    halo = swap_edges(edges, "row")
    kept = halos * PASSES * 2
    *own_stencil, done_rows, saved, control_planes = call(
        functools.partial(prepare_body, halos),
        [planes(own)] * 3 + [planes(own + 1), planes(own), planes(kept), planes(own)],
        resident(control_near, east_near, south_near),
        [planes(own)] * 2,
    )
    members_planes, innovation_planes, huber_planes, matrix, transposed = call(
        columns_body,
        [planes(part * chunks), planes(packed), planes(packed), planes(terms), planes(terms)],
        [members, innovation, huber_class, band, level_group_index],
        [planes(part * chunks)],
        specs=[VMEM, VMEM, VMEM, SMEM, SMEM],
    )
    results = call(
        functools.partial(forward_body, halos),
        [planes(tail)] * 4 + [planes(part)] * chunks,
        resident(done_rows, saved, *own_stencil, *halo),
        [planes(own)],
    )
    tail_stencil = results[:4]
    columns = exchange(results[:3:-1], "lev")
    (partial,) = call(
        functools.partial(filter_body, chunks),
        [planes(packed)],
        resident(*columns[::-1], members_planes, matrix),
        [planes(part * chunks)],
    )
    partials = collect(partial, "mem")
    last_coefs, behind = [*own_stencil, *tail_stencil], []
    if halos == 1:
        last_coefs = call(compose_body, [planes((2 * PASSES - 2) * POINTS)], resident(*last_coefs, partial))
        behind = last_coefs
    lifted = call(
        functools.partial(lift_body, chunks, parts, len(behind)),
        [planes(part)] * chunks,
        resident(*partials, innovation_planes, huber_planes, members_planes, transposed, *behind),
        [planes(packed), planes(part * chunks)],
    )
    returned = exchange(lifted[::-1], "lev")
    gathered, *edges = call(
        functools.partial(gather_body, halos, chunks),
        [planes(own)] + [planes(PASSES)] * halos,
        resident(*returned[::-1]),
        [planes(own)],
    )
    halo = swap_edges(edges, "row")
    early, saved = call(
        functools.partial(interior_body, halos),
        [pltpu.VMEM(control.shape, jnp.float32), planes(kept)],
        resident(gathered, control_planes, *own_stencil),
        [planes(own)],
    )
    (gradient,) = call(
        functools.partial(backward_body, halos),
        [jax.ShapeDtypeStruct(control.shape, jnp.float32)],
        resident(control_planes, early, saved, *halo, *last_coefs),
        [planes(PASSES)] * halos
        + [pltpu.VMEM((count, held, PASSES, lon), jnp.float32)] * halos
        + [pltpu.SemaphoreType.DMA((FIELDS * (1 + halos),))],
        out_specs=[HBM],
    )
    return gradient


def solution(mesh):
    placed = (
        P("mem", "lev", "row", None),
        P("mem", None, ("row", "lev")),
        P("lev", "row", None),
        P("lev", "row", None),
        P(None, ("row", "lev")),
        P(None, ("row", "lev")),
        P(),
        P(),
    )
    return jax.shard_map(
        per_device,
        mesh=mesh,
        in_specs=placed,
        out_specs=P("mem", "lev", "row", None),
        check_vma=False,
    )
```

```python
import functools

import jax
import jax.numpy as jnp
from jax import lax
from jax.experimental import pallas as pl
from jax.experimental.pallas import tpu as pltpu
from jax.sharding import PartitionSpec as P

PASSES = 8
HUBER = 1.0
REACH = 3
POINTS = 13
LANES = 128
TILE = 8
HALVES = 2
HELD = 2
FIELDS = 4

VMEM = pl.BlockSpec(memory_space=pltpu.VMEM)
SMEM = pl.BlockSpec(memory_space=pltpu.SMEM)
HBM = pl.BlockSpec(memory_space=pltpu.HBM)


def planes(count):
    return pltpu.VMEM((count * TILE, LANES), jnp.float32)


def call(body, outs, operands, scratch=(), specs=None, out_specs=None, flops=0):
    total = sum(op.size * op.dtype.itemsize for op in operands)
    return pl.pallas_call(
        body,
        out_shape=outs,
        in_specs=specs or [VMEM] * len(operands),
        out_specs=out_specs or [VMEM] * len(outs),
        scratch_shapes=list(scratch),
        compiler_params=pltpu.CompilerParams(vmem_limit_bytes=32 * 1024 * 1024),
        cost_estimate=pl.CostEstimate(flops=flops, bytes_accessed=2 * total, transcendentals=0),
    )(*operands)


def resident(*arrays):
    return [pltpu.with_memory_space_constraint(array, pltpu.VMEM) for array in arrays]


def remote(*arrays):
    return [pltpu.with_memory_space_constraint(array, pltpu.HBM) for array in arrays]


def exchange(chunks, axis):
    count = len(chunks)
    received = list(chunks)
    for step in reversed(range(1, count)):
        received[step] = lax.ppermute(chunks[step], axis, [(i, i ^ step) for i in range(count)])
    return received


def collect(array, axis):
    count = lax.axis_size(axis)
    shifts = [[(i, (i + step) % count) for i in range(count)] for step in range(1, count)]
    return [array] + [lax.ppermute(array, axis, shift) for shift in shifts]


def swap_edges(edges, axis):
    count = lax.axis_size(axis)
    if len(edges) == 1:
        return [lax.ppermute(edges[0], axis, [(0, 1), (1, 0)])]
    head, tail = edges
    south = lax.ppermute(head, axis, [(i + 1, i) for i in range(count - 1)])
    north = lax.ppermute(tail, axis, [(i, i + 1) for i in range(count - 1)])
    return [south, north]


def tile(ref, row):
    return ref[row * TILE : (row + 1) * TILE, :]


def set_tile(ref, row, value):
    ref[row * TILE : (row + 1) * TILE, :] = value


def block(first_row, rows):
    return pl.ds(pl.multiple_of(first_row * TILE, TILE), rows * TILE)


def spread(ref, row, sublane, values):
    ref[pl.ds(row * TILE + sublane, values.shape[0], stride=TILE), :] = values


def places():
    return lax.broadcasted_iota(jnp.int32, (TILE, LANES), 0)


def east_west(value):
    lane = lax.broadcasted_iota(jnp.int32, (TILE, LANES), 1)
    other = pltpu.roll(value, FIELDS, 0)
    east = pltpu.roll(jnp.where(lane == 0, other, value), LANES - 1, 1)
    west = pltpu.roll(jnp.where(lane == LANES - 1, other, value), 1, 1)
    return east, west


def west_of(value):
    lane = lax.broadcasted_iota(jnp.int32, (TILE, LANES), 1)
    return pltpu.roll(jnp.where(lane == LANES - 1, pltpu.roll(value, FIELDS, 0), value), 1, 1)


def halves():
    return [(half, slice(half * LANES, (half + 1) * LANES)) for half in range(HALVES)]


def pack_body(control_hbm, east_hbm, south_hbm, control_ref, east_ref, south_ref, *refs):
    send_refs, semaphores = refs[:-1], refs[-1]
    pieces = [(east_hbm.at[level], east_ref.at[level]) for level in range(HELD)]
    pieces += [(south_hbm.at[level], south_ref.at[level]) for level in range(HELD)]
    for field in range(FIELDS):
        member, level = divmod(field, HELD)
        pieces.append((control_hbm.at[member, level], control_ref.at[member, level]))
    copies = [
        pltpu.make_async_copy(source, target, semaphores.at[index]) for index, (source, target) in enumerate(pieces)
    ]
    for copy in copies:
        copy.start()
    for copy in copies:
        copy.wait()
    own = control_ref.shape[2]
    first = lax.axis_index("row") == 0

    def edges(load):
        head = load(slice(0, 2 * PASSES))[:PASSES].astype(jnp.float32)
        tail = load(slice(own - 2 * PASSES, own))[PASSES:].astype(jnp.float32)
        return [jnp.where(first, tail, head)] if len(send_refs) == 1 else [head, tail]

    for half, lanes in halves():
        for field in range(FIELDS):
            member, level = divmod(field, HELD)
            at = half * FIELDS + field
            values = edges(lambda rows: control_ref[member, level, rows, lanes])
            for send_ref, value in zip(send_refs, values):
                spread(send_ref, 0, at, value)
            for kind, coef_ref in enumerate((east_ref, south_ref)):
                values = edges(lambda rows: coef_ref[level, rows, lanes])
                for send_ref, value in zip(send_refs, values):
                    spread(send_ref, (kind + 1) * PASSES, at, value)


def is_mirrored(halos):
    return halos == 1 and lax.axis_index("row") == 1


def pick(mirrored, count, row):
    return row if mirrored is False else jnp.where(mirrored, count - 1 - row, row)


def stencil(values, row, center, east, west, above, below):
    to_east, to_west = east_west(values[row])
    total = center * values[row] + below * values[row + 1]
    if above is not None:
        total = total + above * values[row - 1]
    return total + (east * to_east + west * to_west)


def interior_passes(halos, field_ref, own_refs, saved_ref, double=False):
    center_ref, east_ref, west_ref, face_ref = own_refs
    own = field_ref.shape[0] // TILE
    values = {row: tile(field_ref, row) for row in range(own)}
    for step in range(1, PASSES + 1):
        for side in range(halos):
            kept = (own - 1 - step, own - step) if side == 0 else (step - 1, step)
            if double:
                kept = range(own - 3 - step, own + 1 - step) if step % 2 else ()
            for index, row in enumerate(kept):
                set_tile(saved_ref, (side * PASSES + step - 1) * 2 + index, values[row])
        after = {}
        for row in range(step if halos == 2 else 0, own - step):
            after[row] = stencil(
                values,
                row,
                tile(center_ref, row),
                tile(east_ref, row),
                tile(west_ref, row),
                tile(face_ref, row) if row else None,
                tile(face_ref, row + 1),
            )
        values = after
    return values


def wedge_passes(halos, halo_rows, own, saved_ref, coefficient, top):
    done = {}
    for side in range(halos):
        values = dict(halo_rows[side])
        for step in range(1, PASSES + 1):
            kept = (own - 1 - step, own - step) if side == 0 else (step - 1, step)
            for index, row in enumerate(kept):
                values[row] = tile(saved_ref, (side * PASSES + step - 1) * 2 + index)
            after = {}
            for row in range(own - step, own + PASSES - step) if side == 0 else range(step - PASSES, step):
                center, east, west, above = (coefficient(kind, row) for kind in range(4))
                after[row] = stencil(values, row, center, east, west, top if row == 0 else above, coefficient(3, row + 1))
            values = after
        done.update(values)
    return done


def shifted(value, distance):
    lane = lax.broadcasted_iota(jnp.int32, (TILE, LANES), 1)
    other = pltpu.roll(value, FIELDS, 0)
    east = pltpu.roll(jnp.where(lane < distance, other, value), LANES - distance, 1)
    west = pltpu.roll(jnp.where(lane >= LANES - distance, other, value), distance, 1)
    return east, west


def compose(coefficient, rows, composed_out):
    for index, row in enumerate(rows):
        center, east, west, above = (coefficient(kind, row) for kind in range(4))
        below = coefficient(3, row + 1)
        (center_e, center_w), (east_e, east_w), (west_e, west_w), (below_e, below_w), (above_e, above_w) = (
            shifted(value, 1) for value in (center, east, west, below, above)
        )
        tiles = (
            center * center + east * west_e + west * east_w + below * below + above * above,
            east * (center + center_e),
            west * (center + center_w),
            east * east_e,
            west * west_w,
            below * (center + coefficient(0, row + 1)),
            east * below_e + below * coefficient(1, row + 1),
            west * below_w + below * coefficient(2, row + 1),
            above * (center + coefficient(0, row - 1)),
            east * above_e + above * coefficient(1, row - 1),
            west * above_w + above * coefficient(2, row - 1),
            below * coefficient(3, row + 2),
            above * coefficient(3, row - 1),
        )
        for place, value in enumerate(tiles):
            set_tile(composed_out, index * POINTS + place, value)


def composed_rows(own):
    return range(own - PASSES, own - 2), range(own - 2, own + PASSES - 2)


def double_wedge(values, own, saved_ref, composed_refs):
    for step in range(1, PASSES // 2 + 1):
        first = own - 2 * step
        for index in range(4):
            values[first - 2 + index] = tile(saved_ref, (step - 1) * 4 + index)
        near = {row: shifted(values[row], 1) for row in range(first - 1, first + PASSES + 1)}
        after = {}
        for row in range(first, first + PASSES):
            def coefficient(place):
                part = int(row >= own - 2)
                return tile(composed_refs[part], (row - composed_rows(own)[part][0]) * POINTS + place)

            east, west = shifted(values[row], 2)
            total = coefficient(0) * values[row] + coefficient(5) * values[row + 1]
            total = total + (coefficient(8) * values[row - 1] + coefficient(11) * values[row + 2])
            total = total + coefficient(12) * values[row - 2]
            sides = coefficient(1) * near[row][0] + coefficient(2) * near[row][1]
            lower = coefficient(6) * near[row + 1][0] + coefficient(7) * near[row + 1][1]
            upper = coefficient(9) * near[row - 1][0] + coefficient(10) * near[row - 1][1]
            far = coefficient(3) * east + coefficient(4) * west
            after[row] = (total + sides) + ((lower + upper) + far)
        values = after
    return values


def prepare_body(halos, control_ref, east_ref, south_ref, *refs):
    own_refs, (rows_out, saved_out, field_ref), refs = refs[:4], refs[4:7], refs[7:]
    raw_east, raw_face = refs[-2:]
    center_out, east_out, west_out, face_out = own_refs
    own = control_ref.shape[2]
    mirrored = is_mirrored(halos)
    for half, lanes in halves():
        for field in range(FIELDS):
            member, level = divmod(field, HELD)
            at = half * FIELDS + field
            spread(rows_out, 0, at, control_ref[member, level, :, lanes].astype(jnp.float32))
            spread(raw_east, 0, at, east_ref[level, :, lanes])
            spread(raw_face, 0, at, south_ref[level, :, lanes])
    for row in range(own):
        source = pick(mirrored, own, row)
        set_tile(field_ref, row, rows_out[block(source, 1), :])
        east = raw_east[block(source, 1), :]
        set_tile(east_out, row, east)
        set_tile(west_out, row, west_of(east))
        if row == 0:
            face = tile(raw_face, 0)
            face = face if mirrored is False else jnp.where(mirrored, 0.0, face)
        else:
            face = raw_face[block(row if mirrored is False else jnp.where(mirrored, own - row, row), 1), :]
        set_tile(face_out, row, face)
    set_tile(face_out, own, tile(raw_face, 0))
    for row in range(own - 1):
        total = 1.0 - tile(east_out, row) - tile(west_out, row)
        set_tile(center_out, row, total - tile(face_out, row + 1) - tile(face_out, row))
    for row, value in interior_passes(halos, field_ref, own_refs, saved_out, halos == 1).items():
        set_tile(rows_out, row, value)
    if halos == 1:
        compose(lambda kind, row: tile(own_refs[kind], row), composed_rows(own)[0], refs[0])


def finish_coefficients(halos, halo_refs, own_refs, tail_refs, own):
    _, east_own, west_own, face_own = own_refs
    center_tail, east_tail, west_tail, face_tail = tail_refs
    mirrored = is_mirrored(halos)

    def halo_tile(side, kind, row):
        return halo_refs[side][block(kind * PASSES + row, 1), :]

    set_tile(east_tail, 0, tile(east_own, own - 1))
    set_tile(west_tail, 0, tile(west_own, own - 1))
    set_tile(face_tail, 0, tile(face_own, own - 1))
    for row in range(PASSES):
        east = halo_tile(0, 1, pick(mirrored, PASSES, row))
        set_tile(east_tail, 1 + row, east)
        set_tile(west_tail, 1 + row, west_of(east))
        if mirrored is False:
            face = halo_tile(0, 2, row)
        elif row == 0:
            face = jnp.where(mirrored, tile(face_own, own), halo_tile(0, 2, 0))
        else:
            face = halo_tile(0, 2, jnp.where(mirrored, PASSES - row, row))
        set_tile(face_tail, 1 + row, face)
    for row in range(PASSES):
        total = 1.0 - tile(east_tail, row) - tile(west_tail, row)
        set_tile(center_tail, row, total - tile(face_tail, row + 1) - tile(face_tail, row))
    if halos == 2:
        for row in range(PASSES):
            at = 1 + PASSES + row
            east, face = halo_tile(1, 1, row), halo_tile(1, 2, row)
            below = halo_tile(1, 2, row + 1) if row + 1 < PASSES else tile(face_own, 0)
            west = west_of(east)
            for ref, value in zip(tail_refs, (1.0 - east - west - below - face, east, west, face)):
                set_tile(ref, at, value)


def coefficient_reader(own_refs, tail_refs, own):
    def coefficient(kind, row):
        if row < 0:
            return tile(tail_refs[kind], 1 + 2 * PASSES + row)
        return tile(own_refs[kind], row) if row < own - 1 else tile(tail_refs[kind], row - own + 1)

    return coefficient


def top_coefficient(halos, own_refs):
    return None if halos == 1 else jnp.where(lax.axis_index("row") == 0, 0.0, tile(own_refs[3], 0))


def forward_body(halos, rows_ref, saved_ref, *refs):
    own_refs, halo_refs, refs = refs[:4], refs[4 : 4 + halos], refs[4 + halos :]
    if halos == 1:
        composed_own, composed_tail, refs, tail_refs = refs[0], refs[1], refs[2:-4], refs[-4:]
    else:
        tail_refs, refs = refs[:4], refs[4:]
    chunk_refs, sorted_ref = refs[:-1], refs[-1]
    own = rows_ref.shape[0] // TILE
    lev_at = lax.axis_index("lev")
    mirrored = is_mirrored(halos)
    finish_coefficients(halos, halo_refs, own_refs, tail_refs, own)
    halo_rows = [{own + row: halo_refs[0][block(pick(mirrored, PASSES, row), 1), :] for row in range(PASSES)}]
    coefficient = coefficient_reader(own_refs, tail_refs, own)
    if halos == 1:
        compose(coefficient, composed_rows(own)[1], composed_tail)
        done = double_wedge(halo_rows[0], own, saved_ref, (composed_own, composed_tail))
    else:
        halo_rows.append({row - PASSES: tile(halo_refs[1], row) for row in range(PASSES)})
        top = top_coefficient(halos, own_refs)
        done = wedge_passes(halos, halo_rows, own, saved_ref, coefficient, top)
    for row in range(own):
        value = done[row] if row in done else tile(rows_ref, row)
        sorted_ref[block(pick(mirrored, own, row), 1), :] = value
    part = own // len(chunk_refs)
    for step, chunk_ref in enumerate(reversed(chunk_refs)):
        chunk_ref[...] = sorted_ref[block(lax.bitwise_xor(lev_at, step) * part, part), :]


def matrix_terms(groups):
    return [
        (group, other, cross)
        for group in range(groups)
        for other in range(max(0, group - 2), min(groups, group + 3))
        for cross in range(2)
        if abs(group - other) < 2 or cross
    ]


def swap_levels(value, sublane):
    return jnp.where(sublane % HELD == 0, pltpu.roll(value, TILE - 1, 0), pltpu.roll(value, 1, 0))


def columns_body(members_ref, innovation_ref, huber_ref, band_ref, group_ref, *refs):
    members_out, innovation_out, huber_out, matrix_out, transposed_out, levels_ref = refs
    count, levels, cells = members_ref.shape
    groups, lon = levels // HELD, HALVES * LANES
    rows, packed = cells // lon, levels // FIELDS
    sublane = places()
    for member in range(count):
        for row in range(rows):
            for half in range(HALVES):
                lanes = slice(row * lon + half * LANES, row * lon + (half + 1) * LANES)
                start = ((member * rows + row) * HALVES + half) * levels
                levels_ref[start : start + levels, :] = members_ref[member, :, lanes].astype(jnp.float32)
                for level in range(HELD):
                    at = half * FIELDS + member * HELD + level
                    spread(members_out, row * groups, at, levels_ref[pl.ds(start + level, groups, stride=HELD), :])
    for row in range(rows):
        for half in range(HALVES):
            lanes = slice(row * lon + half * LANES, row * lon + (half + 1) * LANES)
            for pack in range(packed):
                source = slice(pack * FIELDS, (pack + 1) * FIELDS)
                start = (row * packed + pack) * TILE + half * FIELDS
                innovation_out[start : start + FIELDS, :] = innovation_ref[source, lanes]
                huber_out[start : start + FIELDS, :] = huber_ref[source, lanes].astype(jnp.float32)

    def entry(level, other):
        offset = other - level + REACH
        if not 0 <= offset < 2 * REACH + 1:
            return jnp.float32(0.0)
        value = band_ref[offset, level] + jnp.float32(1.0 if offset == REACH else 0.0)
        return jnp.where(group_ref[level] == group_ref[other], value, jnp.float32(0.0))

    for slot, (group, other, cross) in enumerate(matrix_terms(groups)):
        pairs = [(group * HELD + level, other * HELD + (level ^ cross)) for level in range(HELD)]
        even, odd = (entry(a, b) for a, b in pairs)
        set_tile(matrix_out, slot, jnp.where(sublane % HELD == 0, even, odd))
        even, odd = (entry(b, a) for a, b in pairs)
        set_tile(transposed_out, slot, jnp.where(sublane % HELD == 0, even, odd))


def apply_matrix(matrix_ref, values, sublane):
    crossed = [swap_levels(value, sublane) for value in values]
    totals = [None] * len(values)
    for slot, (group, other, cross) in enumerate(matrix_terms(len(values))):
        term = tile(matrix_ref, slot) * (crossed if cross else values)[other]
        totals[group] = term if totals[group] is None else totals[group] + term
    return totals


def filter_body(chunks, *refs):
    chunk_refs = refs[:chunks]
    members_ref, matrix_ref, partial_ref, columns = refs[chunks:]
    rows = chunk_refs[0].shape[0] // TILE
    lev_at = lax.axis_index("lev")
    sublane = places()
    first_member = sublane % FIELDS < HELD
    for step, chunk_ref in enumerate(reversed(chunk_refs)):
        columns[block(lax.bitwise_xor(lev_at, step) * rows, rows), :] = chunk_ref[...]
    for row in range(rows):
        filtered = apply_matrix(matrix_ref, [tile(columns, group * rows + row) for group in range(chunks)], sublane)
        terms = [tile(members_ref, row * chunks + group) * value for group, value in enumerate(filtered)]
        for pack in range(chunks // 2):
            lower, upper = terms[2 * pack], terms[2 * pack + 1]
            total = jnp.where(first_member, lower, upper)
            total = total + jnp.where(first_member, pltpu.roll(lower, TILE - HELD, 0), pltpu.roll(upper, HELD, 0))
            set_tile(partial_ref, row * (chunks // 2) + pack, total)


def lift_body(chunks, parts, *refs):
    part_refs, refs = refs[:parts], refs[parts:]
    innovation_ref, huber_ref, members_ref, transposed_ref = refs[:4]
    refs = refs[4:]
    chunk_refs, (weighted_ref, sorted_ref) = refs[:chunks], refs[chunks:]
    rows = chunk_refs[0].shape[0] // TILE
    lev_at = lax.axis_index("lev")
    sublane = places()
    first_member = sublane % FIELDS < HELD
    increment = part_refs[0][...]
    for part_ref in part_refs[1:]:
        increment = increment + part_ref[...]
    residual = increment - innovation_ref[...]
    scale = HUBER / jnp.maximum(jnp.abs(residual), HUBER)
    weighted_ref[...] = jnp.where(huber_ref[...] == 1.0, scale, 1.0) * residual
    for row in range(rows):
        adjoint = []
        for pack in range(chunks // 2):
            weighted = tile(weighted_ref, row * (chunks // 2) + pack)
            lower = jnp.where(first_member, weighted, pltpu.roll(weighted, HELD, 0))
            upper = jnp.where(first_member, pltpu.roll(weighted, TILE - HELD, 0), weighted)
            for value in (lower, upper):
                adjoint.append(value * tile(members_ref, row * chunks + len(adjoint)))
        for group, value in enumerate(apply_matrix(transposed_ref, adjoint, sublane)):
            set_tile(sorted_ref, group * rows + row, value)
    for step, chunk_ref in enumerate(reversed(chunk_refs)):
        chunk_ref[...] = sorted_ref[block(lax.bitwise_xor(lev_at, step) * rows, rows), :]


def gather_body(halos, chunks, *refs):
    chunk_refs, field_ref, send_refs, sorted_ref = refs[:chunks], refs[chunks], refs[chunks + 1 : -1], refs[-1]
    lev_at = lax.axis_index("lev")
    mirrored = is_mirrored(halos)
    rows = chunk_refs[0].shape[0] // TILE
    own = rows * chunks
    for step, chunk_ref in enumerate(reversed(chunk_refs)):
        sorted_ref[block(lax.bitwise_xor(lev_at, step) * rows, rows), :] = chunk_ref[...]
    for row in range(own):
        set_tile(field_ref, row, sorted_ref[block(pick(mirrored, own, row), 1), :])
    for row in range(PASSES):
        if halos == 1:
            set_tile(send_refs[0], row, tile(field_ref, own - 1 - row))
        else:
            set_tile(send_refs[0], row, tile(field_ref, row))
            set_tile(send_refs[1], row, tile(field_ref, own - PASSES + row))


def to_fields(planes_ref, fields_ref, rows):
    for field in range(FIELDS):
        member, level = divmod(field, HELD)
        for half, lanes in halves():
            fields_ref[member, level, :, lanes] = planes_ref[pl.ds(half * FIELDS + field, rows, stride=TILE), :]


def interior_body(halos, field_ref, control_ref, *refs):
    own_refs, (fields_out, saved_out, result_ref) = refs[:4], refs[4:]
    own = field_ref.shape[0] // TILE
    mirrored = is_mirrored(halos)
    done = interior_passes(halos, field_ref, own_refs, saved_out, halos == 1)
    for row in range(own):
        value = done[row] + tile(control_ref, row) if row in done else jnp.zeros((TILE, LANES), jnp.float32)
        result_ref[block(pick(mirrored, own, row), 1), :] = value
    to_fields(result_ref, fields_out, own)


def backward_body(halos, control_ref, fields_ref, saved_ref, *refs):
    halo_refs, refs = refs[:halos], refs[halos:]
    coefficient_refs, refs = (refs[:2], refs[2:]) if halos == 1 else (refs[:8], refs[8:])
    gradient_hbm, refs = refs[0], refs[1:]
    result_refs, edge_refs, semaphores = refs[:halos], refs[halos : 2 * halos], refs[-1]
    own = fields_ref.shape[2]
    mirrored = is_mirrored(halos)
    if halos == 1:
        spans = [(PASSES * mirrored.astype(jnp.int32), own - PASSES)]
        spans.append((jnp.where(mirrored, 0, own - PASSES), PASSES))
    else:
        spans = [(PASSES, own - 2 * PASSES), (own - PASSES, PASSES), (0, PASSES)]
    copies = []

    def send(source_ref, source_start, start, rows):
        copy = pltpu.make_async_copy(
            source_ref.at[:, :, pl.ds(source_start, rows), :],
            gradient_hbm.at[:, :, pl.ds(start, rows), :],
            semaphores.at[len(copies)],
        )
        copy.start()
        copies.append(copy)

    start = pl.multiple_of(spans[0][0], TILE)
    send(fields_ref, start, start, spans[0][1])
    halo_rows = [{own + row: tile(halo_refs[0], row) for row in range(PASSES)}]
    if halos == 1:
        done = double_wedge(halo_rows[0], own, saved_ref, coefficient_refs)
    else:
        halo_rows.append({row - PASSES: tile(halo_refs[1], row) for row in range(PASSES)})
        own_refs, tail_refs = coefficient_refs[:4], coefficient_refs[4:]
        coefficient = coefficient_reader(own_refs, tail_refs, own)
        top = top_coefficient(halos, own_refs)
        done = wedge_passes(halos, halo_rows, own, saved_ref, coefficient, top)
    for side in range(halos):
        for row in range(PASSES):
            value = done[own - PASSES + row] + tile(control_ref, own - PASSES + row) if side == 0 else done[row] + tile(control_ref, row)
            result_refs[side][block(pick(mirrored, PASSES, row), 1), :] = value
        to_fields(result_refs[side], edge_refs[side], PASSES)
        send(edge_refs[side], 0, pl.multiple_of(spans[1 + side][0], TILE), PASSES)
    for copy in copies:
        copy.wait()


def per_device(control, members, east_coef, south_coef, innovation, huber_class, band, level_group_index):
    count, held, own, lon = control.shape
    levels, cells = members.shape[1:]
    chunks, parts, row_count = (lax.axis_size(axis) for axis in ("lev", "mem", "row"))
    assert (count * held, held, lon) == (FIELDS, HELD, HALVES * LANES)
    part = own // chunks
    halos = 1 if row_count == 2 else 2
    tail = 1 + halos * PASSES
    terms = len(matrix_terms(chunks))
    packed = part * levels // FIELDS

    control_near, east_near, south_near, *edges = call(
        pack_body,
        [pltpu.VMEM(x.shape, x.dtype) for x in (control, east_coef, south_coef)] + [planes(3 * PASSES)] * halos,
        remote(control, east_coef, south_coef),
        [pltpu.SemaphoreType.DMA((FIELDS + 2 * HELD,))],
        specs=[HBM] * 3,
    )
    halo = swap_edges(edges, "row")
    kept = halos * PASSES * 2
    near, far = ([planes(len(rows) * POINTS)] if halos == 1 else [] for rows in composed_rows(own))
    prepared = call(
        functools.partial(prepare_body, halos),
        [planes(own)] * 3 + [planes(own + 1), planes(own), planes(kept), planes(own)] + near,
        resident(control_near, east_near, south_near),
        [planes(own)] * 2,
    )
    own_stencil, (done_rows, saved, control_planes), composed = prepared[:4], prepared[4:7], prepared[7:]
    members_planes, innovation_planes, huber_planes, matrix, transposed = call(
        columns_body,
        [planes(part * chunks), planes(packed), planes(packed), planes(terms), planes(terms)],
        [members, innovation, huber_class, band, level_group_index],
        [planes(part * chunks)],
        specs=[VMEM, VMEM, VMEM, SMEM, SMEM],
    )
    tail_planes = [planes(tail)] * 4
    first_outs = far or tail_planes
    results = call(
        functools.partial(forward_body, halos),
        first_outs + [planes(part)] * chunks,
        resident(done_rows, saved, *own_stencil, *halo, *composed),
        [planes(own)] + (tail_planes if halos == 1 else []),
    )
    last_coefs = [*composed, *results[:1]] if halos == 1 else [*own_stencil, *results[:4]]
    smoothed = results[len(first_outs) :]
    columns = exchange(smoothed[::-1], "lev")
    (partial,) = call(
        functools.partial(filter_body, chunks),
        [planes(packed)],
        resident(*columns[::-1], members_planes, matrix),
        [planes(part * chunks)],
    )
    partials = collect(partial, "mem")
    lifted = call(
        functools.partial(lift_body, chunks, parts),
        [planes(part)] * chunks,
        resident(*partials, innovation_planes, huber_planes, members_planes, transposed),
        [planes(packed), planes(part * chunks)],
    )
    returned = exchange(lifted[::-1], "lev")
    gathered, *edges = call(
        functools.partial(gather_body, halos, chunks),
        [planes(own)] + [planes(PASSES)] * halos,
        resident(*returned[::-1]),
        [planes(own)],
    )
    halo = swap_edges(edges, "row")
    early, saved = call(
        functools.partial(interior_body, halos),
        [pltpu.VMEM(control.shape, jnp.float32), planes(kept)],
        resident(gathered, control_planes, *own_stencil),
        [planes(own)],
    )
    (gradient,) = call(
        functools.partial(backward_body, halos),
        [jax.ShapeDtypeStruct(control.shape, jnp.float32)],
        resident(control_planes, early, saved, *halo, *last_coefs),
        [planes(PASSES)] * halos
        + [pltpu.VMEM((count, held, PASSES, lon), jnp.float32)] * halos
        + [pltpu.SemaphoreType.DMA((1 + halos,))],
        out_specs=[HBM],
    )
    return gradient


def solution(mesh):
    placed = (
        P("mem", "lev", "row", None),
        P("mem", None, ("row", "lev")),
        P("lev", "row", None),
        P("lev", "row", None),
        P(None, ("row", "lev")),
        P(None, ("row", "lev")),
        P(),
        P(),
    )
    return jax.shard_map(
        per_device,
        mesh=mesh,
        in_specs=placed,
        out_specs=P("mem", "lev", "row", None),
        check_vma=False,
    )
```

```python
import functools

import jax
import jax.numpy as jnp
from jax import lax
from jax.experimental import pallas as pl
from jax.experimental.pallas import tpu as pltpu
from jax.sharding import PartitionSpec as P

PASSES = 8
HUBER = 1.0
REACH = 3
POINTS = 13
LANES = 128
TILE = 8
HALVES = 2
HELD = 2
FIELDS = 4

VMEM = pl.BlockSpec(memory_space=pltpu.VMEM)
SMEM = pl.BlockSpec(memory_space=pltpu.SMEM)
HBM = pl.BlockSpec(memory_space=pltpu.HBM)


def planes(count):
    return pltpu.VMEM((count * TILE, LANES), jnp.float32)


def call(body, outs, operands, scratch=(), specs=None, out_specs=None, flops=0):
    total = sum(op.size * op.dtype.itemsize for op in operands)
    return pl.pallas_call(
        body,
        out_shape=outs,
        in_specs=specs or [VMEM] * len(operands),
        out_specs=out_specs or [VMEM] * len(outs),
        scratch_shapes=list(scratch),
        compiler_params=pltpu.CompilerParams(vmem_limit_bytes=32 * 1024 * 1024),
        cost_estimate=pl.CostEstimate(flops=flops, bytes_accessed=2 * total, transcendentals=0),
    )(*operands)


def resident(*arrays):
    return [pltpu.with_memory_space_constraint(array, pltpu.VMEM) for array in arrays]


def remote(*arrays):
    return [pltpu.with_memory_space_constraint(array, pltpu.HBM) for array in arrays]


def exchange(chunks, axis):
    count = len(chunks)
    received = list(chunks)
    for step in reversed(range(1, count)):
        received[step] = lax.ppermute(chunks[step], axis, [(i, i ^ step) for i in range(count)])
    return received


def collect(array, axis):
    count, rows = lax.axis_size(axis), lax.axis_size("row")
    ring = [i ^ (i >> 1) for i in range(count)]
    received = [array]
    for step in range(1, count):
        pairs = []
        for place, index in enumerate(ring):
            for row in range(rows):
                target = index ^ (count - step) if row % 2 else ring[(place + step) % count]
                pairs.append((index * rows + row, target * rows + row))
        received.append(lax.ppermute(array, (axis, "row"), pairs))
    return received


def swap_edges(edges, axis):
    count = lax.axis_size(axis)
    if len(edges) == 1:
        return [lax.ppermute(edges[0], axis, [(0, 1), (1, 0)])]
    head, tail = edges
    south = lax.ppermute(head, axis, [(i + 1, i) for i in range(count - 1)])
    north = lax.ppermute(tail, axis, [(i, i + 1) for i in range(count - 1)])
    return [south, north]


def tile(ref, row):
    return ref[row * TILE : (row + 1) * TILE, :]


def set_tile(ref, row, value):
    ref[row * TILE : (row + 1) * TILE, :] = value


def block(first_row, rows):
    return pl.ds(pl.multiple_of(first_row * TILE, TILE), rows * TILE)


def spread(ref, row, sublane, values):
    ref[pl.ds(row * TILE + sublane, values.shape[0], stride=TILE), :] = values


def places():
    return lax.broadcasted_iota(jnp.int32, (TILE, LANES), 0)


def east_west(value):
    lane = lax.broadcasted_iota(jnp.int32, (TILE, LANES), 1)
    other = pltpu.roll(value, FIELDS, 0)
    east = pltpu.roll(jnp.where(lane == 0, other, value), LANES - 1, 1)
    west = pltpu.roll(jnp.where(lane == LANES - 1, other, value), 1, 1)
    return east, west


def west_of(value):
    lane = lax.broadcasted_iota(jnp.int32, (TILE, LANES), 1)
    return pltpu.roll(jnp.where(lane == LANES - 1, pltpu.roll(value, FIELDS, 0), value), 1, 1)


def halves():
    return [(half, slice(half * LANES, (half + 1) * LANES)) for half in range(HALVES)]


def pack_body(control_hbm, east_hbm, south_hbm, control_ref, east_ref, south_ref, *refs):
    send_refs, semaphores = refs[:-1], refs[-1]
    pieces = [(east_hbm.at[level], east_ref.at[level]) for level in range(HELD)]
    pieces += [(south_hbm.at[level], south_ref.at[level]) for level in range(HELD)]
    for field in range(FIELDS):
        member, level = divmod(field, HELD)
        pieces.append((control_hbm.at[member, level], control_ref.at[member, level]))
    copies = [
        pltpu.make_async_copy(source, target, semaphores.at[index]) for index, (source, target) in enumerate(pieces)
    ]
    for copy in copies:
        copy.start()
    for copy in copies:
        copy.wait()
    own = control_ref.shape[2]
    first = lax.axis_index("row") == 0

    def edges(load):
        head = load(slice(0, 2 * PASSES))[:PASSES].astype(jnp.float32)
        tail = load(slice(own - 2 * PASSES, own))[PASSES:].astype(jnp.float32)
        return [jnp.where(first, tail, head)] if len(send_refs) == 1 else [head, tail]

    for half, lanes in halves():
        for field in range(FIELDS):
            member, level = divmod(field, HELD)
            at = half * FIELDS + field
            values = edges(lambda rows: control_ref[member, level, rows, lanes])
            for send_ref, value in zip(send_refs, values):
                spread(send_ref, 0, at, value)
            for kind, coef_ref in enumerate((east_ref, south_ref)):
                values = edges(lambda rows: coef_ref[level, rows, lanes])
                for send_ref, value in zip(send_refs, values):
                    spread(send_ref, (kind + 1) * PASSES, at, value)


def is_mirrored(halos):
    return halos == 1 and lax.axis_index("row") == 1


def pick(mirrored, count, row):
    return row if mirrored is False else jnp.where(mirrored, count - 1 - row, row)


def stencil(values, row, center, east, west, above, below):
    to_east, to_west = east_west(values[row])
    total = center * values[row] + below * values[row + 1]
    if above is not None:
        total = total + above * values[row - 1]
    return total + (east * to_east + west * to_west)


def interior_passes(halos, field_ref, own_refs, saved_ref, double=False):
    center_ref, east_ref, west_ref, face_ref = own_refs
    own = field_ref.shape[0] // TILE
    values = {row: tile(field_ref, row) for row in range(own)}
    for step in range(1, PASSES + 1):
        for side in range(halos):
            kept = (own - 1 - step, own - step) if side == 0 else (step - 1, step)
            if double:
                kept = range(own - 3 - step, own + 1 - step) if step % 2 else ()
            for index, row in enumerate(kept):
                set_tile(saved_ref, (side * PASSES + step - 1) * 2 + index, values[row])
        after = {}
        for row in range(step if halos == 2 else 0, own - step):
            after[row] = stencil(
                values,
                row,
                tile(center_ref, row),
                tile(east_ref, row),
                tile(west_ref, row),
                tile(face_ref, row) if row else None,
                tile(face_ref, row + 1),
            )
        values = after
    return values


def wedge_passes(halos, halo_rows, own, saved_ref, coefficient, top):
    done = {}
    for side in range(halos):
        values = dict(halo_rows[side])
        for step in range(1, PASSES + 1):
            kept = (own - 1 - step, own - step) if side == 0 else (step - 1, step)
            for index, row in enumerate(kept):
                values[row] = tile(saved_ref, (side * PASSES + step - 1) * 2 + index)
            after = {}
            for row in range(own - step, own + PASSES - step) if side == 0 else range(step - PASSES, step):
                center, east, west, above = (coefficient(kind, row) for kind in range(4))
                after[row] = stencil(values, row, center, east, west, top if row == 0 else above, coefficient(3, row + 1))
            values = after
        done.update(values)
    return done


def shifted(value, distance):
    lane = lax.broadcasted_iota(jnp.int32, (TILE, LANES), 1)
    other = pltpu.roll(value, FIELDS, 0)
    east = pltpu.roll(jnp.where(lane < distance, other, value), LANES - distance, 1)
    west = pltpu.roll(jnp.where(lane >= LANES - distance, other, value), distance, 1)
    return east, west


def compose(coefficient, rows, composed_out):
    for index, row in enumerate(rows):
        center, east, west, above = (coefficient(kind, row) for kind in range(4))
        below = coefficient(3, row + 1)
        (center_e, center_w), (east_e, east_w), (west_e, west_w), (below_e, below_w), (above_e, above_w) = (
            shifted(value, 1) for value in (center, east, west, below, above)
        )
        tiles = (
            center * center + east * west_e + west * east_w + below * below + above * above,
            east * (center + center_e),
            west * (center + center_w),
            east * east_e,
            west * west_w,
            below * (center + coefficient(0, row + 1)),
            east * below_e + below * coefficient(1, row + 1),
            west * below_w + below * coefficient(2, row + 1),
            above * (center + coefficient(0, row - 1)),
            east * above_e + above * coefficient(1, row - 1),
            west * above_w + above * coefficient(2, row - 1),
            below * coefficient(3, row + 2),
            above * coefficient(3, row - 1),
        )
        for place, value in enumerate(tiles):
            set_tile(composed_out, index * POINTS + place, value)


def composed_rows(own):
    return range(own - PASSES, own - 2), range(own - 2, own + PASSES - 2)


def double_wedge(values, own, saved_ref, composed_refs):
    for step in range(1, PASSES // 2 + 1):
        first = own - 2 * step
        for index in range(4):
            values[first - 2 + index] = tile(saved_ref, (step - 1) * 4 + index)
        near = {row: shifted(values[row], 1) for row in range(first - 1, first + PASSES + 1)}
        after = {}
        for row in range(first, first + PASSES):
            def coefficient(place):
                part = int(row >= own - 2)
                return tile(composed_refs[part], (row - composed_rows(own)[part][0]) * POINTS + place)

            east, west = shifted(values[row], 2)
            total = coefficient(0) * values[row] + coefficient(5) * values[row + 1]
            total = total + (coefficient(8) * values[row - 1] + coefficient(11) * values[row + 2])
            total = total + coefficient(12) * values[row - 2]
            sides = coefficient(1) * near[row][0] + coefficient(2) * near[row][1]
            lower = coefficient(6) * near[row + 1][0] + coefficient(7) * near[row + 1][1]
            upper = coefficient(9) * near[row - 1][0] + coefficient(10) * near[row - 1][1]
            far = coefficient(3) * east + coefficient(4) * west
            after[row] = (total + sides) + ((lower + upper) + far)
        values = after
    return values


def prepare_body(halos, control_ref, east_ref, south_ref, *refs):
    own_refs, (rows_out, saved_out, field_ref), refs = refs[:4], refs[4:7], refs[7:]
    raw_east, raw_face = refs[-2:]
    center_out, east_out, west_out, face_out = own_refs
    own = control_ref.shape[2]
    mirrored = is_mirrored(halos)
    for half, lanes in halves():
        for field in range(FIELDS):
            member, level = divmod(field, HELD)
            at = half * FIELDS + field
            spread(rows_out, 0, at, control_ref[member, level, :, lanes].astype(jnp.float32))
            spread(raw_east, 0, at, east_ref[level, :, lanes])
            spread(raw_face, 0, at, south_ref[level, :, lanes])
    for row in range(own):
        source = pick(mirrored, own, row)
        set_tile(field_ref, row, rows_out[block(source, 1), :])
        east = raw_east[block(source, 1), :]
        set_tile(east_out, row, east)
        set_tile(west_out, row, west_of(east))
        if row == 0:
            face = tile(raw_face, 0)
            face = face if mirrored is False else jnp.where(mirrored, 0.0, face)
        else:
            face = raw_face[block(row if mirrored is False else jnp.where(mirrored, own - row, row), 1), :]
        set_tile(face_out, row, face)
    set_tile(face_out, own, tile(raw_face, 0))
    for row in range(own - 1):
        total = 1.0 - tile(east_out, row) - tile(west_out, row)
        set_tile(center_out, row, total - tile(face_out, row + 1) - tile(face_out, row))
    for row, value in interior_passes(halos, field_ref, own_refs, saved_out, halos == 1).items():
        set_tile(rows_out, row, value)
    if halos == 1:
        compose(lambda kind, row: tile(own_refs[kind], row), composed_rows(own)[0], refs[0])


def finish_coefficients(halos, halo_refs, own_refs, tail_refs, own):
    _, east_own, west_own, face_own = own_refs
    center_tail, east_tail, west_tail, face_tail = tail_refs
    mirrored = is_mirrored(halos)

    def halo_tile(side, kind, row):
        return halo_refs[side][block(kind * PASSES + row, 1), :]

    set_tile(east_tail, 0, tile(east_own, own - 1))
    set_tile(west_tail, 0, tile(west_own, own - 1))
    set_tile(face_tail, 0, tile(face_own, own - 1))
    for row in range(PASSES):
        east = halo_tile(0, 1, pick(mirrored, PASSES, row))
        set_tile(east_tail, 1 + row, east)
        set_tile(west_tail, 1 + row, west_of(east))
        if mirrored is False:
            face = halo_tile(0, 2, row)
        elif row == 0:
            face = jnp.where(mirrored, tile(face_own, own), halo_tile(0, 2, 0))
        else:
            face = halo_tile(0, 2, jnp.where(mirrored, PASSES - row, row))
        set_tile(face_tail, 1 + row, face)
    for row in range(PASSES):
        total = 1.0 - tile(east_tail, row) - tile(west_tail, row)
        set_tile(center_tail, row, total - tile(face_tail, row + 1) - tile(face_tail, row))
    if halos == 2:
        for row in range(PASSES):
            at = 1 + PASSES + row
            east, face = halo_tile(1, 1, row), halo_tile(1, 2, row)
            below = halo_tile(1, 2, row + 1) if row + 1 < PASSES else tile(face_own, 0)
            west = west_of(east)
            for ref, value in zip(tail_refs, (1.0 - east - west - below - face, east, west, face)):
                set_tile(ref, at, value)


def coefficient_reader(own_refs, tail_refs, own):
    def coefficient(kind, row):
        if row < 0:
            return tile(tail_refs[kind], 1 + 2 * PASSES + row)
        return tile(own_refs[kind], row) if row < own - 1 else tile(tail_refs[kind], row - own + 1)

    return coefficient


def top_coefficient(halos, own_refs):
    return None if halos == 1 else jnp.where(lax.axis_index("row") == 0, 0.0, tile(own_refs[3], 0))


def forward_body(halos, rows_ref, saved_ref, *refs):
    own_refs, halo_refs, refs = refs[:4], refs[4 : 4 + halos], refs[4 + halos :]
    if halos == 1:
        composed_own, composed_tail, refs, tail_refs = refs[0], refs[1], refs[2:-4], refs[-4:]
    else:
        tail_refs, refs = refs[:4], refs[4:]
    chunk_refs, sorted_ref = refs[:-1], refs[-1]
    own = rows_ref.shape[0] // TILE
    lev_at = lax.axis_index("lev")
    mirrored = is_mirrored(halos)
    finish_coefficients(halos, halo_refs, own_refs, tail_refs, own)
    halo_rows = [{own + row: halo_refs[0][block(pick(mirrored, PASSES, row), 1), :] for row in range(PASSES)}]
    coefficient = coefficient_reader(own_refs, tail_refs, own)
    if halos == 1:
        compose(coefficient, composed_rows(own)[1], composed_tail)
        done = double_wedge(halo_rows[0], own, saved_ref, (composed_own, composed_tail))
    else:
        halo_rows.append({row - PASSES: tile(halo_refs[1], row) for row in range(PASSES)})
        top = top_coefficient(halos, own_refs)
        done = wedge_passes(halos, halo_rows, own, saved_ref, coefficient, top)
    for row in range(own):
        value = done[row] if row in done else tile(rows_ref, row)
        sorted_ref[block(pick(mirrored, own, row), 1), :] = value
    part = own // len(chunk_refs)
    for step, chunk_ref in enumerate(reversed(chunk_refs)):
        chunk_ref[...] = sorted_ref[block(lax.bitwise_xor(lev_at, step) * part, part), :]


def matrix_terms(groups):
    return [
        (group, other, cross)
        for group in range(groups)
        for other in range(max(0, group - 2), min(groups, group + 3))
        for cross in range(2)
        if abs(group - other) < 2 or cross
    ]


def swap_levels(value, sublane):
    return jnp.where(sublane % HELD == 0, pltpu.roll(value, TILE - 1, 0), pltpu.roll(value, 1, 0))


def columns_body(members_ref, innovation_ref, huber_ref, band_ref, group_ref, *refs):
    members_out, innovation_out, huber_out, matrix_out, transposed_out, levels_ref = refs
    count, levels, cells = members_ref.shape
    groups, lon = levels // HELD, HALVES * LANES
    rows, packed = cells // lon, levels // FIELDS
    sublane = places()
    for member in range(count):
        for row in range(rows):
            for half in range(HALVES):
                lanes = slice(row * lon + half * LANES, row * lon + (half + 1) * LANES)
                start = ((member * rows + row) * HALVES + half) * levels
                levels_ref[start : start + levels, :] = members_ref[member, :, lanes].astype(jnp.float32)
                for level in range(HELD):
                    at = half * FIELDS + member * HELD + level
                    spread(members_out, row * groups, at, levels_ref[pl.ds(start + level, groups, stride=HELD), :])
    for row in range(rows):
        for half in range(HALVES):
            lanes = slice(row * lon + half * LANES, row * lon + (half + 1) * LANES)
            for pack in range(packed):
                source = slice(pack * FIELDS, (pack + 1) * FIELDS)
                start = (row * packed + pack) * TILE + half * FIELDS
                innovation_out[start : start + FIELDS, :] = innovation_ref[source, lanes]
                huber_out[start : start + FIELDS, :] = huber_ref[source, lanes].astype(jnp.float32)

    def entry(level, other):
        offset = other - level + REACH
        if not 0 <= offset < 2 * REACH + 1:
            return jnp.float32(0.0)
        value = band_ref[offset, level] + jnp.float32(1.0 if offset == REACH else 0.0)
        return jnp.where(group_ref[level] == group_ref[other], value, jnp.float32(0.0))

    for slot, (group, other, cross) in enumerate(matrix_terms(groups)):
        pairs = [(group * HELD + level, other * HELD + (level ^ cross)) for level in range(HELD)]
        even, odd = (entry(a, b) for a, b in pairs)
        set_tile(matrix_out, slot, jnp.where(sublane % HELD == 0, even, odd))
        even, odd = (entry(b, a) for a, b in pairs)
        set_tile(transposed_out, slot, jnp.where(sublane % HELD == 0, even, odd))


def apply_matrix(matrix_ref, values, sublane):
    crossed = [swap_levels(value, sublane) for value in values]
    totals = [None] * len(values)
    for slot, (group, other, cross) in enumerate(matrix_terms(len(values))):
        term = tile(matrix_ref, slot) * (crossed if cross else values)[other]
        totals[group] = term if totals[group] is None else totals[group] + term
    return totals


def filter_body(chunks, *refs):
    chunk_refs = refs[:chunks]
    members_ref, matrix_ref, partial_ref, columns = refs[chunks:]
    rows = chunk_refs[0].shape[0] // TILE
    lev_at = lax.axis_index("lev")
    sublane = places()
    first_member = sublane % FIELDS < HELD
    for step, chunk_ref in enumerate(reversed(chunk_refs)):
        columns[block(lax.bitwise_xor(lev_at, step) * rows, rows), :] = chunk_ref[...]
    for row in range(rows):
        filtered = apply_matrix(matrix_ref, [tile(columns, group * rows + row) for group in range(chunks)], sublane)
        terms = [tile(members_ref, row * chunks + group) * value for group, value in enumerate(filtered)]
        for pack in range(chunks // 2):
            lower, upper = terms[2 * pack], terms[2 * pack + 1]
            total = jnp.where(first_member, lower, upper)
            total = total + jnp.where(first_member, pltpu.roll(lower, TILE - HELD, 0), pltpu.roll(upper, HELD, 0))
            set_tile(partial_ref, row * (chunks // 2) + pack, total)


def lift_body(chunks, parts, *refs):
    part_refs, refs = refs[:parts], refs[parts:]
    innovation_ref, huber_ref, members_ref, transposed_ref = refs[:4]
    refs = refs[4:]
    chunk_refs, (weighted_ref, sorted_ref) = refs[:chunks], refs[chunks:]
    rows = chunk_refs[0].shape[0] // TILE
    lev_at = lax.axis_index("lev")
    sublane = places()
    first_member = sublane % FIELDS < HELD
    increment = part_refs[0][...]
    for part_ref in part_refs[1:]:
        increment = increment + part_ref[...]
    residual = increment - innovation_ref[...]
    scale = HUBER / jnp.maximum(jnp.abs(residual), HUBER)
    weighted_ref[...] = jnp.where(huber_ref[...] == 1.0, scale, 1.0) * residual
    for row in range(rows):
        adjoint = []
        for pack in range(chunks // 2):
            weighted = tile(weighted_ref, row * (chunks // 2) + pack)
            lower = jnp.where(first_member, weighted, pltpu.roll(weighted, HELD, 0))
            upper = jnp.where(first_member, pltpu.roll(weighted, TILE - HELD, 0), weighted)
            for value in (lower, upper):
                adjoint.append(value * tile(members_ref, row * chunks + len(adjoint)))
        for group, value in enumerate(apply_matrix(transposed_ref, adjoint, sublane)):
            set_tile(sorted_ref, group * rows + row, value)
    for step, chunk_ref in enumerate(reversed(chunk_refs)):
        chunk_ref[...] = sorted_ref[block(lax.bitwise_xor(lev_at, step) * rows, rows), :]


def gather_body(halos, chunks, *refs):
    chunk_refs, field_ref, send_refs, sorted_ref = refs[:chunks], refs[chunks], refs[chunks + 1 : -1], refs[-1]
    lev_at = lax.axis_index("lev")
    mirrored = is_mirrored(halos)
    rows = chunk_refs[0].shape[0] // TILE
    own = rows * chunks
    for step, chunk_ref in enumerate(reversed(chunk_refs)):
        sorted_ref[block(lax.bitwise_xor(lev_at, step) * rows, rows), :] = chunk_ref[...]
    for row in range(own):
        set_tile(field_ref, row, sorted_ref[block(pick(mirrored, own, row), 1), :])
    for row in range(PASSES):
        if halos == 1:
            set_tile(send_refs[0], row, tile(field_ref, own - 1 - row))
        else:
            set_tile(send_refs[0], row, tile(field_ref, row))
            set_tile(send_refs[1], row, tile(field_ref, own - PASSES + row))


def to_fields(planes_ref, fields_ref, rows):
    for field in range(FIELDS):
        member, level = divmod(field, HELD)
        for half, lanes in halves():
            fields_ref[member, level, :, lanes] = planes_ref[pl.ds(half * FIELDS + field, rows, stride=TILE), :]


def interior_body(halos, field_ref, control_ref, *refs):
    own_refs, (fields_out, saved_out, result_ref) = refs[:4], refs[4:]
    own = field_ref.shape[0] // TILE
    mirrored = is_mirrored(halos)
    done = interior_passes(halos, field_ref, own_refs, saved_out, halos == 1)
    for row in range(own):
        value = done[row] + tile(control_ref, row) if row in done else jnp.zeros((TILE, LANES), jnp.float32)
        result_ref[block(pick(mirrored, own, row), 1), :] = value
    to_fields(result_ref, fields_out, own)


def backward_body(halos, control_ref, fields_ref, saved_ref, *refs):
    halo_refs, refs = refs[:halos], refs[halos:]
    coefficient_refs, refs = (refs[:2], refs[2:]) if halos == 1 else (refs[:8], refs[8:])
    gradient_hbm, refs = refs[0], refs[1:]
    result_refs, edge_refs, semaphores = refs[:halos], refs[halos : 2 * halos], refs[-1]
    own = fields_ref.shape[2]
    mirrored = is_mirrored(halos)
    if halos == 1:
        spans = [(PASSES * mirrored.astype(jnp.int32), own - PASSES)]
        spans.append((jnp.where(mirrored, 0, own - PASSES), PASSES))
    else:
        spans = [(PASSES, own - 2 * PASSES), (own - PASSES, PASSES), (0, PASSES)]
    copies = []

    def send(source_ref, source_start, start, rows):
        copy = pltpu.make_async_copy(
            source_ref.at[:, :, pl.ds(source_start, rows), :],
            gradient_hbm.at[:, :, pl.ds(start, rows), :],
            semaphores.at[len(copies)],
        )
        copy.start()
        copies.append(copy)

    start = pl.multiple_of(spans[0][0], TILE)
    send(fields_ref, start, start, spans[0][1])
    halo_rows = [{own + row: tile(halo_refs[0], row) for row in range(PASSES)}]
    if halos == 1:
        done = double_wedge(halo_rows[0], own, saved_ref, coefficient_refs)
    else:
        halo_rows.append({row - PASSES: tile(halo_refs[1], row) for row in range(PASSES)})
        own_refs, tail_refs = coefficient_refs[:4], coefficient_refs[4:]
        coefficient = coefficient_reader(own_refs, tail_refs, own)
        top = top_coefficient(halos, own_refs)
        done = wedge_passes(halos, halo_rows, own, saved_ref, coefficient, top)
    for side in range(halos):
        for row in range(PASSES):
            value = done[own - PASSES + row] + tile(control_ref, own - PASSES + row) if side == 0 else done[row] + tile(control_ref, row)
            result_refs[side][block(pick(mirrored, PASSES, row), 1), :] = value
        to_fields(result_refs[side], edge_refs[side], PASSES)
        send(edge_refs[side], 0, pl.multiple_of(spans[1 + side][0], TILE), PASSES)
    for copy in copies:
        copy.wait()


def per_device(control, members, east_coef, south_coef, innovation, huber_class, band, level_group_index):
    count, held, own, lon = control.shape
    levels, cells = members.shape[1:]
    chunks, parts, row_count = (lax.axis_size(axis) for axis in ("lev", "mem", "row"))
    assert (count * held, held, lon) == (FIELDS, HELD, HALVES * LANES)
    part = own // chunks
    halos = 1 if row_count == 2 else 2
    tail = 1 + halos * PASSES
    terms = len(matrix_terms(chunks))
    packed = part * levels // FIELDS

    control_near, east_near, south_near, *edges = call(
        pack_body,
        [pltpu.VMEM(x.shape, x.dtype) for x in (control, east_coef, south_coef)] + [planes(3 * PASSES)] * halos,
        remote(control, east_coef, south_coef),
        [pltpu.SemaphoreType.DMA((FIELDS + 2 * HELD,))],
        specs=[HBM] * 3,
    )
    halo = swap_edges(edges, "row")
    kept = halos * PASSES * 2
    near, far = ([planes(len(rows) * POINTS)] if halos == 1 else [] for rows in composed_rows(own))
    prepared = call(
        functools.partial(prepare_body, halos),
        [planes(own)] * 3 + [planes(own + 1), planes(own), planes(kept), planes(own)] + near,
        resident(control_near, east_near, south_near),
        [planes(own)] * 2,
    )
    own_stencil, (done_rows, saved, control_planes), composed = prepared[:4], prepared[4:7], prepared[7:]
    members_planes, innovation_planes, huber_planes, matrix, transposed = call(
        columns_body,
        [planes(part * chunks), planes(packed), planes(packed), planes(terms), planes(terms)],
        [members, innovation, huber_class, band, level_group_index],
        [planes(part * chunks)],
        specs=[VMEM, VMEM, VMEM, SMEM, SMEM],
    )
    tail_planes = [planes(tail)] * 4
    first_outs = far or tail_planes
    results = call(
        functools.partial(forward_body, halos),
        first_outs + [planes(part)] * chunks,
        resident(done_rows, saved, *own_stencil, *halo, *composed),
        [planes(own)] + (tail_planes if halos == 1 else []),
    )
    last_coefs = [*composed, *results[:1]] if halos == 1 else [*own_stencil, *results[:4]]
    smoothed = results[len(first_outs) :]
    columns = exchange(smoothed[::-1], "lev")
    (partial,) = call(
        functools.partial(filter_body, chunks),
        [planes(packed)],
        resident(*columns[::-1], members_planes, matrix),
        [planes(part * chunks)],
    )
    partials = collect(partial, "mem")
    lifted = call(
        functools.partial(lift_body, chunks, parts),
        [planes(part)] * chunks,
        resident(*partials, innovation_planes, huber_planes, members_planes, transposed),
        [planes(packed), planes(part * chunks)],
    )
    returned = exchange(lifted[::-1], "lev")
    gathered, *edges = call(
        functools.partial(gather_body, halos, chunks),
        [planes(own)] + [planes(PASSES)] * halos,
        resident(*returned[::-1]),
        [planes(own)],
    )
    halo = swap_edges(edges, "row")
    early, saved = call(
        functools.partial(interior_body, halos),
        [pltpu.VMEM(control.shape, jnp.float32), planes(kept)],
        resident(gathered, control_planes, *own_stencil),
        [planes(own)],
    )
    (gradient,) = call(
        functools.partial(backward_body, halos),
        [jax.ShapeDtypeStruct(control.shape, jnp.float32)],
        resident(control_planes, early, saved, *halo, *last_coefs),
        [planes(PASSES)] * halos
        + [pltpu.VMEM((count, held, PASSES, lon), jnp.float32)] * halos
        + [pltpu.SemaphoreType.DMA((1 + halos,))],
        out_specs=[HBM],
    )
    return gradient


def solution(mesh):
    placed = (
        P("mem", "lev", "row", None),
        P("mem", None, ("row", "lev")),
        P("lev", "row", None),
        P("lev", "row", None),
        P(None, ("row", "lev")),
        P(None, ("row", "lev")),
        P(),
        P(),
    )
    return jax.shard_map(
        per_device,
        mesh=mesh,
        in_specs=placed,
        out_specs=P("mem", "lev", "row", None),
        check_vma=False,
    )
```

```python
import functools

import jax
import jax.numpy as jnp
from jax import lax
from jax.experimental import pallas as pl
from jax.experimental.pallas import tpu as pltpu
from jax.sharding import PartitionSpec as P

PASSES = 8
HUBER = 1.0
REACH = 3
POINTS = 13
LANES = 128
TILE = 8
HALVES = 2
HELD = 2
FIELDS = 4

VMEM = pl.BlockSpec(memory_space=pltpu.VMEM)
SMEM = pl.BlockSpec(memory_space=pltpu.SMEM)
HBM = pl.BlockSpec(memory_space=pltpu.HBM)


def planes(count):
    return pltpu.VMEM((count * TILE, LANES), jnp.float32)


def call(body, outs, operands, scratch=(), specs=None, out_specs=None, flops=0, aliases=None):
    total = sum(op.size * op.dtype.itemsize for op in operands)
    return pl.pallas_call(
        body,
        out_shape=outs,
        in_specs=specs or [VMEM] * len(operands),
        out_specs=out_specs or [VMEM] * len(outs),
        scratch_shapes=list(scratch),
        input_output_aliases=aliases or {},
        compiler_params=pltpu.CompilerParams(vmem_limit_bytes=32 * 1024 * 1024),
        cost_estimate=pl.CostEstimate(flops=flops, bytes_accessed=2 * total, transcendentals=0),
    )(*operands)


def resident(*arrays):
    return [pltpu.with_memory_space_constraint(array, pltpu.VMEM) for array in arrays]


def remote(*arrays):
    return [pltpu.with_memory_space_constraint(array, pltpu.HBM) for array in arrays]


def exchange(chunks, axis, crossed):
    count = len(chunks)
    received = list(chunks)
    for step in reversed(range(count)):
        if crossed:
            pairs = [(2 * i + row, 2 * (i ^ step) + 1 - row) for i in range(count) for row in range(2)]
            received[step] = lax.ppermute(chunks[step], (axis, "row"), pairs)
        elif step:
            received[step] = lax.ppermute(chunks[step], axis, [(i, i ^ step) for i in range(count)])
    return received


def collect(array, axis):
    count = lax.axis_size(axis)
    shifts = [[(i, (i + step) % count) for i in range(count)] for step in range(1, count)]
    return [array] + [lax.ppermute(array, axis, shift) for shift in shifts]


def swap_edges(edges, axis):
    count = lax.axis_size(axis)
    if len(edges) == 1:
        return [lax.ppermute(edges[0], axis, [(0, 1), (1, 0)])]
    head, tail = edges
    south = lax.ppermute(head, axis, [(i + 1, i) for i in range(count - 1)])
    north = lax.ppermute(tail, axis, [(i, i + 1) for i in range(count - 1)])
    return [south, north]


def tile(ref, row):
    return ref[row * TILE : (row + 1) * TILE, :]


def set_tile(ref, row, value):
    ref[row * TILE : (row + 1) * TILE, :] = value


def block(first_row, rows):
    return pl.ds(pl.multiple_of(first_row * TILE, TILE), rows * TILE)


def spread(ref, row, sublane, values):
    ref[pl.ds(row * TILE + sublane, values.shape[0], stride=TILE), :] = values


def places():
    return lax.broadcasted_iota(jnp.int32, (TILE, LANES), 0)


def east_west(value):
    lane = lax.broadcasted_iota(jnp.int32, (TILE, LANES), 1)
    other = pltpu.roll(value, FIELDS, 0)
    east = pltpu.roll(jnp.where(lane == 0, other, value), LANES - 1, 1)
    west = pltpu.roll(jnp.where(lane == LANES - 1, other, value), 1, 1)
    return east, west


def west_of(value):
    lane = lax.broadcasted_iota(jnp.int32, (TILE, LANES), 1)
    return pltpu.roll(jnp.where(lane == LANES - 1, pltpu.roll(value, FIELDS, 0), value), 1, 1)


def halves():
    return [(half, slice(half * LANES, (half + 1) * LANES)) for half in range(HALVES)]


def pack_body(control_hbm, east_hbm, south_hbm, *refs):
    column_hbms, (control_ref, east_ref, south_ref), column_refs = refs[:3], refs[3:6], refs[6:9]
    send_refs, semaphores = refs[9:-1], refs[-1]
    pieces = [(east_hbm.at[level], east_ref.at[level]) for level in range(HELD)]
    pieces += [(south_hbm.at[level], south_ref.at[level]) for level in range(HELD)]
    pieces += list(zip(column_hbms, column_refs))
    for field in range(FIELDS):
        member, level = divmod(field, HELD)
        pieces.append((control_hbm.at[member, level], control_ref.at[member, level]))
    copies = [
        pltpu.make_async_copy(source, target, semaphores.at[index]) for index, (source, target) in enumerate(pieces)
    ]
    for copy in copies:
        copy.start()
    for copy in copies:
        copy.wait()
    own = control_ref.shape[2]
    first = lax.axis_index("row") == 0

    def edges(load):
        head = load(slice(0, 2 * PASSES))[:PASSES].astype(jnp.float32)
        tail = load(slice(own - 2 * PASSES, own))[PASSES:].astype(jnp.float32)
        return [jnp.where(first, tail, head)] if len(send_refs) == 1 else [head, tail]

    for half, lanes in halves():
        for field in range(FIELDS):
            member, level = divmod(field, HELD)
            at = half * FIELDS + field
            values = edges(lambda rows: control_ref[member, level, rows, lanes])
            for send_ref, value in zip(send_refs, values):
                spread(send_ref, 0, at, value)
            for kind, coef_ref in enumerate((east_ref, south_ref)):
                values = edges(lambda rows: coef_ref[level, rows, lanes])
                for send_ref, value in zip(send_refs, values):
                    spread(send_ref, (kind + 1) * PASSES, at, value)


def is_mirrored(halos):
    return halos == 1 and lax.axis_index("row") == 1


def pick(mirrored, count, row):
    return row if mirrored is False else jnp.where(mirrored, count - 1 - row, row)


def stencil(values, row, center, east, west, above, below):
    to_east, to_west = east_west(values[row])
    total = center * values[row] + below * values[row + 1]
    if above is not None:
        total = total + above * values[row - 1]
    return total + (east * to_east + west * to_west)


def interior_passes(halos, field_ref, own_refs, saved_ref, double=False):
    center_ref, east_ref, west_ref, face_ref = own_refs
    own = field_ref.shape[0] // TILE
    values = {row: tile(field_ref, row) for row in range(own)}
    for step in range(1, PASSES + 1):
        for side in range(halos):
            kept = (own - 1 - step, own - step) if side == 0 else (step - 1, step)
            if double:
                kept = range(own - 3 - step, own + 1 - step) if step % 2 else ()
            for index, row in enumerate(kept):
                set_tile(saved_ref, (side * PASSES + step - 1) * 2 + index, values[row])
        after = {}
        for row in range(step if halos == 2 else 0, own - step):
            after[row] = stencil(
                values,
                row,
                tile(center_ref, row),
                tile(east_ref, row),
                tile(west_ref, row),
                tile(face_ref, row) if row else None,
                tile(face_ref, row + 1),
            )
        values = after
    return values


def wedge_passes(halos, halo_rows, own, saved_ref, coefficient, top):
    done = {}
    for side in range(halos):
        values = dict(halo_rows[side])
        for step in range(1, PASSES + 1):
            kept = (own - 1 - step, own - step) if side == 0 else (step - 1, step)
            for index, row in enumerate(kept):
                values[row] = tile(saved_ref, (side * PASSES + step - 1) * 2 + index)
            after = {}
            for row in range(own - step, own + PASSES - step) if side == 0 else range(step - PASSES, step):
                center, east, west, above = (coefficient(kind, row) for kind in range(4))
                after[row] = stencil(values, row, center, east, west, top if row == 0 else above, coefficient(3, row + 1))
            values = after
        done.update(values)
    return done


def shifted(value, distance):
    lane = lax.broadcasted_iota(jnp.int32, (TILE, LANES), 1)
    other = pltpu.roll(value, FIELDS, 0)
    east = pltpu.roll(jnp.where(lane < distance, other, value), LANES - distance, 1)
    west = pltpu.roll(jnp.where(lane >= LANES - distance, other, value), distance, 1)
    return east, west


def compose(coefficient, rows, composed_out):
    for index, row in enumerate(rows):
        center, east, west, above = (coefficient(kind, row) for kind in range(4))
        below = coefficient(3, row + 1)
        (center_e, center_w), (east_e, east_w), (west_e, west_w), (below_e, below_w), (above_e, above_w) = (
            shifted(value, 1) for value in (center, east, west, below, above)
        )
        tiles = (
            center * center + east * west_e + west * east_w + below * below + above * above,
            east * (center + center_e),
            west * (center + center_w),
            east * east_e,
            west * west_w,
            below * (center + coefficient(0, row + 1)),
            east * below_e + below * coefficient(1, row + 1),
            west * below_w + below * coefficient(2, row + 1),
            above * (center + coefficient(0, row - 1)),
            east * above_e + above * coefficient(1, row - 1),
            west * above_w + above * coefficient(2, row - 1),
            below * coefficient(3, row + 2),
            above * coefficient(3, row - 1),
        )
        for place, value in enumerate(tiles):
            set_tile(composed_out, index * POINTS + place, value)


def composed_rows(own):
    return range(own - PASSES, own - 2), range(own - 2, own + PASSES - 2)


def double_wedge(values, own, saved_ref, composed_refs):
    for step in range(1, PASSES // 2 + 1):
        first = own - 2 * step
        for index in range(4):
            values[first - 2 + index] = tile(saved_ref, (step - 1) * 4 + index)
        near = {row: shifted(values[row], 1) for row in range(first - 1, first + PASSES + 1)}
        after = {}
        for row in range(first, first + PASSES):
            def coefficient(place):
                part = int(row >= own - 2)
                return tile(composed_refs[part], (row - composed_rows(own)[part][0]) * POINTS + place)

            east, west = shifted(values[row], 2)
            total = coefficient(0) * values[row] + coefficient(5) * values[row + 1]
            total = total + (coefficient(8) * values[row - 1] + coefficient(11) * values[row + 2])
            total = total + coefficient(12) * values[row - 2]
            sides = coefficient(1) * near[row][0] + coefficient(2) * near[row][1]
            lower = coefficient(6) * near[row + 1][0] + coefficient(7) * near[row + 1][1]
            upper = coefficient(9) * near[row - 1][0] + coefficient(10) * near[row - 1][1]
            far = coefficient(3) * east + coefficient(4) * west
            after[row] = (total + sides) + ((lower + upper) + far)
        values = after
    return values


def prepare_body(halos, control_ref, east_ref, south_ref, *refs):
    own_refs, (rows_out, saved_out, field_ref), refs = refs[:4], refs[4:7], refs[7:]
    raw_east, raw_face = refs[-2:]
    center_out, east_out, west_out, face_out = own_refs
    own = control_ref.shape[2]
    mirrored = is_mirrored(halos)
    for half, lanes in halves():
        for field in range(FIELDS):
            member, level = divmod(field, HELD)
            at = half * FIELDS + field
            spread(rows_out, 0, at, control_ref[member, level, :, lanes].astype(jnp.float32))
            spread(raw_east, 0, at, east_ref[level, :, lanes])
            spread(raw_face, 0, at, south_ref[level, :, lanes])
    for row in range(own):
        source = pick(mirrored, own, row)
        set_tile(field_ref, row, rows_out[block(source, 1), :])
        east = raw_east[block(source, 1), :]
        set_tile(east_out, row, east)
        set_tile(west_out, row, west_of(east))
        if row == 0:
            face = tile(raw_face, 0)
            face = face if mirrored is False else jnp.where(mirrored, 0.0, face)
        else:
            face = raw_face[block(row if mirrored is False else jnp.where(mirrored, own - row, row), 1), :]
        set_tile(face_out, row, face)
    set_tile(face_out, own, tile(raw_face, 0))
    for row in range(own - 1):
        total = 1.0 - tile(east_out, row) - tile(west_out, row)
        set_tile(center_out, row, total - tile(face_out, row + 1) - tile(face_out, row))
    for row, value in interior_passes(halos, field_ref, own_refs, saved_out, halos == 1).items():
        set_tile(rows_out, row, value)
    if halos == 1:
        compose(lambda kind, row: tile(own_refs[kind], row), composed_rows(own)[0], refs[0])


def finish_coefficients(halos, halo_refs, own_refs, tail_refs, own):
    _, east_own, west_own, face_own = own_refs
    center_tail, east_tail, west_tail, face_tail = tail_refs
    mirrored = is_mirrored(halos)

    def halo_tile(side, kind, row):
        return halo_refs[side][block(kind * PASSES + row, 1), :]

    set_tile(east_tail, 0, tile(east_own, own - 1))
    set_tile(west_tail, 0, tile(west_own, own - 1))
    set_tile(face_tail, 0, tile(face_own, own - 1))
    for row in range(PASSES):
        east = halo_tile(0, 1, pick(mirrored, PASSES, row))
        set_tile(east_tail, 1 + row, east)
        set_tile(west_tail, 1 + row, west_of(east))
        if mirrored is False:
            face = halo_tile(0, 2, row)
        elif row == 0:
            face = jnp.where(mirrored, tile(face_own, own), halo_tile(0, 2, 0))
        else:
            face = halo_tile(0, 2, jnp.where(mirrored, PASSES - row, row))
        set_tile(face_tail, 1 + row, face)
    for row in range(PASSES):
        total = 1.0 - tile(east_tail, row) - tile(west_tail, row)
        set_tile(center_tail, row, total - tile(face_tail, row + 1) - tile(face_tail, row))
    if halos == 2:
        for row in range(PASSES):
            at = 1 + PASSES + row
            east, face = halo_tile(1, 1, row), halo_tile(1, 2, row)
            below = halo_tile(1, 2, row + 1) if row + 1 < PASSES else tile(face_own, 0)
            west = west_of(east)
            for ref, value in zip(tail_refs, (1.0 - east - west - below - face, east, west, face)):
                set_tile(ref, at, value)


def coefficient_reader(own_refs, tail_refs, own):
    def coefficient(kind, row):
        if row < 0:
            return tile(tail_refs[kind], 1 + 2 * PASSES + row)
        return tile(own_refs[kind], row) if row < own - 1 else tile(tail_refs[kind], row - own + 1)

    return coefficient


def top_coefficient(halos, own_refs):
    return None if halos == 1 else jnp.where(lax.axis_index("row") == 0, 0.0, tile(own_refs[3], 0))


def forward_body(halos, rows_ref, saved_ref, *refs):
    own_refs, halo_refs, refs = refs[:4], refs[4 : 4 + halos], refs[4 + halos :]
    if halos == 1:
        composed_own, _, composed_tail, *refs = refs
        chunk_refs, sorted_ref, tail_refs = refs[:-6], refs[-5], refs[-4:]
    else:
        tail_refs, chunk_refs, sorted_ref = refs[:4], refs[4:-1], refs[-1]
    own = rows_ref.shape[0] // TILE
    lev_at = lax.axis_index("lev")
    mirrored = is_mirrored(halos)
    finish_coefficients(halos, halo_refs, own_refs, tail_refs, own)
    halo_rows = [{own + row: halo_refs[0][block(pick(mirrored, PASSES, row), 1), :] for row in range(PASSES)}]
    coefficient = coefficient_reader(own_refs, tail_refs, own)
    if halos == 1:
        compose(coefficient, composed_rows(own)[1], composed_tail)
        done = double_wedge(halo_rows[0], own, saved_ref, (composed_own, composed_tail))
    else:
        halo_rows.append({row - PASSES: tile(halo_refs[1], row) for row in range(PASSES)})
        top = top_coefficient(halos, own_refs)
        done = wedge_passes(halos, halo_rows, own, saved_ref, coefficient, top)
    for row in range(own):
        value = done[row] if row in done else tile(rows_ref, row)
        sorted_ref[block(pick(mirrored, own, row), 1), :] = value
    part = own // len(chunk_refs)
    for step, chunk_ref in enumerate(reversed(chunk_refs)):
        chunk_ref[...] = sorted_ref[block(lax.bitwise_xor(lev_at, step) * part, part), :]


def matrix_terms(groups):
    return [
        (group, other, cross)
        for group in range(groups)
        for other in range(max(0, group - 2), min(groups, group + 3))
        for cross in range(2)
        if abs(group - other) < 2 or cross
    ]


def swap_levels(value, sublane):
    return jnp.where(sublane % HELD == 0, pltpu.roll(value, TILE - 1, 0), pltpu.roll(value, 1, 0))


def columns_body(members_ref, innovation_ref, huber_ref, columns_out, levels_ref):
    count, levels, cells = members_ref.shape
    groups, lon = levels // HELD, HALVES * LANES
    rows, packed = cells // lon, levels // FIELDS
    for member in range(count):
        for row in range(rows):
            for half in range(HALVES):
                lanes = slice(row * lon + half * LANES, row * lon + (half + 1) * LANES)
                start = ((member * rows + row) * HALVES + half) * levels
                levels_ref[start : start + levels, :] = members_ref[member, :, lanes].astype(jnp.float32)
                for level in range(HELD):
                    at = half * FIELDS + member * HELD + level
                    spread(columns_out, row * groups, at, levels_ref[pl.ds(start + level, groups, stride=HELD), :])
    for row in range(rows):
        for half in range(HALVES):
            lanes = slice(row * lon + half * LANES, row * lon + (half + 1) * LANES)
            for pack in range(packed):
                source = slice(pack * FIELDS, (pack + 1) * FIELDS)
                start = (rows * groups + row * packed + pack) * TILE + half * FIELDS
                columns_out[start : start + FIELDS, :] = innovation_ref[source, lanes]
                start = start + rows * packed * TILE
                columns_out[start : start + FIELDS, :] = huber_ref[source, lanes].astype(jnp.float32)


def matrix_body(band_ref, group_ref, matrix_out, transposed_out):
    levels = band_ref.shape[1]
    groups = levels // HELD
    sublane = places()

    def entry(level, other):
        offset = other - level + REACH
        if not 0 <= offset < 2 * REACH + 1:
            return jnp.float32(0.0)
        value = band_ref[offset, level] + jnp.float32(1.0 if offset == REACH else 0.0)
        return jnp.where(group_ref[level] == group_ref[other], value, jnp.float32(0.0))

    for slot, (group, other, cross) in enumerate(matrix_terms(groups)):
        pairs = [(group * HELD + level, other * HELD + (level ^ cross)) for level in range(HELD)]
        even, odd = (entry(a, b) for a, b in pairs)
        set_tile(matrix_out, slot, jnp.where(sublane % HELD == 0, even, odd))
        even, odd = (entry(b, a) for a, b in pairs)
        set_tile(transposed_out, slot, jnp.where(sublane % HELD == 0, even, odd))


def apply_matrix(matrix_ref, values, sublane):
    crossed = [swap_levels(value, sublane) for value in values]
    totals = [None] * len(values)
    for slot, (group, other, cross) in enumerate(matrix_terms(len(values))):
        term = tile(matrix_ref, slot) * (crossed if cross else values)[other]
        totals[group] = term if totals[group] is None else totals[group] + term
    return totals


def filter_body(chunks, *refs):
    chunk_refs = refs[:chunks]
    members_ref, matrix_ref, partial_ref, columns = refs[chunks:]
    rows = chunk_refs[0].shape[0] // TILE
    lev_at = lax.axis_index("lev")
    sublane = places()
    first_member = sublane % FIELDS < HELD
    for step, chunk_ref in enumerate(reversed(chunk_refs)):
        columns[block(lax.bitwise_xor(lev_at, step) * rows, rows), :] = chunk_ref[...]
    for row in range(rows):
        filtered = apply_matrix(matrix_ref, [tile(columns, group * rows + row) for group in range(chunks)], sublane)
        terms = [tile(members_ref, row * chunks + group) * value for group, value in enumerate(filtered)]
        for pack in range(chunks // 2):
            lower, upper = terms[2 * pack], terms[2 * pack + 1]
            total = jnp.where(first_member, lower, upper)
            total = total + jnp.where(first_member, pltpu.roll(lower, TILE - HELD, 0), pltpu.roll(upper, HELD, 0))
            set_tile(partial_ref, row * (chunks // 2) + pack, total)


def lift_body(chunks, parts, *refs):
    part_refs, refs = refs[:parts], refs[parts:]
    columns_ref, transposed_ref, refs = refs[0], refs[1], refs[2:]
    chunk_refs, (weighted_ref, sorted_ref) = refs[:chunks], refs[chunks:]
    rows = chunk_refs[0].shape[0] // TILE
    lev_at = lax.axis_index("lev")
    sublane = places()
    first_member = sublane % FIELDS < HELD
    increment = part_refs[0][...]
    for part_ref in part_refs[1:]:
        increment = increment + part_ref[...]
    start, size = rows * chunks * TILE, weighted_ref.shape[0]
    residual = increment - columns_ref[start : start + size, :]
    scale = HUBER / jnp.maximum(jnp.abs(residual), HUBER)
    weighted_ref[...] = jnp.where(columns_ref[start + size :, :] == 1.0, scale, 1.0) * residual
    for row in range(rows):
        adjoint = []
        for pack in range(chunks // 2):
            weighted = tile(weighted_ref, row * (chunks // 2) + pack)
            lower = jnp.where(first_member, weighted, pltpu.roll(weighted, HELD, 0))
            upper = jnp.where(first_member, pltpu.roll(weighted, TILE - HELD, 0), weighted)
            for value in (lower, upper):
                adjoint.append(value * tile(columns_ref, row * chunks + len(adjoint)))
        for group, value in enumerate(apply_matrix(transposed_ref, adjoint, sublane)):
            set_tile(sorted_ref, group * rows + row, value)
    for step, chunk_ref in enumerate(reversed(chunk_refs)):
        chunk_ref[...] = sorted_ref[block(lax.bitwise_xor(lev_at, step) * rows, rows), :]


def gather_body(halos, chunks, *refs):
    chunk_refs, field_ref, send_refs, sorted_ref = refs[:chunks], refs[chunks], refs[chunks + 1 : -1], refs[-1]
    lev_at = lax.axis_index("lev")
    mirrored = is_mirrored(halos)
    rows = chunk_refs[0].shape[0] // TILE
    own = rows * chunks
    for step, chunk_ref in enumerate(reversed(chunk_refs)):
        sorted_ref[block(lax.bitwise_xor(lev_at, step) * rows, rows), :] = chunk_ref[...]
    for row in range(own):
        set_tile(field_ref, row, sorted_ref[block(pick(mirrored, own, row), 1), :])
    for row in range(PASSES):
        if halos == 1:
            set_tile(send_refs[0], row, tile(field_ref, own - 1 - row))
        else:
            set_tile(send_refs[0], row, tile(field_ref, row))
            set_tile(send_refs[1], row, tile(field_ref, own - PASSES + row))


def to_fields(planes_ref, fields_ref, rows):
    for field in range(FIELDS):
        member, level = divmod(field, HELD)
        for half, lanes in halves():
            fields_ref[member, level, :, lanes] = planes_ref[pl.ds(half * FIELDS + field, rows, stride=TILE), :]


def interior_body(halos, field_ref, control_ref, *refs):
    own_refs, (fields_out, saved_out, result_ref) = refs[:4], refs[4:]
    own = field_ref.shape[0] // TILE
    mirrored = is_mirrored(halos)
    done = interior_passes(halos, field_ref, own_refs, saved_out, halos == 1)
    for row in range(own):
        value = done[row] + tile(control_ref, row) if row in done else jnp.zeros((TILE, LANES), jnp.float32)
        result_ref[block(pick(mirrored, own, row), 1), :] = value
    to_fields(result_ref, fields_out, own)


def backward_body(halos, control_ref, fields_ref, saved_ref, *refs):
    halo_refs, refs = refs[:halos], refs[halos:]
    coefficient_refs, refs = (refs[:2], refs[2:]) if halos == 1 else (refs[:8], refs[8:])
    gradient_hbm, refs = refs[0], refs[1:]
    result_refs, edge_refs, semaphores = refs[:halos], refs[halos : 2 * halos], refs[-1]
    own = fields_ref.shape[2]
    mirrored = is_mirrored(halos)
    if halos == 1:
        spans = [(PASSES * mirrored.astype(jnp.int32), own - PASSES)]
        spans.append((jnp.where(mirrored, 0, own - PASSES), PASSES))
    else:
        spans = [(PASSES, own - 2 * PASSES), (own - PASSES, PASSES), (0, PASSES)]
    copies = []

    def send(source_ref, source_start, start, rows):
        copy = pltpu.make_async_copy(
            source_ref.at[:, :, pl.ds(source_start, rows), :],
            gradient_hbm.at[:, :, pl.ds(start, rows), :],
            semaphores.at[len(copies)],
        )
        copy.start()
        copies.append(copy)

    start = pl.multiple_of(spans[0][0], TILE)
    send(fields_ref, start, start, spans[0][1])
    halo_rows = [{own + row: tile(halo_refs[0], row) for row in range(PASSES)}]
    if halos == 1:
        done = double_wedge(halo_rows[0], own, saved_ref, coefficient_refs)
    else:
        halo_rows.append({row - PASSES: tile(halo_refs[1], row) for row in range(PASSES)})
        own_refs, tail_refs = coefficient_refs[:4], coefficient_refs[4:]
        coefficient = coefficient_reader(own_refs, tail_refs, own)
        top = top_coefficient(halos, own_refs)
        done = wedge_passes(halos, halo_rows, own, saved_ref, coefficient, top)
    for side in range(halos):
        for row in range(PASSES):
            value = done[own - PASSES + row] + tile(control_ref, own - PASSES + row) if side == 0 else done[row] + tile(control_ref, row)
            result_refs[side][block(pick(mirrored, PASSES, row), 1), :] = value
        to_fields(result_refs[side], edge_refs[side], PASSES)
        send(edge_refs[side], 0, pl.multiple_of(spans[1 + side][0], TILE), PASSES)
    for copy in copies:
        copy.wait()


def per_device(control, members, east_coef, south_coef, innovation, huber_class, band, level_group_index):
    count, held, own, lon = control.shape
    levels, cells = members.shape[1:]
    chunks, parts, row_count = (lax.axis_size(axis) for axis in ("lev", "mem", "row"))
    assert (count * held, held, lon) == (FIELDS, HELD, HALVES * LANES)
    part = own // chunks
    halos = 1 if row_count == 2 else 2
    tail = 1 + halos * PASSES
    terms = len(matrix_terms(chunks))
    packed = part * levels // FIELDS
    crossed = row_count == 2

    inputs = (control, east_coef, south_coef, members, innovation, huber_class)
    fetched = call(
        pack_body,
        [pltpu.VMEM(x.shape, x.dtype) for x in inputs] + [planes(3 * PASSES)] * halos,
        remote(*inputs),
        [pltpu.SemaphoreType.DMA((FIELDS + 2 * HELD + 3,))],
        specs=[HBM] * 6,
    )
    control_near, east_near, south_near = fetched[:3]
    edges = fetched[6:]
    halo = swap_edges(edges, "row")
    kept = halos * PASSES * 2
    near, far = ([planes(len(rows) * POINTS)] if halos == 1 else [] for rows in composed_rows(own))
    prepared = call(
        functools.partial(prepare_body, halos),
        [planes(own)] * 3 + [planes(own + 1), planes(own), planes(kept), planes(own)] + near,
        resident(control_near, east_near, south_near),
        [planes(own)] * 2,
    )
    own_stencil, (done_rows, saved, control_planes), composed = prepared[:4], prepared[4:7], prepared[7:]
    (columns,) = call(
        columns_body,
        [planes(part * chunks + 2 * packed)],
        resident(*fetched[3:6]),
        [planes(part * chunks)],
    )
    matrix, transposed = call(
        matrix_body, [planes(terms)] * 2, [band, level_group_index], specs=[SMEM, SMEM]
    )
    tail_planes = [planes(tail)] * 4
    first_outs = far or tail_planes
    operands = [done_rows, saved, *own_stencil, *halo, *composed]
    passed = [columns] if crossed else []
    results = call(
        functools.partial(forward_body, halos),
        first_outs + [planes(part)] * chunks + [planes(part * chunks + 2 * packed)] * len(passed),
        resident(*operands, *passed),
        [planes(own)] + (tail_planes if halos == 1 else []),
        aliases={len(operands): len(first_outs) + chunks} if crossed else None,
    )
    if crossed:
        *results, columns = results
        columns = lax.ppermute(columns, "row", [(0, 1), (1, 0)])
    last_coefs = [*composed, *results[:1]] if halos == 1 else [*own_stencil, *results[:4]]
    smoothed = results[len(first_outs) :]
    received = exchange(smoothed[::-1], "lev", crossed)
    (partial,) = call(
        functools.partial(filter_body, chunks),
        [planes(packed)],
        resident(*received[::-1], columns, matrix),
        [planes(part * chunks)],
    )
    partials = collect(partial, "mem")
    lifted = call(
        functools.partial(lift_body, chunks, parts),
        [planes(part)] * chunks,
        resident(*partials, columns, transposed),
        [planes(packed), planes(part * chunks)],
    )
    returned = exchange(lifted[::-1], "lev", crossed)
    gathered, *edges = call(
        functools.partial(gather_body, halos, chunks),
        [planes(own)] + [planes(PASSES)] * halos,
        resident(*returned[::-1]),
        [planes(own)],
    )
    halo = swap_edges(edges, "row")
    early, saved = call(
        functools.partial(interior_body, halos),
        [pltpu.VMEM(control.shape, jnp.float32), planes(kept)],
        resident(gathered, control_planes, *own_stencil),
        [planes(own)],
    )
    (gradient,) = call(
        functools.partial(backward_body, halos),
        [jax.ShapeDtypeStruct(control.shape, jnp.float32)],
        resident(control_planes, early, saved, *halo, *last_coefs),
        [planes(PASSES)] * halos
        + [pltpu.VMEM((count, held, PASSES, lon), jnp.float32)] * halos
        + [pltpu.SemaphoreType.DMA((1 + halos,))],
        out_specs=[HBM],
    )
    return gradient


def solution(mesh):
    placed = (
        P("mem", "lev", "row", None),
        P("mem", None, ("row", "lev")),
        P("lev", "row", None),
        P("lev", "row", None),
        P(None, ("row", "lev")),
        P(None, ("row", "lev")),
        P(),
        P(),
    )
    return jax.shard_map(
        per_device,
        mesh=mesh,
        in_specs=placed,
        out_specs=P("mem", "lev", "row", None),
        check_vma=False,
    )
```

```python
import functools

import jax
import jax.numpy as jnp
from jax import lax
from jax.experimental import pallas as pl
from jax.experimental.pallas import tpu as pltpu
from jax.sharding import PartitionSpec as P

PASSES = 8
HUBER = 1.0
REACH = 3
POINTS = 13
LANES = 128
TILE = 8
HALVES = 2
HELD = 2
FIELDS = 4

VMEM = pl.BlockSpec(memory_space=pltpu.VMEM)
SMEM = pl.BlockSpec(memory_space=pltpu.SMEM)
HBM = pl.BlockSpec(memory_space=pltpu.HBM)


def planes(count):
    return pltpu.VMEM((count * TILE, LANES), jnp.float32)


def call(body, outs, operands, scratch=(), specs=None, out_specs=None, flops=0, aliases=None):
    total = sum(op.size * op.dtype.itemsize for op in operands)
    return pl.pallas_call(
        body,
        out_shape=outs,
        in_specs=specs or [VMEM] * len(operands),
        out_specs=out_specs or [VMEM] * len(outs),
        scratch_shapes=list(scratch),
        input_output_aliases=aliases or {},
        compiler_params=pltpu.CompilerParams(vmem_limit_bytes=32 * 1024 * 1024),
        cost_estimate=pl.CostEstimate(flops=flops, bytes_accessed=2 * total, transcendentals=0),
    )(*operands)


def resident(*arrays):
    return [pltpu.with_memory_space_constraint(array, pltpu.VMEM) for array in arrays]


def remote(*arrays):
    return [pltpu.with_memory_space_constraint(array, pltpu.HBM) for array in arrays]


def exchange(chunks, axis, crossed):
    count = len(chunks)
    received = list(chunks)
    for step in reversed(range(count)):
        if chunks[step] is None:
            continue
        if crossed:
            pairs = [(2 * i + row, 2 * (i ^ step) + 1 - row) for i in range(count) for row in range(2)]
            received[step] = lax.ppermute(chunks[step], (axis, "row"), pairs)
        elif step:
            received[step] = lax.ppermute(chunks[step], axis, [(i, i ^ step) for i in range(count)])
    return received


def collect(array, axis):
    count = lax.axis_size(axis)
    shifts = [[(i, (i + step) % count) for i in range(count)] for step in range(1, count)]
    return [array] + [lax.ppermute(array, axis, shift) for shift in shifts]


def swap_edges(edges, axis):
    count = lax.axis_size(axis)
    if len(edges) == 1:
        return [lax.ppermute(edges[0], axis, [(0, 1), (1, 0)])]
    head, tail = edges
    south = lax.ppermute(head, axis, [(i + 1, i) for i in range(count - 1)])
    north = lax.ppermute(tail, axis, [(i, i + 1) for i in range(count - 1)])
    return [south, north]


def tile(ref, row):
    return ref[row * TILE : (row + 1) * TILE, :]


def set_tile(ref, row, value):
    ref[row * TILE : (row + 1) * TILE, :] = value


def block(first_row, rows):
    return pl.ds(pl.multiple_of(first_row * TILE, TILE), rows * TILE)


def spread(ref, row, sublane, values):
    ref[pl.ds(row * TILE + sublane, values.shape[0], stride=TILE), :] = values


def places():
    return lax.broadcasted_iota(jnp.int32, (TILE, LANES), 0)


def east_west(value):
    lane = lax.broadcasted_iota(jnp.int32, (TILE, LANES), 1)
    other = pltpu.roll(value, FIELDS, 0)
    east = pltpu.roll(jnp.where(lane == 0, other, value), LANES - 1, 1)
    west = pltpu.roll(jnp.where(lane == LANES - 1, other, value), 1, 1)
    return east, west


def west_of(value):
    lane = lax.broadcasted_iota(jnp.int32, (TILE, LANES), 1)
    return pltpu.roll(jnp.where(lane == LANES - 1, pltpu.roll(value, FIELDS, 0), value), 1, 1)


def halves():
    return [(half, slice(half * LANES, (half + 1) * LANES)) for half in range(HALVES)]


def pack_body(control_hbm, east_hbm, south_hbm, control_ref, east_ref, south_ref, *refs):
    send_refs, semaphores = refs[:-1], refs[-1]
    pieces = [(east_hbm.at[level], east_ref.at[level]) for level in range(HELD)]
    pieces += [(south_hbm.at[level], south_ref.at[level]) for level in range(HELD)]
    for field in range(FIELDS):
        member, level = divmod(field, HELD)
        pieces.append((control_hbm.at[member, level], control_ref.at[member, level]))
    copies = [
        pltpu.make_async_copy(source, target, semaphores.at[index]) for index, (source, target) in enumerate(pieces)
    ]
    for copy in copies:
        copy.start()
    for copy in copies:
        copy.wait()
    own = control_ref.shape[2]
    first = lax.axis_index("row") == 0

    def edges(load):
        head = load(slice(0, 2 * PASSES))[:PASSES].astype(jnp.float32)
        tail = load(slice(own - 2 * PASSES, own))[PASSES:].astype(jnp.float32)
        return [jnp.where(first, tail, head)] if len(send_refs) == 1 else [head, tail]

    for half, lanes in halves():
        for field in range(FIELDS):
            member, level = divmod(field, HELD)
            at = half * FIELDS + field
            values = edges(lambda rows: control_ref[member, level, rows, lanes])
            for send_ref, value in zip(send_refs, values):
                spread(send_ref, 0, at, value)
            for kind, coef_ref in enumerate((east_ref, south_ref)):
                values = edges(lambda rows: coef_ref[level, rows, lanes])
                for send_ref, value in zip(send_refs, values):
                    spread(send_ref, (kind + 1) * PASSES, at, value)


def is_mirrored(halos):
    return halos == 1 and lax.axis_index("row") == 1


def pick(mirrored, count, row):
    return row if mirrored is False else jnp.where(mirrored, count - 1 - row, row)


def stencil(values, row, center, east, west, above, below):
    to_east, to_west = east_west(values[row])
    total = center * values[row] + below * values[row + 1]
    if above is not None:
        total = total + above * values[row - 1]
    return total + (east * to_east + west * to_west)


def interior_passes(halos, field_ref, own_refs, saved_ref, double=False):
    center_ref, east_ref, west_ref, face_ref = own_refs
    own = field_ref.shape[0] // TILE
    values = {row: tile(field_ref, row) for row in range(own)}
    for step in range(1, PASSES + 1):
        for side in range(halos):
            kept = (own - 1 - step, own - step) if side == 0 else (step - 1, step)
            if double:
                kept = range(own - 3 - step, own + 1 - step) if step % 2 else ()
            for index, row in enumerate(kept):
                set_tile(saved_ref, (side * PASSES + step - 1) * 2 + index, values[row])
        after = {}
        for row in range(step if halos == 2 else 0, own - step):
            after[row] = stencil(
                values,
                row,
                tile(center_ref, row),
                tile(east_ref, row),
                tile(west_ref, row),
                tile(face_ref, row) if row else None,
                tile(face_ref, row + 1),
            )
        values = after
    return values


def wedge_passes(halos, halo_rows, own, saved_ref, coefficient, top):
    done = {}
    for side in range(halos):
        values = dict(halo_rows[side])
        for step in range(1, PASSES + 1):
            kept = (own - 1 - step, own - step) if side == 0 else (step - 1, step)
            for index, row in enumerate(kept):
                values[row] = tile(saved_ref, (side * PASSES + step - 1) * 2 + index)
            after = {}
            for row in range(own - step, own + PASSES - step) if side == 0 else range(step - PASSES, step):
                center, east, west, above = (coefficient(kind, row) for kind in range(4))
                after[row] = stencil(values, row, center, east, west, top if row == 0 else above, coefficient(3, row + 1))
            values = after
        done.update(values)
    return done


def shifted(value, distance):
    lane = lax.broadcasted_iota(jnp.int32, (TILE, LANES), 1)
    other = pltpu.roll(value, FIELDS, 0)
    east = pltpu.roll(jnp.where(lane < distance, other, value), LANES - distance, 1)
    west = pltpu.roll(jnp.where(lane >= LANES - distance, other, value), distance, 1)
    return east, west


def compose(coefficient, rows, composed_out):
    for index, row in enumerate(rows):
        center, east, west, above = (coefficient(kind, row) for kind in range(4))
        below = coefficient(3, row + 1)
        (center_e, center_w), (east_e, east_w), (west_e, west_w), (below_e, below_w), (above_e, above_w) = (
            shifted(value, 1) for value in (center, east, west, below, above)
        )
        tiles = (
            center * center + east * west_e + west * east_w + below * below + above * above,
            east * (center + center_e),
            west * (center + center_w),
            east * east_e,
            west * west_w,
            below * (center + coefficient(0, row + 1)),
            east * below_e + below * coefficient(1, row + 1),
            west * below_w + below * coefficient(2, row + 1),
            above * (center + coefficient(0, row - 1)),
            east * above_e + above * coefficient(1, row - 1),
            west * above_w + above * coefficient(2, row - 1),
            below * coefficient(3, row + 2),
            above * coefficient(3, row - 1),
        )
        for place, value in enumerate(tiles):
            set_tile(composed_out, index * POINTS + place, value)


def composed_rows(own):
    return range(own - PASSES, own - 2), range(own - 2, own + PASSES - 2)


def double_wedge(values, own, saved_ref, composed_refs):
    for step in range(1, PASSES // 2 + 1):
        first = own - 2 * step
        for index in range(4):
            values[first - 2 + index] = tile(saved_ref, (step - 1) * 4 + index)
        near = {row: shifted(values[row], 1) for row in range(first - 1, first + PASSES + 1)}
        after = {}
        for row in range(first, first + PASSES):
            def coefficient(place):
                part = int(row >= own - 2)
                return tile(composed_refs[part], (row - composed_rows(own)[part][0]) * POINTS + place)

            east, west = shifted(values[row], 2)
            total = coefficient(0) * values[row] + coefficient(5) * values[row + 1]
            total = total + (coefficient(8) * values[row - 1] + coefficient(11) * values[row + 2])
            total = total + coefficient(12) * values[row - 2]
            sides = coefficient(1) * near[row][0] + coefficient(2) * near[row][1]
            lower = coefficient(6) * near[row + 1][0] + coefficient(7) * near[row + 1][1]
            upper = coefficient(9) * near[row - 1][0] + coefficient(10) * near[row - 1][1]
            far = coefficient(3) * east + coefficient(4) * west
            after[row] = (total + sides) + ((lower + upper) + far)
        values = after
    return values


def prepare_body(halos, control_ref, east_ref, south_ref, *refs):
    own_refs, (rows_out, saved_out, field_ref), refs = refs[:4], refs[4:7], refs[7:]
    raw_east, raw_face = refs[-2:]
    center_out, east_out, west_out, face_out = own_refs
    own = control_ref.shape[2]
    mirrored = is_mirrored(halos)
    for half, lanes in halves():
        for field in range(FIELDS):
            member, level = divmod(field, HELD)
            at = half * FIELDS + field
            spread(rows_out, 0, at, control_ref[member, level, :, lanes].astype(jnp.float32))
            spread(raw_east, 0, at, east_ref[level, :, lanes])
            spread(raw_face, 0, at, south_ref[level, :, lanes])
    for row in range(own):
        source = pick(mirrored, own, row)
        set_tile(field_ref, row, rows_out[block(source, 1), :])
        east = raw_east[block(source, 1), :]
        set_tile(east_out, row, east)
        set_tile(west_out, row, west_of(east))
        if row == 0:
            face = tile(raw_face, 0)
            face = face if mirrored is False else jnp.where(mirrored, 0.0, face)
        else:
            face = raw_face[block(row if mirrored is False else jnp.where(mirrored, own - row, row), 1), :]
        set_tile(face_out, row, face)
    set_tile(face_out, own, tile(raw_face, 0))
    for row in range(own - 1):
        total = 1.0 - tile(east_out, row) - tile(west_out, row)
        set_tile(center_out, row, total - tile(face_out, row + 1) - tile(face_out, row))
    for row, value in interior_passes(halos, field_ref, own_refs, saved_out, halos == 1).items():
        set_tile(rows_out, row, value)
    if halos == 1:
        compose(lambda kind, row: tile(own_refs[kind], row), composed_rows(own)[0], refs[0])


def finish_coefficients(halos, halo_refs, own_refs, tail_refs, own):
    _, east_own, west_own, face_own = own_refs
    center_tail, east_tail, west_tail, face_tail = tail_refs
    mirrored = is_mirrored(halos)

    def halo_tile(side, kind, row):
        return halo_refs[side][block(kind * PASSES + row, 1), :]

    set_tile(east_tail, 0, tile(east_own, own - 1))
    set_tile(west_tail, 0, tile(west_own, own - 1))
    set_tile(face_tail, 0, tile(face_own, own - 1))
    for row in range(PASSES):
        east = halo_tile(0, 1, pick(mirrored, PASSES, row))
        set_tile(east_tail, 1 + row, east)
        set_tile(west_tail, 1 + row, west_of(east))
        if mirrored is False:
            face = halo_tile(0, 2, row)
        elif row == 0:
            face = jnp.where(mirrored, tile(face_own, own), halo_tile(0, 2, 0))
        else:
            face = halo_tile(0, 2, jnp.where(mirrored, PASSES - row, row))
        set_tile(face_tail, 1 + row, face)
    for row in range(PASSES):
        total = 1.0 - tile(east_tail, row) - tile(west_tail, row)
        set_tile(center_tail, row, total - tile(face_tail, row + 1) - tile(face_tail, row))
    if halos == 2:
        for row in range(PASSES):
            at = 1 + PASSES + row
            east, face = halo_tile(1, 1, row), halo_tile(1, 2, row)
            below = halo_tile(1, 2, row + 1) if row + 1 < PASSES else tile(face_own, 0)
            west = west_of(east)
            for ref, value in zip(tail_refs, (1.0 - east - west - below - face, east, west, face)):
                set_tile(ref, at, value)


def coefficient_reader(own_refs, tail_refs, own):
    def coefficient(kind, row):
        if row < 0:
            return tile(tail_refs[kind], 1 + 2 * PASSES + row)
        return tile(own_refs[kind], row) if row < own - 1 else tile(tail_refs[kind], row - own + 1)

    return coefficient


def top_coefficient(halos, own_refs):
    return None if halos == 1 else jnp.where(lax.axis_index("row") == 0, 0.0, tile(own_refs[3], 0))


def forward_body(halos, rows_ref, saved_ref, *refs):
    own_refs, halo_refs, refs = refs[:4], refs[4 : 4 + halos], refs[4 + halos :]
    if halos == 1:
        composed_own, _, composed_tail, *refs = refs
        chunk_refs, columns_ref, sorted_ref, tail_refs = refs[:-6], refs[-6], refs[-5], refs[-4:]
        size = chunk_refs[0].shape[0]
        chunk_refs = [*chunk_refs, columns_ref.at[pl.ds(columns_ref.shape[0] - size, size), :]]
    else:
        tail_refs, chunk_refs, sorted_ref = refs[:4], refs[4:-1], refs[-1]
    own = rows_ref.shape[0] // TILE
    lev_at = lax.axis_index("lev")
    mirrored = is_mirrored(halos)
    finish_coefficients(halos, halo_refs, own_refs, tail_refs, own)
    halo_rows = [{own + row: halo_refs[0][block(pick(mirrored, PASSES, row), 1), :] for row in range(PASSES)}]
    coefficient = coefficient_reader(own_refs, tail_refs, own)
    if halos == 1:
        compose(coefficient, composed_rows(own)[1], composed_tail)
        done = double_wedge(halo_rows[0], own, saved_ref, (composed_own, composed_tail))
    else:
        halo_rows.append({row - PASSES: tile(halo_refs[1], row) for row in range(PASSES)})
        top = top_coefficient(halos, own_refs)
        done = wedge_passes(halos, halo_rows, own, saved_ref, coefficient, top)
    for row in range(own):
        value = done[row] if row in done else tile(rows_ref, row)
        sorted_ref[block(pick(mirrored, own, row), 1), :] = value
    part = own // len(chunk_refs)
    for step, chunk_ref in enumerate(reversed(chunk_refs)):
        chunk_ref[...] = sorted_ref[block(lax.bitwise_xor(lev_at, step) * part, part), :]


def matrix_terms(groups):
    return [
        (group, other, cross)
        for group in range(groups)
        for other in range(max(0, group - 2), min(groups, group + 3))
        for cross in range(2)
        if abs(group - other) < 2 or cross
    ]


def swap_levels(value, sublane):
    return jnp.where(sublane % HELD == 0, pltpu.roll(value, TILE - 1, 0), pltpu.roll(value, 1, 0))


def columns_body(members_ref, innovation_ref, huber_ref, columns_out, levels_ref):
    count, levels, cells = members_ref.shape
    groups, lon = levels // HELD, HALVES * LANES
    rows, packed = cells // lon, levels // FIELDS
    for member in range(count):
        for row in range(rows):
            for half in range(HALVES):
                lanes = slice(row * lon + half * LANES, row * lon + (half + 1) * LANES)
                start = ((member * rows + row) * HALVES + half) * levels
                levels_ref[start : start + levels, :] = members_ref[member, :, lanes].astype(jnp.float32)
                for level in range(HELD):
                    at = half * FIELDS + member * HELD + level
                    spread(columns_out, row * groups, at, levels_ref[pl.ds(start + level, groups, stride=HELD), :])
    for row in range(rows):
        for half in range(HALVES):
            lanes = slice(row * lon + half * LANES, row * lon + (half + 1) * LANES)
            for pack in range(packed):
                source = slice(pack * FIELDS, (pack + 1) * FIELDS)
                start = (rows * groups + row * packed + pack) * TILE + half * FIELDS
                columns_out[start : start + FIELDS, :] = innovation_ref[source, lanes]
                start = start + rows * packed * TILE
                columns_out[start : start + FIELDS, :] = huber_ref[source, lanes].astype(jnp.float32)


def matrix_body(band_ref, group_ref, matrix_out, transposed_out):
    levels = band_ref.shape[1]
    groups = levels // HELD
    sublane = places()

    def entry(level, other):
        offset = other - level + REACH
        if not 0 <= offset < 2 * REACH + 1:
            return jnp.float32(0.0)
        value = band_ref[offset, level] + jnp.float32(1.0 if offset == REACH else 0.0)
        return jnp.where(group_ref[level] == group_ref[other], value, jnp.float32(0.0))

    for slot, (group, other, cross) in enumerate(matrix_terms(groups)):
        pairs = [(group * HELD + level, other * HELD + (level ^ cross)) for level in range(HELD)]
        even, odd = (entry(a, b) for a, b in pairs)
        set_tile(matrix_out, slot, jnp.where(sublane % HELD == 0, even, odd))
        even, odd = (entry(b, a) for a, b in pairs)
        set_tile(transposed_out, slot, jnp.where(sublane % HELD == 0, even, odd))


def apply_matrix(matrix_ref, values, sublane):
    crossed = [swap_levels(value, sublane) for value in values]
    totals = [None] * len(values)
    for slot, (group, other, cross) in enumerate(matrix_terms(len(values))):
        term = tile(matrix_ref, slot) * (crossed if cross else values)[other]
        totals[group] = term if totals[group] is None else totals[group] + term
    return totals


def filter_body(chunks, *refs):
    *chunk_refs, members_ref, matrix_ref, partial_ref, columns = refs
    size = chunk_refs[0].shape[0]
    if len(chunk_refs) < chunks:
        chunk_refs.append(members_ref.at[pl.ds(members_ref.shape[0] - size, size), :])
    rows = size // TILE
    lev_at = lax.axis_index("lev")
    sublane = places()
    first_member = sublane % FIELDS < HELD
    for step, chunk_ref in enumerate(reversed(chunk_refs)):
        columns[block(lax.bitwise_xor(lev_at, step) * rows, rows), :] = chunk_ref[...]
    for row in range(rows):
        filtered = apply_matrix(matrix_ref, [tile(columns, group * rows + row) for group in range(chunks)], sublane)
        terms = [tile(members_ref, row * chunks + group) * value for group, value in enumerate(filtered)]
        for pack in range(chunks // 2):
            lower, upper = terms[2 * pack], terms[2 * pack + 1]
            total = jnp.where(first_member, lower, upper)
            total = total + jnp.where(first_member, pltpu.roll(lower, TILE - HELD, 0), pltpu.roll(upper, HELD, 0))
            set_tile(partial_ref, row * (chunks // 2) + pack, total)


def lift_body(chunks, parts, *refs):
    part_refs, refs = refs[:parts], refs[parts:]
    columns_ref, transposed_ref, refs = refs[0], refs[1], refs[2:]
    chunk_refs, (weighted_ref, sorted_ref) = refs[:chunks], refs[chunks:]
    rows = chunk_refs[0].shape[0] // TILE
    lev_at = lax.axis_index("lev")
    sublane = places()
    first_member = sublane % FIELDS < HELD
    increment = part_refs[0][...]
    for part_ref in part_refs[1:]:
        increment = increment + part_ref[...]
    start, size = rows * chunks * TILE, weighted_ref.shape[0]
    residual = increment - columns_ref[start : start + size, :]
    scale = HUBER / jnp.maximum(jnp.abs(residual), HUBER)
    weighted_ref[...] = jnp.where(columns_ref[start + size : start + 2 * size, :] == 1.0, scale, 1.0) * residual
    for row in range(rows):
        adjoint = []
        for pack in range(chunks // 2):
            weighted = tile(weighted_ref, row * (chunks // 2) + pack)
            lower = jnp.where(first_member, weighted, pltpu.roll(weighted, HELD, 0))
            upper = jnp.where(first_member, pltpu.roll(weighted, TILE - HELD, 0), weighted)
            for value in (lower, upper):
                adjoint.append(value * tile(columns_ref, row * chunks + len(adjoint)))
        for group, value in enumerate(apply_matrix(transposed_ref, adjoint, sublane)):
            set_tile(sorted_ref, group * rows + row, value)
    for step, chunk_ref in enumerate(reversed(chunk_refs)):
        chunk_ref[...] = sorted_ref[block(lax.bitwise_xor(lev_at, step) * rows, rows), :]


def gather_body(halos, chunks, *refs):
    chunk_refs, field_ref, send_refs, sorted_ref = refs[:chunks], refs[chunks], refs[chunks + 1 : -1], refs[-1]
    lev_at = lax.axis_index("lev")
    mirrored = is_mirrored(halos)
    rows = chunk_refs[0].shape[0] // TILE
    own = rows * chunks
    for step, chunk_ref in enumerate(reversed(chunk_refs)):
        sorted_ref[block(lax.bitwise_xor(lev_at, step) * rows, rows), :] = chunk_ref[...]
    for row in range(own):
        set_tile(field_ref, row, sorted_ref[block(pick(mirrored, own, row), 1), :])
    for row in range(PASSES):
        if halos == 1:
            set_tile(send_refs[0], row, tile(field_ref, own - 1 - row))
        else:
            set_tile(send_refs[0], row, tile(field_ref, row))
            set_tile(send_refs[1], row, tile(field_ref, own - PASSES + row))


def to_fields(planes_ref, fields_ref, rows):
    for field in range(FIELDS):
        member, level = divmod(field, HELD)
        for half, lanes in halves():
            fields_ref[member, level, :, lanes] = planes_ref[pl.ds(half * FIELDS + field, rows, stride=TILE), :]


def interior_body(halos, field_ref, control_ref, *refs):
    own_refs, (fields_out, saved_out, result_ref) = refs[:4], refs[4:]
    own = field_ref.shape[0] // TILE
    mirrored = is_mirrored(halos)
    done = interior_passes(halos, field_ref, own_refs, saved_out, halos == 1)
    for row in range(own):
        value = done[row] + tile(control_ref, row) if row in done else jnp.zeros((TILE, LANES), jnp.float32)
        result_ref[block(pick(mirrored, own, row), 1), :] = value
    to_fields(result_ref, fields_out, own)


def backward_body(halos, control_ref, fields_ref, saved_ref, *refs):
    halo_refs, refs = refs[:halos], refs[halos:]
    coefficient_refs, refs = (refs[:2], refs[2:]) if halos == 1 else (refs[:8], refs[8:])
    gradient_hbm, refs = refs[0], refs[1:]
    result_refs, edge_refs, semaphores = refs[:halos], refs[halos : 2 * halos], refs[-1]
    own = fields_ref.shape[2]
    mirrored = is_mirrored(halos)
    if halos == 1:
        spans = [(PASSES * mirrored.astype(jnp.int32), own - PASSES)]
        spans.append((jnp.where(mirrored, 0, own - PASSES), PASSES))
    else:
        spans = [(PASSES, own - 2 * PASSES), (own - PASSES, PASSES), (0, PASSES)]
    copies = []

    def send(source_ref, source_start, start, rows):
        copy = pltpu.make_async_copy(
            source_ref.at[:, :, pl.ds(source_start, rows), :],
            gradient_hbm.at[:, :, pl.ds(start, rows), :],
            semaphores.at[len(copies)],
        )
        copy.start()
        copies.append(copy)

    start = pl.multiple_of(spans[0][0], TILE)
    send(fields_ref, start, start, spans[0][1])
    halo_rows = [{own + row: tile(halo_refs[0], row) for row in range(PASSES)}]
    if halos == 1:
        done = double_wedge(halo_rows[0], own, saved_ref, coefficient_refs)
    else:
        halo_rows.append({row - PASSES: tile(halo_refs[1], row) for row in range(PASSES)})
        own_refs, tail_refs = coefficient_refs[:4], coefficient_refs[4:]
        coefficient = coefficient_reader(own_refs, tail_refs, own)
        top = top_coefficient(halos, own_refs)
        done = wedge_passes(halos, halo_rows, own, saved_ref, coefficient, top)
    for side in range(halos):
        for row in range(PASSES):
            value = done[own - PASSES + row] + tile(control_ref, own - PASSES + row) if side == 0 else done[row] + tile(control_ref, row)
            result_refs[side][block(pick(mirrored, PASSES, row), 1), :] = value
        to_fields(result_refs[side], edge_refs[side], PASSES)
        send(edge_refs[side], 0, pl.multiple_of(spans[1 + side][0], TILE), PASSES)
    for copy in copies:
        copy.wait()


def per_device(control, members, east_coef, south_coef, innovation, huber_class, band, level_group_index):
    count, held, own, lon = control.shape
    levels, cells = members.shape[1:]
    chunks, parts, row_count = (lax.axis_size(axis) for axis in ("lev", "mem", "row"))
    assert (count * held, held, lon) == (FIELDS, HELD, HALVES * LANES)
    part = own // chunks
    halos = 1 if row_count == 2 else 2
    tail = 1 + halos * PASSES
    terms = len(matrix_terms(chunks))
    packed = part * levels // FIELDS
    crossed = row_count == 2

    control_near, east_near, south_near, *edges = call(
        pack_body,
        [pltpu.VMEM(x.shape, x.dtype) for x in (control, east_coef, south_coef)] + [planes(3 * PASSES)] * halos,
        remote(control, east_coef, south_coef),
        [pltpu.SemaphoreType.DMA((FIELDS + 2 * HELD,))],
        specs=[HBM] * 3,
    )
    halo = swap_edges(edges, "row")
    kept = halos * PASSES * 2
    near, far = ([planes(len(rows) * POINTS)] if halos == 1 else [] for rows in composed_rows(own))
    prepared = call(
        functools.partial(prepare_body, halos),
        [planes(own)] * 3 + [planes(own + 1), planes(own), planes(kept), planes(own)] + near,
        resident(control_near, east_near, south_near),
        [planes(own)] * 2,
    )
    own_stencil, (done_rows, saved, control_planes), composed = prepared[:4], prepared[4:7], prepared[7:]
    columns_planes = planes(part * chunks + 2 * packed + (part if crossed else 0))
    (columns,) = call(
        columns_body, [columns_planes], [members, innovation, huber_class], [planes(part * chunks)]
    )
    matrix, transposed = call(
        matrix_body, [planes(terms)] * 2, [band, level_group_index], specs=[SMEM, SMEM]
    )
    tail_planes = [planes(tail)] * 4
    first_outs = far or tail_planes
    operands = [done_rows, saved, *own_stencil, *halo, *composed]
    passed, sent = ([columns], chunks - 1) if crossed else ([], chunks)
    results = call(
        functools.partial(forward_body, halos),
        first_outs + [planes(part)] * sent + [columns_planes] * len(passed),
        resident(*operands, *passed),
        [planes(own)] + (tail_planes if halos == 1 else []),
        aliases={len(operands): len(first_outs) + sent} if crossed else None,
    )
    if crossed:
        *results, columns = results
        columns = lax.ppermute(columns, "row", [(0, 1), (1, 0)])
    last_coefs = [*composed, *results[:1]] if halos == 1 else [*own_stencil, *results[:4]]
    smoothed = results[len(first_outs) :]
    kept_back = [None] * (chunks - sent)
    received = exchange([*kept_back, *smoothed[::-1]], "lev", crossed)[chunks - sent :]
    (partial,) = call(
        functools.partial(filter_body, chunks),
        [planes(packed)],
        resident(*received[::-1], columns, matrix),
        [planes(part * chunks)],
    )
    partials = collect(partial, "mem")
    lifted = call(
        functools.partial(lift_body, chunks, parts),
        [planes(part)] * chunks,
        resident(*partials, columns, transposed),
        [planes(packed), planes(part * chunks)],
    )
    returned = exchange(lifted[::-1], "lev", crossed)
    gathered, *edges = call(
        functools.partial(gather_body, halos, chunks),
        [planes(own)] + [planes(PASSES)] * halos,
        resident(*returned[::-1]),
        [planes(own)],
    )
    halo = swap_edges(edges, "row")
    early, saved = call(
        functools.partial(interior_body, halos),
        [pltpu.VMEM(control.shape, jnp.float32), planes(kept)],
        resident(gathered, control_planes, *own_stencil),
        [planes(own)],
    )
    (gradient,) = call(
        functools.partial(backward_body, halos),
        [jax.ShapeDtypeStruct(control.shape, jnp.float32)],
        resident(control_planes, early, saved, *halo, *last_coefs),
        [planes(PASSES)] * halos
        + [pltpu.VMEM((count, held, PASSES, lon), jnp.float32)] * halos
        + [pltpu.SemaphoreType.DMA((1 + halos,))],
        out_specs=[HBM],
    )
    return gradient


def solution(mesh):
    placed = (
        P("mem", "lev", "row", None),
        P("mem", None, ("row", "lev")),
        P("lev", "row", None),
        P("lev", "row", None),
        P(None, ("row", "lev")),
        P(None, ("row", "lev")),
        P(),
        P(),
    )
    return jax.shard_map(
        per_device,
        mesh=mesh,
        in_specs=placed,
        out_specs=P("mem", "lev", "row", None),
        check_vma=False,
    )
```

```python
import functools

import jax
import jax.numpy as jnp
from jax import lax
from jax.experimental import pallas as pl
from jax.experimental.pallas import tpu as pltpu
from jax.sharding import PartitionSpec as P

PASSES = 8
HUBER = 1.0
REACH = 3
POINTS = 13
LANES = 128
TILE = 8
HALVES = 2
HELD = 2
FIELDS = 4

VMEM = pl.BlockSpec(memory_space=pltpu.VMEM)
SMEM = pl.BlockSpec(memory_space=pltpu.SMEM)
HBM = pl.BlockSpec(memory_space=pltpu.HBM)


def planes(count):
    return pltpu.VMEM((count * TILE, LANES), jnp.float32)


def call(body, outs, operands, scratch=(), specs=None, out_specs=None, flops=0, aliases=None):
    total = sum(op.size * op.dtype.itemsize for op in operands)
    return pl.pallas_call(
        body,
        out_shape=outs,
        in_specs=specs or [VMEM] * len(operands),
        out_specs=out_specs or [VMEM] * len(outs),
        scratch_shapes=list(scratch),
        input_output_aliases=aliases or {},
        compiler_params=pltpu.CompilerParams(vmem_limit_bytes=32 * 1024 * 1024),
        cost_estimate=pl.CostEstimate(flops=flops, bytes_accessed=2 * total, transcendentals=0),
    )(*operands)


def resident(*arrays):
    return [pltpu.with_memory_space_constraint(array, pltpu.VMEM) for array in arrays]


def remote(*arrays):
    return [pltpu.with_memory_space_constraint(array, pltpu.HBM) for array in arrays]


def exchange(chunks, axis, crossed):
    count = len(chunks)
    received = list(chunks)
    for step in reversed(range(count)):
        if chunks[step] is None:
            continue
        if crossed:
            pairs = [(2 * i + row, 2 * (i ^ step) + 1 - row) for i in range(count) for row in range(2)]
            received[step] = lax.ppermute(chunks[step], (axis, "row"), pairs)
        elif step:
            received[step] = lax.ppermute(chunks[step], axis, [(i, i ^ step) for i in range(count)])
    return received


def collect(array, axis):
    count, rows = lax.axis_size(axis), lax.axis_size("row")
    partners = [count - 1, *range(1, count - 1)]
    received = [array]
    for step in range(1, count):
        pairs = []
        for index in range(count):
            for row in range(rows):
                target = index ^ partners[step - 1] if row % 2 else (index + step) % count
                pairs.append((index * rows + row, target * rows + row))
        received.append(lax.ppermute(array, (axis, "row"), pairs))
    return received


def swap_edges(edges, axis):
    count = lax.axis_size(axis)
    if len(edges) == 1:
        return [lax.ppermute(edges[0], axis, [(0, 1), (1, 0)])]
    head, tail = edges
    south = lax.ppermute(head, axis, [(i + 1, i) for i in range(count - 1)])
    north = lax.ppermute(tail, axis, [(i, i + 1) for i in range(count - 1)])
    return [south, north]


def tile(ref, row):
    return ref[row * TILE : (row + 1) * TILE, :]


def set_tile(ref, row, value):
    ref[row * TILE : (row + 1) * TILE, :] = value


def block(first_row, rows):
    return pl.ds(pl.multiple_of(first_row * TILE, TILE), rows * TILE)


def spread(ref, row, sublane, values):
    ref[pl.ds(row * TILE + sublane, values.shape[0], stride=TILE), :] = values


def places():
    return lax.broadcasted_iota(jnp.int32, (TILE, LANES), 0)


def east_west(value):
    lane = lax.broadcasted_iota(jnp.int32, (TILE, LANES), 1)
    other = pltpu.roll(value, FIELDS, 0)
    east = pltpu.roll(jnp.where(lane == 0, other, value), LANES - 1, 1)
    west = pltpu.roll(jnp.where(lane == LANES - 1, other, value), 1, 1)
    return east, west


def west_of(value):
    lane = lax.broadcasted_iota(jnp.int32, (TILE, LANES), 1)
    return pltpu.roll(jnp.where(lane == LANES - 1, pltpu.roll(value, FIELDS, 0), value), 1, 1)


def halves():
    return [(half, slice(half * LANES, (half + 1) * LANES)) for half in range(HALVES)]


def pack_body(control_hbm, east_hbm, south_hbm, control_ref, east_ref, south_ref, *refs):
    send_refs, semaphores = refs[:-1], refs[-1]
    pieces = [(east_hbm.at[level], east_ref.at[level]) for level in range(HELD)]
    pieces += [(south_hbm.at[level], south_ref.at[level]) for level in range(HELD)]
    for field in range(FIELDS):
        member, level = divmod(field, HELD)
        pieces.append((control_hbm.at[member, level], control_ref.at[member, level]))
    copies = [
        pltpu.make_async_copy(source, target, semaphores.at[index]) for index, (source, target) in enumerate(pieces)
    ]
    for copy in copies:
        copy.start()
    for copy in copies:
        copy.wait()
    own = control_ref.shape[2]
    first = lax.axis_index("row") == 0

    def edges(load):
        head = load(slice(0, 2 * PASSES))[:PASSES].astype(jnp.float32)
        tail = load(slice(own - 2 * PASSES, own))[PASSES:].astype(jnp.float32)
        return [jnp.where(first, tail, head)] if len(send_refs) == 1 else [head, tail]

    for half, lanes in halves():
        for field in range(FIELDS):
            member, level = divmod(field, HELD)
            at = half * FIELDS + field
            values = edges(lambda rows: control_ref[member, level, rows, lanes])
            for send_ref, value in zip(send_refs, values):
                spread(send_ref, 0, at, value)
            for kind, coef_ref in enumerate((east_ref, south_ref)):
                values = edges(lambda rows: coef_ref[level, rows, lanes])
                for send_ref, value in zip(send_refs, values):
                    spread(send_ref, (kind + 1) * PASSES, at, value)


def is_mirrored(halos):
    return halos == 1 and lax.axis_index("row") == 1


def pick(mirrored, count, row):
    return row if mirrored is False else jnp.where(mirrored, count - 1 - row, row)


def stencil(values, row, center, east, west, above, below):
    to_east, to_west = east_west(values[row])
    total = center * values[row] + below * values[row + 1]
    if above is not None:
        total = total + above * values[row - 1]
    return total + (east * to_east + west * to_west)


def interior_passes(halos, field_ref, own_refs, saved_ref, double=False):
    center_ref, east_ref, west_ref, face_ref = own_refs
    own = field_ref.shape[0] // TILE
    values = {row: tile(field_ref, row) for row in range(own)}
    for step in range(1, PASSES + 1):
        for side in range(halos):
            kept = (own - 1 - step, own - step) if side == 0 else (step - 1, step)
            if double:
                kept = range(own - 3 - step, own + 1 - step) if step % 2 else ()
            for index, row in enumerate(kept):
                set_tile(saved_ref, (side * PASSES + step - 1) * 2 + index, values[row])
        after = {}
        for row in range(step if halos == 2 else 0, own - step):
            after[row] = stencil(
                values,
                row,
                tile(center_ref, row),
                tile(east_ref, row),
                tile(west_ref, row),
                tile(face_ref, row) if row else None,
                tile(face_ref, row + 1),
            )
        values = after
    return values


def wedge_passes(halos, halo_rows, own, saved_ref, coefficient, top):
    done = {}
    for side in range(halos):
        values = dict(halo_rows[side])
        for step in range(1, PASSES + 1):
            kept = (own - 1 - step, own - step) if side == 0 else (step - 1, step)
            for index, row in enumerate(kept):
                values[row] = tile(saved_ref, (side * PASSES + step - 1) * 2 + index)
            after = {}
            for row in range(own - step, own + PASSES - step) if side == 0 else range(step - PASSES, step):
                center, east, west, above = (coefficient(kind, row) for kind in range(4))
                after[row] = stencil(values, row, center, east, west, top if row == 0 else above, coefficient(3, row + 1))
            values = after
        done.update(values)
    return done


def shifted(value, distance):
    lane = lax.broadcasted_iota(jnp.int32, (TILE, LANES), 1)
    other = pltpu.roll(value, FIELDS, 0)
    east = pltpu.roll(jnp.where(lane < distance, other, value), LANES - distance, 1)
    west = pltpu.roll(jnp.where(lane >= LANES - distance, other, value), distance, 1)
    return east, west


def compose(coefficient, rows, composed_out):
    for index, row in enumerate(rows):
        center, east, west, above = (coefficient(kind, row) for kind in range(4))
        below = coefficient(3, row + 1)
        (center_e, center_w), (east_e, east_w), (west_e, west_w), (below_e, below_w), (above_e, above_w) = (
            shifted(value, 1) for value in (center, east, west, below, above)
        )
        tiles = (
            center * center + east * west_e + west * east_w + below * below + above * above,
            east * (center + center_e),
            west * (center + center_w),
            east * east_e,
            west * west_w,
            below * (center + coefficient(0, row + 1)),
            east * below_e + below * coefficient(1, row + 1),
            west * below_w + below * coefficient(2, row + 1),
            above * (center + coefficient(0, row - 1)),
            east * above_e + above * coefficient(1, row - 1),
            west * above_w + above * coefficient(2, row - 1),
            below * coefficient(3, row + 2),
            above * coefficient(3, row - 1),
        )
        for place, value in enumerate(tiles):
            set_tile(composed_out, index * POINTS + place, value)


def composed_rows(own):
    return range(own - PASSES, own - 2), range(own - 2, own + PASSES - 2)


def double_wedge(values, own, saved_ref, composed_refs):
    for step in range(1, PASSES // 2 + 1):
        first = own - 2 * step
        for index in range(4):
            values[first - 2 + index] = tile(saved_ref, (step - 1) * 4 + index)
        near = {row: shifted(values[row], 1) for row in range(first - 1, first + PASSES + 1)}
        after = {}
        for row in range(first, first + PASSES):
            def coefficient(place):
                part = int(row >= own - 2)
                return tile(composed_refs[part], (row - composed_rows(own)[part][0]) * POINTS + place)

            east, west = shifted(values[row], 2)
            total = coefficient(0) * values[row] + coefficient(5) * values[row + 1]
            total = total + (coefficient(8) * values[row - 1] + coefficient(11) * values[row + 2])
            total = total + coefficient(12) * values[row - 2]
            sides = coefficient(1) * near[row][0] + coefficient(2) * near[row][1]
            lower = coefficient(6) * near[row + 1][0] + coefficient(7) * near[row + 1][1]
            upper = coefficient(9) * near[row - 1][0] + coefficient(10) * near[row - 1][1]
            far = coefficient(3) * east + coefficient(4) * west
            after[row] = (total + sides) + ((lower + upper) + far)
        values = after
    return values


def prepare_body(halos, control_ref, east_ref, south_ref, *refs):
    own_refs, (rows_out, saved_out, field_ref), refs = refs[:4], refs[4:7], refs[7:]
    raw_east, raw_face = refs[-2:]
    center_out, east_out, west_out, face_out = own_refs
    own = control_ref.shape[2]
    mirrored = is_mirrored(halos)
    for half, lanes in halves():
        for field in range(FIELDS):
            member, level = divmod(field, HELD)
            at = half * FIELDS + field
            spread(rows_out, 0, at, control_ref[member, level, :, lanes].astype(jnp.float32))
            spread(raw_east, 0, at, east_ref[level, :, lanes])
            spread(raw_face, 0, at, south_ref[level, :, lanes])
    for row in range(own):
        source = pick(mirrored, own, row)
        set_tile(field_ref, row, rows_out[block(source, 1), :])
        east = raw_east[block(source, 1), :]
        set_tile(east_out, row, east)
        set_tile(west_out, row, west_of(east))
        if row == 0:
            face = tile(raw_face, 0)
            face = face if mirrored is False else jnp.where(mirrored, 0.0, face)
        else:
            face = raw_face[block(row if mirrored is False else jnp.where(mirrored, own - row, row), 1), :]
        set_tile(face_out, row, face)
    set_tile(face_out, own, tile(raw_face, 0))
    for row in range(own - 1):
        total = 1.0 - tile(east_out, row) - tile(west_out, row)
        set_tile(center_out, row, total - tile(face_out, row + 1) - tile(face_out, row))
    for row, value in interior_passes(halos, field_ref, own_refs, saved_out, halos == 1).items():
        set_tile(rows_out, row, value)
    if halos == 1:
        compose(lambda kind, row: tile(own_refs[kind], row), composed_rows(own)[0], refs[0])


def finish_coefficients(halos, halo_refs, own_refs, tail_refs, own):
    _, east_own, west_own, face_own = own_refs
    center_tail, east_tail, west_tail, face_tail = tail_refs
    mirrored = is_mirrored(halos)

    def halo_tile(side, kind, row):
        return halo_refs[side][block(kind * PASSES + row, 1), :]

    set_tile(east_tail, 0, tile(east_own, own - 1))
    set_tile(west_tail, 0, tile(west_own, own - 1))
    set_tile(face_tail, 0, tile(face_own, own - 1))
    for row in range(PASSES):
        east = halo_tile(0, 1, pick(mirrored, PASSES, row))
        set_tile(east_tail, 1 + row, east)
        set_tile(west_tail, 1 + row, west_of(east))
        if mirrored is False:
            face = halo_tile(0, 2, row)
        elif row == 0:
            face = jnp.where(mirrored, tile(face_own, own), halo_tile(0, 2, 0))
        else:
            face = halo_tile(0, 2, jnp.where(mirrored, PASSES - row, row))
        set_tile(face_tail, 1 + row, face)
    for row in range(PASSES):
        total = 1.0 - tile(east_tail, row) - tile(west_tail, row)
        set_tile(center_tail, row, total - tile(face_tail, row + 1) - tile(face_tail, row))
    if halos == 2:
        for row in range(PASSES):
            at = 1 + PASSES + row
            east, face = halo_tile(1, 1, row), halo_tile(1, 2, row)
            below = halo_tile(1, 2, row + 1) if row + 1 < PASSES else tile(face_own, 0)
            west = west_of(east)
            for ref, value in zip(tail_refs, (1.0 - east - west - below - face, east, west, face)):
                set_tile(ref, at, value)


def coefficient_reader(own_refs, tail_refs, own):
    def coefficient(kind, row):
        if row < 0:
            return tile(tail_refs[kind], 1 + 2 * PASSES + row)
        return tile(own_refs[kind], row) if row < own - 1 else tile(tail_refs[kind], row - own + 1)

    return coefficient


def top_coefficient(halos, own_refs):
    return None if halos == 1 else jnp.where(lax.axis_index("row") == 0, 0.0, tile(own_refs[3], 0))


def forward_body(halos, rows_ref, saved_ref, *refs):
    own_refs, halo_refs, refs = refs[:4], refs[4 : 4 + halos], refs[4 + halos :]
    if halos == 1:
        composed_own, _, composed_tail, *refs = refs
        chunk_refs, columns_ref, sorted_ref, tail_refs = refs[:-6], refs[-6], refs[-5], refs[-4:]
        size = chunk_refs[0].shape[0]
        chunk_refs = [*chunk_refs, columns_ref.at[pl.ds(columns_ref.shape[0] - size, size), :]]
    else:
        tail_refs, chunk_refs, sorted_ref = refs[:4], refs[4:-1], refs[-1]
    own = rows_ref.shape[0] // TILE
    lev_at = lax.axis_index("lev")
    mirrored = is_mirrored(halos)
    finish_coefficients(halos, halo_refs, own_refs, tail_refs, own)
    halo_rows = [{own + row: halo_refs[0][block(pick(mirrored, PASSES, row), 1), :] for row in range(PASSES)}]
    coefficient = coefficient_reader(own_refs, tail_refs, own)
    if halos == 1:
        compose(coefficient, composed_rows(own)[1], composed_tail)
        done = double_wedge(halo_rows[0], own, saved_ref, (composed_own, composed_tail))
    else:
        halo_rows.append({row - PASSES: tile(halo_refs[1], row) for row in range(PASSES)})
        top = top_coefficient(halos, own_refs)
        done = wedge_passes(halos, halo_rows, own, saved_ref, coefficient, top)
    for row in range(own):
        value = done[row] if row in done else tile(rows_ref, row)
        sorted_ref[block(pick(mirrored, own, row), 1), :] = value
    part = own // len(chunk_refs)
    for step, chunk_ref in enumerate(reversed(chunk_refs)):
        chunk_ref[...] = sorted_ref[block(lax.bitwise_xor(lev_at, step) * part, part), :]


def matrix_terms(groups):
    return [
        (group, other, cross)
        for group in range(groups)
        for other in range(max(0, group - 2), min(groups, group + 3))
        for cross in range(2)
        if abs(group - other) < 2 or cross
    ]


def swap_levels(value, sublane):
    return jnp.where(sublane % HELD == 0, pltpu.roll(value, TILE - 1, 0), pltpu.roll(value, 1, 0))


def columns_body(members_ref, innovation_ref, huber_ref, columns_out, levels_ref):
    count, levels, cells = members_ref.shape
    groups, lon = levels // HELD, HALVES * LANES
    rows, packed = cells // lon, levels // FIELDS
    for member in range(count):
        for row in range(rows):
            for half in range(HALVES):
                lanes = slice(row * lon + half * LANES, row * lon + (half + 1) * LANES)
                start = ((member * rows + row) * HALVES + half) * levels
                levels_ref[start : start + levels, :] = members_ref[member, :, lanes].astype(jnp.float32)
                for level in range(HELD):
                    at = half * FIELDS + member * HELD + level
                    spread(columns_out, row * groups, at, levels_ref[pl.ds(start + level, groups, stride=HELD), :])
    for row in range(rows):
        for half in range(HALVES):
            lanes = slice(row * lon + half * LANES, row * lon + (half + 1) * LANES)
            for pack in range(packed):
                source = slice(pack * FIELDS, (pack + 1) * FIELDS)
                start = (rows * groups + row * packed + pack) * TILE + half * FIELDS
                columns_out[start : start + FIELDS, :] = innovation_ref[source, lanes]
                start = start + rows * packed * TILE
                columns_out[start : start + FIELDS, :] = huber_ref[source, lanes].astype(jnp.float32)


def matrix_body(band_ref, group_ref, matrix_out, transposed_out):
    levels = band_ref.shape[1]
    groups = levels // HELD
    sublane = places()

    def entry(level, other):
        offset = other - level + REACH
        if not 0 <= offset < 2 * REACH + 1:
            return jnp.float32(0.0)
        value = band_ref[offset, level] + jnp.float32(1.0 if offset == REACH else 0.0)
        return jnp.where(group_ref[level] == group_ref[other], value, jnp.float32(0.0))

    for slot, (group, other, cross) in enumerate(matrix_terms(groups)):
        pairs = [(group * HELD + level, other * HELD + (level ^ cross)) for level in range(HELD)]
        even, odd = (entry(a, b) for a, b in pairs)
        set_tile(matrix_out, slot, jnp.where(sublane % HELD == 0, even, odd))
        even, odd = (entry(b, a) for a, b in pairs)
        set_tile(transposed_out, slot, jnp.where(sublane % HELD == 0, even, odd))


def apply_matrix(matrix_ref, values, sublane):
    crossed = [swap_levels(value, sublane) for value in values]
    totals = [None] * len(values)
    for slot, (group, other, cross) in enumerate(matrix_terms(len(values))):
        term = tile(matrix_ref, slot) * (crossed if cross else values)[other]
        totals[group] = term if totals[group] is None else totals[group] + term
    return totals


def filter_body(chunks, *refs):
    *chunk_refs, members_ref, matrix_ref, partial_ref, columns = refs
    size = chunk_refs[0].shape[0]
    if len(chunk_refs) < chunks:
        chunk_refs.append(members_ref.at[pl.ds(members_ref.shape[0] - size, size), :])
    rows = size // TILE
    lev_at = lax.axis_index("lev")
    sublane = places()
    first_member = sublane % FIELDS < HELD
    for step, chunk_ref in enumerate(reversed(chunk_refs)):
        columns[block(lax.bitwise_xor(lev_at, step) * rows, rows), :] = chunk_ref[...]
    for row in range(rows):
        filtered = apply_matrix(matrix_ref, [tile(columns, group * rows + row) for group in range(chunks)], sublane)
        terms = [tile(members_ref, row * chunks + group) * value for group, value in enumerate(filtered)]
        for pack in range(chunks // 2):
            lower, upper = terms[2 * pack], terms[2 * pack + 1]
            total = jnp.where(first_member, lower, upper)
            total = total + jnp.where(first_member, pltpu.roll(lower, TILE - HELD, 0), pltpu.roll(upper, HELD, 0))
            set_tile(partial_ref, row * (chunks // 2) + pack, total)


def lift_body(chunks, parts, *refs):
    part_refs, refs = refs[:parts], refs[parts:]
    columns_ref, transposed_ref, refs = refs[0], refs[1], refs[2:]
    chunk_refs, (weighted_ref, sorted_ref) = refs[:chunks], refs[chunks:]
    rows = chunk_refs[0].shape[0] // TILE
    lev_at = lax.axis_index("lev")
    sublane = places()
    first_member = sublane % FIELDS < HELD
    increment = part_refs[0][...]
    for part_ref in part_refs[1:]:
        increment = increment + part_ref[...]
    start, size = rows * chunks * TILE, weighted_ref.shape[0]
    residual = increment - columns_ref[start : start + size, :]
    scale = HUBER / jnp.maximum(jnp.abs(residual), HUBER)
    weighted_ref[...] = jnp.where(columns_ref[start + size : start + 2 * size, :] == 1.0, scale, 1.0) * residual
    for row in range(rows):
        adjoint = []
        for pack in range(chunks // 2):
            weighted = tile(weighted_ref, row * (chunks // 2) + pack)
            lower = jnp.where(first_member, weighted, pltpu.roll(weighted, HELD, 0))
            upper = jnp.where(first_member, pltpu.roll(weighted, TILE - HELD, 0), weighted)
            for value in (lower, upper):
                adjoint.append(value * tile(columns_ref, row * chunks + len(adjoint)))
        for group, value in enumerate(apply_matrix(transposed_ref, adjoint, sublane)):
            set_tile(sorted_ref, group * rows + row, value)
    for step, chunk_ref in enumerate(reversed(chunk_refs)):
        chunk_ref[...] = sorted_ref[block(lax.bitwise_xor(lev_at, step) * rows, rows), :]


def gather_body(halos, chunks, *refs):
    chunk_refs, field_ref, send_refs, sorted_ref = refs[:chunks], refs[chunks], refs[chunks + 1 : -1], refs[-1]
    lev_at = lax.axis_index("lev")
    mirrored = is_mirrored(halos)
    rows = chunk_refs[0].shape[0] // TILE
    own = rows * chunks
    for step, chunk_ref in enumerate(reversed(chunk_refs)):
        sorted_ref[block(lax.bitwise_xor(lev_at, step) * rows, rows), :] = chunk_ref[...]
    for row in range(own):
        set_tile(field_ref, row, sorted_ref[block(pick(mirrored, own, row), 1), :])
    for row in range(PASSES):
        if halos == 1:
            set_tile(send_refs[0], row, tile(field_ref, own - 1 - row))
        else:
            set_tile(send_refs[0], row, tile(field_ref, row))
            set_tile(send_refs[1], row, tile(field_ref, own - PASSES + row))


def to_fields(planes_ref, fields_ref, rows):
    for field in range(FIELDS):
        member, level = divmod(field, HELD)
        for half, lanes in halves():
            fields_ref[member, level, :, lanes] = planes_ref[pl.ds(half * FIELDS + field, rows, stride=TILE), :]


def interior_body(halos, field_ref, control_ref, *refs):
    own_refs, (fields_out, saved_out, result_ref) = refs[:4], refs[4:]
    own = field_ref.shape[0] // TILE
    mirrored = is_mirrored(halos)
    done = interior_passes(halos, field_ref, own_refs, saved_out, halos == 1)
    for row in range(own):
        value = done[row] + tile(control_ref, row) if row in done else jnp.zeros((TILE, LANES), jnp.float32)
        result_ref[block(pick(mirrored, own, row), 1), :] = value
    to_fields(result_ref, fields_out, own)


def backward_body(halos, control_ref, fields_ref, saved_ref, *refs):
    halo_refs, refs = refs[:halos], refs[halos:]
    coefficient_refs, refs = (refs[:2], refs[2:]) if halos == 1 else (refs[:8], refs[8:])
    gradient_hbm, refs = refs[0], refs[1:]
    result_refs, edge_refs, semaphores = refs[:halos], refs[halos : 2 * halos], refs[-1]
    own = fields_ref.shape[2]
    mirrored = is_mirrored(halos)
    if halos == 1:
        spans = [(PASSES * mirrored.astype(jnp.int32), own - PASSES)]
        spans.append((jnp.where(mirrored, 0, own - PASSES), PASSES))
    else:
        spans = [(PASSES, own - 2 * PASSES), (own - PASSES, PASSES), (0, PASSES)]
    copies = []

    def send(source_ref, source_start, start, rows):
        copy = pltpu.make_async_copy(
            source_ref.at[:, :, pl.ds(source_start, rows), :],
            gradient_hbm.at[:, :, pl.ds(start, rows), :],
            semaphores.at[len(copies)],
        )
        copy.start()
        copies.append(copy)

    start = pl.multiple_of(spans[0][0], TILE)
    send(fields_ref, start, start, spans[0][1])
    halo_rows = [{own + row: tile(halo_refs[0], row) for row in range(PASSES)}]
    if halos == 1:
        done = double_wedge(halo_rows[0], own, saved_ref, coefficient_refs)
    else:
        halo_rows.append({row - PASSES: tile(halo_refs[1], row) for row in range(PASSES)})
        own_refs, tail_refs = coefficient_refs[:4], coefficient_refs[4:]
        coefficient = coefficient_reader(own_refs, tail_refs, own)
        top = top_coefficient(halos, own_refs)
        done = wedge_passes(halos, halo_rows, own, saved_ref, coefficient, top)
    for side in range(halos):
        for row in range(PASSES):
            value = done[own - PASSES + row] + tile(control_ref, own - PASSES + row) if side == 0 else done[row] + tile(control_ref, row)
            result_refs[side][block(pick(mirrored, PASSES, row), 1), :] = value
        to_fields(result_refs[side], edge_refs[side], PASSES)
        send(edge_refs[side], 0, pl.multiple_of(spans[1 + side][0], TILE), PASSES)
    for copy in copies:
        copy.wait()


def per_device(control, members, east_coef, south_coef, innovation, huber_class, band, level_group_index):
    count, held, own, lon = control.shape
    levels, cells = members.shape[1:]
    chunks, parts, row_count = (lax.axis_size(axis) for axis in ("lev", "mem", "row"))
    assert (count * held, held, lon) == (FIELDS, HELD, HALVES * LANES)
    part = own // chunks
    halos = 1 if row_count == 2 else 2
    tail = 1 + halos * PASSES
    terms = len(matrix_terms(chunks))
    packed = part * levels // FIELDS
    crossed = row_count == 2

    control_near, east_near, south_near, *edges = call(
        pack_body,
        [pltpu.VMEM(x.shape, x.dtype) for x in (control, east_coef, south_coef)] + [planes(3 * PASSES)] * halos,
        remote(control, east_coef, south_coef),
        [pltpu.SemaphoreType.DMA((FIELDS + 2 * HELD,))],
        specs=[HBM] * 3,
    )
    halo = swap_edges(edges, "row")
    kept = halos * PASSES * 2
    near, far = ([planes(len(rows) * POINTS)] if halos == 1 else [] for rows in composed_rows(own))
    prepared = call(
        functools.partial(prepare_body, halos),
        [planes(own)] * 3 + [planes(own + 1), planes(own), planes(kept), planes(own)] + near,
        resident(control_near, east_near, south_near),
        [planes(own)] * 2,
    )
    own_stencil, (done_rows, saved, control_planes), composed = prepared[:4], prepared[4:7], prepared[7:]
    columns_planes = planes(part * chunks + 2 * packed + (part if crossed else 0))
    (columns,) = call(
        columns_body, [columns_planes], [members, innovation, huber_class], [planes(part * chunks)]
    )
    matrix, transposed = call(
        matrix_body, [planes(terms)] * 2, [band, level_group_index], specs=[SMEM, SMEM]
    )
    tail_planes = [planes(tail)] * 4
    first_outs = far or tail_planes
    operands = [done_rows, saved, *own_stencil, *halo, *composed]
    passed, sent = ([columns], chunks - 1) if crossed else ([], chunks)
    results = call(
        functools.partial(forward_body, halos),
        first_outs + [planes(part)] * sent + [columns_planes] * len(passed),
        resident(*operands, *passed),
        [planes(own)] + (tail_planes if halos == 1 else []),
        aliases={len(operands): len(first_outs) + sent} if crossed else None,
    )
    if crossed:
        *results, columns = results
        columns = lax.ppermute(columns, "row", [(0, 1), (1, 0)])
    last_coefs = [*composed, *results[:1]] if halos == 1 else [*own_stencil, *results[:4]]
    smoothed = results[len(first_outs) :]
    kept_back = [None] * (chunks - sent)
    received = exchange([*kept_back, *smoothed[::-1]], "lev", crossed)[chunks - sent :]
    (partial,) = call(
        functools.partial(filter_body, chunks),
        [planes(packed)],
        resident(*received[::-1], columns, matrix),
        [planes(part * chunks)],
    )
    partials = collect(partial, "mem")
    lifted = call(
        functools.partial(lift_body, chunks, parts),
        [planes(part)] * chunks,
        resident(*partials, columns, transposed),
        [planes(packed), planes(part * chunks)],
    )
    returned = exchange(lifted[::-1], "lev", crossed)
    gathered, *edges = call(
        functools.partial(gather_body, halos, chunks),
        [planes(own)] + [planes(PASSES)] * halos,
        resident(*returned[::-1]),
        [planes(own)],
    )
    halo = swap_edges(edges, "row")
    early, saved = call(
        functools.partial(interior_body, halos),
        [pltpu.VMEM(control.shape, jnp.float32), planes(kept)],
        resident(gathered, control_planes, *own_stencil),
        [planes(own)],
    )
    (gradient,) = call(
        functools.partial(backward_body, halos),
        [jax.ShapeDtypeStruct(control.shape, jnp.float32)],
        resident(control_planes, early, saved, *halo, *last_coefs),
        [planes(PASSES)] * halos
        + [pltpu.VMEM((count, held, PASSES, lon), jnp.float32)] * halos
        + [pltpu.SemaphoreType.DMA((1 + halos,))],
        out_specs=[HBM],
    )
    return gradient


def solution(mesh):
    placed = (
        P("mem", "lev", "row", None),
        P("mem", None, ("row", "lev")),
        P("lev", "row", None),
        P("lev", "row", None),
        P(None, ("row", "lev")),
        P(None, ("row", "lev")),
        P(),
        P(),
    )
    return jax.shard_map(
        per_device,
        mesh=mesh,
        in_specs=placed,
        out_specs=P("mem", "lev", "row", None),
        check_vma=False,
    )
```

```python
import functools

import jax
import jax.numpy as jnp
from jax import lax
from jax.experimental import pallas as pl
from jax.experimental.pallas import tpu as pltpu
from jax.sharding import PartitionSpec as P

PASSES = 8
HUBER = 1.0
REACH = 3
POINTS = 13
LANES = 128
TILE = 8
HALVES = 2
HELD = 2
FIELDS = 4

VMEM = pl.BlockSpec(memory_space=pltpu.VMEM)
SMEM = pl.BlockSpec(memory_space=pltpu.SMEM)
HBM = pl.BlockSpec(memory_space=pltpu.HBM)


def planes(count):
    return pltpu.VMEM((count * TILE, LANES), jnp.float32)


def call(body, outs, operands, scratch=(), specs=None, out_specs=None, flops=0, aliases=None):
    total = sum(op.size * op.dtype.itemsize for op in operands)
    return pl.pallas_call(
        body,
        out_shape=outs,
        in_specs=specs or [VMEM] * len(operands),
        out_specs=out_specs or [VMEM] * len(outs),
        scratch_shapes=list(scratch),
        input_output_aliases=aliases or {},
        compiler_params=pltpu.CompilerParams(vmem_limit_bytes=32 * 1024 * 1024),
        cost_estimate=pl.CostEstimate(flops=flops, bytes_accessed=2 * total, transcendentals=0),
    )(*operands)


def resident(*arrays):
    return [pltpu.with_memory_space_constraint(array, pltpu.VMEM) for array in arrays]


def remote(*arrays):
    return [pltpu.with_memory_space_constraint(array, pltpu.HBM) for array in arrays]


def exchange(chunks, axis, crossed):
    count = len(chunks)
    received = list(chunks)
    for step in reversed(range(count)):
        if chunks[step] is None:
            continue
        if crossed:
            pairs = [(2 * i + row, 2 * (i ^ step) + 1 - row) for i in range(count) for row in range(2)]
            received[step] = lax.ppermute(chunks[step], (axis, "row"), pairs)
        elif step:
            received[step] = lax.ppermute(chunks[step], axis, [(i, i ^ step) for i in range(count)])
    return received


def collect(array, axis):
    count, rows = lax.axis_size(axis), lax.axis_size("row")
    partners = [count - 1, *range(1, count - 1)]
    ring = [i ^ (i >> 1) for i in range(count)]
    received = [array]
    for step in range(1, count):
        pairs = []
        for place, index in enumerate(ring):
            for row in range(rows):
                target = ring[(place + step) % count] if row % 2 else index ^ partners[step - 1]
                pairs.append((index * rows + row, target * rows + row))
        received.append(lax.ppermute(array, (axis, "row"), pairs))
    return received


def swap_edges(edges, axis):
    count = lax.axis_size(axis)
    if len(edges) == 1:
        return [lax.ppermute(edges[0], axis, [(0, 1), (1, 0)])]
    head, tail = edges
    south = lax.ppermute(head, axis, [(i + 1, i) for i in range(count - 1)])
    north = lax.ppermute(tail, axis, [(i, i + 1) for i in range(count - 1)])
    return [south, north]


def tile(ref, row):
    return ref[row * TILE : (row + 1) * TILE, :]


def set_tile(ref, row, value):
    ref[row * TILE : (row + 1) * TILE, :] = value


def block(first_row, rows):
    return pl.ds(pl.multiple_of(first_row * TILE, TILE), rows * TILE)


def spread(ref, row, sublane, values):
    ref[pl.ds(row * TILE + sublane, values.shape[0], stride=TILE), :] = values


def places():
    return lax.broadcasted_iota(jnp.int32, (TILE, LANES), 0)


def east_west(value):
    lane = lax.broadcasted_iota(jnp.int32, (TILE, LANES), 1)
    other = pltpu.roll(value, FIELDS, 0)
    east = pltpu.roll(jnp.where(lane == 0, other, value), LANES - 1, 1)
    west = pltpu.roll(jnp.where(lane == LANES - 1, other, value), 1, 1)
    return east, west


def west_of(value):
    lane = lax.broadcasted_iota(jnp.int32, (TILE, LANES), 1)
    return pltpu.roll(jnp.where(lane == LANES - 1, pltpu.roll(value, FIELDS, 0), value), 1, 1)


def halves():
    return [(half, slice(half * LANES, (half + 1) * LANES)) for half in range(HALVES)]


def pack_body(control_hbm, east_hbm, south_hbm, control_ref, east_ref, south_ref, *refs):
    send_refs, semaphores = refs[:-1], refs[-1]
    pieces = [(east_hbm.at[level], east_ref.at[level]) for level in range(HELD)]
    pieces += [(south_hbm.at[level], south_ref.at[level]) for level in range(HELD)]
    for field in range(FIELDS):
        member, level = divmod(field, HELD)
        pieces.append((control_hbm.at[member, level], control_ref.at[member, level]))
    copies = [
        pltpu.make_async_copy(source, target, semaphores.at[index]) for index, (source, target) in enumerate(pieces)
    ]
    for copy in copies:
        copy.start()
    for copy in copies:
        copy.wait()
    own = control_ref.shape[2]
    first = lax.axis_index("row") == 0

    def edges(load):
        head = load(slice(0, 2 * PASSES))[:PASSES].astype(jnp.float32)
        tail = load(slice(own - 2 * PASSES, own))[PASSES:].astype(jnp.float32)
        return [jnp.where(first, tail, head)] if len(send_refs) == 1 else [head, tail]

    for half, lanes in halves():
        for field in range(FIELDS):
            member, level = divmod(field, HELD)
            at = half * FIELDS + field
            values = edges(lambda rows: control_ref[member, level, rows, lanes])
            for send_ref, value in zip(send_refs, values):
                spread(send_ref, 0, at, value)
            for kind, coef_ref in enumerate((east_ref, south_ref)):
                values = edges(lambda rows: coef_ref[level, rows, lanes])
                for send_ref, value in zip(send_refs, values):
                    spread(send_ref, (kind + 1) * PASSES, at, value)


def is_mirrored(halos):
    return halos == 1 and lax.axis_index("row") == 1


def pick(mirrored, count, row):
    return row if mirrored is False else jnp.where(mirrored, count - 1 - row, row)


def stencil(values, row, center, east, west, above, below):
    to_east, to_west = east_west(values[row])
    total = center * values[row] + below * values[row + 1]
    if above is not None:
        total = total + above * values[row - 1]
    return total + (east * to_east + west * to_west)


def interior_passes(halos, field_ref, own_refs, saved_ref, double=False):
    center_ref, east_ref, west_ref, face_ref = own_refs
    own = field_ref.shape[0] // TILE
    values = {row: tile(field_ref, row) for row in range(own)}
    for step in range(1, PASSES + 1):
        for side in range(halos):
            kept = (own - 1 - step, own - step) if side == 0 else (step - 1, step)
            if double:
                kept = range(own - 3 - step, own + 1 - step) if step % 2 else ()
            for index, row in enumerate(kept):
                set_tile(saved_ref, (side * PASSES + step - 1) * 2 + index, values[row])
        after = {}
        for row in range(step if halos == 2 else 0, own - step):
            after[row] = stencil(
                values,
                row,
                tile(center_ref, row),
                tile(east_ref, row),
                tile(west_ref, row),
                tile(face_ref, row) if row else None,
                tile(face_ref, row + 1),
            )
        values = after
    return values


def wedge_passes(halos, halo_rows, own, saved_ref, coefficient, top):
    done = {}
    for side in range(halos):
        values = dict(halo_rows[side])
        for step in range(1, PASSES + 1):
            kept = (own - 1 - step, own - step) if side == 0 else (step - 1, step)
            for index, row in enumerate(kept):
                values[row] = tile(saved_ref, (side * PASSES + step - 1) * 2 + index)
            after = {}
            for row in range(own - step, own + PASSES - step) if side == 0 else range(step - PASSES, step):
                center, east, west, above = (coefficient(kind, row) for kind in range(4))
                after[row] = stencil(values, row, center, east, west, top if row == 0 else above, coefficient(3, row + 1))
            values = after
        done.update(values)
    return done


def shifted(value, distance):
    lane = lax.broadcasted_iota(jnp.int32, (TILE, LANES), 1)
    other = pltpu.roll(value, FIELDS, 0)
    east = pltpu.roll(jnp.where(lane < distance, other, value), LANES - distance, 1)
    west = pltpu.roll(jnp.where(lane >= LANES - distance, other, value), distance, 1)
    return east, west


def compose(coefficient, rows, composed_out):
    for index, row in enumerate(rows):
        center, east, west, above = (coefficient(kind, row) for kind in range(4))
        below = coefficient(3, row + 1)
        (center_e, center_w), (east_e, east_w), (west_e, west_w), (below_e, below_w), (above_e, above_w) = (
            shifted(value, 1) for value in (center, east, west, below, above)
        )
        tiles = (
            center * center + east * west_e + west * east_w + below * below + above * above,
            east * (center + center_e),
            west * (center + center_w),
            east * east_e,
            west * west_w,
            below * (center + coefficient(0, row + 1)),
            east * below_e + below * coefficient(1, row + 1),
            west * below_w + below * coefficient(2, row + 1),
            above * (center + coefficient(0, row - 1)),
            east * above_e + above * coefficient(1, row - 1),
            west * above_w + above * coefficient(2, row - 1),
            below * coefficient(3, row + 2),
            above * coefficient(3, row - 1),
        )
        for place, value in enumerate(tiles):
            set_tile(composed_out, index * POINTS + place, value)


def composed_rows(own):
    return range(own - PASSES, own - 2), range(own - 2, own + PASSES - 2)


def double_wedge(values, own, saved_ref, composed_refs):
    for step in range(1, PASSES // 2 + 1):
        first = own - 2 * step
        for index in range(4):
            values[first - 2 + index] = tile(saved_ref, (step - 1) * 4 + index)
        near = {row: shifted(values[row], 1) for row in range(first - 1, first + PASSES + 1)}
        after = {}
        for row in range(first, first + PASSES):
            def coefficient(place):
                part = int(row >= own - 2)
                return tile(composed_refs[part], (row - composed_rows(own)[part][0]) * POINTS + place)

            east, west = shifted(values[row], 2)
            total = coefficient(0) * values[row] + coefficient(5) * values[row + 1]
            total = total + (coefficient(8) * values[row - 1] + coefficient(11) * values[row + 2])
            total = total + coefficient(12) * values[row - 2]
            sides = coefficient(1) * near[row][0] + coefficient(2) * near[row][1]
            lower = coefficient(6) * near[row + 1][0] + coefficient(7) * near[row + 1][1]
            upper = coefficient(9) * near[row - 1][0] + coefficient(10) * near[row - 1][1]
            far = coefficient(3) * east + coefficient(4) * west
            after[row] = (total + sides) + ((lower + upper) + far)
        values = after
    return values


def prepare_body(halos, control_ref, east_ref, south_ref, *refs):
    own_refs, (rows_out, saved_out, field_ref), refs = refs[:4], refs[4:7], refs[7:]
    raw_east, raw_face = refs[-2:]
    center_out, east_out, west_out, face_out = own_refs
    own = control_ref.shape[2]
    mirrored = is_mirrored(halos)
    for half, lanes in halves():
        for field in range(FIELDS):
            member, level = divmod(field, HELD)
            at = half * FIELDS + field
            spread(rows_out, 0, at, control_ref[member, level, :, lanes].astype(jnp.float32))
            spread(raw_east, 0, at, east_ref[level, :, lanes])
            spread(raw_face, 0, at, south_ref[level, :, lanes])
    for row in range(own):
        source = pick(mirrored, own, row)
        set_tile(field_ref, row, rows_out[block(source, 1), :])
        east = raw_east[block(source, 1), :]
        set_tile(east_out, row, east)
        set_tile(west_out, row, west_of(east))
        if row == 0:
            face = tile(raw_face, 0)
            face = face if mirrored is False else jnp.where(mirrored, 0.0, face)
        else:
            face = raw_face[block(row if mirrored is False else jnp.where(mirrored, own - row, row), 1), :]
        set_tile(face_out, row, face)
    set_tile(face_out, own, tile(raw_face, 0))
    for row in range(own - 1):
        total = 1.0 - tile(east_out, row) - tile(west_out, row)
        set_tile(center_out, row, total - tile(face_out, row + 1) - tile(face_out, row))
    for row, value in interior_passes(halos, field_ref, own_refs, saved_out, halos == 1).items():
        set_tile(rows_out, row, value)
    if halos == 1:
        compose(lambda kind, row: tile(own_refs[kind], row), composed_rows(own)[0], refs[0])


def finish_coefficients(halos, halo_refs, own_refs, tail_refs, own):
    _, east_own, west_own, face_own = own_refs
    center_tail, east_tail, west_tail, face_tail = tail_refs
    mirrored = is_mirrored(halos)

    def halo_tile(side, kind, row):
        return halo_refs[side][block(kind * PASSES + row, 1), :]

    set_tile(east_tail, 0, tile(east_own, own - 1))
    set_tile(west_tail, 0, tile(west_own, own - 1))
    set_tile(face_tail, 0, tile(face_own, own - 1))
    for row in range(PASSES):
        east = halo_tile(0, 1, pick(mirrored, PASSES, row))
        set_tile(east_tail, 1 + row, east)
        set_tile(west_tail, 1 + row, west_of(east))
        if mirrored is False:
            face = halo_tile(0, 2, row)
        elif row == 0:
            face = jnp.where(mirrored, tile(face_own, own), halo_tile(0, 2, 0))
        else:
            face = halo_tile(0, 2, jnp.where(mirrored, PASSES - row, row))
        set_tile(face_tail, 1 + row, face)
    for row in range(PASSES):
        total = 1.0 - tile(east_tail, row) - tile(west_tail, row)
        set_tile(center_tail, row, total - tile(face_tail, row + 1) - tile(face_tail, row))
    if halos == 2:
        for row in range(PASSES):
            at = 1 + PASSES + row
            east, face = halo_tile(1, 1, row), halo_tile(1, 2, row)
            below = halo_tile(1, 2, row + 1) if row + 1 < PASSES else tile(face_own, 0)
            west = west_of(east)
            for ref, value in zip(tail_refs, (1.0 - east - west - below - face, east, west, face)):
                set_tile(ref, at, value)


def coefficient_reader(own_refs, tail_refs, own):
    def coefficient(kind, row):
        if row < 0:
            return tile(tail_refs[kind], 1 + 2 * PASSES + row)
        return tile(own_refs[kind], row) if row < own - 1 else tile(tail_refs[kind], row - own + 1)

    return coefficient


def top_coefficient(halos, own_refs):
    return None if halos == 1 else jnp.where(lax.axis_index("row") == 0, 0.0, tile(own_refs[3], 0))


def forward_body(halos, rows_ref, saved_ref, *refs):
    own_refs, halo_refs, refs = refs[:4], refs[4 : 4 + halos], refs[4 + halos :]
    if halos == 1:
        composed_own, _, composed_tail, *refs = refs
        chunk_refs, columns_ref, sorted_ref, tail_refs = refs[:-6], refs[-6], refs[-5], refs[-4:]
        size = chunk_refs[0].shape[0]
        chunk_refs = [*chunk_refs, columns_ref.at[pl.ds(columns_ref.shape[0] - size, size), :]]
    else:
        tail_refs, chunk_refs, sorted_ref = refs[:4], refs[4:-1], refs[-1]
    own = rows_ref.shape[0] // TILE
    lev_at = lax.axis_index("lev")
    mirrored = is_mirrored(halos)
    finish_coefficients(halos, halo_refs, own_refs, tail_refs, own)
    halo_rows = [{own + row: halo_refs[0][block(pick(mirrored, PASSES, row), 1), :] for row in range(PASSES)}]
    coefficient = coefficient_reader(own_refs, tail_refs, own)
    if halos == 1:
        compose(coefficient, composed_rows(own)[1], composed_tail)
        done = double_wedge(halo_rows[0], own, saved_ref, (composed_own, composed_tail))
    else:
        halo_rows.append({row - PASSES: tile(halo_refs[1], row) for row in range(PASSES)})
        top = top_coefficient(halos, own_refs)
        done = wedge_passes(halos, halo_rows, own, saved_ref, coefficient, top)
    for row in range(own):
        value = done[row] if row in done else tile(rows_ref, row)
        sorted_ref[block(pick(mirrored, own, row), 1), :] = value
    part = own // len(chunk_refs)
    for step, chunk_ref in enumerate(reversed(chunk_refs)):
        chunk_ref[...] = sorted_ref[block(lax.bitwise_xor(lev_at, step) * part, part), :]


def matrix_terms(groups):
    return [
        (group, other, cross)
        for group in range(groups)
        for other in range(max(0, group - 2), min(groups, group + 3))
        for cross in range(2)
        if abs(group - other) < 2 or cross
    ]


def swap_levels(value, sublane):
    return jnp.where(sublane % HELD == 0, pltpu.roll(value, TILE - 1, 0), pltpu.roll(value, 1, 0))


def columns_body(members_ref, innovation_ref, huber_ref, columns_out, levels_ref):
    count, levels, cells = members_ref.shape
    groups, lon = levels // HELD, HALVES * LANES
    rows, packed = cells // lon, levels // FIELDS
    for member in range(count):
        for row in range(rows):
            for half in range(HALVES):
                lanes = slice(row * lon + half * LANES, row * lon + (half + 1) * LANES)
                start = ((member * rows + row) * HALVES + half) * levels
                levels_ref[start : start + levels, :] = members_ref[member, :, lanes].astype(jnp.float32)
                for level in range(HELD):
                    at = half * FIELDS + member * HELD + level
                    spread(columns_out, row * groups, at, levels_ref[pl.ds(start + level, groups, stride=HELD), :])
    for row in range(rows):
        for half in range(HALVES):
            lanes = slice(row * lon + half * LANES, row * lon + (half + 1) * LANES)
            for pack in range(packed):
                source = slice(pack * FIELDS, (pack + 1) * FIELDS)
                start = (rows * groups + row * packed + pack) * TILE + half * FIELDS
                columns_out[start : start + FIELDS, :] = innovation_ref[source, lanes]
                start = start + rows * packed * TILE
                columns_out[start : start + FIELDS, :] = huber_ref[source, lanes].astype(jnp.float32)


def matrix_body(band_ref, group_ref, matrix_out, transposed_out):
    levels = band_ref.shape[1]
    groups = levels // HELD
    sublane = places()

    def entry(level, other):
        offset = other - level + REACH
        if not 0 <= offset < 2 * REACH + 1:
            return jnp.float32(0.0)
        value = band_ref[offset, level] + jnp.float32(1.0 if offset == REACH else 0.0)
        return jnp.where(group_ref[level] == group_ref[other], value, jnp.float32(0.0))

    for slot, (group, other, cross) in enumerate(matrix_terms(groups)):
        pairs = [(group * HELD + level, other * HELD + (level ^ cross)) for level in range(HELD)]
        even, odd = (entry(a, b) for a, b in pairs)
        set_tile(matrix_out, slot, jnp.where(sublane % HELD == 0, even, odd))
        even, odd = (entry(b, a) for a, b in pairs)
        set_tile(transposed_out, slot, jnp.where(sublane % HELD == 0, even, odd))


def apply_matrix(matrix_ref, values, sublane):
    crossed = [swap_levels(value, sublane) for value in values]
    totals = [None] * len(values)
    for slot, (group, other, cross) in enumerate(matrix_terms(len(values))):
        term = tile(matrix_ref, slot) * (crossed if cross else values)[other]
        totals[group] = term if totals[group] is None else totals[group] + term
    return totals


def filter_body(chunks, *refs):
    *chunk_refs, members_ref, matrix_ref, partial_ref, columns = refs
    size = chunk_refs[0].shape[0]
    if len(chunk_refs) < chunks:
        chunk_refs.append(members_ref.at[pl.ds(members_ref.shape[0] - size, size), :])
    rows = size // TILE
    lev_at = lax.axis_index("lev")
    sublane = places()
    first_member = sublane % FIELDS < HELD
    for step, chunk_ref in enumerate(reversed(chunk_refs)):
        columns[block(lax.bitwise_xor(lev_at, step) * rows, rows), :] = chunk_ref[...]
    for row in range(rows):
        filtered = apply_matrix(matrix_ref, [tile(columns, group * rows + row) for group in range(chunks)], sublane)
        terms = [tile(members_ref, row * chunks + group) * value for group, value in enumerate(filtered)]
        for pack in range(chunks // 2):
            lower, upper = terms[2 * pack], terms[2 * pack + 1]
            total = jnp.where(first_member, lower, upper)
            total = total + jnp.where(first_member, pltpu.roll(lower, TILE - HELD, 0), pltpu.roll(upper, HELD, 0))
            set_tile(partial_ref, row * (chunks // 2) + pack, total)


def lift_body(chunks, parts, *refs):
    part_refs, refs = refs[:parts], refs[parts:]
    columns_ref, transposed_ref, refs = refs[0], refs[1], refs[2:]
    chunk_refs, (weighted_ref, sorted_ref) = refs[:chunks], refs[chunks:]
    rows = chunk_refs[0].shape[0] // TILE
    lev_at = lax.axis_index("lev")
    sublane = places()
    first_member = sublane % FIELDS < HELD
    increment = part_refs[0][...]
    for part_ref in part_refs[1:]:
        increment = increment + part_ref[...]
    start, size = rows * chunks * TILE, weighted_ref.shape[0]
    residual = increment - columns_ref[start : start + size, :]
    scale = HUBER / jnp.maximum(jnp.abs(residual), HUBER)
    weighted_ref[...] = jnp.where(columns_ref[start + size : start + 2 * size, :] == 1.0, scale, 1.0) * residual
    for row in range(rows):
        adjoint = []
        for pack in range(chunks // 2):
            weighted = tile(weighted_ref, row * (chunks // 2) + pack)
            lower = jnp.where(first_member, weighted, pltpu.roll(weighted, HELD, 0))
            upper = jnp.where(first_member, pltpu.roll(weighted, TILE - HELD, 0), weighted)
            for value in (lower, upper):
                adjoint.append(value * tile(columns_ref, row * chunks + len(adjoint)))
        for group, value in enumerate(apply_matrix(transposed_ref, adjoint, sublane)):
            set_tile(sorted_ref, group * rows + row, value)
    for step, chunk_ref in enumerate(reversed(chunk_refs)):
        chunk_ref[...] = sorted_ref[block(lax.bitwise_xor(lev_at, step) * rows, rows), :]


def gather_body(halos, chunks, *refs):
    chunk_refs, field_ref, send_refs, sorted_ref = refs[:chunks], refs[chunks], refs[chunks + 1 : -1], refs[-1]
    lev_at = lax.axis_index("lev")
    mirrored = is_mirrored(halos)
    rows = chunk_refs[0].shape[0] // TILE
    own = rows * chunks
    for step, chunk_ref in enumerate(reversed(chunk_refs)):
        sorted_ref[block(lax.bitwise_xor(lev_at, step) * rows, rows), :] = chunk_ref[...]
    for row in range(own):
        set_tile(field_ref, row, sorted_ref[block(pick(mirrored, own, row), 1), :])
    for row in range(PASSES):
        if halos == 1:
            set_tile(send_refs[0], row, tile(field_ref, own - 1 - row))
        else:
            set_tile(send_refs[0], row, tile(field_ref, row))
            set_tile(send_refs[1], row, tile(field_ref, own - PASSES + row))


def to_fields(planes_ref, fields_ref, rows):
    for field in range(FIELDS):
        member, level = divmod(field, HELD)
        for half, lanes in halves():
            fields_ref[member, level, :, lanes] = planes_ref[pl.ds(half * FIELDS + field, rows, stride=TILE), :]


def interior_body(halos, field_ref, control_ref, *refs):
    own_refs, (fields_out, saved_out, result_ref) = refs[:4], refs[4:]
    own = field_ref.shape[0] // TILE
    mirrored = is_mirrored(halos)
    done = interior_passes(halos, field_ref, own_refs, saved_out, halos == 1)
    for row in range(own):
        value = done[row] + tile(control_ref, row) if row in done else jnp.zeros((TILE, LANES), jnp.float32)
        result_ref[block(pick(mirrored, own, row), 1), :] = value
    to_fields(result_ref, fields_out, own)


def backward_body(halos, control_ref, fields_ref, saved_ref, *refs):
    halo_refs, refs = refs[:halos], refs[halos:]
    coefficient_refs, refs = (refs[:2], refs[2:]) if halos == 1 else (refs[:8], refs[8:])
    gradient_hbm, refs = refs[0], refs[1:]
    result_refs, edge_refs, semaphores = refs[:halos], refs[halos : 2 * halos], refs[-1]
    own = fields_ref.shape[2]
    mirrored = is_mirrored(halos)
    if halos == 1:
        spans = [(PASSES * mirrored.astype(jnp.int32), own - PASSES)]
        spans.append((jnp.where(mirrored, 0, own - PASSES), PASSES))
    else:
        spans = [(PASSES, own - 2 * PASSES), (own - PASSES, PASSES), (0, PASSES)]
    copies = []

    def send(source_ref, source_start, start, rows):
        copy = pltpu.make_async_copy(
            source_ref.at[:, :, pl.ds(source_start, rows), :],
            gradient_hbm.at[:, :, pl.ds(start, rows), :],
            semaphores.at[len(copies)],
        )
        copy.start()
        copies.append(copy)

    start = pl.multiple_of(spans[0][0], TILE)
    send(fields_ref, start, start, spans[0][1])
    halo_rows = [{own + row: tile(halo_refs[0], row) for row in range(PASSES)}]
    if halos == 1:
        done = double_wedge(halo_rows[0], own, saved_ref, coefficient_refs)
    else:
        halo_rows.append({row - PASSES: tile(halo_refs[1], row) for row in range(PASSES)})
        own_refs, tail_refs = coefficient_refs[:4], coefficient_refs[4:]
        coefficient = coefficient_reader(own_refs, tail_refs, own)
        top = top_coefficient(halos, own_refs)
        done = wedge_passes(halos, halo_rows, own, saved_ref, coefficient, top)
    for side in range(halos):
        for row in range(PASSES):
            value = done[own - PASSES + row] + tile(control_ref, own - PASSES + row) if side == 0 else done[row] + tile(control_ref, row)
            result_refs[side][block(pick(mirrored, PASSES, row), 1), :] = value
        to_fields(result_refs[side], edge_refs[side], PASSES)
        send(edge_refs[side], 0, pl.multiple_of(spans[1 + side][0], TILE), PASSES)
    for copy in copies:
        copy.wait()


def per_device(control, members, east_coef, south_coef, innovation, huber_class, band, level_group_index):
    count, held, own, lon = control.shape
    levels, cells = members.shape[1:]
    chunks, parts, row_count = (lax.axis_size(axis) for axis in ("lev", "mem", "row"))
    assert (count * held, held, lon) == (FIELDS, HELD, HALVES * LANES)
    part = own // chunks
    halos = 1 if row_count == 2 else 2
    tail = 1 + halos * PASSES
    terms = len(matrix_terms(chunks))
    packed = part * levels // FIELDS
    crossed = row_count == 2

    control_near, east_near, south_near, *edges = call(
        pack_body,
        [pltpu.VMEM(x.shape, x.dtype) for x in (control, east_coef, south_coef)] + [planes(3 * PASSES)] * halos,
        remote(control, east_coef, south_coef),
        [pltpu.SemaphoreType.DMA((FIELDS + 2 * HELD,))],
        specs=[HBM] * 3,
    )
    halo = swap_edges(edges, "row")
    kept = halos * PASSES * 2
    near, far = ([planes(len(rows) * POINTS)] if halos == 1 else [] for rows in composed_rows(own))
    prepared = call(
        functools.partial(prepare_body, halos),
        [planes(own)] * 3 + [planes(own + 1), planes(own), planes(kept), planes(own)] + near,
        resident(control_near, east_near, south_near),
        [planes(own)] * 2,
    )
    own_stencil, (done_rows, saved, control_planes), composed = prepared[:4], prepared[4:7], prepared[7:]
    columns_planes = planes(part * chunks + 2 * packed + (part if crossed else 0))
    (columns,) = call(
        columns_body, [columns_planes], [members, innovation, huber_class], [planes(part * chunks)]
    )
    matrix, transposed = call(
        matrix_body, [planes(terms)] * 2, [band, level_group_index], specs=[SMEM, SMEM]
    )
    tail_planes = [planes(tail)] * 4
    first_outs = far or tail_planes
    operands = [done_rows, saved, *own_stencil, *halo, *composed]
    passed, sent = ([columns], chunks - 1) if crossed else ([], chunks)
    results = call(
        functools.partial(forward_body, halos),
        first_outs + [planes(part)] * sent + [columns_planes] * len(passed),
        resident(*operands, *passed),
        [planes(own)] + (tail_planes if halos == 1 else []),
        aliases={len(operands): len(first_outs) + sent} if crossed else None,
    )
    if crossed:
        *results, columns = results
        columns = lax.ppermute(columns, "row", [(0, 1), (1, 0)])
    last_coefs = [*composed, *results[:1]] if halos == 1 else [*own_stencil, *results[:4]]
    smoothed = results[len(first_outs) :]
    kept_back = [None] * (chunks - sent)
    received = exchange([*kept_back, *smoothed[::-1]], "lev", crossed)[chunks - sent :]
    (partial,) = call(
        functools.partial(filter_body, chunks),
        [planes(packed)],
        resident(*received[::-1], columns, matrix),
        [planes(part * chunks)],
    )
    partials = collect(partial, "mem")
    lifted = call(
        functools.partial(lift_body, chunks, parts),
        [planes(part)] * chunks,
        resident(*partials, columns, transposed),
        [planes(packed), planes(part * chunks)],
    )
    returned = exchange(lifted[::-1], "lev", crossed)
    gathered, *edges = call(
        functools.partial(gather_body, halos, chunks),
        [planes(own)] + [planes(PASSES)] * halos,
        resident(*returned[::-1]),
        [planes(own)],
    )
    halo = swap_edges(edges, "row")
    early, saved = call(
        functools.partial(interior_body, halos),
        [pltpu.VMEM(control.shape, jnp.float32), planes(kept)],
        resident(gathered, control_planes, *own_stencil),
        [planes(own)],
    )
    (gradient,) = call(
        functools.partial(backward_body, halos),
        [jax.ShapeDtypeStruct(control.shape, jnp.float32)],
        resident(control_planes, early, saved, *halo, *last_coefs),
        [planes(PASSES)] * halos
        + [pltpu.VMEM((count, held, PASSES, lon), jnp.float32)] * halos
        + [pltpu.SemaphoreType.DMA((1 + halos,))],
        out_specs=[HBM],
    )
    return gradient


def solution(mesh):
    placed = (
        P("mem", "lev", "row", None),
        P("mem", None, ("row", "lev")),
        P("lev", "row", None),
        P("lev", "row", None),
        P(None, ("row", "lev")),
        P(None, ("row", "lev")),
        P(),
        P(),
    )
    return jax.shard_map(
        per_device,
        mesh=mesh,
        in_specs=placed,
        out_specs=P("mem", "lev", "row", None),
        check_vma=False,
    )
```

```python
import functools

import jax
import jax.numpy as jnp
from jax import lax
from jax.experimental import pallas as pl
from jax.experimental.pallas import tpu as pltpu
from jax.sharding import PartitionSpec as P

PASSES = 8
HUBER = 1.0
REACH = 3
POINTS = 13
LANES = 128
TILE = 8
HALVES = 2
HELD = 2
FIELDS = 4

VMEM = pl.BlockSpec(memory_space=pltpu.VMEM)
SMEM = pl.BlockSpec(memory_space=pltpu.SMEM)
HBM = pl.BlockSpec(memory_space=pltpu.HBM)


def planes(count):
    return pltpu.VMEM((count * TILE, LANES), jnp.float32)


def call(body, outs, operands, scratch=(), specs=None, out_specs=None, flops=0, aliases=None):
    total = sum(op.size * op.dtype.itemsize for op in operands)
    return pl.pallas_call(
        body,
        out_shape=outs,
        in_specs=specs or [VMEM] * len(operands),
        out_specs=out_specs or [VMEM] * len(outs),
        scratch_shapes=list(scratch),
        input_output_aliases=aliases or {},
        compiler_params=pltpu.CompilerParams(vmem_limit_bytes=32 * 1024 * 1024),
        cost_estimate=pl.CostEstimate(flops=flops, bytes_accessed=2 * total, transcendentals=0),
    )(*operands)


def resident(*arrays):
    return [pltpu.with_memory_space_constraint(array, pltpu.VMEM) for array in arrays]


def remote(*arrays):
    return [pltpu.with_memory_space_constraint(array, pltpu.HBM) for array in arrays]


def exchange(chunks, axis, crossed):
    count = len(chunks)
    received = list(chunks)
    for step in reversed(range(count)):
        if chunks[step] is None:
            continue
        if crossed:
            pairs = [(2 * i + row, 2 * (i ^ step) + 1 - row) for i in range(count) for row in range(2)]
            received[step] = lax.ppermute(chunks[step], (axis, "row"), pairs)
        elif step:
            received[step] = lax.ppermute(chunks[step], axis, [(i, i ^ step) for i in range(count)])
    return received


def collect(array, axis):
    count, rows = lax.axis_size(axis), lax.axis_size("row")
    shifts = [count - 1, *range(1, count - 1)]
    ring = [i ^ (i >> 1) for i in range(count)]
    received = [array]
    for step in range(1, count):
        pairs = []
        for place, index in enumerate(ring):
            for row in range(rows):
                target = index ^ (count - step) if row % 2 else ring[(place + shifts[step - 1]) % count]
                pairs.append((index * rows + row, target * rows + row))
        received.append(lax.ppermute(array, (axis, "row"), pairs))
    return received


def swap_edges(edges, axis):
    count = lax.axis_size(axis)
    if len(edges) == 1:
        return [lax.ppermute(edges[0], axis, [(0, 1), (1, 0)])]
    head, tail = edges
    south = lax.ppermute(head, axis, [(i + 1, i) for i in range(count - 1)])
    north = lax.ppermute(tail, axis, [(i, i + 1) for i in range(count - 1)])
    return [south, north]


def tile(ref, row):
    return ref[row * TILE : (row + 1) * TILE, :]


def set_tile(ref, row, value):
    ref[row * TILE : (row + 1) * TILE, :] = value


def block(first_row, rows):
    return pl.ds(pl.multiple_of(first_row * TILE, TILE), rows * TILE)


def spread(ref, row, sublane, values):
    ref[pl.ds(row * TILE + sublane, values.shape[0], stride=TILE), :] = values


def places():
    return lax.broadcasted_iota(jnp.int32, (TILE, LANES), 0)


def east_west(value):
    lane = lax.broadcasted_iota(jnp.int32, (TILE, LANES), 1)
    other = pltpu.roll(value, FIELDS, 0)
    east = pltpu.roll(jnp.where(lane == 0, other, value), LANES - 1, 1)
    west = pltpu.roll(jnp.where(lane == LANES - 1, other, value), 1, 1)
    return east, west


def west_of(value):
    lane = lax.broadcasted_iota(jnp.int32, (TILE, LANES), 1)
    return pltpu.roll(jnp.where(lane == LANES - 1, pltpu.roll(value, FIELDS, 0), value), 1, 1)


def halves():
    return [(half, slice(half * LANES, (half + 1) * LANES)) for half in range(HALVES)]


def pack_body(control_hbm, east_hbm, south_hbm, control_ref, east_ref, south_ref, *refs):
    send_refs, semaphores = refs[:-1], refs[-1]
    pieces = [(east_hbm.at[level], east_ref.at[level]) for level in range(HELD)]
    pieces += [(south_hbm.at[level], south_ref.at[level]) for level in range(HELD)]
    for field in range(FIELDS):
        member, level = divmod(field, HELD)
        pieces.append((control_hbm.at[member, level], control_ref.at[member, level]))
    copies = [
        pltpu.make_async_copy(source, target, semaphores.at[index]) for index, (source, target) in enumerate(pieces)
    ]
    for copy in copies:
        copy.start()
    for copy in copies:
        copy.wait()
    own = control_ref.shape[2]
    first = lax.axis_index("row") == 0

    def edges(load):
        head = load(slice(0, 2 * PASSES))[:PASSES].astype(jnp.float32)
        tail = load(slice(own - 2 * PASSES, own))[PASSES:].astype(jnp.float32)
        return [jnp.where(first, tail, head)] if len(send_refs) == 1 else [head, tail]

    for half, lanes in halves():
        for field in range(FIELDS):
            member, level = divmod(field, HELD)
            at = half * FIELDS + field
            values = edges(lambda rows: control_ref[member, level, rows, lanes])
            for send_ref, value in zip(send_refs, values):
                spread(send_ref, 0, at, value)
            for kind, coef_ref in enumerate((east_ref, south_ref)):
                values = edges(lambda rows: coef_ref[level, rows, lanes])
                for send_ref, value in zip(send_refs, values):
                    spread(send_ref, (kind + 1) * PASSES, at, value)


def is_mirrored(halos):
    return halos == 1 and lax.axis_index("row") == 1


def pick(mirrored, count, row):
    return row if mirrored is False else jnp.where(mirrored, count - 1 - row, row)


def stencil(values, row, center, east, west, above, below):
    to_east, to_west = east_west(values[row])
    total = center * values[row] + below * values[row + 1]
    if above is not None:
        total = total + above * values[row - 1]
    return total + (east * to_east + west * to_west)


def interior_passes(halos, field_ref, own_refs, saved_ref, double=False):
    center_ref, east_ref, west_ref, face_ref = own_refs
    own = field_ref.shape[0] // TILE
    values = {row: tile(field_ref, row) for row in range(own)}
    for step in range(1, PASSES + 1):
        for side in range(halos):
            kept = (own - 1 - step, own - step) if side == 0 else (step - 1, step)
            if double:
                kept = range(own - 3 - step, own + 1 - step) if step % 2 else ()
            for index, row in enumerate(kept):
                set_tile(saved_ref, (side * PASSES + step - 1) * 2 + index, values[row])
        after = {}
        for row in range(step if halos == 2 else 0, own - step):
            after[row] = stencil(
                values,
                row,
                tile(center_ref, row),
                tile(east_ref, row),
                tile(west_ref, row),
                tile(face_ref, row) if row else None,
                tile(face_ref, row + 1),
            )
        values = after
    return values


def wedge_passes(halos, halo_rows, own, saved_ref, coefficient, top):
    done = {}
    for side in range(halos):
        values = dict(halo_rows[side])
        for step in range(1, PASSES + 1):
            kept = (own - 1 - step, own - step) if side == 0 else (step - 1, step)
            for index, row in enumerate(kept):
                values[row] = tile(saved_ref, (side * PASSES + step - 1) * 2 + index)
            after = {}
            for row in range(own - step, own + PASSES - step) if side == 0 else range(step - PASSES, step):
                center, east, west, above = (coefficient(kind, row) for kind in range(4))
                after[row] = stencil(values, row, center, east, west, top if row == 0 else above, coefficient(3, row + 1))
            values = after
        done.update(values)
    return done


def shifted(value, distance):
    lane = lax.broadcasted_iota(jnp.int32, (TILE, LANES), 1)
    other = pltpu.roll(value, FIELDS, 0)
    east = pltpu.roll(jnp.where(lane < distance, other, value), LANES - distance, 1)
    west = pltpu.roll(jnp.where(lane >= LANES - distance, other, value), distance, 1)
    return east, west


def compose(coefficient, rows, composed_out):
    for index, row in enumerate(rows):
        center, east, west, above = (coefficient(kind, row) for kind in range(4))
        below = coefficient(3, row + 1)
        (center_e, center_w), (east_e, east_w), (west_e, west_w), (below_e, below_w), (above_e, above_w) = (
            shifted(value, 1) for value in (center, east, west, below, above)
        )
        tiles = (
            center * center + east * west_e + west * east_w + below * below + above * above,
            east * (center + center_e),
            west * (center + center_w),
            east * east_e,
            west * west_w,
            below * (center + coefficient(0, row + 1)),
            east * below_e + below * coefficient(1, row + 1),
            west * below_w + below * coefficient(2, row + 1),
            above * (center + coefficient(0, row - 1)),
            east * above_e + above * coefficient(1, row - 1),
            west * above_w + above * coefficient(2, row - 1),
            below * coefficient(3, row + 2),
            above * coefficient(3, row - 1),
        )
        for place, value in enumerate(tiles):
            set_tile(composed_out, index * POINTS + place, value)


def composed_rows(own):
    return range(own - PASSES, own - 2), range(own - 2, own + PASSES - 2)


def double_wedge(values, own, saved_ref, composed_refs):
    for step in range(1, PASSES // 2 + 1):
        first = own - 2 * step
        for index in range(4):
            values[first - 2 + index] = tile(saved_ref, (step - 1) * 4 + index)
        near = {row: shifted(values[row], 1) for row in range(first - 1, first + PASSES + 1)}
        after = {}
        for row in range(first, first + PASSES):
            def coefficient(place):
                part = int(row >= own - 2)
                return tile(composed_refs[part], (row - composed_rows(own)[part][0]) * POINTS + place)

            east, west = shifted(values[row], 2)
            total = coefficient(0) * values[row] + coefficient(5) * values[row + 1]
            total = total + (coefficient(8) * values[row - 1] + coefficient(11) * values[row + 2])
            total = total + coefficient(12) * values[row - 2]
            sides = coefficient(1) * near[row][0] + coefficient(2) * near[row][1]
            lower = coefficient(6) * near[row + 1][0] + coefficient(7) * near[row + 1][1]
            upper = coefficient(9) * near[row - 1][0] + coefficient(10) * near[row - 1][1]
            far = coefficient(3) * east + coefficient(4) * west
            after[row] = (total + sides) + ((lower + upper) + far)
        values = after
    return values


def prepare_body(halos, control_ref, east_ref, south_ref, *refs):
    own_refs, (rows_out, saved_out, field_ref), refs = refs[:4], refs[4:7], refs[7:]
    raw_east, raw_face = refs[-2:]
    center_out, east_out, west_out, face_out = own_refs
    own = control_ref.shape[2]
    mirrored = is_mirrored(halos)
    for half, lanes in halves():
        for field in range(FIELDS):
            member, level = divmod(field, HELD)
            at = half * FIELDS + field
            spread(rows_out, 0, at, control_ref[member, level, :, lanes].astype(jnp.float32))
            spread(raw_east, 0, at, east_ref[level, :, lanes])
            spread(raw_face, 0, at, south_ref[level, :, lanes])
    for row in range(own):
        source = pick(mirrored, own, row)
        set_tile(field_ref, row, rows_out[block(source, 1), :])
        east = raw_east[block(source, 1), :]
        set_tile(east_out, row, east)
        set_tile(west_out, row, west_of(east))
        if row == 0:
            face = tile(raw_face, 0)
            face = face if mirrored is False else jnp.where(mirrored, 0.0, face)
        else:
            face = raw_face[block(row if mirrored is False else jnp.where(mirrored, own - row, row), 1), :]
        set_tile(face_out, row, face)
    set_tile(face_out, own, tile(raw_face, 0))
    for row in range(own - 1):
        total = 1.0 - tile(east_out, row) - tile(west_out, row)
        set_tile(center_out, row, total - tile(face_out, row + 1) - tile(face_out, row))
    for row, value in interior_passes(halos, field_ref, own_refs, saved_out, halos == 1).items():
        set_tile(rows_out, row, value)
    if halos == 1:
        compose(lambda kind, row: tile(own_refs[kind], row), composed_rows(own)[0], refs[0])


def finish_coefficients(halos, halo_refs, own_refs, tail_refs, own):
    _, east_own, west_own, face_own = own_refs
    center_tail, east_tail, west_tail, face_tail = tail_refs
    mirrored = is_mirrored(halos)

    def halo_tile(side, kind, row):
        return halo_refs[side][block(kind * PASSES + row, 1), :]

    set_tile(east_tail, 0, tile(east_own, own - 1))
    set_tile(west_tail, 0, tile(west_own, own - 1))
    set_tile(face_tail, 0, tile(face_own, own - 1))
    for row in range(PASSES):
        east = halo_tile(0, 1, pick(mirrored, PASSES, row))
        set_tile(east_tail, 1 + row, east)
        set_tile(west_tail, 1 + row, west_of(east))
        if mirrored is False:
            face = halo_tile(0, 2, row)
        elif row == 0:
            face = jnp.where(mirrored, tile(face_own, own), halo_tile(0, 2, 0))
        else:
            face = halo_tile(0, 2, jnp.where(mirrored, PASSES - row, row))
        set_tile(face_tail, 1 + row, face)
    for row in range(PASSES):
        total = 1.0 - tile(east_tail, row) - tile(west_tail, row)
        set_tile(center_tail, row, total - tile(face_tail, row + 1) - tile(face_tail, row))
    if halos == 2:
        for row in range(PASSES):
            at = 1 + PASSES + row
            east, face = halo_tile(1, 1, row), halo_tile(1, 2, row)
            below = halo_tile(1, 2, row + 1) if row + 1 < PASSES else tile(face_own, 0)
            west = west_of(east)
            for ref, value in zip(tail_refs, (1.0 - east - west - below - face, east, west, face)):
                set_tile(ref, at, value)


def coefficient_reader(own_refs, tail_refs, own):
    def coefficient(kind, row):
        if row < 0:
            return tile(tail_refs[kind], 1 + 2 * PASSES + row)
        return tile(own_refs[kind], row) if row < own - 1 else tile(tail_refs[kind], row - own + 1)

    return coefficient


def top_coefficient(halos, own_refs):
    return None if halos == 1 else jnp.where(lax.axis_index("row") == 0, 0.0, tile(own_refs[3], 0))


def forward_body(halos, rows_ref, saved_ref, *refs):
    own_refs, halo_refs, refs = refs[:4], refs[4 : 4 + halos], refs[4 + halos :]
    if halos == 1:
        composed_own, _, composed_tail, *refs = refs
        chunk_refs, columns_ref, sorted_ref, tail_refs = refs[:-6], refs[-6], refs[-5], refs[-4:]
        size = chunk_refs[0].shape[0]
        chunk_refs = [*chunk_refs, columns_ref.at[pl.ds(columns_ref.shape[0] - size, size), :]]
    else:
        tail_refs, chunk_refs, sorted_ref = refs[:4], refs[4:-1], refs[-1]
    own = rows_ref.shape[0] // TILE
    lev_at = lax.axis_index("lev")
    mirrored = is_mirrored(halos)
    finish_coefficients(halos, halo_refs, own_refs, tail_refs, own)
    halo_rows = [{own + row: halo_refs[0][block(pick(mirrored, PASSES, row), 1), :] for row in range(PASSES)}]
    coefficient = coefficient_reader(own_refs, tail_refs, own)
    if halos == 1:
        compose(coefficient, composed_rows(own)[1], composed_tail)
        done = double_wedge(halo_rows[0], own, saved_ref, (composed_own, composed_tail))
    else:
        halo_rows.append({row - PASSES: tile(halo_refs[1], row) for row in range(PASSES)})
        top = top_coefficient(halos, own_refs)
        done = wedge_passes(halos, halo_rows, own, saved_ref, coefficient, top)
    for row in range(own):
        value = done[row] if row in done else tile(rows_ref, row)
        sorted_ref[block(pick(mirrored, own, row), 1), :] = value
    part = own // len(chunk_refs)
    for step, chunk_ref in enumerate(reversed(chunk_refs)):
        chunk_ref[...] = sorted_ref[block(lax.bitwise_xor(lev_at, step) * part, part), :]


def matrix_terms(groups):
    return [
        (group, other, cross)
        for group in range(groups)
        for other in range(max(0, group - 2), min(groups, group + 3))
        for cross in range(2)
        if abs(group - other) < 2 or cross
    ]


def swap_levels(value, sublane):
    return jnp.where(sublane % HELD == 0, pltpu.roll(value, TILE - 1, 0), pltpu.roll(value, 1, 0))


def columns_body(members_ref, innovation_ref, huber_ref, columns_out, levels_ref):
    count, levels, cells = members_ref.shape
    groups, lon = levels // HELD, HALVES * LANES
    rows, packed = cells // lon, levels // FIELDS
    for member in range(count):
        for row in range(rows):
            for half in range(HALVES):
                lanes = slice(row * lon + half * LANES, row * lon + (half + 1) * LANES)
                start = ((member * rows + row) * HALVES + half) * levels
                levels_ref[start : start + levels, :] = members_ref[member, :, lanes].astype(jnp.float32)
                for level in range(HELD):
                    at = half * FIELDS + member * HELD + level
                    spread(columns_out, row * groups, at, levels_ref[pl.ds(start + level, groups, stride=HELD), :])
    for row in range(rows):
        for half in range(HALVES):
            lanes = slice(row * lon + half * LANES, row * lon + (half + 1) * LANES)
            for pack in range(packed):
                source = slice(pack * FIELDS, (pack + 1) * FIELDS)
                start = (rows * groups + row * packed + pack) * TILE + half * FIELDS
                columns_out[start : start + FIELDS, :] = innovation_ref[source, lanes]
                start = start + rows * packed * TILE
                columns_out[start : start + FIELDS, :] = huber_ref[source, lanes].astype(jnp.float32)


def matrix_body(band_ref, group_ref, matrix_out, transposed_out):
    levels = band_ref.shape[1]
    groups = levels // HELD
    sublane = places()

    def entry(level, other):
        offset = other - level + REACH
        if not 0 <= offset < 2 * REACH + 1:
            return jnp.float32(0.0)
        value = band_ref[offset, level] + jnp.float32(1.0 if offset == REACH else 0.0)
        return jnp.where(group_ref[level] == group_ref[other], value, jnp.float32(0.0))

    for slot, (group, other, cross) in enumerate(matrix_terms(groups)):
        pairs = [(group * HELD + level, other * HELD + (level ^ cross)) for level in range(HELD)]
        even, odd = (entry(a, b) for a, b in pairs)
        set_tile(matrix_out, slot, jnp.where(sublane % HELD == 0, even, odd))
        even, odd = (entry(b, a) for a, b in pairs)
        set_tile(transposed_out, slot, jnp.where(sublane % HELD == 0, even, odd))


def apply_matrix(matrix_ref, values, sublane):
    crossed = [swap_levels(value, sublane) for value in values]
    totals = [None] * len(values)
    for slot, (group, other, cross) in enumerate(matrix_terms(len(values))):
        term = tile(matrix_ref, slot) * (crossed if cross else values)[other]
        totals[group] = term if totals[group] is None else totals[group] + term
    return totals


def filter_body(chunks, *refs):
    *chunk_refs, members_ref, matrix_ref, partial_ref, columns = refs
    size = chunk_refs[0].shape[0]
    if len(chunk_refs) < chunks:
        chunk_refs.append(members_ref.at[pl.ds(members_ref.shape[0] - size, size), :])
    rows = size // TILE
    lev_at = lax.axis_index("lev")
    sublane = places()
    first_member = sublane % FIELDS < HELD
    for step, chunk_ref in enumerate(reversed(chunk_refs)):
        columns[block(lax.bitwise_xor(lev_at, step) * rows, rows), :] = chunk_ref[...]
    for row in range(rows):
        filtered = apply_matrix(matrix_ref, [tile(columns, group * rows + row) for group in range(chunks)], sublane)
        terms = [tile(members_ref, row * chunks + group) * value for group, value in enumerate(filtered)]
        for pack in range(chunks // 2):
            lower, upper = terms[2 * pack], terms[2 * pack + 1]
            total = jnp.where(first_member, lower, upper)
            total = total + jnp.where(first_member, pltpu.roll(lower, TILE - HELD, 0), pltpu.roll(upper, HELD, 0))
            set_tile(partial_ref, row * (chunks // 2) + pack, total)


def lift_body(chunks, parts, *refs):
    part_refs, refs = refs[:parts], refs[parts:]
    columns_ref, transposed_ref, refs = refs[0], refs[1], refs[2:]
    chunk_refs, (weighted_ref, sorted_ref) = refs[:chunks], refs[chunks:]
    rows = chunk_refs[0].shape[0] // TILE
    lev_at = lax.axis_index("lev")
    sublane = places()
    first_member = sublane % FIELDS < HELD
    increment = part_refs[0][...]
    for part_ref in part_refs[1:]:
        increment = increment + part_ref[...]
    start, size = rows * chunks * TILE, weighted_ref.shape[0]
    residual = increment - columns_ref[start : start + size, :]
    scale = HUBER / jnp.maximum(jnp.abs(residual), HUBER)
    weighted_ref[...] = jnp.where(columns_ref[start + size : start + 2 * size, :] == 1.0, scale, 1.0) * residual
    for row in range(rows):
        adjoint = []
        for pack in range(chunks // 2):
            weighted = tile(weighted_ref, row * (chunks // 2) + pack)
            lower = jnp.where(first_member, weighted, pltpu.roll(weighted, HELD, 0))
            upper = jnp.where(first_member, pltpu.roll(weighted, TILE - HELD, 0), weighted)
            for value in (lower, upper):
                adjoint.append(value * tile(columns_ref, row * chunks + len(adjoint)))
        for group, value in enumerate(apply_matrix(transposed_ref, adjoint, sublane)):
            set_tile(sorted_ref, group * rows + row, value)
    for step, chunk_ref in enumerate(reversed(chunk_refs)):
        chunk_ref[...] = sorted_ref[block(lax.bitwise_xor(lev_at, step) * rows, rows), :]


def gather_body(halos, chunks, *refs):
    chunk_refs, field_ref, send_refs, sorted_ref = refs[:chunks], refs[chunks], refs[chunks + 1 : -1], refs[-1]
    lev_at = lax.axis_index("lev")
    mirrored = is_mirrored(halos)
    rows = chunk_refs[0].shape[0] // TILE
    own = rows * chunks
    for step, chunk_ref in enumerate(reversed(chunk_refs)):
        sorted_ref[block(lax.bitwise_xor(lev_at, step) * rows, rows), :] = chunk_ref[...]
    for row in range(own):
        set_tile(field_ref, row, sorted_ref[block(pick(mirrored, own, row), 1), :])
    for row in range(PASSES):
        if halos == 1:
            set_tile(send_refs[0], row, tile(field_ref, own - 1 - row))
        else:
            set_tile(send_refs[0], row, tile(field_ref, row))
            set_tile(send_refs[1], row, tile(field_ref, own - PASSES + row))


def to_fields(planes_ref, fields_ref, rows):
    for field in range(FIELDS):
        member, level = divmod(field, HELD)
        for half, lanes in halves():
            fields_ref[member, level, :, lanes] = planes_ref[pl.ds(half * FIELDS + field, rows, stride=TILE), :]


def interior_body(halos, field_ref, control_ref, *refs):
    own_refs, (fields_out, saved_out, result_ref) = refs[:4], refs[4:]
    own = field_ref.shape[0] // TILE
    mirrored = is_mirrored(halos)
    done = interior_passes(halos, field_ref, own_refs, saved_out, halos == 1)
    for row in range(own):
        value = done[row] + tile(control_ref, row) if row in done else jnp.zeros((TILE, LANES), jnp.float32)
        result_ref[block(pick(mirrored, own, row), 1), :] = value
    to_fields(result_ref, fields_out, own)


def backward_body(halos, control_ref, fields_ref, saved_ref, *refs):
    halo_refs, refs = refs[:halos], refs[halos:]
    coefficient_refs, refs = (refs[:2], refs[2:]) if halos == 1 else (refs[:8], refs[8:])
    gradient_hbm, refs = refs[0], refs[1:]
    result_refs, edge_refs, semaphores = refs[:halos], refs[halos : 2 * halos], refs[-1]
    own = fields_ref.shape[2]
    mirrored = is_mirrored(halos)
    if halos == 1:
        spans = [(PASSES * mirrored.astype(jnp.int32), own - PASSES)]
        spans.append((jnp.where(mirrored, 0, own - PASSES), PASSES))
    else:
        spans = [(PASSES, own - 2 * PASSES), (own - PASSES, PASSES), (0, PASSES)]
    copies = []

    def send(source_ref, source_start, start, rows):
        copy = pltpu.make_async_copy(
            source_ref.at[:, :, pl.ds(source_start, rows), :],
            gradient_hbm.at[:, :, pl.ds(start, rows), :],
            semaphores.at[len(copies)],
        )
        copy.start()
        copies.append(copy)

    start = pl.multiple_of(spans[0][0], TILE)
    send(fields_ref, start, start, spans[0][1])
    halo_rows = [{own + row: tile(halo_refs[0], row) for row in range(PASSES)}]
    if halos == 1:
        done = double_wedge(halo_rows[0], own, saved_ref, coefficient_refs)
    else:
        halo_rows.append({row - PASSES: tile(halo_refs[1], row) for row in range(PASSES)})
        own_refs, tail_refs = coefficient_refs[:4], coefficient_refs[4:]
        coefficient = coefficient_reader(own_refs, tail_refs, own)
        top = top_coefficient(halos, own_refs)
        done = wedge_passes(halos, halo_rows, own, saved_ref, coefficient, top)
    for side in range(halos):
        for row in range(PASSES):
            value = done[own - PASSES + row] + tile(control_ref, own - PASSES + row) if side == 0 else done[row] + tile(control_ref, row)
            result_refs[side][block(pick(mirrored, PASSES, row), 1), :] = value
        to_fields(result_refs[side], edge_refs[side], PASSES)
        send(edge_refs[side], 0, pl.multiple_of(spans[1 + side][0], TILE), PASSES)
    for copy in copies:
        copy.wait()


def per_device(control, members, east_coef, south_coef, innovation, huber_class, band, level_group_index):
    count, held, own, lon = control.shape
    levels, cells = members.shape[1:]
    chunks, parts, row_count = (lax.axis_size(axis) for axis in ("lev", "mem", "row"))
    assert (count * held, held, lon) == (FIELDS, HELD, HALVES * LANES)
    part = own // chunks
    halos = 1 if row_count == 2 else 2
    tail = 1 + halos * PASSES
    terms = len(matrix_terms(chunks))
    packed = part * levels // FIELDS
    crossed = row_count == 2

    control_near, east_near, south_near, *edges = call(
        pack_body,
        [pltpu.VMEM(x.shape, x.dtype) for x in (control, east_coef, south_coef)] + [planes(3 * PASSES)] * halos,
        remote(control, east_coef, south_coef),
        [pltpu.SemaphoreType.DMA((FIELDS + 2 * HELD,))],
        specs=[HBM] * 3,
    )
    halo = swap_edges(edges, "row")
    kept = halos * PASSES * 2
    near, far = ([planes(len(rows) * POINTS)] if halos == 1 else [] for rows in composed_rows(own))
    prepared = call(
        functools.partial(prepare_body, halos),
        [planes(own)] * 3 + [planes(own + 1), planes(own), planes(kept), planes(own)] + near,
        resident(control_near, east_near, south_near),
        [planes(own)] * 2,
    )
    own_stencil, (done_rows, saved, control_planes), composed = prepared[:4], prepared[4:7], prepared[7:]
    columns_planes = planes(part * chunks + 2 * packed + (part if crossed else 0))
    (columns,) = call(
        columns_body, [columns_planes], [members, innovation, huber_class], [planes(part * chunks)]
    )
    matrix, transposed = call(
        matrix_body, [planes(terms)] * 2, [band, level_group_index], specs=[SMEM, SMEM]
    )
    tail_planes = [planes(tail)] * 4
    first_outs = far or tail_planes
    operands = [done_rows, saved, *own_stencil, *halo, *composed]
    passed, sent = ([columns], chunks - 1) if crossed else ([], chunks)
    results = call(
        functools.partial(forward_body, halos),
        first_outs + [planes(part)] * sent + [columns_planes] * len(passed),
        resident(*operands, *passed),
        [planes(own)] + (tail_planes if halos == 1 else []),
        aliases={len(operands): len(first_outs) + sent} if crossed else None,
    )
    if crossed:
        *results, columns = results
        columns = lax.ppermute(columns, "row", [(0, 1), (1, 0)])
    last_coefs = [*composed, *results[:1]] if halos == 1 else [*own_stencil, *results[:4]]
    smoothed = results[len(first_outs) :]
    kept_back = [None] * (chunks - sent)
    received = exchange([*kept_back, *smoothed[::-1]], "lev", crossed)[chunks - sent :]
    (partial,) = call(
        functools.partial(filter_body, chunks),
        [planes(packed)],
        resident(*received[::-1], columns, matrix),
        [planes(part * chunks)],
    )
    partials = collect(partial, "mem")
    lifted = call(
        functools.partial(lift_body, chunks, parts),
        [planes(part)] * chunks,
        resident(*partials, columns, transposed),
        [planes(packed), planes(part * chunks)],
    )
    returned = exchange(lifted[::-1], "lev", crossed)
    gathered, *edges = call(
        functools.partial(gather_body, halos, chunks),
        [planes(own)] + [planes(PASSES)] * halos,
        resident(*returned[::-1]),
        [planes(own)],
    )
    halo = swap_edges(edges, "row")
    early, saved = call(
        functools.partial(interior_body, halos),
        [pltpu.VMEM(control.shape, jnp.float32), planes(kept)],
        resident(gathered, control_planes, *own_stencil),
        [planes(own)],
    )
    (gradient,) = call(
        functools.partial(backward_body, halos),
        [jax.ShapeDtypeStruct(control.shape, jnp.float32)],
        resident(control_planes, early, saved, *halo, *last_coefs),
        [planes(PASSES)] * halos
        + [pltpu.VMEM((count, held, PASSES, lon), jnp.float32)] * halos
        + [pltpu.SemaphoreType.DMA((1 + halos,))],
        out_specs=[HBM],
    )
    return gradient


def solution(mesh):
    placed = (
        P("mem", "lev", "row", None),
        P("mem", None, ("row", "lev")),
        P("lev", "row", None),
        P("lev", "row", None),
        P(None, ("row", "lev")),
        P(None, ("row", "lev")),
        P(),
        P(),
    )
    return jax.shard_map(
        per_device,
        mesh=mesh,
        in_specs=placed,
        out_specs=P("mem", "lev", "row", None),
        check_vma=False,
    )
```
